32 devices in a mesh: head: 4 (over z), batch: 8 (over y, x, core).
Axes of the slice: x: 2, y: 2, z: 4, core: 2. Of those that a mesh axis runs over, the one named last changes fastest.
Arguments:
- layer_input: bfloat16 [16384, 1024], P('batch', 'head'), may hold values from -6 to 6
- cotangent: bfloat16 [16384, 1024], P('batch', 'head'), may hold values from -6 to 6
- positions: int32 [16384], P('batch'), may hold values from 0 to 2047, as said below
- w_qkv: float32 [1024, 3, 1024], P('batch', None, 'head'), may hold values from -2 to 2
- w_out: float32 [1024, 1024], P('head', 'batch'), may hold values from -2 to 2
- w_up: float32 [1024, 2, 4096], P('batch', None, 'head'), may hold values from -2 to 2
- w_down: float32 [4096, 1024], P('head', 'batch'), may hold values from -2 to 2
- moment_qkv: float32 [1024, 3, 1024], P('batch', None, 'head'), may hold values from -12 to 12
- moment_out: float32 [1024, 1024], P('head', 'batch'), may hold values from -12 to 12
- moment_up: float32 [1024, 2, 4096], P('batch', None, 'head'), may hold values from -12 to 12
- moment_down: float32 [4096, 1024], P('head', 'batch'), may hold values from -12 to 12
- square_qkv: float32 [1024, 3, 1024], P('batch', None, 'head'), may hold values from 16 to 256
- square_out: float32 [1024, 1024], P('head', 'batch'), may hold values from 16 to 256
- square_up: float32 [1024, 2, 4096], P('batch', None, 'head'), may hold values from 8 to 128
- square_down: float32 [4096, 1024], P('head', 'batch'), may hold values from 16 to 256
- s_qk: float32 [1024], P('head'), may hold values from 0.7 to 1.4
- alpha_attn: float32 [1024], replicated, may hold values from 0.15 to 0.6
- alpha_mlp: float32 [1024], replicated, may hold values from 0.15 to 0.6
- s_uv: float32 [2, 4096], P(None, 'head'), may hold values from 0.5 to 2
Outputs:
- hidden: float32 [16384, 1024], P('batch', 'head')
- input_grad: float32 [16384, 1024], P('batch', 'head')
- grad_qkv: float32 [1024, 3, 1024], P('batch', None, 'head')
- grad_out: float32 [1024, 1024], P('head', 'batch')
- grad_up: float32 [1024, 2, 4096], P('batch', None, 'head')
- grad_down: float32 [4096, 1024], P('head', 'batch')
- moment_qkv_new: float32 [1024, 3, 1024], P('batch', None, 'head')
- moment_out_new: float32 [1024, 1024], P('head', 'batch')
- moment_up_new: float32 [1024, 2, 4096], P('batch', None, 'head')
- moment_down_new: float32 [4096, 1024], P('head', 'batch')
- square_qkv_new: float32 [1024, 3, 1024], P('batch', None, 'head')
- square_out_new: float32 [1024, 1024], P('head', 'batch')
- square_up_new: float32 [1024, 2, 4096], P('batch', None, 'head')
- square_down_new: float32 [4096, 1024], P('head', 'batch')
- new_qkv: float32 [1024, 3, 1024], P('batch', None, 'head')
- new_out: float32 [1024, 1024], P('head', 'batch')
- new_up: float32 [1024, 2, 4096], P('batch', None, 'head')
- new_down: float32 [4096, 1024], P('head', 'batch')
- grad_s_qk: float32 [1024], P(('head', 'batch'))
- grad_alpha_attn: float32 [1024], P(('head', 'batch'))
- grad_alpha_mlp: float32 [1024], P(('head', 'batch'))
- grad_s_uv: float32 [2, 4096], P(None, ('head', 'batch'))
The draws below stay inside these ranges and needn't reach their ends.
Inputs may be any that keep to these rules, and one draw needn't show every extreme that they name: Each block of 2048 tokens (one index of batch) holds either one sequence of 2048 tokens or sequences of 1024 tokens that fill it; positions count 0, 1, 2 within each sequence; exactly 4 blocks hold a long sequence.
All inputs are finite; a program needn't handle non-finite values.
Results may differ from the reference program's by a relative error of at most 0.017.
Values may be sent and summed in bfloat16 or wider, within the bound.
No kernel may reach another device: no remote copies, remote signals or barrier semaphores. Data moves between devices by JAX's collectives and lax.ppermute only.
A program may use at most 256 MiB of HBM per device.

```python
import math
import jax
import jax.numpy as jnp
from jax import lax

D = 1024
HEADS = 16
HEAD_DIM = 64
FF = 4096
SHORT = 1024
GROUP_TOK = 2048
GROUPS = 8
LONG_GROUPS = 4
TOKENS = 16384


def draw_positions(key, part):
    order = jax.random.permutation(key, GROUPS)
    is_long = order < LONG_GROUPS
    counter = jnp.arange(GROUP_TOK, dtype=jnp.int32)
    table = jnp.where(is_long[:, None], counter[None, :], counter[None, :] % SHORT)
    return table.reshape(-1).astype(jnp.int32)


def rising_weight(key, shape, along, fan_in):
    count = shape[along]
    place = jnp.arange(count, dtype=jnp.float32) / max(count - 1, 1)
    trend = jnp.exp(place * math.log(8.0))
    jitter = jnp.exp(jax.random.uniform(jax.random.fold_in(key, 11), (count,), jnp.float32, math.log(0.7), math.log(1.4)))
    factor = trend * jitter / 4.1
    layout = [1] * len(shape)
    layout[along] = count
    factor = factor.reshape(layout)
    base = jnp.clip(jax.random.normal(jax.random.fold_in(key, 12), shape, jnp.float32), -6.0, 6.0)
    return (base * float(fan_in) ** (-0.5) * factor).astype(jnp.float32)


def draw_w_qkv(key, part):
    return rising_weight(key, (D, 3, D), 0, D)


def draw_w_out(key, part):
    return rising_weight(key, (D, D), 1, D)


def draw_w_up(key, part):
    return rising_weight(key, (D, 2, FF), 0, D)


def draw_w_down(key, part):
    return rising_weight(key, (FF, D), 1, FF)


def block_levels(stream_key, dims, cuts, smallest, top_value):
    level = 1.0
    for position, shards_of in cuts:
        draws = jax.random.uniform(jax.random.fold_in(jax.random.fold_in(stream_key, 6), position), (shards_of,), jnp.float32, smallest / len(cuts), top_value / len(cuts))
        level = level * jnp.repeat(jnp.exp(draws), dims[position] // shards_of).reshape((-1,) + (1,) * (len(dims) - 1 - position))
    return level


def centred(own_key, dims, deviation, limit, shards=(), held_as=jnp.bfloat16):
    array = deviation * jax.random.normal(own_key, dims, jnp.float32)
    if shards:
        array = array * block_levels(own_key, dims, shards, -0.22, 0.18)
    return jnp.clip(array, -limit, limit).astype(held_as)


def setup_inputs(seed: int = 0) -> dict:
    seeds = jax.random.split(jax.random.key(seed), 20)
    return {
        "layer_input": centred(seeds[0], (TOKENS, D), 1.0, 6.0, ((0, 8), (1, 4))),
        "cotangent": centred(seeds[1], (TOKENS, D), 1.0, 6.0, ((0, 8), (1, 4))),
        "positions": draw_positions(jax.random.fold_in(seeds[19], 71), 0),
        "w_qkv": draw_w_qkv(jax.random.fold_in(seeds[19], 71), 0),
        "w_out": draw_w_out(jax.random.fold_in(seeds[19], 71), 0),
        "w_up": draw_w_up(jax.random.fold_in(seeds[19], 71), 0),
        "w_down": draw_w_down(jax.random.fold_in(seeds[19], 71), 0),
        "moment_qkv": centred(seeds[7], (D, 3, D), (max(1, TOKENS // 8192)), 12.0, ((0, 8), (2, 4)), jnp.float32),
        "moment_out": centred(seeds[8], (D, D), (max(1, TOKENS // 8192)), 12.0, ((0, 4), (1, 8)), jnp.float32),
        "moment_up": centred(seeds[9], (D, 2, FF), (max(1, TOKENS // 8192)), 12.0, ((0, 8), (2, 4)), jnp.float32),
        "moment_down": centred(seeds[10], (FF, D), (max(1, TOKENS // 8192)), 12.0, ((0, 4), (1, 8)), jnp.float32),
        "square_qkv": jnp.clip(jnp.exp(math.log(256.0) - 2.7725887 * jax.random.uniform(seeds[11], (D, 3, D), jnp.float32) ** block_levels(seeds[11], (D, 3, D), ((0, 8), (2, 4)), -0.2, 0.2)), 16.0, 256.0),
        "square_out": jnp.clip(jnp.exp(math.log(256.0) - 2.7725887 * jax.random.uniform(seeds[12], (D, D), jnp.float32) ** block_levels(seeds[12], (D, D), ((0, 4), (1, 8)), -0.2, 0.2)), 16.0, 256.0),
        "square_up": jnp.clip(jnp.exp(math.log(128.0) - 2.7725887 * jax.random.uniform(seeds[13], (D, 2, FF), jnp.float32) ** block_levels(seeds[13], (D, 2, FF), ((0, 8), (2, 4)), -0.2, 0.2)), 8.0, 128.0),
        "square_down": jnp.clip(jnp.exp(math.log(256.0) - 2.7725887 * jax.random.uniform(seeds[14], (FF, D), jnp.float32) ** block_levels(seeds[14], (FF, D), ((0, 4), (1, 8)), -0.2, 0.2)), 16.0, 256.0),
        "s_qk": jnp.clip(jnp.exp(math.log(1.4) - 0.6931472 * jax.random.uniform(seeds[15], (D,), jnp.float32) ** block_levels(seeds[15], (D,), ((0, 4),), -0.2, 0.2)), 0.7, 1.4),
        "alpha_attn": jnp.clip(jax.random.uniform(seeds[16], (D,), jnp.float32, 0.15, 0.6), 0.15, 0.6),
        "alpha_mlp": jnp.clip(jax.random.uniform(seeds[17], (D,), jnp.float32, 0.15, 0.6), 0.15, 0.6),
        "s_uv": jnp.clip(jnp.exp(math.log(2.0) - 1.3862944 * jax.random.uniform(seeds[18], (2, FF), jnp.float32) ** block_levels(seeds[18], (2, FF), ((1, 4),), -0.2, 0.2)), 0.5, 2.0),
    }


@jax.custom_vjp
def low(v):
    return lax.optimization_barrier(v.astype(jnp.bfloat16)).astype(jnp.float32)

@jax.custom_vjp
def low_back(v):
    return v

def low_keep(v):
    return (low(v), None)

def low_pass(kept, grad):
    return (grad,)

def back_keep(v):
    return (v, None)

def back_low(kept, grad):
    return (low(grad),)
low.defvjp(low_keep, low_pass)
low_back.defvjp(back_keep, back_low)
layer_eps = 1e-06
learn_rate = 0.008
beta_one = 0.9
beta_two = 0.95
adam_eps = 1e-08
bias_one = 1.0 - math.exp(100.0 * math.log(0.9))
bias_two = 1.0 - math.exp(100.0 * math.log(0.95))
score_scale = 8.0

def rotate(value, cosine, sine):
    half = value.shape[-1] // 2
    first = value[..., :half]
    second = value[..., half:]
    return jnp.concatenate([first * cosine - second * sine, second * cosine + first * sine], axis=-1)

def angles(places, head_dim):
    freqs = jnp.exp(jnp.arange(head_dim // 2, dtype=jnp.float32) * (-2.0 * math.log(10000.0) / head_dim))
    phase = places.astype(jnp.float32)[:, None] * freqs[None, :]
    return (jnp.cos(phase)[:, None, :], jnp.sin(phase)[:, None, :])

def norm_rows(value):
    return value * lax.rsqrt(lax.optimization_barrier(jnp.mean(value * value, axis=-1, keepdims=True)) + layer_eps)

def unit_heads(value):
    return value * lax.rsqrt(lax.optimization_barrier(jnp.sum(value * value, axis=-1, keepdims=True)) + layer_eps)

def group_layer(weights, tokens, places):
    w_qkv, w_out, w_up, w_down, s_qk, alpha_attn, alpha_mlp, s_uv = weights
    rows = tokens.shape[0]
    high = lax.Precision.HIGHEST
    token_low = low(tokens)
    proj = jnp.einsum('td,dcn->tcn', token_low, low(w_qkv), precision=high)
    cosine, sine = angles(places, HEAD_DIM)
    query = low_back(proj[:, 0]).reshape(rows, HEADS, HEAD_DIM)
    keys = low_back(proj[:, 1]).reshape(rows, HEADS, HEAD_DIM)
    values = low(low_back(proj[:, 2])).reshape(rows, HEADS, HEAD_DIM)
    gain = s_qk.reshape(HEADS, HEAD_DIM)
    query_s = low(unit_heads(rotate(query, cosine, sine)) * gain)
    key_s = low(unit_heads(rotate(keys, cosine, sine)) * gain)
    row_ids = jnp.arange(rows, dtype=jnp.int32)
    first_ids = row_ids - places.astype(jnp.int32)
    allowed = (row_ids[None, :] <= row_ids[:, None]) & (row_ids[None, :] >= first_ids[:, None])
    scores = low_back(score_scale * jnp.einsum('qhd,khd->hqk', query_s, key_s, precision=high))
    scores = jnp.where(allowed[None], scores, -1e+30)
    probs = low(jax.nn.softmax(scores, axis=-1))
    attended = jnp.einsum('hqk,khd->qhd', probs, values, precision=high).reshape(rows, D)
    attended = low(low_back(attended))
    out_sum = low_back(jnp.dot(attended, low(w_out), preferred_element_type=jnp.float32, precision=high))
    attn_hidden = norm_rows(out_sum)
    first_hidden = norm_rows(tokens + alpha_attn * (attn_hidden - tokens))
    first_low = low(first_hidden)
    up_gate = jnp.einsum('td,dcf->tcf', first_low, low(w_up), precision=high)
    up_val = low_back(up_gate[:, 0])
    gate_val = low_back(up_gate[:, 1])
    lifted = s_uv[0] * up_val
    gated = s_uv[1] * gate_val
    act = low(lifted * gated * jax.nn.sigmoid(gated))
    mlp_sum = low_back(jnp.dot(act, low(w_down), preferred_element_type=jnp.float32, precision=high))
    mlp_hidden = norm_rows(mlp_sum)
    return norm_rows(first_hidden + alpha_mlp * (mlp_hidden - first_hidden))

def adam_step(weight, grad, first, second, axis):
    first_new = beta_one * first + (1.0 - beta_one) * grad
    second_new = beta_two * second + (1.0 - beta_two) * grad * grad
    moved = weight - learn_rate * (first_new / bias_one) / (jnp.sqrt(second_new / bias_two) + adam_eps)
    renorm = moved * lax.rsqrt(lax.optimization_barrier(jnp.mean(moved * moved, axis=axis, keepdims=True)) + layer_eps)
    return (first_new, second_new, renorm)

def reference(layer_input, cotangent, positions, w_qkv, w_out, w_up, w_down, moment_qkv, moment_out, moment_up, moment_down, square_qkv, square_out, square_up, square_down, s_qk, alpha_attn, alpha_mlp, s_uv):
    params = (w_qkv, w_out, w_up, w_down, s_qk, alpha_attn, alpha_mlp, s_uv)
    inputs = layer_input.astype(jnp.float32).reshape(GROUPS, GROUP_TOK, D)
    places = positions.astype(jnp.int32).reshape(GROUPS, GROUP_TOK)

    def forward(weights, tokens):

        def one(pair):
            return group_layer(weights, pair[0], pair[1])
        return lax.map(jax.checkpoint(one), (tokens, places))
    hidden, pull = jax.vjp(forward, params, inputs)
    grads, grad_inputs = pull(cotangent.astype(jnp.float32).reshape(GROUPS, GROUP_TOK, D))
    g_qkv, g_out, g_up, g_down, g_sqk, g_attn, g_mlp, g_suv = grads
    m_a, v_a, n_a = adam_step(w_qkv, g_qkv, moment_qkv, square_qkv, 0)
    m_b, v_b, n_b = adam_step(w_out, g_out, moment_out, square_out, 1)
    m_c, v_c, n_c = adam_step(w_up, g_up, moment_up, square_up, 0)
    m_d, v_d, n_d = adam_step(w_down, g_down, moment_down, square_down, 1)
    return (hidden.reshape(TOKENS, D), grad_inputs.reshape(TOKENS, D), g_qkv, g_out, g_up, g_down, m_a, m_b, m_c, m_d, v_a, v_b, v_c, v_d, n_a, n_b, n_c, n_d, g_sqk, g_attn, g_mlp, g_suv)
```

```python
import functools
import math

import jax
import jax.numpy as jnp
from jax import lax
from jax.experimental import pallas as pl
from jax.experimental.pallas import tpu as pltpu
from jax.sharding import PartitionSpec as P

HEAD_DIM = 64
SHORT = 1024

layer_eps = 1e-06
learn_rate = 0.008
beta_one = 0.9
beta_two = 0.95
adam_eps = 1e-08
bias_one = 1.0 - math.exp(100.0 * math.log(0.9))
bias_two = 1.0 - math.exp(100.0 * math.log(0.95))
score_scale = 8.0
LOG2E = math.log2(math.e)
LN2 = math.log(2.0)

bf16 = jnp.bfloat16
f32 = jnp.float32
VMEM_LIMIT = 56 * 1024 * 1024


def dot(a, b):
    return jnp.dot(a, b, preferred_element_type=f32)


def dot_t(a, b):
    return lax.dot_general(a, b, (((1,), (1,)), ((), ())), preferred_element_type=f32)


def t_dot(a, b):
    return lax.dot_general(a, b, (((0,), (0,)), ((), ())), preferred_element_type=f32)


def params():
    return pltpu.CompilerParams(vmem_limit_bytes=VMEM_LIMIT)


def full_spec(shape):
    return pl.BlockSpec(shape, lambda *_: (0,) * len(shape))


def head_sum(value, ones):
    high = value.astype(bf16)
    low = (value - high.astype(f32)).astype(bf16)
    return dot(high, ones) + dot(low, ones)


def swap_halves(value):
    cols = value.shape[-1]
    half = HEAD_DIM // 2
    lane = lax.broadcasted_iota(jnp.int32, value.shape, 1)
    first = (lane % HEAD_DIM) < half
    up = pltpu.roll(value, cols - half, 1)
    down = pltpu.roll(value, half, 1)
    return jnp.where(first, up, down)


def qkv_kernel(z_ref, *refs, parts):
    lefts = refs[: parts - 1]
    own_ref = refs[parts - 1]
    rights = refs[parts : 2 * parts - 1]
    w_ref, cos_ref, sin_ref, gain_ref, ones_ref, x_ref, q_ref, k_ref, v_ref, rq_ref, rk_ref = refs[2 * parts - 1 :]
    cols = v_ref.shape[1]
    z = z_ref[0]
    for s in range(parts):
        value = own_ref[...]
        for at in range(parts):
            if at != s:
                other = lefts[s - at - 1] if s > at else rights[at - s - 1]
                value = jnp.where(z == at, other[...], value)
        x_ref[:, s * cols : (s + 1) * cols] = value
    proj = dot(x_ref[...], w_ref[...])
    cosine = cos_ref[...]
    sine = sin_ref[...]
    ones = ones_ref[...]
    gain = gain_ref[...]
    for c, (out, rho_ref, scale) in enumerate(
        ((q_ref, rq_ref, score_scale * LOG2E), (k_ref, rk_ref, 1.0))
    ):
        part = proj[:, c * cols : (c + 1) * cols]
        rho = lax.rsqrt(head_sum(part * part, ones) + layer_eps)
        rot = part * cosine + swap_halves(part) * sine
        out[...] = (rot * rho * (gain * scale)).astype(bf16)
        rho_ref[...] = rho
    v_ref[...] = proj[:, 2 * cols :].astype(bf16)


def qkv_project(z, lefts, own, rights, w, cosine, sine, gain, ones):
    rows, cols = own.shape
    parts = len(lefts) + 1
    width = parts * cols
    blk = 512
    row = lambda n: pl.BlockSpec((blk, n), lambda i, s: (i, 0))
    return pl.pallas_call(
        functools.partial(qkv_kernel, parts=parts),
        grid_spec=pltpu.PrefetchScalarGridSpec(
            num_scalar_prefetch=1,
            grid=(rows // blk,),
            in_specs=[row(cols)] * (2 * parts - 1)
            + [full_spec((width, 3 * cols)), row(cols), row(cols)]
            + [full_spec((1, cols)), full_spec((cols, cols))],
            out_specs=[row(width)] + [row(cols)] * 5,
        ),
        out_shape=[jax.ShapeDtypeStruct((rows, width), bf16)]
        + [jax.ShapeDtypeStruct((rows, cols), bf16)] * 3
        + [jax.ShapeDtypeStruct((rows, cols), f32)] * 2,
        compiler_params=params(),
    )(z, *lefts, own, *rights, w, cosine, sine, gain, ones)


def head_masks(cols, heads):
    lane = lax.broadcasted_iota(jnp.int32, (1, cols), 1) // HEAD_DIM
    return [(lane == h) for h in range(heads)]


def masked(value, mask):
    return jnp.where(mask, value, jnp.zeros_like(value))


def attn_fwd_kernel(long_ref, q_ref, k_ref, v_ref, y_ref, l_ref, acc, mass, *, heads, blk, sub):
    i = pl.program_id(0)
    cols = q_ref.shape[1]
    masks = head_masks(cols, heads)
    per = SHORT // blk
    low = jnp.where(long_ref[0] != 0, 0, (i // per) * per)
    acc[...] = jnp.zeros_like(acc)
    mass[...] = jnp.zeros_like(mass)

    def lanes(p):
        total = p[:, 0:128]
        for n in range(1, p.shape[1] // 128):
            total = total + p[:, n * 128 : (n + 1) * 128]
        return total

    def body(j, carry):
        start = pl.multiple_of(j * blk, blk)
        keys = k_ref[pl.ds(start, blk), :]
        vals = v_ref[pl.ds(start, blk), :]
        q = q_ref[...]
        total = jnp.zeros(acc.shape, f32)
        for h in range(heads):
            p = jnp.exp2(dot_t(masked(q, masks[h]), keys))
            mass[h] += lanes(p)
            total += dot(p.astype(bf16), masked(vals, masks[h]))
        acc[...] += total
        return carry

    lax.fori_loop(low, i, body, 0)
    start = pl.multiple_of(i * blk, blk)
    causal = lax.broadcasted_iota(jnp.int32, (sub, sub), 0) >= lax.broadcasted_iota(
        jnp.int32, (sub, sub), 1
    )
    for a in range(blk // sub):
        rows = slice(a * sub, (a + 1) * sub)
        q = q_ref[rows, :]
        for b in range(a + 1):
            at = pl.multiple_of(start + b * sub, sub)
            keys = k_ref[pl.ds(at, sub), :]
            vals = v_ref[pl.ds(at, sub), :]
            total = jnp.zeros((sub, cols), f32)
            for h in range(heads):
                p = jnp.exp2(dot_t(masked(q, masks[h]), keys))
                if a == b:
                    p = jnp.where(causal, p, 0.0)
                mass[h, rows, :] += lanes(p)
                total += dot(p.astype(bf16), masked(vals, masks[h]))
            acc[rows, :] += total
    inverse = jnp.zeros(acc.shape, f32)
    logs = jnp.zeros(l_ref.shape, f32)
    lane = lax.broadcasted_iota(jnp.int32, l_ref.shape, 1)
    for h in range(heads):
        column = jnp.sum(mass[h], axis=1, keepdims=True)
        inverse = jnp.where(masks[h], 1.0 / column, inverse)
        logs = jnp.where(lane == h, jnp.log2(column), logs)
    y_ref[...] = (acc[...] * inverse).astype(bf16)
    l_ref[...] = logs


def attn_fwd(is_long, q, k, v):
    rows, cols = q.shape
    heads = cols // HEAD_DIM
    blk, sub = 512, 256
    row = lambda n: pl.BlockSpec((blk, n), lambda i, s: (i, 0))
    return pl.pallas_call(
        functools.partial(attn_fwd_kernel, heads=heads, blk=blk, sub=sub),
        grid_spec=pltpu.PrefetchScalarGridSpec(
            num_scalar_prefetch=1,
            grid=(rows // blk,),
            in_specs=[row(cols), full_spec((rows, cols)), full_spec((rows, cols))],
            out_specs=[row(cols), row(128)],
            scratch_shapes=[pltpu.VMEM((blk, cols), f32), pltpu.VMEM((heads, blk, 128), f32)],
        ),
        out_shape=[
            jax.ShapeDtypeStruct((rows, cols), bf16),
            jax.ShapeDtypeStruct((rows, 128), f32),
        ],
        compiler_params=params(),
    )(is_long, q, k, v)


def attn_bwd_kernel(
    long_ref, q_ref, qk_ref, dy_ref, y_ref, l_ref, k_ref, v_ref, rq_ref, rk_ref, cos_ref, sin_ref, gain_ref,
    ones_ref, dk_in, dv_in, out_ref, dk_out, dv_out, s_ref, acc, dk_acc, dv_acc, stats, *, heads, blk, sub, first, count
):
    step = pl.program_id(0)
    local = count - 1 - step
    i = first + local
    cols = q_ref.shape[1]
    masks = head_masks(cols, heads)
    per = SHORT // blk
    low = jnp.where(long_ref[0] != 0, 0, (i // per) * per)
    ones = ones_ref[...]
    gain = gain_ref[...]

    @pl.when(step == 0)
    def _():
        dk_acc[...] = jnp.zeros_like(dk_acc)
        dv_acc[...] = jnp.zeros_like(dv_acc)
        s_ref[...] = jnp.zeros_like(s_ref)
        if dk_in is not None:
            dk_acc[...] = dk_in[...]
            dv_acc[...] = dv_in[...]

    acc[...] = jnp.zeros_like(acc)
    prod = dy_ref[...].astype(f32) * y_ref[...].astype(f32)
    high = prod.astype(bf16)
    rest = (prod - high.astype(f32)).astype(bf16)
    pickers = (
        lax.broadcasted_iota(jnp.int32, (8, cols), 1) // HEAD_DIM
        == lax.broadcasted_iota(jnp.int32, (8, cols), 0)
    ).astype(bf16)
    stats[0:8, :] = dot_t(pickers, high) + dot_t(pickers, rest)
    stats[8:16, :] = l_ref[...].T[0:8, :]

    def piece(at, size, rows, causal):
        keys = k_ref[pl.ds(at, size), :]
        vals = v_ref[pl.ds(at, size), :]
        q = q_ref[rows, :]
        dy = dy_ref[rows, :]
        total_q = jnp.zeros(q.shape, f32)
        total_k = jnp.zeros(keys.shape, f32)
        total_v = jnp.zeros(keys.shape, f32)
        for h in range(heads):
            qm = masked(q, masks[h])
            dym = masked(dy, masks[h])
            p = jnp.exp2(dot_t(keys, qm) - stats[8 + h : 9 + h, rows])
            if causal is not None:
                p = jnp.where(causal, p, 0.0)
            ds = (p * (dot_t(vals, dym) - stats[h : h + 1, rows])).astype(bf16)
            total_v += dot(p.astype(bf16), dym)
            total_k += dot(ds, qm)
            total_q += t_dot(ds, masked(keys, masks[h]))
        acc[rows, :] += total_q
        dk_acc[pl.ds(at, size), :] += total_k
        dv_acc[pl.ds(at, size), :] += total_v

    def body(j, carry):
        piece(pl.multiple_of(j * blk, blk), blk, slice(0, blk), None)
        return carry

    lax.fori_loop(low, i, body, 0)
    start = pl.multiple_of(i * blk, blk)
    causal = lax.broadcasted_iota(jnp.int32, (sub, sub), 0) <= lax.broadcasted_iota(
        jnp.int32, (sub, sub), 1
    )
    for a in range(blk // sub):
        for b in range(a + 1):
            piece(
                pl.multiple_of(start + b * sub, sub),
                sub,
                slice(a * sub, (a + 1) * sub),
                causal if a == b else None,
            )
    cosine = cos_ref[...]
    sine = sin_ref[...]
    total = jnp.zeros((1, cols), f32)
    here = pl.ds(start, blk)
    for c, (value, unit, rho_ref, up, scale) in enumerate(
        (
            (acc[...], q_ref[...], rq_ref, score_scale, score_scale * LOG2E),
            (dk_acc[here, :], k_ref[here, :], rk_ref, LN2, 1.0),
        )
    ):
        grad = value * up
        unit = unit.astype(f32) * (1.0 / (gain * scale))
        total += jnp.sum(grad * unit, axis=0, keepdims=True)
        grad = grad * gain
        back = rho_ref[...] * (grad - unit * head_sum(grad * unit, ones))
        turned = back * cosine - swap_halves(back) * sine
        out_ref[:, c * cols : (c + 1) * cols] = turned.astype(bf16)
    out_ref[:, 2 * cols :] = dv_acc[here, :].astype(bf16)
    s_ref[0:1, :] += total
    if dk_out is not None:
        @pl.when(step == count - 1)
        def _():
            dk_out[...] = dk_acc[0 : first * blk, :]
            dv_out[...] = dv_acc[0 : first * blk, :]


def attn_bwd(is_long, q, k, v, dy, y, logs, rq, rk, cosine, sine, gain, ones, first, count, carry):
    rows, cols = q.shape
    heads = cols // HEAD_DIM
    blk, sub = 512, 256
    top = (first + count) * blk
    at = lambda s: first + count - 1 - s
    row = lambda n: pl.BlockSpec((blk, n), lambda s, m: (at(s), 0))
    whole = pl.BlockSpec((top, cols), lambda s, m: (0, 0))
    ins = [q, k, dy, y, logs, k, v, rq, rk, cosine, sine, gain, ones]
    in_specs = [row(cols)] * 4 + [row(128), whole, whole] + [row(cols)] * 4
    in_specs += [full_spec((1, cols)), full_spec((cols, cols))]
    body = functools.partial(
        attn_bwd_kernel, heads=heads, blk=blk, sub=sub, first=first, count=count
    )
    outs = [jax.ShapeDtypeStruct((count * blk, 3 * cols), bf16)]
    out_specs = [pl.BlockSpec((blk, 3 * cols), lambda s, m: (count - 1 - s, 0))]
    if first:
        outs += [jax.ShapeDtypeStruct((first * blk, cols), f32)] * 2
        out_specs += [full_spec((first * blk, cols))] * 2
        inner = lambda *r: body(*r[:14], None, None, *r[14:])
    else:
        ins += carry
        in_specs += [full_spec((top, cols))] * 2
        inner = lambda *r: body(*r[:17], None, None, *r[17:])
    outs.append(jax.ShapeDtypeStruct((8, cols), f32))
    out_specs.append(full_spec((8, cols)))
    return pl.pallas_call(
        inner,
        grid_spec=pltpu.PrefetchScalarGridSpec(
            num_scalar_prefetch=1,
            grid=(count,),
            in_specs=in_specs,
            out_specs=out_specs,
            scratch_shapes=[
                pltpu.VMEM((blk, cols), f32),
                pltpu.VMEM((top, cols), f32),
                pltpu.VMEM((top, cols), f32),
                pltpu.VMEM((16, blk), f32),
            ],
        ),
        out_shape=outs,
        compiler_params=params(),
    )(is_long, *ins)


def row_norm(value):
    return lax.rsqrt(jnp.mean(value * value, axis=1, keepdims=True) + layer_eps)


def norm_back(scale, result, grad):
    return scale * (grad - result * jnp.mean(grad * result, axis=1, keepdims=True))


def pack_kernel(core_ref, up_ref, down_ref, out_ref, qkv_ref, mine_ref, theirs_ref, q_ref, o_ref):
    half = up_ref.shape[2] // 2
    low = core_ref[0] == 0
    down = down_ref[...].astype(bf16).T
    o_ref[...] = out_ref[...].astype(bf16).T
    for ref, first in ((mine_ref, low), (theirs_ref, jnp.logical_not(low))):
        for c in range(2):
            ref[:, c * half : (c + 1) * half] = jnp.where(
                first, up_ref[:, c, :half], up_ref[:, c, half:]
            ).astype(bf16)
        ref[:, 2 * half : 3 * half] = jnp.where(first, down[:, :half], down[:, half:])
    cols = qkv_ref.shape[2]
    for c in range(3):
        q_ref[:, c * cols : (c + 1) * cols] = qkv_ref[:, c, :].astype(bf16)


def pack(core, w_up, w_down, w_out, w_qkv):
    span, _, hid = w_up.shape
    cols = w_qkv.shape[2]
    vmem = pl.BlockSpec(memory_space=pltpu.VMEM)
    return pl.pallas_call(
        pack_kernel,
        in_specs=[pl.BlockSpec(memory_space=pltpu.SMEM)] + [vmem] * 4,
        out_specs=[vmem] * 4,
        out_shape=[jax.ShapeDtypeStruct((span, 3 * hid // 2), bf16)] * 2
        + [jax.ShapeDtypeStruct((span, 3 * cols), bf16), jax.ShapeDtypeStruct((span, cols), bf16)],
        compiler_params=params(),
    )(core, w_up, w_down, w_out, w_qkv)


def attn_out_kernel(place_ref, *refs, parts, chips):
    ys = refs[:parts]
    w_ref, x_ref, alpha_ref, ha_ref, h1_ref, hb_ref, stat_ref, acc = refs[parts:]
    z, chip = place_ref[0], place_ref[1]
    chunk = x_ref.shape[1] // chips
    for r in range(chips):
        at = pl.ds(pl.multiple_of((r ^ chip) * chunk, chunk), chunk)
        part = jnp.zeros((x_ref.shape[0], chunk), f32)
        for k in range(parts):
            part += dot_t(ys[k][...], w_ref[lax.rem(z + k, parts), at, :])
        acc[:, r * chunk : (r + 1) * chunk] = part
    total = acc[...]
    norm = row_norm(total)
    hidden = total * norm
    start = x_ref[...].astype(f32)
    mixed = start + alpha_ref[...] * (hidden - start)
    first_norm = row_norm(mixed)
    out = mixed * first_norm
    ha_ref[...] = hidden
    h1_ref[...] = out
    hb_ref[...] = out.astype(bf16)
    lane = lax.broadcasted_iota(jnp.int32, stat_ref.shape, 1)
    stat_ref[...] = jnp.where(lane == 0, norm, first_norm)


def attn_out(place, ys, w, x, alpha, chips):
    rows, width = x.shape
    cols = ys[0].shape[1]
    blk = 256
    row = lambda n: pl.BlockSpec((blk, n), lambda i, s: (i, 0))
    return pl.pallas_call(
        functools.partial(attn_out_kernel, parts=len(ys), chips=chips),
        grid_spec=pltpu.PrefetchScalarGridSpec(
            num_scalar_prefetch=1,
            grid=(rows // blk,),
            in_specs=[row(cols)] * len(ys)
            + [full_spec(w.shape), row(width), full_spec((1, width))],
            out_specs=[row(width)] * 3 + [row(128)],
            scratch_shapes=[pltpu.VMEM((blk, width), f32)],
        ),
        out_shape=[jax.ShapeDtypeStruct((rows, width), d) for d in (f32, f32, bf16)]
        + [jax.ShapeDtypeStruct((rows, 128), f32)],
        compiler_params=params(),
    )(place, *ys, w, x, alpha)


def loss_kernel(own_ref, got_ref, h1_ref, cot_ref, alpha_ref, hidden_ref, dmo_ref, base_ref, ga_ref):
    total = own_ref[...] + got_ref[...].astype(f32)
    alpha = alpha_ref[...]
    norm = row_norm(total)
    inner = total * norm
    h1 = h1_ref[...]
    mixed = h1 + alpha * (inner - h1)
    last = row_norm(mixed)
    hidden = mixed * last
    grad = norm_back(last, hidden, cot_ref[...].astype(f32))
    hidden_ref[...] = hidden.astype(bf16)
    base_ref[...] = (1.0 - alpha) * grad
    dmo_ref[...] = norm_back(norm, inner, alpha * grad).astype(bf16)

    @pl.when(pl.program_id(0) == 0)
    def _():
        ga_ref[...] = jnp.zeros_like(ga_ref)

    ga_ref[0:1, :] += jnp.sum(grad * (inner - h1), axis=0, keepdims=True)


def loss(own, got, h1, cot, alpha):
    rows, width = own.shape
    blk = 256
    row = pl.BlockSpec((blk, width), lambda i: (i, 0))
    return pl.pallas_call(
        loss_kernel,
        grid=(rows // blk,),
        in_specs=[row] * 4 + [full_spec((1, width))],
        out_specs=[row] * 3 + [full_spec((8, width))],
        out_shape=[jax.ShapeDtypeStruct((rows, width), d) for d in (bf16, bf16, f32)]
        + [jax.ShapeDtypeStruct((8, width), f32)],
        compiler_params=params(),
    )(own, got, h1, cot, alpha)


def first_back_kernel(place_ref, own_ref, got_ref, base_ref, h1_ref, ha_ref, x_ref, stat_ref, alpha_ref, w_ref, *outs, parts, chips):
    do_ref, through_ref, ga_ref = outs[:3]
    dys = outs[3:]
    z, chip = place_ref[0], place_ref[1]
    alpha = alpha_ref[...]
    grad = base_ref[...] + own_ref[...] + got_ref[...].astype(f32)
    grad = norm_back(stat_ref[:, 1:2], h1_ref[...], grad)
    ha = ha_ref[...]
    through_ref[...] = ((1.0 - alpha) * grad).astype(bf16)
    back = norm_back(stat_ref[:, 0:1], ha, alpha * grad).astype(bf16)
    do_ref[...] = back
    chunk = back.shape[1] // chips
    for k in range(parts):
        part = jnp.zeros(dys[k].shape, f32)
        for r in range(chips):
            at = pl.ds(pl.multiple_of((r ^ chip) * chunk, chunk), chunk)
            part += dot(
                do_ref[:, r * chunk : (r + 1) * chunk], w_ref[lax.rem(z + k, parts), at, :]
            )
        dys[k][...] = part.astype(bf16)

    @pl.when(pl.program_id(0) == 0)
    def _():
        ga_ref[...] = jnp.zeros_like(ga_ref)

    ga_ref[0:1, :] += jnp.sum(grad * (ha - x_ref[...].astype(f32)), axis=0, keepdims=True)


def first_back(place, own, got, base, h1, ha, x, stat, alpha, w, chips):
    rows, width = own.shape
    parts, _, cols = w.shape
    blk = 256
    row = lambda n: pl.BlockSpec((blk, n), lambda i, s: (i, 0))
    return pl.pallas_call(
        functools.partial(first_back_kernel, parts=parts, chips=chips),
        grid_spec=pltpu.PrefetchScalarGridSpec(
            num_scalar_prefetch=1,
            grid=(rows // blk,),
            in_specs=[row(width)] * 6
            + [row(128), full_spec((1, width)), full_spec(w.shape)],
            out_specs=[row(width)] * 2 + [full_spec((8, width))] + [row(cols)] * parts,
        ),
        out_shape=[jax.ShapeDtypeStruct((rows, width), bf16)] * 2
        + [jax.ShapeDtypeStruct((8, width), f32)]
        + [jax.ShapeDtypeStruct((rows, cols), bf16)] * parts,
        compiler_params=params(),
    )(place, own, got, base, h1, ha, x, stat, alpha, w)


def fetch_weights(q, slots, wbuf, sems):
    def copies(j):
        at = 0
        found = []
        for p, piece in enumerate(slots[j]):
            size = piece.shape[0]
            found.append(
                pltpu.make_async_copy(
                    piece, wbuf.at[j % 2, at : at + size, :], sems.at[j % 2, p]
                )
            )
            at += size
        return found

    for j in range(len(slots)):

        @pl.when(q == j)
        def _(j=j):
            if j == 0:
                for copy in copies(0):
                    copy.start()
            if j + 1 < len(slots):
                for copy in copies(j + 1):
                    copy.start()
            for copy in copies(j):
                copy.wait()


def mlp_fwd_kernel(*refs, half, counts, carried):
    total = sum(counts)
    flat, refs = refs[:total], refs[total:]
    slots, at = [], 0
    for n in counts:
        slots.append(flat[at : at + n])
        at += n
    ha_ref, hb_ref, suv_ref = refs[:3]
    refs = refs[3:]
    if carried:
        own_in, got_in = refs[:2]
        refs = refs[4:]
    act_ref, uv_ref, own_ref, got_ref, wbuf, sems = refs
    rows = ha_ref.shape[0]
    q = pl.program_id(0)

    @pl.when(q == 0)
    def _():
        if carried:
            own_ref[...] = own_in[...]
            got_ref[...] = got_in[...]
        else:
            own_ref[...] = jnp.zeros_like(own_ref)
            got_ref[...] = jnp.zeros_like(got_ref)

    fetch_weights(q, slots, wbuf, sems)
    w = wbuf.at[lax.rem(q, 2)]
    for base, h_ref, sum_ref in ((0, ha_ref, own_ref), (rows, hb_ref, got_ref)):
        at = slice(base, base + rows)
        pair = dot(h_ref[...], w[:, : 2 * half])
        lifted = pair[:, :half] * suv_ref[0:1, :]
        gated = pair[:, half:] * suv_ref[1:2, :]
        act = (lifted * gated * jax.nn.sigmoid(gated)).astype(bf16)
        uv_ref[at, :] = pair.astype(bf16)
        act_ref[at, :] = act
        sum_ref[...] += dot_t(act, w[:, 2 * half : 3 * half])


def mlp_fwd(ha, hb, slots, suv, first, carry):
    rows, width = ha.shape
    parts, _, half = suv.shape
    take = lambda n: pl.BlockSpec((None, 2 * rows, n), lambda q: (first + q, 0, 0))
    whole = full_spec((rows, width))
    anywhere = pl.BlockSpec(memory_space=pl.ANY)
    flat = [p for slot in slots for p in slot]
    ins = [*flat, ha, hb, suv]
    in_specs = [anywhere] * len(flat) + [
        whole,
        whole,
        pl.BlockSpec((None, 2, half), lambda q: (first + q, 0, 0)),
    ]
    alias = {}
    if carry:
        act, uv, own, got = carry
        ins += [own, got, act, uv]
        in_specs += [whole, whole, anywhere, anywhere]
        alias = {len(ins) - 2: 0, len(ins) - 1: 1}
    return pl.pallas_call(
        functools.partial(
            mlp_fwd_kernel, half=half, counts=[len(s) for s in slots], carried=bool(carry)
        ),
        grid=(len(slots),),
        in_specs=in_specs,
        out_specs=[take(half), take(2 * half), whole, whole],
        out_shape=[
            jax.ShapeDtypeStruct((parts, 2 * rows, half), bf16),
            jax.ShapeDtypeStruct((parts, 2 * rows, 2 * half), bf16),
            jax.ShapeDtypeStruct((rows, width), f32),
            jax.ShapeDtypeStruct((rows, width), f32),
        ],
        scratch_shapes=[
            pltpu.VMEM((2, width, 3 * half), bf16),
            pltpu.SemaphoreType.DMA((2, max(len(s) for s in slots))),
        ],
        input_output_aliases=alias,
        compiler_params=params(),
    )(*ins)


def mlp_bwd_kernel(*refs, half, counts):
    total = sum(counts)
    flat, refs = refs[:total], refs[total:]
    slots, at = [], 0
    for n in counts:
        slots.append(flat[at : at + n])
        at += n
    da_ref, db_ref, uv_ref, suv_ref, duv_ref, own_ref, got_ref, gs_ref, acc, wbuf, sems = refs
    rows = da_ref.shape[0]
    q = pl.program_id(0)

    @pl.when(q == 0)
    def _():
        own_ref[...] = jnp.zeros_like(own_ref)
        acc[...] = jnp.zeros_like(acc)

    gs_ref[...] = jnp.zeros_like(gs_ref)
    fetch_weights(q, slots, wbuf, sems)
    w = wbuf.at[lax.rem(q, 2)]
    for base, d_ref, sum_ref in ((0, da_ref, own_ref), (rows, db_ref, acc)):
        at = slice(base, base + rows)
        grad = dot(d_ref[...], w[:, 2 * half : 3 * half])
        up = uv_ref[at, :half].astype(f32)
        gate = uv_ref[at, half:].astype(f32)
        su = suv_ref[0:1, :]
        sv = suv_ref[1:2, :]
        lifted = up * su
        gated = gate * sv
        sigma = jax.nn.sigmoid(gated)
        da = grad * gated * sigma
        db = grad * lifted * sigma * (1.0 + gated * (1.0 - sigma))
        gs_ref[0:1, :] += jnp.sum(da * up, axis=0, keepdims=True)
        gs_ref[1:2, :] += jnp.sum(db * gate, axis=0, keepdims=True)
        duv_ref[at, :half] = (da * su).astype(bf16)
        duv_ref[at, half:] = (db * sv).astype(bf16)
        sum_ref[...] += dot_t(duv_ref[at, :], w[:, : 2 * half])

    @pl.when(q == pl.num_programs(0) - 1)
    def _():
        got_ref[...] = acc[...].astype(bf16)


def mlp_bwd(da, db, slots, uv, suv):
    rows, width = da.shape
    parts, _, half = suv.shape
    take = lambda n: pl.BlockSpec((None, 2 * rows, n), lambda q: (q, 0, 0))
    whole = full_spec((rows, width))
    anywhere = pl.BlockSpec(memory_space=pl.ANY)
    flat = [p for slot in slots for p in slot]
    return pl.pallas_call(
        functools.partial(mlp_bwd_kernel, half=half, counts=[len(s) for s in slots]),
        grid=(parts,),
        in_specs=[anywhere] * len(flat)
        + [
            whole,
            whole,
            take(2 * half),
            pl.BlockSpec((None, 2, half), lambda q: (q, 0, 0)),
        ],
        out_specs=[
            take(2 * half),
            whole,
            whole,
            pl.BlockSpec((None, 8, half), lambda q: (q, 0, 0)),
        ],
        out_shape=[
            jax.ShapeDtypeStruct((parts, 2 * rows, 2 * half), bf16),
            jax.ShapeDtypeStruct((rows, width), f32),
            jax.ShapeDtypeStruct((rows, width), bf16),
            jax.ShapeDtypeStruct((parts, 8, half), f32),
        ],
        scratch_shapes=[
            pltpu.VMEM((rows, width), f32),
            pltpu.VMEM((2, width, 3 * half), bf16),
            pltpu.SemaphoreType.DMA((2, max(len(s) for s in slots))),
        ],
        compiler_params=params(),
    )(*flat, da, db, uv, suv)


EXTRA = 16


def grad_kernel(*refs, count, chunk, more):
    ha, hb = refs[:count], refs[count : 2 * count]
    refs = refs[2 * count :]
    if more:
        oa, ob = refs[:count], refs[count : 2 * count]
        ya_ref, yb_ref, extra_ref = refs[2 * count : 2 * count + 3]
        refs = refs[2 * count + 3 :]
        val_ref, out_ref, turned, turned_o = refs
    else:
        val_ref, out_ref, turned = refs
    rows = ha[0].shape[0]

    @pl.when(pl.program_id(0) == 0)
    def _():
        for j in range(count):
            at = slice(j * chunk, (j + 1) * chunk)
            turned[at, :rows] = ha[j][...].T
            turned[at, rows:] = hb[j][...].T
            if more:
                turned_o[at, :rows] = oa[j][...].T
                turned_o[at, rows:] = ob[j][...].T

    value = dot(turned[...], val_ref[...]).astype(bf16)
    size = value.shape[1]
    for j in range(count):
        at = slice(j * chunk, (j + 1) * chunk)
        out_ref[j, :chunk, :size] = value[at, :]
        if more:
            out_ref[j, :chunk, size:] = (
                dot(turned_o[at, :rows], ya_ref[...]) + dot(turned_o[at, rows:], yb_ref[...])
            ).astype(bf16)
            out_ref[j, chunk:, :] = extra_ref[...].astype(bf16)


def weight_grads(which, parts, chips, hs, value, os=None, ys=None, extra=None):
    rows, width = hs[0].shape
    chunk = width // chips
    size = value.shape[2]
    more = os is not None
    lo, count, nw = parts[0], len(parts), len(which)
    hc = ys[0].shape[1] // value.shape[0] if more else 0
    tall = chunk + (EXTRA if more else 0)
    if chunk % 128:
        cut = lambda pair: jnp.concatenate(
            [jnp.concatenate(pair, axis=0)[:, r * chunk : (r + 1) * chunk] for r in which], axis=1
        )
        found = []
        for k in parts:
            one = t_dot(cut(hs), value[k])
            if more:
                y = jnp.concatenate(ys, axis=0)[:, k * hc : (k + 1) * hc]
                one = jnp.concatenate([one, t_dot(cut(os), y)], axis=1)
            one = one.reshape(nw, chunk, size + hc)
            if more:
                wide = jnp.broadcast_to(extra[k][None], (nw, EXTRA, size + hc))
                one = jnp.concatenate([one, wide], axis=1)
            found.append(one.astype(bf16))
        return jnp.stack(found)
    columns = [pl.BlockSpec((rows, chunk), lambda k, r=r: (0, r)) for r in which]
    ins = [hs[0]] * nw + [hs[1]] * nw
    in_specs = columns * 2
    scratch = [pltpu.VMEM((nw * chunk, 2 * rows), bf16)]
    if more:
        ins += [os[0]] * nw + [os[1]] * nw + [ys[0], ys[1], extra]
        in_specs += columns * 2
        in_specs += [pl.BlockSpec((rows, hc), lambda k: (0, lo + k))] * 2
        in_specs.append(pl.BlockSpec((None, EXTRA, size + hc), lambda k: (lo + k, 0, 0)))
        scratch = scratch * 2
    ins.append(value)
    in_specs.append(pl.BlockSpec((None, 2 * rows, size), lambda k: (lo + k, 0, 0)))
    return pl.pallas_call(
        functools.partial(grad_kernel, count=nw, chunk=chunk, more=more),
        grid=(count,),
        in_specs=in_specs,
        out_specs=pl.BlockSpec((None, nw, tall, size + hc), lambda k: (k, 0, 0, 0)),
        out_shape=jax.ShapeDtypeStruct((count, nw, tall, size + hc), bf16),
        scratch_shapes=scratch,
        compiler_params=params(),
    )(*ins)


def adam_step(weight, grad, first, second):
    first_new = beta_one * first + (1.0 - beta_one) * grad
    second_new = beta_two * second + (1.0 - beta_two) * grad * grad
    moved = weight - learn_rate * (first_new / bias_one) / (
        jnp.sqrt(second_new / bias_two) + adam_eps
    )
    return (first_new, second_new, moved)


def after(value, *others):
    return lax.optimization_barrier((value, *others))[0]


def per_device(
    layer_input,
    cotangent,
    positions,
    w_qkv,
    w_out,
    w_up,
    w_down,
    moment_qkv,
    moment_out,
    moment_up,
    moment_down,
    square_qkv,
    square_out,
    square_up,
    square_down,
    s_qk,
    alpha_attn,
    alpha_mlp,
    s_uv,
):
    nz = lax.axis_size("head")
    nb = lax.axis_size("batch")
    z = lax.axis_index("head")
    b = lax.axis_index("batch")
    core = b % 2
    chip = b // 2
    chips = nb // 2
    bits = [1 << n for n in range(int(math.log2(chips)))]
    rows, cols = layer_input.shape
    width = cols * nz
    own = rows // nz
    hid = w_down.shape[0]
    half = hid // 2
    hc = cols // 2
    heads = cols // HEAD_DIM
    span = w_qkv.shape[0]
    chunk = width // chips
    core_s = core.reshape(1).astype(jnp.int32)
    place = jnp.stack([z, chip]).astype(jnp.int32)
    near_first = [
        sorted(range(nz), key=lambda s, at=at: (abs(s - at), (s < at) == (at < nz // 2)))
        for at in range(nz)
    ]

    def swap_batch(value, bit):
        return lax.ppermute(value, "batch", [(i, i ^ bit) for i in range(nb)])

    def swap_core(value):
        return swap_batch(value, 1)

    def swap_chip(value, bit):
        return swap_batch(value, 2 * bit)

    def turn(value, k):
        return lax.ppermute(value, "head", [(i, (i - k) % nz) for i in range(nz)])

    def from_left(value):
        return lax.ppermute(value, "head", [(i, i + 1) for i in range(nz - 1)])

    def from_right(value):
        return lax.ppermute(value, "head", [(i + 1, i) for i in range(nz - 1)])

    def pick(pair, index):
        return jnp.where(index == 0, pair[0], pair[1])

    def relative(value):
        return jnp.concatenate(
            [
                lax.dynamic_slice_in_dim(value, (chip ^ r) * chunk, chunk, value.ndim - 1)
                for r in range(chips)
            ],
            axis=-1,
        )

    lefts, rights = [from_right(layer_input)], [from_left(layer_input)]
    mine, theirs, qkv_own, out_own = pack(core_s, w_up, w_down, w_out, w_qkv)
    qkv_full = lax.all_gather(qkv_own, "batch", axis=0, tiled=True)
    theirs = swap_core(theirs)
    packet = jnp.concatenate([pick((mine, theirs), core), pick((theirs, mine), core)], axis=0)

    def spread(value):
        if len(bits) == 2:
            return [value, swap_chip(value, 1), swap_chip(value, 2)]
        for bit in bits:
            value = jnp.concatenate([value, swap_chip(value, bit)], axis=0)
        return [value]

    def spread_more(found, *wait):
        if len(bits) == 2:
            near, far = found[1:]
            middle = near.shape[0] // 2
            top, bottom = far[:middle], near[middle:]
            if wait:
                top, bottom, *_ = lax.optimization_barrier((top, bottom, *wait))
            found = found + [swap_chip(top, 1), swap_chip(bottom, 2)]
        return found

    for _ in range(nz - 2):
        lefts.append(from_right(lefts[-1]))
        rights.append(from_left(rights[-1]))
    slots = [spread_more(spread(packet))]

    suv_parts = [s_uv.reshape(2, 2, half)]
    for k in range(1, nz):
        suv_parts.append(turn(suv_parts[0], k))
    suv_all = jnp.stack(suv_parts)
    suv_all = pick((suv_all[:, :, 0], suv_all[:, :, 1]), core)
    order_z = jnp.asarray(near_first, jnp.int32)[z]
    suv = jnp.take(suv_all, (order_z - z) % nz, axis=0)

    freqs = jnp.exp(
        jnp.arange(HEAD_DIM // 2, dtype=f32) * (-2.0 * math.log(10000.0) / HEAD_DIM)
    )
    phase = positions.astype(f32)[:, None] * freqs[None, :]
    cosine, sine = jnp.cos(phase), jnp.sin(phase)
    cosine = jnp.tile(cosine, (1, 2 * heads))
    sine = jnp.tile(jnp.concatenate([-sine, sine], axis=1), (1, heads))
    lane = jnp.arange(cols) // HEAD_DIM
    ones = (lane[:, None] == lane[None, :]).astype(bf16)
    gain = s_qk.reshape(1, cols)
    is_long = (positions[SHORT : SHORT + 1] != 0).astype(jnp.int32)
    attn_gain = relative(alpha_attn[None])
    mlp_gain = relative(alpha_mlp[None])

    packet_z, out_own, lefts[-1], rights[-1] = lax.optimization_barrier(
        (packet, out_own, lefts[-1], rights[-1])
    )
    hops = [[from_right(packet_z)], [from_left(packet_z)]]
    out_full = lax.all_gather(out_own, ("head", "batch"), axis=0, tiled=True)
    out_full = out_full.reshape(nz, width, cols)

    def slot_value(k):
        value = None
        for at in range(nz):
            s = near_first[at][k]
            one = hops[0][s - at - 1] if s > at else hops[1][at - s - 1]
            value = one if value is None else jnp.where(z == at, one, value)
        return value

    tokens_full, q, k, v, rho_q, rho_k = qkv_project(
        place, lefts, layer_input, rights, qkv_full, cosine, sine, gain, ones
    )
    waits = [q]
    held = []

    def next_hop():
        hops[0][-1], hops[1][-1], *_ = lax.optimization_barrier((hops[0][-1], hops[1][-1], *waits))
        count = len(hops[0])
        if count < nz - 1:
            hops[0].append(from_right(hops[0][-1]))
            hops[1].append(from_left(hops[1][-1]))
        held.append(spread(slot_value(count)))

    attended, logs = attn_fwd(is_long, q, k, v)
    next_hop()

    def to_tokens(value):
        parts = []
        for n in range(nz):
            part = lax.dynamic_slice_in_dim(value, ((z - n) % nz) * own, own, 0)
            parts.append(part if n == 0 else turn(part, n))
        return parts

    def natural_z(parts, axis):
        size = parts[0].shape[axis]
        out = jnp.concatenate(parts, axis=axis)
        return jnp.concatenate(
            [
                lax.dynamic_slice_in_dim(out, ((n - z) % nz) * size, size, axis)
                for n in range(nz)
            ],
            axis=axis,
        )

    def to_columns(value):
        parts = []
        for n in range(nz):
            part = lax.dynamic_slice_in_dim(value, ((z - n) % nz) * cols, cols, 1)
            parts.append(part if n == 0 else turn(part, n))
        return natural_z(parts, 0)

    y_parts = to_tokens(attended)
    waits = [attended]
    for _ in range(nz - 3):
        next_hop()
    if len(held) > 0:
        slots.append(spread_more(held[0], attended))
    start = relative(lax.dynamic_slice_in_dim(tokens_full, z * own, own, 0))
    hA, h1, h_own, stat = attn_out(place, y_parts, out_full, start, attn_gain, chips)
    h_got = swap_core(h_own)
    waits = [h_own]
    next_hop()
    for found in held[1 : nz - 2]:
        slots.append(spread_more(found, h_own))
    cot_parts = to_tokens(after(cotangent, h_own))

    some = mlp_fwd(h_own, h_got, slots, suv, 0, None)
    slots.append(spread_more(held[nz - 2]))
    act, uv, mo_own, mo_other = mlp_fwd(h_own, h_got, slots[nz - 1 :], suv, nz - 1, some)
    cot = relative(natural_z(cot_parts, 1))
    hidden, d_own, base, ga_mlp = loss(
        mo_own, swap_core(mo_other.astype(bf16)), h1, cot, mlp_gain
    )
    d_got = swap_core(d_own)
    hidden_t = to_columns(relative(hidden))

    groups = [(list(range(nz // 2)), bits), (list(range(nz // 2, nz)), bits[::-1])]
    sides = lambda order: (
        [r for r in range(chips) if r & order[0]],
        [r for r in range(chips) if not r & order[0]],
    )

    def first_sent(*args):
        made = [weight_grads(sides(order)[0], parts, chips, *args) for parts, order in groups]
        return made, [swap_chip(one, order[0]) for one, (_, order) in zip(made, groups)]

    def first_kept(*args):
        return [weight_grads(sides(order)[1], parts, chips, *args) for parts, order in groups]

    def second(kept, sent):
        found = []
        for (_, order), got, keep in zip(groups, sent, kept):
            left = sides(order)[1]
            for bit in order[1:]:
                send_at = [n for n, r in enumerate(left) if r & bit]
                keep_at = [n for n, r in enumerate(left) if not r & bit]
                left = [left[n] for n in keep_at]
                cut = lambda v, at: jnp.concatenate([v[:, n : n + 1] for n in at], axis=1).astype(f32)
                send = (cut(keep, send_at) + cut(got, send_at)).astype(bf16)
                keep = cut(keep, keep_at) + cut(got, keep_at)
                got = swap_chip(send, bit)
            found.append((keep, got))
        return found

    slot_of = [[near_first[at].index(s) for s in range(nz)] for at in range(nz)]
    slot_of = jnp.asarray(slot_of, jnp.int32)[z]

    def along_z(found):
        pieces = jnp.concatenate([keep[:, 0] + got[:, 0].astype(f32) for keep, got in found], axis=0)
        total = pieces[0]
        low = pieces[1:].astype(bf16)
        for n in range(1, nz):
            at = slot_of[(z + n) % nz] - 1
            one = lax.dynamic_index_in_dim(low, at, 0, keepdims=False)
            total = total + turn(one, nz - n).astype(f32)
        return total

    down_made, down_sent = first_sent((d_own, d_got), act)
    d_own, d_got, *_ = lax.optimization_barrier((d_own, d_got, *down_made))
    duv, dh_own, dh_other, gsuv = mlp_bwd(d_own, d_got, slots, uv, suv)
    dh_got = swap_core(dh_other)
    down_kept = first_kept((after(d_own, dh_other), d_got), act)
    do_own, through, ga_attn, *dy_parts = first_back(
        place, dh_own, dh_got, base, h1, hA, start, stat, attn_gain, out_full, chips
    )
    down_sent = [after(one, do_own) for one in down_sent]
    down_part = second(down_kept, down_sent)
    do_got = swap_core(do_own)
    y_mine = jnp.concatenate([pick((p[:, :hc], p[:, hc:]), core) for p in y_parts], axis=1)
    y_other = jnp.concatenate([pick((p[:, hc:], p[:, :hc]), core) for p in y_parts], axis=1)
    y_got = swap_core(y_other)
    in_slots = lambda value: jnp.concatenate(
        [
            lax.dynamic_slice_in_dim(value, ((order_z[n] - z) % nz) * hc, hc, 1)
            for n in range(nz)
        ],
        axis=1,
    )
    ys = (in_slots(y_mine), in_slots(y_got))

    dy_parts = [p if n == 0 else turn(p, nz - n) for n, p in enumerate(dy_parts)]
    dy = natural_z([dy_parts[(nz - n) % nz] for n in range(nz)], 0)

    alphas = [relative(ga_attn[0:1]), relative(ga_mlp[0:1])]
    extra = []
    wide = 2 * half + hc
    fill = lambda r: jnp.pad(r, ((0, 0), (0, wide - r.shape[1])))
    for n in range(nz):
        at = order_z[n] * cols
        line = jnp.concatenate([lax.dynamic_slice_in_dim(g, at, cols, 1) for g in alphas], axis=1)
        first = gsuv[n, :2].reshape(1, 2 * half)
        extra.append(jnp.pad(jnp.concatenate([fill(first), fill(line)]), ((0, EXTRA - 2), (0, 0))))
    extra = jnp.stack(extra)
    up_args = ((h_own, h_got), duv, (do_own, do_got), ys, extra)
    up_made, up_sent = first_sent(*up_args)
    up_kept = first_kept(*up_args)

    blocks = rows // 512
    middle = blocks // 2
    dy = after(dy, *up_made)
    common = (is_long, q, k, v, dy, attended, logs, rho_q, rho_k, cosine, sine, gain, ones)
    sum_down_t = along_z([(keep, after(got, dy)) for keep, got in down_part])
    dqkv_b, dk_part, dv_part, sqk_b = attn_bwd(*common, middle, blocks - middle, None)

    through = relative(through).astype(f32)
    where_rows = (z % (nz // 2)) * own

    def input_part(dqkv, side):
        part = dot_t(dqkv, qkv_full)
        here = lax.dynamic_slice_in_dim(part, where_rows, own, 0)
        here = here + jnp.where(z // (nz // 2) == side, through, 0.0)
        part = lax.dynamic_update_slice_in_dim(part.astype(bf16), here.astype(bf16), where_rows, 0)
        return lax.psum_scatter(part, "head", scatter_dimension=1, tiled=True)

    input_b = input_part(dqkv_b, 1)
    up_part = second(up_kept, [after(one, dqkv_b) for one in up_sent])
    dqkv_a, sqk_a = attn_bwd(*common, 0, middle, [dk_part, dv_part])
    input_a = input_part(dqkv_a, 0)
    input_grad = jnp.concatenate([input_a, input_b], axis=0).astype(f32)
    sum_up_t = along_z([(keep, after(got, dqkv_a)) for keep, got in up_part])

    dqkv = jnp.concatenate([dqkv_a, dqkv_b], axis=0)
    grad_qkv = t_dot(tokens_full, dqkv).astype(bf16)
    sqk = jnp.pad((sqk_a + sqk_b), ((0, EXTRA - 8), (0, 2 * cols)))
    shard = [lax.dynamic_slice_in_dim(grad_qkv, (b ^ r) * span, span, 0) for r in range(nb)]
    shard = [jnp.concatenate([s, sqk.astype(bf16)], axis=0) for s in shard]
    qbits = [1 << n for n in range(int(math.log2(nb)))]
    held = {r: shard[r] for r in range(nb)}
    for bit in qbits:
        send_at = [r for r in held if r & bit]
        send = jnp.concatenate([held[r] for r in send_at], axis=0).astype(bf16)
        got = swap_batch(send, bit)
        size = span + EXTRA
        held = {
            r ^ bit: held[r ^ bit].astype(f32) + got[n * size : (n + 1) * size].astype(f32)
            for n, r in enumerate(send_at)
        }
    sum_qkv = held[0][:span].reshape(span, 3, cols)
    cell = width // (nz * nb)
    sum_sqk = lax.dynamic_slice_in_dim(held[0][span, :cols], b * cell, cell, 0)

    def both_halves(total):
        two = (total[:span], total[span : 2 * span])
        here = jnp.concatenate([pick(two, core), total[2 * span :]], axis=0)
        there = jnp.concatenate([pick(two, 1 - core), total[2 * span :]], axis=0)
        there = swap_core(there.astype(bf16)).astype(f32)
        return [pick((here, there), core), pick((there, here), core)]

    join = lambda halves, at, size: jnp.concatenate([p[:span, at : at + size] for p in halves], axis=1)
    halves = both_halves(sum_down_t)
    sum_down = join(halves, 0, half).T
    halves = both_halves(sum_up_t)
    sum_up = jnp.stack([join(halves, c * half, half) for c in range(2)], axis=1)
    sum_out = join(halves, 2 * half, hc).T
    suv_rows = jnp.stack(
        [jnp.concatenate([p[span, c * half : (c + 1) * half] for p in halves]) for c in range(2)]
    )
    sum_suv = lax.dynamic_slice_in_dim(suv_rows, b * (hid // nb), hid // nb, 1)
    alphas = halves[0][span + 1] + halves[1][span + 1]
    sum_attn = lax.dynamic_slice_in_dim(alphas[:cols], b * cell, cell, 0)
    sum_mlp = lax.dynamic_slice_in_dim(alphas[cols : 2 * cols], b * cell, cell, 0)

    hidden = hidden_t.astype(f32)

    first_a, second_a, moved_a = adam_step(w_qkv, sum_qkv, moment_qkv, square_qkv)
    first_b, second_b, moved_b = adam_step(w_out, sum_out, moment_out, square_out)
    first_c, second_c, moved_c = adam_step(w_up, sum_up, moment_up, square_up)
    first_d, second_d, moved_d = adam_step(w_down, sum_down, moment_down, square_down)
    squares = [
        jnp.sum(moved_a * moved_a, axis=0).reshape(-1),
        jnp.sum(moved_b * moved_b, axis=1),
        jnp.sum(moved_c * moved_c, axis=0).reshape(-1),
        jnp.sum(moved_d * moved_d, axis=1),
    ]
    sizes = [s.shape[0] for s in squares]
    norms = jnp.concatenate(squares).reshape(-1, 128)
    for bit in qbits:
        norms = norms + swap_batch(norms, bit)
    norms = norms.reshape(-1)
    ends = [sum(sizes[: n + 1]) for n in range(4)]
    norm_a = norms[: ends[0]].reshape(3, cols)
    norm_b = norms[ends[0] : ends[1]]
    norm_c = norms[ends[1] : ends[2]].reshape(2, hid)
    norm_d = norms[ends[2] :]
    new_qkv = moved_a * lax.rsqrt(norm_a / width + layer_eps)[None]
    new_out = moved_b * lax.rsqrt(norm_b / width + layer_eps)[:, None]
    new_up = moved_c * lax.rsqrt(norm_c / width + layer_eps)[None]
    new_down = moved_d * lax.rsqrt(norm_d / width + layer_eps)[:, None]
    return (
        hidden,
        input_grad,
        sum_qkv,
        sum_out,
        sum_up,
        sum_down,
        first_a,
        first_b,
        first_c,
        first_d,
        second_a,
        second_b,
        second_c,
        second_d,
        new_qkv,
        new_out,
        new_up,
        new_down,
        sum_sqk,
        sum_attn,
        sum_mlp,
        sum_suv,
    )


def solution(mesh):
    tokens = P("batch", "head")
    wide = P("batch", None, "head")
    tall = P("head", "batch")
    flat = P(("head", "batch"))
    weights = (wide, tall, wide, tall)
    return jax.shard_map(
        per_device,
        mesh=mesh,
        in_specs=(tokens, tokens, P("batch"))
        + weights * 3
        + (P("head"), P(), P(), P(None, "head")),
        out_specs=(tokens, tokens) + weights * 4 + (flat, flat, flat, P(None, ("head", "batch"))),
        check_vma=False,
    )
```

```python
import functools
import math

import jax
import jax.numpy as jnp
from jax import lax
from jax.experimental import pallas as pl
from jax.experimental.pallas import tpu as pltpu
from jax.sharding import PartitionSpec as P

HEAD_DIM = 64
SHORT = 1024

layer_eps = 1e-06
learn_rate = 0.008
beta_one = 0.9
beta_two = 0.95
adam_eps = 1e-08
bias_one = 1.0 - math.exp(100.0 * math.log(0.9))
bias_two = 1.0 - math.exp(100.0 * math.log(0.95))
score_scale = 8.0
LOG2E = math.log2(math.e)
LN2 = math.log(2.0)

bf16 = jnp.bfloat16
f32 = jnp.float32
VMEM_LIMIT = 56 * 1024 * 1024


def dot(a, b):
    return jnp.dot(a, b, preferred_element_type=f32)


def dot_t(a, b):
    return lax.dot_general(a, b, (((1,), (1,)), ((), ())), preferred_element_type=f32)


def t_dot(a, b):
    return lax.dot_general(a, b, (((0,), (0,)), ((), ())), preferred_element_type=f32)


def params():
    return pltpu.CompilerParams(vmem_limit_bytes=VMEM_LIMIT)


def full_spec(shape):
    return pl.BlockSpec(shape, lambda *_: (0,) * len(shape))


def head_sum(value, ones):
    high = value.astype(bf16)
    low = (value - high.astype(f32)).astype(bf16)
    return dot(high, ones) + dot(low, ones)


def widen(value, cols):
    return jnp.concatenate([value] * (cols // value.shape[1]), axis=1)


def swap_halves(value):
    cols = value.shape[-1]
    half = HEAD_DIM // 2
    lane = lax.broadcasted_iota(jnp.int32, value.shape, 1)
    first = (lane % HEAD_DIM) < half
    up = pltpu.roll(value, cols - half, 1)
    down = pltpu.roll(value, half, 1)
    return jnp.where(first, up, down)


def qkv_kernel(place_ref, *refs, parts):
    tokens = refs[:parts]
    w_ref, cos_ref, sin_ref, gain_ref, ones_ref, x_ref, q_ref, k_ref, v_ref, rho_ref = refs[parts:]
    cols = v_ref.shape[1]
    z = place_ref[0]
    for n in range(parts):
        at = pl.multiple_of(lax.rem(z + parts - n, parts) * cols, cols)
        x_ref[:, pl.ds(at, cols)] = tokens[n][...]
    proj = dot(x_ref[...], w_ref[...])
    cosine = widen(cos_ref[...], cols)
    sine = widen(sin_ref[...], cols)
    ones = ones_ref[...]
    gain = gain_ref[...]
    heads = cols // HEAD_DIM
    lane = lax.broadcasted_iota(jnp.int32, rho_ref.shape, 1)
    stats = jnp.zeros(rho_ref.shape, f32)
    for c, (out, scale) in enumerate(((q_ref, score_scale * LOG2E), (k_ref, 1.0))):
        part = proj[:, c * cols : (c + 1) * cols]
        rho = lax.rsqrt(head_sum(part * part, ones) + layer_eps)
        rot = part * cosine + swap_halves(part) * sine
        out[...] = (rot * rho * (gain * scale)).astype(bf16)
        for h in range(heads):
            stats = jnp.where(lane == c * heads + h, rho[:, h * HEAD_DIM : h * HEAD_DIM + 1], stats)
    rho_ref[...] = stats
    v_ref[...] = proj[:, 2 * cols :].astype(bf16)


def qkv_project(place, tokens, w, cosine, sine, gain, ones):
    rows, cols = tokens[0].shape
    parts = len(tokens)
    width = parts * cols
    blk = 512
    row = lambda n: pl.BlockSpec((blk, n), lambda i, s: (i, 0))
    return pl.pallas_call(
        functools.partial(qkv_kernel, parts=parts),
        grid_spec=pltpu.PrefetchScalarGridSpec(
            num_scalar_prefetch=1,
            grid=(rows // blk,),
            in_specs=[row(cols)] * parts
            + [full_spec((width, 3 * cols)), row(128), row(128)]
            + [full_spec((1, cols)), full_spec((cols, cols))],
            out_specs=[row(width)] + [row(cols)] * 3 + [row(128)],
        ),
        out_shape=[jax.ShapeDtypeStruct((rows, width), bf16)]
        + [jax.ShapeDtypeStruct((rows, cols), bf16)] * 3
        + [jax.ShapeDtypeStruct((rows, 128), f32)],
        compiler_params=params(),
    )(place, *tokens, w, cosine, sine, gain, ones)


def head_masks(cols, heads):
    lane = lax.broadcasted_iota(jnp.int32, (1, cols), 1) // HEAD_DIM
    return [(lane == h) for h in range(heads)]


def masked(value, mask):
    return jnp.where(mask, value, jnp.zeros_like(value))


def attn_fwd_kernel(long_ref, q_ref, k_ref, v_ref, y_ref, l_ref, acc, mass, *, heads, blk, sub, first):
    i = first + pl.program_id(0)
    cols = q_ref.shape[1]
    masks = head_masks(cols, heads)
    per = SHORT // blk
    low = jnp.where(long_ref[0] != 0, 0, (i // per) * per)
    acc[...] = jnp.zeros_like(acc)
    mass[...] = jnp.zeros_like(mass)

    def lanes(p):
        total = p[:, 0:128]
        for n in range(1, p.shape[1] // 128):
            total = total + p[:, n * 128 : (n + 1) * 128]
        return total

    def body(j, carry):
        start = pl.multiple_of(j * blk, blk)
        keys = k_ref[pl.ds(start, blk), :]
        vals = v_ref[pl.ds(start, blk), :]
        q = q_ref[...]
        total = jnp.zeros(acc.shape, f32)
        for h in range(heads):
            p = jnp.exp2(dot_t(masked(q, masks[h]), keys))
            mass[h] += lanes(p)
            total += dot(p.astype(bf16), masked(vals, masks[h]))
        acc[...] += total
        return carry

    lax.fori_loop(low, i, body, 0)
    start = pl.multiple_of(i * blk, blk)
    causal = lax.broadcasted_iota(jnp.int32, (sub, sub), 0) >= lax.broadcasted_iota(
        jnp.int32, (sub, sub), 1
    )
    for a in range(blk // sub):
        rows = slice(a * sub, (a + 1) * sub)
        q = q_ref[rows, :]
        for b in range(a + 1):
            at = pl.multiple_of(start + b * sub, sub)
            keys = k_ref[pl.ds(at, sub), :]
            vals = v_ref[pl.ds(at, sub), :]
            total = jnp.zeros((sub, cols), f32)
            for h in range(heads):
                p = jnp.exp2(dot_t(masked(q, masks[h]), keys))
                if a == b:
                    p = jnp.where(causal, p, 0.0)
                mass[h, rows, :] += lanes(p)
                total += dot(p.astype(bf16), masked(vals, masks[h]))
            acc[rows, :] += total
    inverse = jnp.zeros(acc.shape, f32)
    logs = jnp.zeros(l_ref.shape, f32)
    lane = lax.broadcasted_iota(jnp.int32, l_ref.shape, 1)
    for h in range(heads):
        column = jnp.sum(mass[h], axis=1, keepdims=True)
        inverse = jnp.where(masks[h], 1.0 / column, inverse)
        logs = jnp.where(lane == h, jnp.log2(column), logs)
    y_ref[...] = (acc[...] * inverse).astype(bf16)
    l_ref[...] = logs


def attn_fwd(is_long, q, k, v, first, count):
    rows, cols = q.shape
    heads = cols // HEAD_DIM
    blk, sub = 512, 256
    row = lambda n: pl.BlockSpec((blk, n), lambda i, s: (i, 0))
    whole = pl.BlockSpec(((first + count) * blk, cols), lambda i, s: (0, 0))
    return pl.pallas_call(
        functools.partial(attn_fwd_kernel, heads=heads, blk=blk, sub=sub, first=first),
        grid_spec=pltpu.PrefetchScalarGridSpec(
            num_scalar_prefetch=1,
            grid=(count,),
            in_specs=[pl.BlockSpec((blk, cols), lambda i, s: (first + i, 0)), whole, whole],
            out_specs=[row(cols), row(128)],
            scratch_shapes=[pltpu.VMEM((blk, cols), f32), pltpu.VMEM((heads, blk, 128), f32)],
        ),
        out_shape=[
            jax.ShapeDtypeStruct((count * blk, cols), bf16),
            jax.ShapeDtypeStruct((count * blk, 128), f32),
        ],
        compiler_params=params(),
    )(is_long, q, k, v)


def attn_bwd_kernel(
    long_ref, q_ref, qk_ref, dy_ref, y_ref, l_ref, k_ref, v_ref, rho_ref, cos_ref, sin_ref, gain_ref,
    ones_ref, dk_in, dv_in, out_ref, dk_out, dv_out, s_ref, acc, dk_acc, dv_acc, stats, *, heads, blk, sub, first, count
):
    step = pl.program_id(0)
    local = count - 1 - step
    i = first + local
    cols = q_ref.shape[1]
    masks = head_masks(cols, heads)
    per = SHORT // blk
    low = jnp.where(long_ref[0] != 0, 0, (i // per) * per)
    ones = ones_ref[...]
    gain = gain_ref[...]

    @pl.when(step == 0)
    def _():
        dk_acc[...] = jnp.zeros_like(dk_acc)
        dv_acc[...] = jnp.zeros_like(dv_acc)
        s_ref[...] = jnp.zeros_like(s_ref)
        if dk_in is not None:
            dk_acc[...] = dk_in[...]
            dv_acc[...] = dv_in[...]

    acc[...] = jnp.zeros_like(acc)
    prod = dy_ref[...].astype(f32) * y_ref[...].astype(f32)
    high = prod.astype(bf16)
    rest = (prod - high.astype(f32)).astype(bf16)
    pickers = (
        lax.broadcasted_iota(jnp.int32, (8, cols), 1) // HEAD_DIM
        == lax.broadcasted_iota(jnp.int32, (8, cols), 0)
    ).astype(bf16)
    stats[0:8, :] = dot_t(pickers, high) + dot_t(pickers, rest)
    stats[8:16, :] = l_ref[...].T[0:8, :]

    def piece(at, size, rows, causal):
        keys = k_ref[pl.ds(at, size), :]
        vals = v_ref[pl.ds(at, size), :]
        q = q_ref[rows, :]
        dy = dy_ref[rows, :]
        total_q = jnp.zeros(q.shape, f32)
        total_k = jnp.zeros(keys.shape, f32)
        total_v = jnp.zeros(keys.shape, f32)
        for h in range(heads):
            qm = masked(q, masks[h])
            dym = masked(dy, masks[h])
            p = jnp.exp2(dot_t(keys, qm) - stats[8 + h : 9 + h, rows])
            if causal is not None:
                p = jnp.where(causal, p, 0.0)
            ds = (p * (dot_t(vals, dym) - stats[h : h + 1, rows])).astype(bf16)
            total_v += dot(p.astype(bf16), dym)
            total_k += dot(ds, qm)
            total_q += t_dot(ds, masked(keys, masks[h]))
        acc[rows, :] += total_q
        dk_acc[pl.ds(at, size), :] += total_k
        dv_acc[pl.ds(at, size), :] += total_v

    def body(j, carry):
        piece(pl.multiple_of(j * blk, blk), blk, slice(0, blk), None)
        return carry

    lax.fori_loop(low, i, body, 0)
    start = pl.multiple_of(i * blk, blk)
    causal = lax.broadcasted_iota(jnp.int32, (sub, sub), 0) <= lax.broadcasted_iota(
        jnp.int32, (sub, sub), 1
    )
    for a in range(blk // sub):
        for b in range(a + 1):
            piece(
                pl.multiple_of(start + b * sub, sub),
                sub,
                slice(a * sub, (a + 1) * sub),
                causal if a == b else None,
            )
    cosine = widen(cos_ref[...], cols)
    sine = widen(sin_ref[...], cols)
    total = jnp.zeros((1, cols), f32)
    here = pl.ds(start, blk)
    for c, (value, unit, up, scale) in enumerate(
        (
            (acc[...], q_ref[...], score_scale, score_scale * LOG2E),
            (dk_acc[here, :], k_ref[here, :], LN2, 1.0),
        )
    ):
        rho = jnp.zeros(value.shape, f32)
        for h in range(heads):
            at = c * heads + h
            rho = jnp.where(masks[h], rho_ref[:, at : at + 1], rho)
        grad = value * up
        unit = unit.astype(f32) * (1.0 / (gain * scale))
        total += jnp.sum(grad * unit, axis=0, keepdims=True)
        grad = grad * gain
        back = rho * (grad - unit * head_sum(grad * unit, ones))
        turned = back * cosine - swap_halves(back) * sine
        out_ref[:, c * cols : (c + 1) * cols] = turned.astype(bf16)
    out_ref[:, 2 * cols :] = dv_acc[here, :].astype(bf16)
    s_ref[0:1, :] += total
    if dk_out is not None:
        @pl.when(step == count - 1)
        def _():
            dk_out[...] = dk_acc[0 : first * blk, :]
            dv_out[...] = dv_acc[0 : first * blk, :]


def attn_bwd(is_long, q, k, v, dy, y, logs, rho, cosine, sine, gain, ones, first, count, carry):
    rows, cols = q.shape
    heads = cols // HEAD_DIM
    blk, sub = 512, 256
    top = (first + count) * blk
    at = lambda s: first + count - 1 - s
    row = lambda n: pl.BlockSpec((blk, n), lambda s, m: (at(s), 0))
    whole = pl.BlockSpec((top, cols), lambda s, m: (0, 0))
    ins = [q, k, dy, y, logs, k, v, rho, cosine, sine, gain, ones]
    mine = lambda n: pl.BlockSpec((blk, n), lambda s, m: (count - 1 - s, 0))
    in_specs = [row(cols)] * 2 + [mine(cols)] * 2 + [mine(128), whole, whole] + [row(128)] * 3
    in_specs += [full_spec((1, cols)), full_spec((cols, cols))]
    body = functools.partial(
        attn_bwd_kernel, heads=heads, blk=blk, sub=sub, first=first, count=count
    )
    outs = [jax.ShapeDtypeStruct((count * blk, 3 * cols), bf16)]
    out_specs = [pl.BlockSpec((blk, 3 * cols), lambda s, m: (count - 1 - s, 0))]
    if first:
        outs += [jax.ShapeDtypeStruct((first * blk, cols), f32)] * 2
        out_specs += [full_spec((first * blk, cols))] * 2
        inner = lambda *r: body(*r[:13], None, None, *r[13:])
    else:
        ins += carry
        in_specs += [full_spec((top, cols))] * 2
        inner = lambda *r: body(*r[:16], None, None, *r[16:])
    outs.append(jax.ShapeDtypeStruct((8, cols), f32))
    out_specs.append(full_spec((8, cols)))
    return pl.pallas_call(
        inner,
        grid_spec=pltpu.PrefetchScalarGridSpec(
            num_scalar_prefetch=1,
            grid=(count,),
            in_specs=in_specs,
            out_specs=out_specs,
            scratch_shapes=[
                pltpu.VMEM((blk, cols), f32),
                pltpu.VMEM((top, cols), f32),
                pltpu.VMEM((top, cols), f32),
                pltpu.VMEM((16, blk), f32),
            ],
        ),
        out_shape=outs,
        compiler_params=params(),
    )(is_long, *ins)


def row_norm(value):
    return lax.rsqrt(jnp.mean(value * value, axis=1, keepdims=True) + layer_eps)


def norm_back(scale, result, grad):
    return scale * (grad - result * jnp.mean(grad * result, axis=1, keepdims=True))


def pack_kernel(core_ref, up_ref, down_ref, out_ref, qkv_ref, mine_ref, theirs_ref, q_ref):
    half = up_ref.shape[2] // 2
    low = core_ref[0] == 0
    down = down_ref[...].astype(bf16).T
    out = out_ref[...].astype(bf16).T
    for ref, first in ((mine_ref, low), (theirs_ref, jnp.logical_not(low))):
        for c in range(2):
            ref[:, c * half : (c + 1) * half] = jnp.where(
                first, up_ref[:, c, :half], up_ref[:, c, half:]
            ).astype(bf16)
        ref[:, 2 * half : 3 * half] = jnp.where(first, down[:, :half], down[:, half:])
        ref[:, 3 * half :] = out
    cols = qkv_ref.shape[2]
    for c in range(3):
        q_ref[:, c * cols : (c + 1) * cols] = qkv_ref[:, c, :].astype(bf16)


def pack(core, w_up, w_down, w_out, w_qkv):
    span, _, hid = w_up.shape
    cols = w_qkv.shape[2]
    vmem = pl.BlockSpec(memory_space=pltpu.VMEM)
    return pl.pallas_call(
        pack_kernel,
        in_specs=[pl.BlockSpec(memory_space=pltpu.SMEM)] + [vmem] * 4,
        out_specs=[vmem] * 3,
        out_shape=[jax.ShapeDtypeStruct((span, 3 * hid // 2 + cols), bf16)] * 2
        + [jax.ShapeDtypeStruct((span, 3 * cols), bf16)],
        compiler_params=params(),
    )(core, w_up, w_down, w_out, w_qkv)


def place_of(r, chip, chunk):
    return pl.ds(pl.multiple_of((r ^ chip) * chunk, chunk), chunk)


def put_relative(ref, chip, chips, fast):
    if not fast:
        return ref[...]
    if len(ref.shape) == 3:
        return jnp.concatenate([ref[r ^ chip] for r in range(chips)], axis=1)
    chunk = ref.shape[1] // chips
    return jnp.concatenate([ref[:, place_of(r, chip, chunk)] for r in range(chips)], axis=1)


def put_natural(ref, value, chip, chips, fast):
    if not fast:
        ref[...] = value
        return
    chunk = value.shape[1] // chips
    for r in range(chips):
        part = value[:, r * chunk : (r + 1) * chunk]
        if len(ref.shape) == 3:
            ref[r ^ chip] = part
        else:
            ref[:, place_of(r, chip, chunk)] = part


def attn_out_kernel(place_ref, *refs, counts, chips, fast):
    total = sum(counts)
    flat, refs = refs[:total], refs[total:]
    ya_ref, yb_ref, x_ref, alpha_ref, ha_ref, h1_ref, hb_ref, stat_ref, acc = refs
    z, chip = place_ref[0], place_ref[1]
    parts = len(counts)
    early = pl.program_id(0) == 0
    index = 0
    for n in range(parts):
        at = lax.rem(z + parts - n, parts)
        y = jnp.where(early, ya_ref[at], yb_ref[at])
        column = 0
        for piece in flat[index : index + counts[n]]:
            part = slice(column, column + piece.shape[0])
            if n == 0:
                acc[:, part] = dot_t(y, piece[...])
            else:
                acc[:, part] += dot_t(y, piece[...])
            column += piece.shape[0]
        index += counts[n]
    total = acc[...]
    norm = row_norm(total)
    hidden = total * norm
    start = put_relative(x_ref, chip, chips, fast).astype(f32)
    mixed = start + alpha_ref[...] * (hidden - start)
    first_norm = row_norm(mixed)
    out = mixed * first_norm
    ha_ref[...] = hidden
    h1_ref[...] = out
    hb_ref[...] = out.astype(bf16)
    lane = lax.broadcasted_iota(jnp.int32, stat_ref.shape, 1)
    stat_ref[...] = jnp.where(lane == 0, norm, first_norm)


def own_rows(blk, parts, width, fast):
    if fast:
        return pl.BlockSpec((blk, width), lambda i, s: (i * parts + s[0], 0))
    return pl.BlockSpec((blk, width), lambda i, s: (i, 0))


def out_weights(slots, cols):
    flat = [p for slot in slots for p in slot]
    last = flat[0].shape[1] // cols - 1
    return flat, [pl.BlockSpec((p.shape[0], cols), lambda i, s: (0, last)) for p in flat]


def attn_out(place, ya, yb, slots, x, alpha, chips, fast):
    parts, blk, cols = ya.shape
    width = x.shape[1]
    rows = 2 * blk
    row = lambda n: pl.BlockSpec((blk, n), lambda i, s: (i, 0))
    flat, specs = out_weights(slots, cols)
    return pl.pallas_call(
        functools.partial(attn_out_kernel, counts=[len(t) for t in slots], chips=chips, fast=fast),
        grid_spec=pltpu.PrefetchScalarGridSpec(
            num_scalar_prefetch=1,
            grid=(2,),
            in_specs=specs
            + [full_spec(ya.shape)] * 2
            + [own_rows(blk, parts, width, fast), full_spec((1, width))],
            out_specs=[row(width)] * 3 + [row(128)],
            scratch_shapes=[pltpu.VMEM((blk, width), f32)],
        ),
        out_shape=[jax.ShapeDtypeStruct((rows, width), d) for d in (f32, f32, bf16)]
        + [jax.ShapeDtypeStruct((rows, 128), f32)],
        compiler_params=params(),
    )(place, *flat, ya, yb, x, alpha)


def loss_kernel(place_ref, own_ref, got_ref, h1_ref, cot_ref, alpha_ref, hidden_ref, dmo_ref, base_ref, ga_ref, *, chips, fast):
    chip = place_ref[1]
    total = own_ref[...] + got_ref[...].astype(f32)
    alpha = alpha_ref[...]
    norm = row_norm(total)
    inner = total * norm
    h1 = h1_ref[...]
    mixed = h1 + alpha * (inner - h1)
    last = row_norm(mixed)
    hidden = mixed * last
    grad = norm_back(last, hidden, put_relative(cot_ref, chip, chips, fast).astype(f32))
    put_natural(hidden_ref, hidden.astype(bf16), chip, chips, fast)
    base_ref[...] = (1.0 - alpha) * grad
    dmo_ref[...] = norm_back(norm, inner, alpha * grad).astype(bf16)

    @pl.when(pl.program_id(0) == 0)
    def _():
        ga_ref[...] = jnp.zeros_like(ga_ref)

    ga_ref[0:1, :] += jnp.sum(grad * (inner - h1), axis=0, keepdims=True)


def loss(place, own, got, h1, cot, alpha, chips, fast):
    rows, width = own.shape
    blk = rows // 2
    row = pl.BlockSpec((blk, width), lambda i, s: (i, 0))
    part = row
    if fast:
        part = pl.BlockSpec((chips, blk, width // chips), lambda i, s: (0, i, 0))
    return pl.pallas_call(
        functools.partial(loss_kernel, chips=chips, fast=fast),
        grid_spec=pltpu.PrefetchScalarGridSpec(
            num_scalar_prefetch=1,
            grid=(rows // blk,),
            in_specs=[row] * 3 + [part, full_spec((1, width))],
            out_specs=[part] + [row] * 2 + [full_spec((8, width))],
        ),
        out_shape=[jax.ShapeDtypeStruct(cot.shape, bf16)]
        + [jax.ShapeDtypeStruct((rows, width), d) for d in (bf16, f32)]
        + [jax.ShapeDtypeStruct((8, width), f32)],
        compiler_params=params(),
    )(place, own, got, h1, cot, alpha)


def first_back_kernel(place_ref, *refs, counts, chips, fast):
    total = sum(counts)
    flat, refs = refs[:total], refs[total:]
    own_ref, got_ref, base_ref, h1_ref, ha_ref, x_ref, stat_ref, alpha_ref = refs[:8]
    do_ref, through_ref, ga_ref, dya_ref, dyb_ref = refs[8:]
    z, chip = place_ref[0], place_ref[1]
    alpha = alpha_ref[...]
    grad = base_ref[...] + own_ref[...] + got_ref[...].astype(f32)
    grad = norm_back(stat_ref[:, 1:2], h1_ref[...], grad)
    ha = ha_ref[...]
    put_natural(through_ref, ((1.0 - alpha) * grad).astype(bf16), chip, chips, fast)
    back = norm_back(stat_ref[:, 0:1], ha, alpha * grad).astype(bf16)
    do_ref[...] = back
    parts = len(counts)
    step = pl.program_id(0)
    index = 0
    for n in range(parts):
        at = lax.rem(z + parts - n, parts)
        part = jnp.zeros(dya_ref.shape[1:], f32)
        column = 0
        for piece in flat[index : index + counts[n]]:
            part += dot(do_ref[:, column : column + piece.shape[0]], piece[...])
            column += piece.shape[0]
        index += counts[n]
        part = part.astype(bf16)
        for side, ref in enumerate((dya_ref, dyb_ref)):

            @pl.when(step == side)
            def _(ref=ref, part=part, at=at):
                ref[at] = part

    @pl.when(step == 0)
    def _():
        ga_ref[...] = jnp.zeros_like(ga_ref)

    start = put_relative(x_ref, chip, chips, fast).astype(f32)
    ga_ref[0:1, :] += jnp.sum(grad * (ha - start), axis=0, keepdims=True)


def first_back(place, own, got, base, h1, ha, x, stat, alpha, slots, chips, fast, cols):
    rows, width = own.shape
    parts = len(slots)
    blk = rows // 2
    row = lambda n: pl.BlockSpec((blk, n), lambda i, s: (i, 0))
    flat, specs = out_weights(slots, cols)
    return pl.pallas_call(
        functools.partial(first_back_kernel, counts=[len(t) for t in slots], chips=chips, fast=fast),
        grid_spec=pltpu.PrefetchScalarGridSpec(
            num_scalar_prefetch=1,
            grid=(2,),
            in_specs=specs
            + [row(width)] * 5
            + [own_rows(blk, parts, width, fast), row(128), full_spec((1, width))],
            out_specs=[row(width)] * 2
            + [full_spec((8, width))]
            + [full_spec((parts, blk, cols))] * 2,
        ),
        out_shape=[jax.ShapeDtypeStruct((rows, width), bf16)] * 2
        + [jax.ShapeDtypeStruct((8, width), f32)]
        + [jax.ShapeDtypeStruct((parts, blk, cols), bf16)] * 2,
        compiler_params=params(),
    )(place, *flat, own, got, base, h1, ha, x, stat, alpha)


def fetch_weights(q, slots, wbuf, sems):
    def copies(j):
        at = 0
        found = []
        for p, piece in enumerate(slots[j]):
            size = piece.shape[0]
            found.append(
                pltpu.make_async_copy(
                    piece.at[:, : wbuf.shape[2]], wbuf.at[j % 2, at : at + size, :], sems.at[j % 2, p]
                )
            )
            at += size
        return found

    for j in range(len(slots)):

        @pl.when(q == j)
        def _(j=j):
            if j == 0:
                for copy in copies(0):
                    copy.start()
            if j + 1 < len(slots):
                for copy in copies(j + 1):
                    copy.start()
            for copy in copies(j):
                copy.wait()


def mlp_fwd_kernel(*refs, half, counts):
    total = sum(counts)
    flat, refs = refs[:total], refs[total:]
    slots, at = [], 0
    for n in counts:
        slots.append(flat[at : at + n])
        at += n
    ha_ref, hb_ref, suv_ref, act_ref, uv_ref, own_ref, got_ref, acc, wbuf, sems = refs
    rows = ha_ref.shape[0]
    q = pl.program_id(0)

    @pl.when(q == 0)
    def _():
        own_ref[...] = jnp.zeros_like(own_ref)
        acc[...] = jnp.zeros_like(acc)

    fetch_weights(q, slots, wbuf, sems)
    w = wbuf.at[lax.rem(q, 2)]
    for base, h_ref, sum_ref in ((0, ha_ref, own_ref), (rows, hb_ref, acc)):
        at = slice(base, base + rows)
        pair = dot(h_ref[...], w[:, : 2 * half])
        lifted = pair[:, :half] * suv_ref[0:1, :]
        gated = pair[:, half:] * suv_ref[1:2, :]
        act = (lifted * gated * jax.nn.sigmoid(gated)).astype(bf16)
        uv_ref[at, :] = pair.astype(bf16)
        act_ref[at, :] = act
        sum_ref[...] += dot_t(act, w[:, 2 * half : 3 * half])

    @pl.when(q == pl.num_programs(0) - 1)
    def _():
        got_ref[...] = acc[...].astype(bf16)


def mlp_fwd(ha, hb, slots, suv):
    rows, width = ha.shape
    parts, _, half = suv.shape
    take = lambda n: pl.BlockSpec((None, 2 * rows, n), lambda q: (q, 0, 0))
    whole = full_spec((rows, width))
    anywhere = pl.BlockSpec(memory_space=pl.ANY)
    flat = [p for slot in slots for p in slot]
    return pl.pallas_call(
        functools.partial(mlp_fwd_kernel, half=half, counts=[len(s) for s in slots]),
        grid=(parts,),
        in_specs=[anywhere] * len(flat)
        + [whole, whole, pl.BlockSpec((None, 2, half), lambda q: (q, 0, 0))],
        out_specs=[take(half), take(2 * half), whole, whole],
        out_shape=[
            jax.ShapeDtypeStruct((parts, 2 * rows, half), bf16),
            jax.ShapeDtypeStruct((parts, 2 * rows, 2 * half), bf16),
            jax.ShapeDtypeStruct((rows, width), f32),
            jax.ShapeDtypeStruct((rows, width), bf16),
        ],
        scratch_shapes=[
            pltpu.VMEM((rows, width), f32),
            pltpu.VMEM((2, width, 3 * half), bf16),
            pltpu.SemaphoreType.DMA((2, max(len(s) for s in slots))),
        ],
        compiler_params=params(),
    )(*flat, ha, hb, suv)


def mlp_bwd_kernel(*refs, half, counts):
    total = sum(counts)
    flat, refs = refs[:total], refs[total:]
    slots, at = [], 0
    for n in counts:
        slots.append(flat[at : at + n])
        at += n
    da_ref, db_ref, uv_ref, suv_ref, duv_ref, own_ref, got_ref, gs_ref, acc, wbuf, sems = refs
    rows = da_ref.shape[0]
    q = pl.program_id(0)

    @pl.when(q == 0)
    def _():
        own_ref[...] = jnp.zeros_like(own_ref)
        acc[...] = jnp.zeros_like(acc)

    gs_ref[...] = jnp.zeros_like(gs_ref)
    fetch_weights(q, slots, wbuf, sems)
    w = wbuf.at[lax.rem(q, 2)]
    for base, d_ref, sum_ref in ((0, da_ref, own_ref), (rows, db_ref, acc)):
        at = slice(base, base + rows)
        grad = dot(d_ref[...], w[:, 2 * half : 3 * half])
        up = uv_ref[at, :half].astype(f32)
        gate = uv_ref[at, half:].astype(f32)
        su = suv_ref[0:1, :]
        sv = suv_ref[1:2, :]
        lifted = up * su
        gated = gate * sv
        sigma = jax.nn.sigmoid(gated)
        da = grad * gated * sigma
        db = grad * lifted * sigma * (1.0 + gated * (1.0 - sigma))
        gs_ref[0:1, :] += jnp.sum(da * up, axis=0, keepdims=True)
        gs_ref[1:2, :] += jnp.sum(db * gate, axis=0, keepdims=True)
        duv_ref[at, :half] = (da * su).astype(bf16)
        duv_ref[at, half:] = (db * sv).astype(bf16)
        sum_ref[...] += dot_t(duv_ref[at, :], w[:, : 2 * half])

    @pl.when(q == pl.num_programs(0) - 1)
    def _():
        got_ref[...] = acc[...].astype(bf16)


def mlp_bwd(da, db, slots, uv, suv):
    rows, width = da.shape
    parts, _, half = suv.shape
    take = lambda n: pl.BlockSpec((None, 2 * rows, n), lambda q: (q, 0, 0))
    whole = full_spec((rows, width))
    anywhere = pl.BlockSpec(memory_space=pl.ANY)
    flat = [p for slot in slots for p in slot]
    return pl.pallas_call(
        functools.partial(mlp_bwd_kernel, half=half, counts=[len(s) for s in slots]),
        grid=(parts,),
        in_specs=[anywhere] * len(flat)
        + [
            whole,
            whole,
            take(2 * half),
            pl.BlockSpec((None, 2, half), lambda q: (q, 0, 0)),
        ],
        out_specs=[
            take(2 * half),
            whole,
            whole,
            pl.BlockSpec((None, 8, half), lambda q: (q, 0, 0)),
        ],
        out_shape=[
            jax.ShapeDtypeStruct((parts, 2 * rows, 2 * half), bf16),
            jax.ShapeDtypeStruct((rows, width), f32),
            jax.ShapeDtypeStruct((rows, width), bf16),
            jax.ShapeDtypeStruct((parts, 8, half), f32),
        ],
        scratch_shapes=[
            pltpu.VMEM((rows, width), f32),
            pltpu.VMEM((2, width, 3 * half), bf16),
            pltpu.SemaphoreType.DMA((2, max(len(s) for s in slots))),
        ],
        compiler_params=params(),
    )(*flat, da, db, uv, suv)


EXTRA = 16


def grad_kernel(place_ref, *refs, orders, parts, chunk, more):
    ha_ref, hb_ref = refs[:2]
    refs = refs[2:]
    if more:
        oa_ref, ob_ref, ya_ref, yb_ref, extra_ref = refs[:5]
        refs = refs[5:]
    val_ref, *outs = refs[:5]
    turned = refs[5]
    rows = ha_ref.shape[0]
    k = pl.program_id(0)

    @pl.when(k == 0)
    def _():
        turned[:, :rows] = ha_ref[...].T
        turned[:, rows:] = hb_ref[...].T
        if more:
            refs[6][:, :rows] = oa_ref[...].T
            refs[6][:, rows:] = ob_ref[...].T

    for side in range(2):

        @pl.when((k < parts // 2) == (side == 0))
        def _(side=side):
            for which, ref in zip(orders[side], outs[2 * side : 2 * side + 2]):
                for j, r in enumerate(which):
                    at = slice(r * chunk, (r + 1) * chunk)
                    value = dot(turned[at, :], val_ref[...]).astype(bf16)
                    size = value.shape[1]
                    ref[j, :chunk, :size] = value
                    if more:
                        ref[j, :chunk, size:] = (
                            dot(refs[6][at, :rows], ya_ref[...]) + dot(refs[6][at, rows:], yb_ref[...])
                        ).astype(bf16)
                        ref[j, chunk:, :] = extra_ref[...].astype(bf16)


def weight_grads(place, sends, keeps, chips, hs, value, os=None, ys=None, extra=None):
    rows, width = hs[0].shape
    chunk = width // chips
    parts, _, size = value.shape
    more = os is not None
    hc = ys[1].shape[2] if more else 0
    tall = chunk + (EXTRA if more else 0)
    middle = parts // 2
    if chunk % 128:
        result = []
        for which, lo in ((sends[0], 0), (keeps[0], 0), (sends[1], middle), (keeps[1], middle)):
            cut = lambda pair: jnp.concatenate(
                [jnp.concatenate(pair, axis=0)[:, r * chunk : (r + 1) * chunk] for r in which], axis=1
            )
            found = []
            for k in range(lo, lo + middle):
                one = t_dot(cut(hs), value[k])
                if more:
                    at = (place[0] - k) % parts
                    y = lax.dynamic_index_in_dim(ys[0], at, 0, keepdims=False)
                    y = lax.dynamic_slice_in_dim(y, place[2] * hc, hc, 1)
                    y = jnp.concatenate([y, lax.dynamic_index_in_dim(ys[1], at, 0, keepdims=False)])
                    one = jnp.concatenate([one, t_dot(cut(os), y)], axis=1)
                one = one.reshape(len(which), chunk, size + hc)
                if more:
                    wide = jnp.broadcast_to(extra[k][None], (len(which), EXTRA, size + hc))
                    one = jnp.concatenate([one, wide], axis=1)
                found.append(one.astype(bf16))
            result.append(jnp.stack(found, axis=1))
        return [result[0], result[2]], [result[1], result[3]]
    whole = full_spec((rows, width))
    ins = list(hs)
    in_specs = [whole] * 2
    scratch = [pltpu.VMEM((width, 2 * rows), bf16)]
    if more:
        slot = lambda k, p: lax.rem(p[0] + parts - k, parts)
        ins += [*os, ys[0], ys[1], extra]
        in_specs += [whole] * 2
        in_specs += [
            pl.BlockSpec((None, rows, hc), lambda k, p: (slot(k, p), 0, p[2])),
            pl.BlockSpec((None, rows, hc), lambda k, p: (slot(k, p), 0, 0)),
            pl.BlockSpec((None, EXTRA, size + hc), lambda k, p: (k, 0, 0)),
        ]
        scratch = scratch * 2
    ins.append(value)
    in_specs.append(pl.BlockSpec((None, 2 * rows, size), lambda k, p: (k, 0, 0)))
    lists = [sends[0], keeps[0], sends[1], keeps[1]]
    block = lambda one: (len(one), None, tall, size + hc)
    early = lambda k, p: (0, jnp.minimum(k, middle - 1), 0, 0)
    late = lambda k, p: (0, jnp.maximum(k - middle, 0), 0, 0)
    out = pl.pallas_call(
        functools.partial(
            grad_kernel, orders=(lists[:2], lists[2:]), parts=parts, chunk=chunk, more=more
        ),
        grid_spec=pltpu.PrefetchScalarGridSpec(
            num_scalar_prefetch=1,
            grid=(parts,),
            in_specs=in_specs,
            out_specs=[
                pl.BlockSpec(block(one), early if n < 2 else late) for n, one in enumerate(lists)
            ],
            scratch_shapes=scratch,
        ),
        out_shape=[
            jax.ShapeDtypeStruct((len(one), middle, tall, size + hc), bf16) for one in lists
        ],
        compiler_params=params(),
    )(place, *ins)
    return [out[0], out[2]], [out[1], out[3]]


def adam_values(weight, grad, first, second):
    first_new = beta_one * first + (1.0 - beta_one) * grad
    second_new = beta_two * second + (1.0 - beta_two) * grad * grad
    moved = weight - learn_rate * (first_new / bias_one) / (
        jnp.sqrt(second_new / bias_two) + adam_eps
    )
    return first_new, second_new, moved


def lane_sums(value):
    ones = jnp.ones((8, value.shape[1]), bf16)
    high = value.astype(bf16)
    low = (value - high.astype(f32)).astype(bf16)
    return dot_t(ones, high) + dot_t(ones, low)


def adam_wide_kernel(w_ref, g_ref, m_ref, v_ref, g_out, m_out, v_out, n_out, s_out):
    cols = w_ref.shape[2]
    for c in range(w_ref.shape[1]):
        grad = g_ref[:, c * cols : (c + 1) * cols]
        first, second, moved = adam_values(w_ref[:, c, :], grad, m_ref[:, c, :], v_ref[:, c, :])
        g_out[:, c, :] = grad
        m_out[:, c, :] = first
        v_out[:, c, :] = second
        n_out[:, c, :] = moved
        s_out[c : c + 1, :] = jnp.sum(moved * moved, axis=0, keepdims=True)


def adam_wide(w, g, m, v):
    vmem = pl.BlockSpec(memory_space=pltpu.VMEM)
    return pl.pallas_call(
        adam_wide_kernel,
        in_specs=[vmem] * 4,
        out_specs=[vmem] * 5,
        out_shape=[jax.ShapeDtypeStruct(w.shape, f32)] * 4
        + [jax.ShapeDtypeStruct(w.shape[1:], f32)],
        compiler_params=params(),
    )(w, g, m, v)


def adam_tall_kernel(w_ref, g_ref, m_ref, v_ref, g_out, m_out, v_out, n_out, s_out):
    grad = g_ref[...].T
    first, second, moved = adam_values(w_ref[...], grad, m_ref[...], v_ref[...])
    g_out[...] = grad
    m_out[...] = first
    v_out[...] = second
    n_out[...] = moved
    s_out[...] = lane_sums(moved * moved)


def adam_tall(w, g, m, v):
    vmem = pl.BlockSpec(memory_space=pltpu.VMEM)
    return pl.pallas_call(
        adam_tall_kernel,
        in_specs=[vmem] * 4,
        out_specs=[vmem] * 5,
        out_shape=[jax.ShapeDtypeStruct(w.shape, f32)] * 4
        + [jax.ShapeDtypeStruct((8, w.shape[0]), f32)],
        compiler_params=params(),
    )(w, g, m, v)


def scale_kernel(na_ref, nb_ref, nc_ref, nd_ref, a_ref, b_ref, c_ref, d_ref, ao_ref, bo_ref, co_ref, do_ref, *, width):
    factor = lambda value: lax.rsqrt(value / width + layer_eps)
    for norm, ref, out in ((na_ref, a_ref, ao_ref), (nc_ref, c_ref, co_ref)):
        for c in range(ref.shape[1]):
            out[:, c, :] = ref[:, c, :] * factor(norm[c : c + 1, :])
    for norm, ref, out in ((nb_ref, b_ref, bo_ref), (nd_ref, d_ref, do_ref)):
        out[...] = ref[...] * factor(norm[...]).T[:, 0:1]


def scale_weights(norms, weights, width):
    vmem = pl.BlockSpec(memory_space=pltpu.VMEM)
    return pl.pallas_call(
        functools.partial(scale_kernel, width=width),
        in_specs=[vmem] * 8,
        out_specs=[vmem] * 4,
        out_shape=[jax.ShapeDtypeStruct(w.shape, f32) for w in weights],
        compiler_params=params(),
    )(*norms, *weights)


def after(value, *others):
    return lax.optimization_barrier((value, *others))[0]


def per_device(
    layer_input,
    cotangent,
    positions,
    w_qkv,
    w_out,
    w_up,
    w_down,
    moment_qkv,
    moment_out,
    moment_up,
    moment_down,
    square_qkv,
    square_out,
    square_up,
    square_down,
    s_qk,
    alpha_attn,
    alpha_mlp,
    s_uv,
):
    nz = lax.axis_size("head")
    nb = lax.axis_size("batch")
    z = lax.axis_index("head")
    b = lax.axis_index("batch")
    core = b % 2
    chip = b // 2
    chips = nb // 2
    bits = [1 << n for n in range(int(math.log2(chips)))]
    rows, cols = layer_input.shape
    width = cols * nz
    own = rows // nz
    hid = w_down.shape[0]
    half = hid // 2
    hc = cols // 2
    heads = cols // HEAD_DIM
    span = w_qkv.shape[0]
    chunk = width // chips
    core_s = core.reshape(1).astype(jnp.int32)
    place = jnp.stack([z, chip, core]).astype(jnp.int32)
    fast = chunk == cols and chunk % 128 == 0

    def swap_batch(value, bit):
        return lax.ppermute(value, "batch", [(i, i ^ bit) for i in range(nb)])

    def swap_core(value):
        return swap_batch(value, 1)

    def swap_chip(value, bit):
        return swap_batch(value, 2 * bit)

    def onward(value, k=1):
        return lax.ppermute(value, "head", [(i, (i + k) % nz) for i in range(nz)])

    def exchange(value):
        return lax.all_to_all(value, "head", split_axis=0, concat_axis=0)

    def pick(pair, index):
        return jnp.where(index == 0, pair[0], pair[1])

    def relative(value):
        return jnp.concatenate(
            [
                lax.dynamic_slice_in_dim(value, (chip ^ r) * chunk, chunk, value.ndim - 1)
                for r in range(chips)
            ],
            axis=-1,
        )

    def spread(value):
        if chips <= 4:
            return [value] + [swap_chip(value, r) for r in range(1, chips)]
        for bit in bits:
            value = jnp.concatenate([value, swap_chip(value, bit)], axis=0)
        return [value]

    tokens = [layer_input, onward(layer_input)]
    mine, theirs, qkv_own = pack(core_s, w_up, w_down, w_out, w_qkv)
    qkv_full = lax.all_gather(qkv_own, "batch", axis=0, tiled=True)
    theirs = swap_core(theirs)
    packet = jnp.concatenate([pick((mine, theirs), core), pick((theirs, mine), core)], axis=0)
    tokens[1], packet, places, s_uv, alpha_attn, alpha_mlp = lax.optimization_barrier(
        (tokens[1], packet, positions, s_uv, alpha_attn, alpha_mlp)
    )

    suv_own = pick((s_uv[:, :half], s_uv[:, half:]), core)
    freqs = jnp.exp(
        (jnp.arange(128) % (HEAD_DIM // 2)).astype(f32) * (-2.0 * math.log(10000.0) / HEAD_DIM)
    )
    phase = places.astype(f32)[:, None] * freqs[None, :]
    side = jnp.where(jnp.arange(128) % HEAD_DIM < HEAD_DIM // 2, -1.0, 1.0).astype(f32)
    cosine, sine = jnp.cos(phase), jnp.sin(phase) * side[None, :]
    lane = jnp.arange(cols) // HEAD_DIM
    ones = (lane[:, None] == lane[None, :]).astype(bf16)
    gain = s_qk.reshape(1, cols)
    is_long = (places[SHORT : SHORT + 1] != 0).astype(jnp.int32)
    attn_gain = relative(alpha_attn[None])
    mlp_gain = relative(alpha_mlp[None])

    suv = jnp.stack([suv_own] + [onward(suv_own, n) for n in range(1, nz)])
    hops = [packet]
    slots = [spread(packet)]
    for n in range(2, nz):
        tokens.append(onward(tokens[-1]))
        hops.append(onward(hops[-1]))
        tokens[-1], hops[-1], cosine, sine, ones, attn_gain, mlp_gain, suv, *last = lax.optimization_barrier(
            (tokens[-1], hops[-1], cosine, sine, ones, attn_gain, mlp_gain, suv, *slots[-1])
        )
        slots[-1] = list(last)
        slots.append(spread(hops[-1]))
    hops.append(onward(hops[-1]))

    blocks = rows // 512
    middle = blocks // 2
    tokens_full, q, k, v, rho = qkv_project(place, tokens, qkv_full, cosine, sine, gain, ones)
    y_a, logs_a = attn_fwd(is_long, q, k, v, 0, middle)
    q_b, hops[-1] = lax.optimization_barrier((after(q, y_a), hops[-1]))
    y_b, logs_b = attn_fwd(is_long, q_b, k, v, middle, blocks - middle)
    y_one = exchange(y_a.reshape(nz, own // 2, cols))
    y_in, y_one = lax.optimization_barrier((y_b, y_one))
    y_two = exchange(y_in.reshape(nz, own // 2, cols))
    hop = after(hops[-1], y_b)
    slots.append(spread(hop))
    flat = lambda value: value.transpose(1, 0, 2).reshape(own, width)
    start = tokens_full
    if not fast:
        start = jnp.concatenate(
            [
                lax.dynamic_slice_in_dim(tokens_full, h * (rows // 2) + z * (own // 2), own // 2, 0)
                for h in range(2)
            ]
        )
        start = relative(start)
    hA, h1, h_own, stat = attn_out(place, y_one, y_two, slots, start, attn_gain, chips, fast)
    h_got = swap_core(h_own)
    cot = after(cotangent, h_own).reshape(2, nz, own // 2, cols).transpose(1, 0, 2, 3)
    cot = exchange(cot.reshape(nz, own, cols))

    act, uv, mo_own, mo_other = mlp_fwd(h_own, h_got, slots, suv)
    mo_got = swap_core(mo_other)
    if not fast:
        cot = relative(flat(cot))
    hidden, d_own, base, ga_mlp = loss(place, mo_own, mo_got, h1, cot, mlp_gain, chips, fast)
    d_got = swap_core(d_own)
    if not fast:
        hidden = relative(hidden).reshape(own, nz, cols).transpose(1, 0, 2)
    hidden = exchange(hidden)

    orders = [bits, bits[::-1]]
    sent_at = [[r for r in range(chips) if r & order[0]] for order in orders]
    kept_at = [[r for r in range(chips) if not r & order[0]] for order in orders]

    def second(kept, sent):
        found, sends = [], []
        for order, left, got, keep in zip(orders, kept_at, sent, kept):
            for bit in order[1:]:
                send_at = [n for n, r in enumerate(left) if r & bit]
                keep_at = [n for n, r in enumerate(left) if not r & bit]
                left = [left[n] for n in keep_at]
                cut = lambda v, at: jnp.concatenate([v[n : n + 1] for n in at], axis=0).astype(f32)
                send = (cut(keep, send_at) + cut(got, send_at)).astype(bf16)
                keep = cut(keep, keep_at) + cut(got, keep_at)
                got = swap_chip(send, bit)
                sends.append(send)
            found.append((keep, got))
        return found, sends

    def slot_sums(found):
        return [(keep[0, n] + got[0, n].astype(f32)) for keep, got in found for n in range(nz // 2)]

    down_made, down_kept = weight_grads(place, sent_at, kept_at, chips, (d_own, d_got), act)
    down_sent = [swap_chip(one, order[0]) for one, order in zip(down_made, orders)]
    d_own, d_got, *_ = lax.optimization_barrier((d_own, d_got, *down_made))
    duv, dh_own, dh_other, gsuv = mlp_bwd(d_own, d_got, slots, uv, suv)
    dh_got = swap_core(dh_other)
    dh_own, hidden, *down_sent = lax.optimization_barrier((dh_own, hidden, *down_sent))
    do_own, through, ga_attn, dy_a, dy_b = first_back(
        place, dh_own, dh_got, base, h1, hA, start, stat, attn_gain, slots, chips, fast, cols
    )
    dy_b = exchange(dy_b)
    do_got = swap_core(do_own)
    y_mine = jnp.concatenate([y_one, y_two], axis=1)
    y_got = swap_core(lax.dynamic_slice_in_dim(after(y_mine, h_own), (1 - core) * hc, hc, 2))
    down_sent = [after(one, do_own) for one in down_sent]
    down_part, down_next = second(down_kept, down_sent)

    alphas = [relative(ga_attn[0:1]), relative(ga_mlp[0:1])]
    extra = []
    wide = 2 * half + hc
    fill = lambda r: jnp.pad(r, ((0, 0), (0, wide - r.shape[1])))
    for n in range(nz):
        at = ((z - n) % nz) * cols
        line = jnp.concatenate([lax.dynamic_slice_in_dim(g, at, cols, 1) for g in alphas], axis=1)
        first = gsuv[n, :2].reshape(1, 2 * half)
        extra.append(jnp.pad(jnp.concatenate([fill(first), fill(line)]), ((0, EXTRA - 2), (0, 0))))
    extra = jnp.stack(extra)
    h_own, *_ = lax.optimization_barrier((h_own, *down_next))
    up_made, up_kept = weight_grads(
        place, sent_at, kept_at, chips, (h_own, h_got), duv, (do_own, do_got), (y_mine, y_got), extra
    )
    dy_b, dy_a, *up_made = lax.optimization_barrier((dy_b, dy_a, *up_made))
    up_sent = [swap_chip(one, order[0]) for one, order in zip(up_made, orders)]

    dy_a = exchange(dy_a)
    common = lambda dy, y, logs: (
        is_long, q, k, v, dy.reshape(y.shape), y, logs, rho, cosine, sine, gain, ones
    )
    dqkv_b, dk_part, dv_part, sqk_b = attn_bwd(
        *common(dy_b, y_b, logs_b), middle, blocks - middle, None
    )

    if not fast:
        through = relative(through)
    through = through.astype(f32)

    def input_part(dqkv, side):
        part = dot_t(dqkv, qkv_full)
        mine_at = z * (own // 2)
        here = lax.dynamic_slice_in_dim(part, mine_at, own // 2, 0)
        here = here + through[side * (own // 2) : (side + 1) * (own // 2)]
        return lax.dynamic_update_slice_in_dim(part.astype(bf16), here.astype(bf16), mine_at, 0)

    dqkv_b, dk_part, dy_a = lax.optimization_barrier((dqkv_b, dk_part, dy_a))
    part_b = input_part(dqkv_b, 1)
    cut = lambda n: lax.dynamic_slice_in_dim(part_b, ((z + n) % nz) * cols, cols, 1)
    part_cuts = [cut(n) for n in range(nz)]
    down_part = [(keep, after(got, dqkv_b)) for keep, got in down_part]
    down_slots = slot_sums(down_part)
    up_part, up_next = second(up_kept, [after(one, dqkv_b) for one in up_sent])
    part_got = [onward(part_cuts[n], n) for n in range(1, nz)]
    dk_part, dy_a, *_ = lax.optimization_barrier((dk_part, dy_a, *up_next, *part_cuts, *down_slots))
    dqkv_a, sqk_a = attn_bwd(*common(dy_a, y_a, logs_a), 0, middle, [dk_part, dv_part])
    part_got = [after(one, dqkv_a) for one in part_got]
    input_b = part_cuts[0].astype(f32) + sum(one.astype(f32) for one in part_got)
    up_part = [(keep, after(got, dqkv_a)) for keep, got in up_part]
    input_a = lax.psum_scatter(input_part(dqkv_a, 0), "head", scatter_dimension=1, tiled=True)
    down_along = [onward(after(down_slots[n].astype(bf16), input_b), nz - n) for n in range(1, nz)]
    sum_down_t = down_slots[0] + sum(one.astype(f32) for one in down_along)
    up_slots = slot_sums(up_part)
    passed = onward(up_slots[1].astype(bf16))
    for n in range(2, nz):
        passed = onward((up_slots[n] + passed.astype(f32)).astype(bf16))
    sum_up_t = up_slots[0] + passed.astype(f32)
    input_grad = jnp.concatenate([input_a.astype(f32), input_b], axis=0)
    hidden_t = hidden.reshape(nz, 2, own // 2, cols).transpose(1, 0, 2, 3).reshape(rows, cols)

    dqkv = jnp.concatenate([dqkv_a, dqkv_b], axis=0)
    grad_qkv = t_dot(tokens_full, dqkv).astype(bf16)
    sqk = jnp.pad((sqk_a + sqk_b), ((0, EXTRA - 8), (0, 2 * cols)))
    shard = [lax.dynamic_slice_in_dim(grad_qkv, (b ^ r) * span, span, 0) for r in range(nb)]
    shard = [jnp.concatenate([s, sqk.astype(bf16)], axis=0) for s in shard]
    qbits = [1 << n for n in range(int(math.log2(nb)))]
    held = {r: shard[r] for r in range(nb)}
    for bit in qbits:
        send_at = [r for r in held if r & bit]
        send = jnp.concatenate([held[r] for r in send_at], axis=0).astype(bf16)
        got = swap_batch(send, bit)
        size = span + EXTRA
        held = {
            r ^ bit: held[r ^ bit].astype(f32) + got[n * size : (n + 1) * size].astype(f32)
            for n, r in enumerate(send_at)
        }
    cell = width // (nz * nb)
    sum_sqk = lax.dynamic_slice_in_dim(held[0][span, :cols], b * cell, cell, 0)
    qkv_new = adam_wide(w_qkv, held[0][:span], moment_qkv, square_qkv)

    def both_halves(total):
        two = (total[:span], total[span : 2 * span])
        here = jnp.concatenate([pick(two, core), total[2 * span :]], axis=0)
        there = jnp.concatenate([pick(two, 1 - core), total[2 * span :]], axis=0)
        there = swap_core(there.astype(bf16)).astype(f32)
        return [pick((here, there), core), pick((there, here), core)]

    join = lambda halves, at, size: [p[:span, at : at + size] for p in halves]
    halves = both_halves(sum_down_t)
    down_new = adam_tall(w_down, jnp.concatenate(join(halves, 0, half), axis=1), moment_down, square_down)
    halves = both_halves(sum_up_t)
    grad_up = jnp.concatenate(join(halves, 0, half) + join(halves, half, half), axis=1)
    up_new = adam_wide(w_up, grad_up, moment_up, square_up)
    out_new = adam_tall(w_out, jnp.concatenate(join(halves, 2 * half, hc), axis=1), moment_out, square_out)
    suv_rows = jnp.stack(
        [jnp.concatenate([p[span, c * half : (c + 1) * half] for p in halves]) for c in range(2)]
    )
    sum_suv = lax.dynamic_slice_in_dim(suv_rows, b * (hid // nb), hid // nb, 1)
    alphas = halves[0][span + 1] + halves[1][span + 1]
    sum_attn = lax.dynamic_slice_in_dim(alphas[:cols], b * cell, cell, 0)
    sum_mlp = lax.dynamic_slice_in_dim(alphas[cols : 2 * cols], b * cell, cell, 0)

    hidden = hidden_t.astype(f32)

    squares = [qkv_new[4], out_new[4][:1], up_new[4], down_new[4][:1]]
    sizes = [t.size for t in squares]
    norms = jnp.concatenate([t.reshape(-1) for t in squares]).reshape(-1, 128)
    for bit in qbits:
        norms = norms + swap_batch(norms, bit)
    norms = norms.reshape(-1)
    ends = [0] + [sum(sizes[: n + 1]) for n in range(4)]
    back = lambda n, shape: norms[ends[n] : ends[n + 1]].reshape(shape)
    eight = lambda value: jnp.broadcast_to(value, (8, value.shape[1]))
    new_qkv, new_out, new_up, new_down = scale_weights(
        [back(0, (3, cols)), eight(back(1, (1, cols))), back(2, (2, hid)), eight(back(3, (1, hid)))],
        [qkv_new[3], out_new[3], up_new[3], down_new[3]],
        width,
    )
    sum_qkv, first_a, second_a = qkv_new[:3]
    sum_out, first_b, second_b = out_new[:3]
    sum_up, first_c, second_c = up_new[:3]
    sum_down, first_d, second_d = down_new[:3]
    return (
        hidden,
        input_grad,
        sum_qkv,
        sum_out,
        sum_up,
        sum_down,
        first_a,
        first_b,
        first_c,
        first_d,
        second_a,
        second_b,
        second_c,
        second_d,
        new_qkv,
        new_out,
        new_up,
        new_down,
        sum_sqk,
        sum_attn,
        sum_mlp,
        sum_suv,
    )


def solution(mesh):
    tokens = P("batch", "head")
    wide = P("batch", None, "head")
    tall = P("head", "batch")
    flat = P(("head", "batch"))
    weights = (wide, tall, wide, tall)
    return jax.shard_map(
        per_device,
        mesh=mesh,
        in_specs=(tokens, tokens, P("batch"))
        + weights * 3
        + (P("head"), P(), P(), P(None, "head")),
        out_specs=(tokens, tokens) + weights * 4 + (flat, flat, flat, P(None, ("head", "batch"))),
        check_vma=False,
    )
```

```python
import functools
import math

import jax
import jax.numpy as jnp
from jax import lax
from jax.experimental import pallas as pl
from jax.experimental.pallas import tpu as pltpu
from jax.sharding import PartitionSpec as P

HEAD_DIM = 64
SHORT = 1024

layer_eps = 1e-06
learn_rate = 0.008
beta_one = 0.9
beta_two = 0.95
adam_eps = 1e-08
bias_one = 1.0 - math.exp(100.0 * math.log(0.9))
bias_two = 1.0 - math.exp(100.0 * math.log(0.95))
score_scale = 8.0
LOG2E = math.log2(math.e)
LN2 = math.log(2.0)

bf16 = jnp.bfloat16
f32 = jnp.float32
VMEM_LIMIT = 56 * 1024 * 1024


def dot(a, b):
    return jnp.dot(a, b, preferred_element_type=f32)


def dot_t(a, b):
    return lax.dot_general(a, b, (((1,), (1,)), ((), ())), preferred_element_type=f32)


def t_dot(a, b):
    return lax.dot_general(a, b, (((0,), (0,)), ((), ())), preferred_element_type=f32)


def params():
    return pltpu.CompilerParams(vmem_limit_bytes=VMEM_LIMIT)


def full_spec(shape):
    return pl.BlockSpec(shape, lambda *_: (0,) * len(shape))


def head_sum(value, ones):
    high = value.astype(bf16)
    low = (value - high.astype(f32)).astype(bf16)
    return dot(high, ones) + dot(low, ones)


def widen(value, cols):
    return jnp.concatenate([value] * (cols // value.shape[1]), axis=1)


def swap_halves(value):
    cols = value.shape[-1]
    half = HEAD_DIM // 2
    lane = lax.broadcasted_iota(jnp.int32, value.shape, 1)
    first = (lane % HEAD_DIM) < half
    up = pltpu.roll(value, cols - half, 1)
    down = pltpu.roll(value, half, 1)
    return jnp.where(first, up, down)


def qkv_kernel(place_ref, *refs, parts):
    tokens = refs[:parts]
    w_ref, cos_ref, sin_ref, gain_ref, ones_ref, x_ref, q_ref, k_ref, v_ref, rho_ref = refs[parts:]
    cols = v_ref.shape[1]
    z = place_ref[0]
    for n in range(parts):
        at = pl.multiple_of(lax.rem(z + parts - n, parts) * cols, cols)
        x_ref[:, pl.ds(at, cols)] = tokens[n][...]
    proj = dot(x_ref[...], w_ref[...])
    cosine = widen(cos_ref[...], cols)
    sine = widen(sin_ref[...], cols)
    ones = ones_ref[...]
    gain = gain_ref[...]
    heads = cols // HEAD_DIM
    lane = lax.broadcasted_iota(jnp.int32, rho_ref.shape, 1)
    stats = jnp.zeros(rho_ref.shape, f32)
    for c, (out, scale) in enumerate(((q_ref, score_scale * LOG2E), (k_ref, 1.0))):
        part = proj[:, c * cols : (c + 1) * cols]
        rho = lax.rsqrt(head_sum(part * part, ones) + layer_eps)
        rot = part * cosine + swap_halves(part) * sine
        out[...] = (rot * rho * (gain * scale)).astype(bf16)
        for h in range(heads):
            stats = jnp.where(lane == c * heads + h, rho[:, h * HEAD_DIM : h * HEAD_DIM + 1], stats)
    rho_ref[...] = stats
    v_ref[...] = proj[:, 2 * cols :].astype(bf16)


def qkv_project(place, tokens, w, cosine, sine, gain, ones):
    rows, cols = tokens[0].shape
    parts = len(tokens)
    width = parts * cols
    blk = 512
    row = lambda n: pl.BlockSpec((blk, n), lambda i, s: (i, 0))
    return pl.pallas_call(
        functools.partial(qkv_kernel, parts=parts),
        grid_spec=pltpu.PrefetchScalarGridSpec(
            num_scalar_prefetch=1,
            grid=(rows // blk,),
            in_specs=[row(cols)] * parts
            + [full_spec((width, 3 * cols)), row(128), row(128)]
            + [full_spec((1, cols)), full_spec((cols, cols))],
            out_specs=[row(width)] + [row(cols)] * 3 + [row(128)],
        ),
        out_shape=[jax.ShapeDtypeStruct((rows, width), bf16)]
        + [jax.ShapeDtypeStruct((rows, cols), bf16)] * 3
        + [jax.ShapeDtypeStruct((rows, 128), f32)],
        compiler_params=params(),
    )(place, *tokens, w, cosine, sine, gain, ones)


def head_masks(cols, heads):
    lane = lax.broadcasted_iota(jnp.int32, (1, cols), 1) // HEAD_DIM
    return [(lane == h) for h in range(heads)]


def masked(value, mask):
    return jnp.where(mask, value, jnp.zeros_like(value))


def attn_fwd_kernel(long_ref, q_ref, k_ref, v_ref, y_ref, l_ref, acc, mass, *, heads, blk, sub, first):
    i = first + pl.program_id(0)
    cols = q_ref.shape[1]
    masks = head_masks(cols, heads)
    per = SHORT // blk
    low = jnp.where(long_ref[0] != 0, 0, (i // per) * per)
    acc[...] = jnp.zeros_like(acc)
    mass[...] = jnp.zeros_like(mass)

    def lanes(p):
        total = p[:, 0:128]
        for n in range(1, p.shape[1] // 128):
            total = total + p[:, n * 128 : (n + 1) * 128]
        return total

    def body(j, carry):
        start = pl.multiple_of(j * blk, blk)
        keys = k_ref[pl.ds(start, blk), :]
        vals = v_ref[pl.ds(start, blk), :]
        q = q_ref[...]
        total = jnp.zeros(acc.shape, f32)
        for h in range(heads):
            p = jnp.exp2(dot_t(masked(q, masks[h]), keys))
            mass[h] += lanes(p)
            total += dot(p.astype(bf16), masked(vals, masks[h]))
        acc[...] += total
        return carry

    lax.fori_loop(low, i, body, 0)
    start = pl.multiple_of(i * blk, blk)
    causal = lax.broadcasted_iota(jnp.int32, (sub, sub), 0) >= lax.broadcasted_iota(
        jnp.int32, (sub, sub), 1
    )
    for a in range(blk // sub):
        rows = slice(a * sub, (a + 1) * sub)
        q = q_ref[rows, :]
        for b in range(a + 1):
            at = pl.multiple_of(start + b * sub, sub)
            keys = k_ref[pl.ds(at, sub), :]
            vals = v_ref[pl.ds(at, sub), :]
            total = jnp.zeros((sub, cols), f32)
            for h in range(heads):
                p = jnp.exp2(dot_t(masked(q, masks[h]), keys))
                if a == b:
                    p = jnp.where(causal, p, 0.0)
                mass[h, rows, :] += lanes(p)
                total += dot(p.astype(bf16), masked(vals, masks[h]))
            acc[rows, :] += total
    inverse = jnp.zeros(acc.shape, f32)
    logs = jnp.zeros(l_ref.shape, f32)
    lane = lax.broadcasted_iota(jnp.int32, l_ref.shape, 1)
    for h in range(heads):
        column = jnp.sum(mass[h], axis=1, keepdims=True)
        inverse = jnp.where(masks[h], 1.0 / column, inverse)
        logs = jnp.where(lane == h, jnp.log2(column), logs)
    y_ref[...] = (acc[...] * inverse).astype(bf16)
    l_ref[...] = logs


def attn_fwd(is_long, q, k, v, first, count):
    rows, cols = q.shape
    heads = cols // HEAD_DIM
    blk, sub = 512, 256
    row = lambda n: pl.BlockSpec((blk, n), lambda i, s: (i, 0))
    whole = pl.BlockSpec(((first + count) * blk, cols), lambda i, s: (0, 0))
    return pl.pallas_call(
        functools.partial(attn_fwd_kernel, heads=heads, blk=blk, sub=sub, first=first),
        grid_spec=pltpu.PrefetchScalarGridSpec(
            num_scalar_prefetch=1,
            grid=(count,),
            in_specs=[pl.BlockSpec((blk, cols), lambda i, s: (first + i, 0)), whole, whole],
            out_specs=[row(cols), row(128)],
            scratch_shapes=[pltpu.VMEM((blk, cols), f32), pltpu.VMEM((heads, blk, 128), f32)],
        ),
        out_shape=[
            jax.ShapeDtypeStruct((count * blk, cols), bf16),
            jax.ShapeDtypeStruct((count * blk, 128), f32),
        ],
        compiler_params=params(),
    )(is_long, q, k, v)


def attn_bwd_kernel(
    long_ref, q_ref, qk_ref, dy_ref, y_ref, l_ref, k_ref, v_ref, rho_ref, cos_ref, sin_ref, gain_ref,
    ones_ref, dk_in, dv_in, out_ref, dk_out, dv_out, s_ref, acc, dk_acc, dv_acc, stats, *, heads, blk, sub, first, count
):
    step = pl.program_id(0)
    local = count - 1 - step
    i = first + local
    cols = q_ref.shape[1]
    masks = head_masks(cols, heads)
    per = SHORT // blk
    low = jnp.where(long_ref[0] != 0, 0, (i // per) * per)
    ones = ones_ref[...]
    gain = gain_ref[...]

    @pl.when(step == 0)
    def _():
        dk_acc[...] = jnp.zeros_like(dk_acc)
        dv_acc[...] = jnp.zeros_like(dv_acc)
        s_ref[...] = jnp.zeros_like(s_ref)
        if dk_in is not None:
            dk_acc[...] = dk_in[...]
            dv_acc[...] = dv_in[...]

    acc[...] = jnp.zeros_like(acc)
    prod = dy_ref[...].astype(f32) * y_ref[...].astype(f32)
    high = prod.astype(bf16)
    rest = (prod - high.astype(f32)).astype(bf16)
    pickers = (
        lax.broadcasted_iota(jnp.int32, (8, cols), 1) // HEAD_DIM
        == lax.broadcasted_iota(jnp.int32, (8, cols), 0)
    ).astype(bf16)
    stats[0:8, :] = dot_t(pickers, high) + dot_t(pickers, rest)
    stats[8:16, :] = l_ref[...].T[0:8, :]

    def piece(at, size, rows, causal):
        keys = k_ref[pl.ds(at, size), :]
        vals = v_ref[pl.ds(at, size), :]
        q = q_ref[rows, :]
        dy = dy_ref[rows, :]
        total_q = jnp.zeros(q.shape, f32)
        total_k = jnp.zeros(keys.shape, f32)
        total_v = jnp.zeros(keys.shape, f32)
        for h in range(heads):
            qm = masked(q, masks[h])
            dym = masked(dy, masks[h])
            p = jnp.exp2(dot_t(keys, qm) - stats[8 + h : 9 + h, rows])
            if causal is not None:
                p = jnp.where(causal, p, 0.0)
            ds = (p * (dot_t(vals, dym) - stats[h : h + 1, rows])).astype(bf16)
            total_v += dot(p.astype(bf16), dym)
            total_k += dot(ds, qm)
            total_q += t_dot(ds, masked(keys, masks[h]))
        acc[rows, :] += total_q
        dk_acc[pl.ds(at, size), :] += total_k
        dv_acc[pl.ds(at, size), :] += total_v

    def body(j, carry):
        piece(pl.multiple_of(j * blk, blk), blk, slice(0, blk), None)
        return carry

    lax.fori_loop(low, i, body, 0)
    start = pl.multiple_of(i * blk, blk)
    causal = lax.broadcasted_iota(jnp.int32, (sub, sub), 0) <= lax.broadcasted_iota(
        jnp.int32, (sub, sub), 1
    )
    for a in range(blk // sub):
        for b in range(a + 1):
            piece(
                pl.multiple_of(start + b * sub, sub),
                sub,
                slice(a * sub, (a + 1) * sub),
                causal if a == b else None,
            )
    cosine = widen(cos_ref[...], cols)
    sine = widen(sin_ref[...], cols)
    total = jnp.zeros((1, cols), f32)
    here = pl.ds(start, blk)
    for c, (value, unit, up, scale) in enumerate(
        (
            (acc[...], q_ref[...], score_scale, score_scale * LOG2E),
            (dk_acc[here, :], k_ref[here, :], LN2, 1.0),
        )
    ):
        rho = jnp.zeros(value.shape, f32)
        for h in range(heads):
            at = c * heads + h
            rho = jnp.where(masks[h], rho_ref[:, at : at + 1], rho)
        grad = value * up
        unit = unit.astype(f32) * (1.0 / (gain * scale))
        total += jnp.sum(grad * unit, axis=0, keepdims=True)
        grad = grad * gain
        back = rho * (grad - unit * head_sum(grad * unit, ones))
        turned = back * cosine - swap_halves(back) * sine
        out_ref[:, c * cols : (c + 1) * cols] = turned.astype(bf16)
    out_ref[:, 2 * cols :] = dv_acc[here, :].astype(bf16)
    s_ref[0:1, :] += total
    if dk_out is not None:
        @pl.when(step == count - 1)
        def _():
            dk_out[...] = dk_acc[0 : first * blk, :]
            dv_out[...] = dv_acc[0 : first * blk, :]


def attn_bwd(is_long, q, k, v, dy, y, logs, rho, cosine, sine, gain, ones, first, count, carry):
    rows, cols = q.shape
    heads = cols // HEAD_DIM
    blk, sub = 512, 256
    top = (first + count) * blk
    at = lambda s: first + count - 1 - s
    row = lambda n: pl.BlockSpec((blk, n), lambda s, m: (at(s), 0))
    whole = pl.BlockSpec((top, cols), lambda s, m: (0, 0))
    ins = [q, k, dy, y, logs, k, v, rho, cosine, sine, gain, ones]
    mine = lambda n: pl.BlockSpec((blk, n), lambda s, m: (count - 1 - s, 0))
    in_specs = [row(cols)] * 2 + [mine(cols)] * 2 + [mine(128), whole, whole] + [row(128)] * 3
    in_specs += [full_spec((1, cols)), full_spec((cols, cols))]
    body = functools.partial(
        attn_bwd_kernel, heads=heads, blk=blk, sub=sub, first=first, count=count
    )
    outs = [jax.ShapeDtypeStruct((count * blk, 3 * cols), bf16)]
    out_specs = [pl.BlockSpec((blk, 3 * cols), lambda s, m: (count - 1 - s, 0))]
    if first:
        outs += [jax.ShapeDtypeStruct((first * blk, cols), f32)] * 2
        out_specs += [full_spec((first * blk, cols))] * 2
        inner = lambda *r: body(*r[:13], None, None, *r[13:])
    else:
        ins += carry
        in_specs += [full_spec((top, cols))] * 2
        inner = lambda *r: body(*r[:16], None, None, *r[16:])
    outs.append(jax.ShapeDtypeStruct((8, cols), f32))
    out_specs.append(full_spec((8, cols)))
    return pl.pallas_call(
        inner,
        grid_spec=pltpu.PrefetchScalarGridSpec(
            num_scalar_prefetch=1,
            grid=(count,),
            in_specs=in_specs,
            out_specs=out_specs,
            scratch_shapes=[
                pltpu.VMEM((blk, cols), f32),
                pltpu.VMEM((top, cols), f32),
                pltpu.VMEM((top, cols), f32),
                pltpu.VMEM((16, blk), f32),
            ],
        ),
        out_shape=outs,
        compiler_params=params(),
    )(is_long, *ins)


def row_norm(value):
    return lax.rsqrt(jnp.mean(value * value, axis=1, keepdims=True) + layer_eps)


def norm_back(scale, result, grad):
    return scale * (grad - result * jnp.mean(grad * result, axis=1, keepdims=True))


def pack_kernel(core_ref, up_ref, down_ref, out_ref, qkv_ref, mine_ref, theirs_ref, q_ref):
    half = up_ref.shape[2] // 2
    low = core_ref[0] == 0
    down = down_ref[...].astype(bf16).T
    out = out_ref[...].astype(bf16).T
    for ref, first in ((mine_ref, low), (theirs_ref, jnp.logical_not(low))):
        for c in range(2):
            ref[:, c * half : (c + 1) * half] = jnp.where(
                first, up_ref[:, c, :half], up_ref[:, c, half:]
            ).astype(bf16)
        ref[:, 2 * half : 3 * half] = jnp.where(first, down[:, :half], down[:, half:])
        ref[:, 3 * half :] = out
    cols = qkv_ref.shape[2]
    for c in range(3):
        q_ref[:, c * cols : (c + 1) * cols] = qkv_ref[:, c, :].astype(bf16)


def pack(core, w_up, w_down, w_out, w_qkv):
    span, _, hid = w_up.shape
    cols = w_qkv.shape[2]
    vmem = pl.BlockSpec(memory_space=pltpu.VMEM)
    return pl.pallas_call(
        pack_kernel,
        in_specs=[pl.BlockSpec(memory_space=pltpu.SMEM)] + [vmem] * 4,
        out_specs=[vmem] * 3,
        out_shape=[jax.ShapeDtypeStruct((span, 3 * hid // 2 + cols), bf16)] * 2
        + [jax.ShapeDtypeStruct((span, 3 * cols), bf16)],
        compiler_params=params(),
    )(core, w_up, w_down, w_out, w_qkv)


def place_of(r, chip, chunk):
    return pl.ds(pl.multiple_of((r ^ chip) * chunk, chunk), chunk)


def put_relative(ref, chip, chips, fast):
    if not fast:
        return ref[...]
    if len(ref.shape) == 3:
        return jnp.concatenate([ref[r ^ chip] for r in range(chips)], axis=1)
    chunk = ref.shape[1] // chips
    return jnp.concatenate([ref[:, place_of(r, chip, chunk)] for r in range(chips)], axis=1)


def put_natural(ref, value, chip, chips, fast):
    if not fast:
        ref[...] = value
        return
    chunk = value.shape[1] // chips
    for r in range(chips):
        part = value[:, r * chunk : (r + 1) * chunk]
        if len(ref.shape) == 3:
            ref[r ^ chip] = part
        else:
            ref[:, place_of(r, chip, chunk)] = part


def attn_out_kernel(place_ref, *refs, counts, chips, fast):
    total = sum(counts)
    flat, refs = refs[:total], refs[total:]
    ya_ref, yb_ref, x_ref, alpha_ref, ha_ref, h1_ref, hb_ref, stat_ref, acc = refs
    z, chip = place_ref[0], place_ref[1]
    parts = len(counts)
    early = pl.program_id(0) == 0
    index = 0
    for n in range(parts):
        at = lax.rem(z + parts - n, parts)
        y = jnp.where(early, ya_ref[at], yb_ref[at])
        column = 0
        for piece in flat[index : index + counts[n]]:
            part = slice(column, column + piece.shape[0])
            if n == 0:
                acc[:, part] = dot_t(y, piece[...])
            else:
                acc[:, part] += dot_t(y, piece[...])
            column += piece.shape[0]
        index += counts[n]
    total = acc[...]
    norm = row_norm(total)
    hidden = total * norm
    start = put_relative(x_ref, chip, chips, fast).astype(f32)
    mixed = start + alpha_ref[...] * (hidden - start)
    first_norm = row_norm(mixed)
    out = mixed * first_norm
    ha_ref[...] = hidden
    h1_ref[...] = out
    hb_ref[...] = out.astype(bf16)
    lane = lax.broadcasted_iota(jnp.int32, stat_ref.shape, 1)
    stat_ref[...] = jnp.where(lane == 0, norm, first_norm)


def own_rows(blk, parts, width, fast):
    if fast:
        return pl.BlockSpec((blk, width), lambda i, s: (i * parts + s[0], 0))
    return pl.BlockSpec((blk, width), lambda i, s: (i, 0))


def out_weights(slots, cols):
    flat = [p for slot in slots for p in slot]
    last = flat[0].shape[1] // cols - 1
    return flat, [pl.BlockSpec((p.shape[0], cols), lambda i, s: (0, last)) for p in flat]


def attn_out(place, ya, yb, slots, x, alpha, chips, fast):
    parts, blk, cols = ya.shape
    width = x.shape[1]
    rows = 2 * blk
    row = lambda n: pl.BlockSpec((blk, n), lambda i, s: (i, 0))
    flat, specs = out_weights(slots, cols)
    return pl.pallas_call(
        functools.partial(attn_out_kernel, counts=[len(t) for t in slots], chips=chips, fast=fast),
        grid_spec=pltpu.PrefetchScalarGridSpec(
            num_scalar_prefetch=1,
            grid=(2,),
            in_specs=specs
            + [full_spec(ya.shape)] * 2
            + [own_rows(blk, parts, width, fast), full_spec((1, width))],
            out_specs=[row(width)] * 3 + [row(128)],
            scratch_shapes=[pltpu.VMEM((blk, width), f32)],
        ),
        out_shape=[jax.ShapeDtypeStruct((rows, width), d) for d in (f32, f32, bf16)]
        + [jax.ShapeDtypeStruct((rows, 128), f32)],
        compiler_params=params(),
    )(place, *flat, ya, yb, x, alpha)


def loss_kernel(place_ref, own_ref, got_ref, h1_ref, cot_ref, alpha_ref, hidden_ref, dmo_ref, base_ref, ga_ref, *, chips, fast):
    chip = place_ref[1]
    total = own_ref[...] + got_ref[...].astype(f32)
    alpha = alpha_ref[...]
    norm = row_norm(total)
    inner = total * norm
    h1 = h1_ref[...]
    mixed = h1 + alpha * (inner - h1)
    last = row_norm(mixed)
    hidden = mixed * last
    grad = norm_back(last, hidden, put_relative(cot_ref, chip, chips, fast).astype(f32))
    put_natural(hidden_ref, hidden.astype(bf16), chip, chips, fast)
    base_ref[...] = (1.0 - alpha) * grad
    dmo_ref[...] = norm_back(norm, inner, alpha * grad).astype(bf16)

    @pl.when(pl.program_id(0) == 0)
    def _():
        ga_ref[...] = jnp.zeros_like(ga_ref)

    ga_ref[0:1, :] += jnp.sum(grad * (inner - h1), axis=0, keepdims=True)


def loss(place, own, got, h1, cot, alpha, chips, fast):
    rows, width = own.shape
    blk = rows // 2
    row = pl.BlockSpec((blk, width), lambda i, s: (i, 0))
    part = row
    if fast:
        part = pl.BlockSpec((chips, blk, width // chips), lambda i, s: (0, i, 0))
    return pl.pallas_call(
        functools.partial(loss_kernel, chips=chips, fast=fast),
        grid_spec=pltpu.PrefetchScalarGridSpec(
            num_scalar_prefetch=1,
            grid=(rows // blk,),
            in_specs=[row] * 3 + [part, full_spec((1, width))],
            out_specs=[part] + [row] * 2 + [full_spec((8, width))],
        ),
        out_shape=[jax.ShapeDtypeStruct(cot.shape, bf16)]
        + [jax.ShapeDtypeStruct((rows, width), d) for d in (bf16, f32)]
        + [jax.ShapeDtypeStruct((8, width), f32)],
        compiler_params=params(),
    )(place, own, got, h1, cot, alpha)


def first_back_kernel(place_ref, *refs, counts, chips, fast):
    total = sum(counts)
    flat, refs = refs[:total], refs[total:]
    own_ref, got_ref, base_ref, h1_ref, ha_ref, x_ref, stat_ref, alpha_ref = refs[:8]
    do_ref, through_ref, ga_ref, dya_ref, dyb_ref = refs[8:]
    z, chip = place_ref[0], place_ref[1]
    alpha = alpha_ref[...]
    grad = base_ref[...] + own_ref[...] + got_ref[...].astype(f32)
    grad = norm_back(stat_ref[:, 1:2], h1_ref[...], grad)
    ha = ha_ref[...]
    put_natural(through_ref, ((1.0 - alpha) * grad).astype(bf16), chip, chips, fast)
    back = norm_back(stat_ref[:, 0:1], ha, alpha * grad).astype(bf16)
    do_ref[...] = back
    parts = len(counts)
    step = pl.program_id(0)
    index = 0
    for n in range(parts):
        at = lax.rem(z + parts - n, parts)
        part = jnp.zeros(dya_ref.shape[1:], f32)
        column = 0
        for piece in flat[index : index + counts[n]]:
            part += dot(do_ref[:, column : column + piece.shape[0]], piece[...])
            column += piece.shape[0]
        index += counts[n]
        part = part.astype(bf16)
        for side, ref in enumerate((dya_ref, dyb_ref)):

            @pl.when(step == side)
            def _(ref=ref, part=part, at=at):
                ref[at] = part

    @pl.when(step == 0)
    def _():
        ga_ref[...] = jnp.zeros_like(ga_ref)

    start = put_relative(x_ref, chip, chips, fast).astype(f32)
    ga_ref[0:1, :] += jnp.sum(grad * (ha - start), axis=0, keepdims=True)


def first_back(place, own, got, base, h1, ha, x, stat, alpha, slots, chips, fast, cols):
    rows, width = own.shape
    parts = len(slots)
    blk = rows // 2
    row = lambda n: pl.BlockSpec((blk, n), lambda i, s: (i, 0))
    flat, specs = out_weights(slots, cols)
    return pl.pallas_call(
        functools.partial(first_back_kernel, counts=[len(t) for t in slots], chips=chips, fast=fast),
        grid_spec=pltpu.PrefetchScalarGridSpec(
            num_scalar_prefetch=1,
            grid=(2,),
            in_specs=specs
            + [row(width)] * 5
            + [own_rows(blk, parts, width, fast), row(128), full_spec((1, width))],
            out_specs=[row(width)] * 2
            + [full_spec((8, width))]
            + [full_spec((parts, blk, cols))] * 2,
        ),
        out_shape=[jax.ShapeDtypeStruct((rows, width), bf16)] * 2
        + [jax.ShapeDtypeStruct((8, width), f32)]
        + [jax.ShapeDtypeStruct((parts, blk, cols), bf16)] * 2,
        compiler_params=params(),
    )(place, *flat, own, got, base, h1, ha, x, stat, alpha)


def fetch_weights(q, slots, wbuf, sems):
    def copies(j):
        at = 0
        found = []
        for p, piece in enumerate(slots[j]):
            size = piece.shape[0]
            found.append(
                pltpu.make_async_copy(
                    piece.at[:, : wbuf.shape[2]], wbuf.at[j % 2, at : at + size, :], sems.at[j % 2, p]
                )
            )
            at += size
        return found

    for j in range(len(slots)):

        @pl.when(q == j)
        def _(j=j):
            if j == 0:
                for copy in copies(0):
                    copy.start()
            if j + 1 < len(slots):
                for copy in copies(j + 1):
                    copy.start()
            for copy in copies(j):
                copy.wait()


def mlp_fwd_kernel(*refs, half, counts):
    total = sum(counts)
    flat, refs = refs[:total], refs[total:]
    slots, at = [], 0
    for n in counts:
        slots.append(flat[at : at + n])
        at += n
    ha_ref, hb_ref, suv_ref, act_ref, uv_ref, own_ref, got_ref, acc, wbuf, sems = refs
    rows = ha_ref.shape[0]
    q = pl.program_id(0)

    @pl.when(q == 0)
    def _():
        own_ref[...] = jnp.zeros_like(own_ref)
        acc[...] = jnp.zeros_like(acc)

    fetch_weights(q, slots, wbuf, sems)
    w = wbuf.at[lax.rem(q, 2)]
    for base, h_ref, sum_ref in ((0, ha_ref, own_ref), (rows, hb_ref, acc)):
        at = slice(base, base + rows)
        pair = dot(h_ref[...], w[:, : 2 * half])
        lifted = pair[:, :half] * suv_ref[0:1, :]
        gated = pair[:, half:] * suv_ref[1:2, :]
        act = (lifted * gated * jax.nn.sigmoid(gated)).astype(bf16)
        uv_ref[at, :] = pair.astype(bf16)
        act_ref[at, :] = act
        sum_ref[...] += dot_t(act, w[:, 2 * half : 3 * half])

    @pl.when(q == pl.num_programs(0) - 1)
    def _():
        got_ref[...] = acc[...].astype(bf16)


def mlp_fwd(ha, hb, slots, suv):
    rows, width = ha.shape
    parts, _, half = suv.shape
    take = lambda n: pl.BlockSpec((None, 2 * rows, n), lambda q: (q, 0, 0))
    whole = full_spec((rows, width))
    anywhere = pl.BlockSpec(memory_space=pl.ANY)
    flat = [p for slot in slots for p in slot]
    return pl.pallas_call(
        functools.partial(mlp_fwd_kernel, half=half, counts=[len(s) for s in slots]),
        grid=(parts,),
        in_specs=[anywhere] * len(flat)
        + [whole, whole, pl.BlockSpec((None, 2, half), lambda q: (q, 0, 0))],
        out_specs=[take(half), take(2 * half), whole, whole],
        out_shape=[
            jax.ShapeDtypeStruct((parts, 2 * rows, half), bf16),
            jax.ShapeDtypeStruct((parts, 2 * rows, 2 * half), bf16),
            jax.ShapeDtypeStruct((rows, width), f32),
            jax.ShapeDtypeStruct((rows, width), bf16),
        ],
        scratch_shapes=[
            pltpu.VMEM((rows, width), f32),
            pltpu.VMEM((2, width, 3 * half), bf16),
            pltpu.SemaphoreType.DMA((2, max(len(s) for s in slots))),
        ],
        compiler_params=params(),
    )(*flat, ha, hb, suv)


def mlp_bwd_kernel(*refs, half, counts):
    total = sum(counts)
    flat, refs = refs[:total], refs[total:]
    slots, at = [], 0
    for n in counts:
        slots.append(flat[at : at + n])
        at += n
    da_ref, db_ref, uv_ref, suv_ref, duv_ref, own_ref, got_ref, gs_ref, acc, wbuf, sems = refs
    rows = da_ref.shape[0]
    q = pl.program_id(0)

    @pl.when(q == 0)
    def _():
        own_ref[...] = jnp.zeros_like(own_ref)
        acc[...] = jnp.zeros_like(acc)

    gs_ref[...] = jnp.zeros_like(gs_ref)
    fetch_weights(q, slots, wbuf, sems)
    w = wbuf.at[lax.rem(q, 2)]
    for base, d_ref, sum_ref in ((0, da_ref, own_ref), (rows, db_ref, acc)):
        at = slice(base, base + rows)
        grad = dot(d_ref[...], w[:, 2 * half : 3 * half])
        up = uv_ref[at, :half].astype(f32)
        gate = uv_ref[at, half:].astype(f32)
        su = suv_ref[0:1, :]
        sv = suv_ref[1:2, :]
        lifted = up * su
        gated = gate * sv
        sigma = jax.nn.sigmoid(gated)
        da = grad * gated * sigma
        db = grad * lifted * sigma * (1.0 + gated * (1.0 - sigma))
        gs_ref[0:1, :] += jnp.sum(da * up, axis=0, keepdims=True)
        gs_ref[1:2, :] += jnp.sum(db * gate, axis=0, keepdims=True)
        duv_ref[at, :half] = (da * su).astype(bf16)
        duv_ref[at, half:] = (db * sv).astype(bf16)
        sum_ref[...] += dot_t(duv_ref[at, :], w[:, : 2 * half])

    @pl.when(q == pl.num_programs(0) - 1)
    def _():
        got_ref[...] = acc[...].astype(bf16)


def mlp_bwd(da, db, slots, uv, suv):
    rows, width = da.shape
    parts, _, half = suv.shape
    take = lambda n: pl.BlockSpec((None, 2 * rows, n), lambda q: (q, 0, 0))
    whole = full_spec((rows, width))
    anywhere = pl.BlockSpec(memory_space=pl.ANY)
    flat = [p for slot in slots for p in slot]
    return pl.pallas_call(
        functools.partial(mlp_bwd_kernel, half=half, counts=[len(s) for s in slots]),
        grid=(parts,),
        in_specs=[anywhere] * len(flat)
        + [
            whole,
            whole,
            take(2 * half),
            pl.BlockSpec((None, 2, half), lambda q: (q, 0, 0)),
        ],
        out_specs=[
            take(2 * half),
            whole,
            whole,
            pl.BlockSpec((None, 8, half), lambda q: (q, 0, 0)),
        ],
        out_shape=[
            jax.ShapeDtypeStruct((parts, 2 * rows, 2 * half), bf16),
            jax.ShapeDtypeStruct((rows, width), f32),
            jax.ShapeDtypeStruct((rows, width), bf16),
            jax.ShapeDtypeStruct((parts, 8, half), f32),
        ],
        scratch_shapes=[
            pltpu.VMEM((rows, width), f32),
            pltpu.VMEM((2, width, 3 * half), bf16),
            pltpu.SemaphoreType.DMA((2, max(len(s) for s in slots))),
        ],
        compiler_params=params(),
    )(*flat, da, db, uv, suv)


EXTRA = 16


def grad_kernel(place_ref, *refs, orders, parts, chunk, more):
    ha_ref, hb_ref = refs[:2]
    refs = refs[2:]
    if more:
        oa_ref, ob_ref, ya_ref, yb_ref, extra_ref = refs[:5]
        refs = refs[5:]
    val_ref, *outs = refs[:5]
    turned = refs[5]
    rows = ha_ref.shape[0]
    k = pl.program_id(0)

    @pl.when(k == 0)
    def _():
        turned[:, :rows] = ha_ref[...].T
        turned[:, rows:] = hb_ref[...].T
        if more:
            refs[6][:, :rows] = oa_ref[...].T
            refs[6][:, rows:] = ob_ref[...].T

    for side in range(2):

        @pl.when((k < parts // 2) == (side == 0))
        def _(side=side):
            for which, ref in zip(orders[side], outs[2 * side : 2 * side + 2]):
                for j, r in enumerate(which):
                    at = slice(r * chunk, (r + 1) * chunk)
                    value = dot(turned[at, :], val_ref[...]).astype(bf16)
                    size = value.shape[1]
                    ref[j, :chunk, :size] = value
                    if more:
                        ref[j, :chunk, size:] = (
                            dot(refs[6][at, :rows], ya_ref[...]) + dot(refs[6][at, rows:], yb_ref[...])
                        ).astype(bf16)
                        ref[j, chunk:, :] = extra_ref[...].astype(bf16)


def weight_grads(place, sends, keeps, chips, hs, value, os=None, ys=None, extra=None):
    rows, width = hs[0].shape
    chunk = width // chips
    parts, _, size = value.shape
    more = os is not None
    hc = ys[1].shape[2] if more else 0
    tall = chunk + (EXTRA if more else 0)
    middle = parts // 2
    if chunk % 128:
        result = []
        for which, lo in ((sends[0], 0), (keeps[0], 0), (sends[1], middle), (keeps[1], middle)):
            cut = lambda pair: jnp.concatenate(
                [jnp.concatenate(pair, axis=0)[:, r * chunk : (r + 1) * chunk] for r in which], axis=1
            )
            found = []
            for k in range(lo, lo + middle):
                one = t_dot(cut(hs), value[k])
                if more:
                    at = (place[0] - k) % parts
                    y = lax.dynamic_index_in_dim(ys[0], at, 0, keepdims=False)
                    y = lax.dynamic_slice_in_dim(y, place[2] * hc, hc, 1)
                    y = jnp.concatenate([y, lax.dynamic_index_in_dim(ys[1], at, 0, keepdims=False)])
                    one = jnp.concatenate([one, t_dot(cut(os), y)], axis=1)
                one = one.reshape(len(which), chunk, size + hc)
                if more:
                    wide = jnp.broadcast_to(extra[k][None], (len(which), EXTRA, size + hc))
                    one = jnp.concatenate([one, wide], axis=1)
                found.append(one.astype(bf16))
            result.append(jnp.stack(found, axis=1))
        return [result[0], result[2]], [result[1], result[3]]
    whole = full_spec((rows, width))
    ins = list(hs)
    in_specs = [whole] * 2
    scratch = [pltpu.VMEM((width, 2 * rows), bf16)]
    if more:
        slot = lambda k, p: lax.rem(p[0] + parts - k, parts)
        ins += [*os, ys[0], ys[1], extra]
        in_specs += [whole] * 2
        in_specs += [
            pl.BlockSpec((None, rows, hc), lambda k, p: (slot(k, p), 0, p[2])),
            pl.BlockSpec((None, rows, hc), lambda k, p: (slot(k, p), 0, 0)),
            pl.BlockSpec((None, EXTRA, size + hc), lambda k, p: (k, 0, 0)),
        ]
        scratch = scratch * 2
    ins.append(value)
    in_specs.append(pl.BlockSpec((None, 2 * rows, size), lambda k, p: (k, 0, 0)))
    lists = [sends[0], keeps[0], sends[1], keeps[1]]
    block = lambda one: (len(one), None, tall, size + hc)
    early = lambda k, p: (0, jnp.minimum(k, middle - 1), 0, 0)
    late = lambda k, p: (0, jnp.maximum(k - middle, 0), 0, 0)
    out = pl.pallas_call(
        functools.partial(
            grad_kernel, orders=(lists[:2], lists[2:]), parts=parts, chunk=chunk, more=more
        ),
        grid_spec=pltpu.PrefetchScalarGridSpec(
            num_scalar_prefetch=1,
            grid=(parts,),
            in_specs=in_specs,
            out_specs=[
                pl.BlockSpec(block(one), early if n < 2 else late) for n, one in enumerate(lists)
            ],
            scratch_shapes=scratch,
        ),
        out_shape=[
            jax.ShapeDtypeStruct((len(one), middle, tall, size + hc), bf16) for one in lists
        ],
        compiler_params=params(),
    )(place, *ins)
    return [out[0], out[2]], [out[1], out[3]]


def adam_values(weight, grad, first, second):
    first_new = beta_one * first + (1.0 - beta_one) * grad
    second_new = beta_two * second + (1.0 - beta_two) * grad * grad
    moved = weight - learn_rate * (first_new / bias_one) / (
        jnp.sqrt(second_new / bias_two) + adam_eps
    )
    return first_new, second_new, moved


def lane_sums(value):
    ones = jnp.ones((8, value.shape[1]), bf16)
    high = value.astype(bf16)
    low = (value - high.astype(f32)).astype(bf16)
    return dot_t(ones, high) + dot_t(ones, low)


def adam_wide_kernel(w_ref, g_ref, m_ref, v_ref, g_out, m_out, v_out, n_out, s_out):
    cols = w_ref.shape[2]
    for c in range(w_ref.shape[1]):
        grad = g_ref[:, c * cols : (c + 1) * cols]
        first, second, moved = adam_values(w_ref[:, c, :], grad, m_ref[:, c, :], v_ref[:, c, :])
        g_out[:, c, :] = grad
        m_out[:, c, :] = first
        v_out[:, c, :] = second
        n_out[:, c, :] = moved
        s_out[c : c + 1, :] = jnp.sum(moved * moved, axis=0, keepdims=True)


def adam_wide(w, g, m, v):
    vmem = pl.BlockSpec(memory_space=pltpu.VMEM)
    return pl.pallas_call(
        adam_wide_kernel,
        in_specs=[vmem] * 4,
        out_specs=[vmem] * 5,
        out_shape=[jax.ShapeDtypeStruct(w.shape, f32)] * 4
        + [jax.ShapeDtypeStruct(w.shape[1:], f32)],
        compiler_params=params(),
    )(w, g, m, v)


def adam_tall_kernel(w_ref, g_ref, m_ref, v_ref, g_out, m_out, v_out, n_out, s_out):
    grad = g_ref[...].T
    first, second, moved = adam_values(w_ref[...], grad, m_ref[...], v_ref[...])
    g_out[...] = grad
    m_out[...] = first
    v_out[...] = second
    n_out[...] = moved
    s_out[...] = lane_sums(moved * moved)


def adam_tall(w, g, m, v):
    vmem = pl.BlockSpec(memory_space=pltpu.VMEM)
    return pl.pallas_call(
        adam_tall_kernel,
        in_specs=[vmem] * 4,
        out_specs=[vmem] * 5,
        out_shape=[jax.ShapeDtypeStruct(w.shape, f32)] * 4
        + [jax.ShapeDtypeStruct((8, w.shape[0]), f32)],
        compiler_params=params(),
    )(w, g, m, v)


def scale_kernel(na_ref, nb_ref, nc_ref, nd_ref, a_ref, b_ref, c_ref, d_ref, ao_ref, bo_ref, co_ref, do_ref, *, width):
    factor = lambda value: lax.rsqrt(value / width + layer_eps)
    for norm, ref, out in ((na_ref, a_ref, ao_ref), (nc_ref, c_ref, co_ref)):
        for c in range(ref.shape[1]):
            out[:, c, :] = ref[:, c, :] * factor(norm[c : c + 1, :])
    for norm, ref, out in ((nb_ref, b_ref, bo_ref), (nd_ref, d_ref, do_ref)):
        out[...] = ref[...] * factor(norm[...]).T[:, 0:1]


def scale_weights(norms, weights, width):
    vmem = pl.BlockSpec(memory_space=pltpu.VMEM)
    return pl.pallas_call(
        functools.partial(scale_kernel, width=width),
        in_specs=[vmem] * 8,
        out_specs=[vmem] * 4,
        out_shape=[jax.ShapeDtypeStruct(w.shape, f32) for w in weights],
        compiler_params=params(),
    )(*norms, *weights)


def after(value, *others):
    return lax.optimization_barrier((value, *others))[0]


def per_device(
    layer_input,
    cotangent,
    positions,
    w_qkv,
    w_out,
    w_up,
    w_down,
    moment_qkv,
    moment_out,
    moment_up,
    moment_down,
    square_qkv,
    square_out,
    square_up,
    square_down,
    s_qk,
    alpha_attn,
    alpha_mlp,
    s_uv,
):
    nz = lax.axis_size("head")
    nb = lax.axis_size("batch")
    z = lax.axis_index("head")
    b = lax.axis_index("batch")
    core = b % 2
    chip = b // 2
    chips = nb // 2
    bits = [1 << n for n in range(int(math.log2(chips)))]
    rows, cols = layer_input.shape
    width = cols * nz
    own = rows // nz
    hid = w_down.shape[0]
    half = hid // 2
    hc = cols // 2
    heads = cols // HEAD_DIM
    span = w_qkv.shape[0]
    chunk = width // chips
    core_s = core.reshape(1).astype(jnp.int32)
    place = jnp.stack([z, chip, core]).astype(jnp.int32)
    fast = chunk == cols and chunk % 128 == 0

    def swap_batch(value, bit):
        return lax.ppermute(value, "batch", [(i, i ^ bit) for i in range(nb)])

    def swap_core(value):
        return swap_batch(value, 1)

    def swap_chip(value, bit):
        return swap_batch(value, 2 * bit)

    def onward(value, k=1):
        return lax.ppermute(value, "head", [(i, (i + k) % nz) for i in range(nz)])

    def exchange(value):
        return lax.all_to_all(value, "head", split_axis=0, concat_axis=0)

    def pick(pair, index):
        return jnp.where(index == 0, pair[0], pair[1])

    def relative(value):
        return jnp.concatenate(
            [
                lax.dynamic_slice_in_dim(value, (chip ^ r) * chunk, chunk, value.ndim - 1)
                for r in range(chips)
            ],
            axis=-1,
        )

    def spread(value):
        if chips <= 4:
            return [value] + [swap_chip(value, r) for r in range(1, chips)]
        for bit in bits:
            value = jnp.concatenate([value, swap_chip(value, bit)], axis=0)
        return [value]

    tokens = [layer_input, onward(layer_input)]
    mine, theirs, qkv_own = pack(core_s, w_up, w_down, w_out, w_qkv)
    qkv_full = lax.all_gather(qkv_own, "batch", axis=0, tiled=True)
    theirs = swap_core(theirs)
    packet = jnp.concatenate([pick((mine, theirs), core), pick((theirs, mine), core)], axis=0)
    hops = [packet, onward(packet)]
    slots = [spread(packet)]
    tokens[1], hops[1], places, s_uv, alpha_attn, alpha_mlp, *last = lax.optimization_barrier(
        (tokens[1], hops[1], positions, s_uv, alpha_attn, alpha_mlp, *slots[0])
    )
    slots[0] = list(last)

    suv_own = pick((s_uv[:, :half], s_uv[:, half:]), core)
    freqs = jnp.exp(
        (jnp.arange(128) % (HEAD_DIM // 2)).astype(f32) * (-2.0 * math.log(10000.0) / HEAD_DIM)
    )
    phase = places.astype(f32)[:, None] * freqs[None, :]
    side = jnp.where(jnp.arange(128) % HEAD_DIM < HEAD_DIM // 2, -1.0, 1.0).astype(f32)
    cosine, sine = jnp.cos(phase), jnp.sin(phase) * side[None, :]
    lane = jnp.arange(cols) // HEAD_DIM
    ones = (lane[:, None] == lane[None, :]).astype(bf16)
    gain = s_qk.reshape(1, cols)
    is_long = (places[SHORT : SHORT + 1] != 0).astype(jnp.int32)
    attn_gain = relative(alpha_attn[None])
    mlp_gain = relative(alpha_mlp[None])

    for n in range(2, nz):
        slots.append(spread(hops[-1]))
        tokens.append(onward(tokens[-1]))
        if n < nz - 1:
            hops.append(onward(hops[-1]))
            tokens[-1], hops[-1], cosine, sine, ones, attn_gain, mlp_gain, suv_own, *last = (
                lax.optimization_barrier(
                    (tokens[-1], hops[-1], cosine, sine, ones, attn_gain, mlp_gain, suv_own, *slots[-1])
                )
            )
            slots[-1] = list(last)
    last_hop, tokens[-1] = lax.optimization_barrier((hops[-1], tokens[-1]))
    hops.append(onward(last_hop))
    suv = jnp.stack([suv_own] + [onward(suv_own, n) for n in range(1, nz)])

    blocks = rows // 512
    middle = blocks // 2
    tokens_full, q, k, v, rho = qkv_project(place, tokens, qkv_full, cosine, sine, gain, ones)
    y_a, logs_a = attn_fwd(is_long, q, k, v, 0, middle)
    q_b, suv, hops[-1], *last = lax.optimization_barrier((after(q, y_a), suv, hops[-1], *slots[-1]))
    slots[-1] = list(last)
    slots.append(spread(hops[-1]))
    y_b, logs_b = attn_fwd(is_long, q_b, k, v, middle, blocks - middle)
    y_one = exchange(y_a.reshape(nz, own // 2, cols))
    y_in, y_one = lax.optimization_barrier((y_b, y_one))
    y_two = exchange(y_in.reshape(nz, own // 2, cols))
    flat = lambda value: value.transpose(1, 0, 2).reshape(own, width)
    start = tokens_full
    if not fast:
        start = jnp.concatenate(
            [
                lax.dynamic_slice_in_dim(tokens_full, h * (rows // 2) + z * (own // 2), own // 2, 0)
                for h in range(2)
            ]
        )
        start = relative(start)
    hA, h1, h_own, stat = attn_out(place, y_one, y_two, slots, start, attn_gain, chips, fast)
    h_got = swap_core(h_own)
    cot = after(cotangent, h_own).reshape(2, nz, own // 2, cols).transpose(1, 0, 2, 3)
    cot = exchange(cot.reshape(nz, own, cols))

    act, uv, mo_own, mo_other = mlp_fwd(h_own, h_got, slots, suv)
    mo_got = swap_core(mo_other)
    if not fast:
        cot = relative(flat(cot))
    hidden, d_own, base, ga_mlp = loss(place, mo_own, mo_got, h1, cot, mlp_gain, chips, fast)
    d_got = swap_core(d_own)
    if not fast:
        hidden = relative(hidden).reshape(own, nz, cols).transpose(1, 0, 2)
    hidden = exchange(hidden)

    orders = [bits, bits[::-1]]
    sent_at = [[r for r in range(chips) if r & order[0]] for order in orders]
    kept_at = [[r for r in range(chips) if not r & order[0]] for order in orders]

    def second(kept, sent):
        found, sends = [], []
        for order, left, got, keep in zip(orders, kept_at, sent, kept):
            for bit in order[1:]:
                send_at = [n for n, r in enumerate(left) if r & bit]
                keep_at = [n for n, r in enumerate(left) if not r & bit]
                left = [left[n] for n in keep_at]
                cut = lambda v, at: jnp.concatenate([v[n : n + 1] for n in at], axis=0).astype(f32)
                send = (cut(keep, send_at) + cut(got, send_at)).astype(bf16)
                keep = cut(keep, keep_at) + cut(got, keep_at)
                got = swap_chip(send, bit)
                sends.append(send)
            found.append((keep, got))
        return found, sends

    def slot_sums(found):
        return [(keep[0, n] + got[0, n].astype(f32)) for keep, got in found for n in range(nz // 2)]

    down_made, down_kept = weight_grads(place, sent_at, kept_at, chips, (d_own, d_got), act)
    down_sent = [swap_chip(one, order[0]) for one, order in zip(down_made, orders)]
    d_own, d_got, *_ = lax.optimization_barrier((d_own, d_got, *down_made))
    duv, dh_own, dh_other, gsuv = mlp_bwd(d_own, d_got, slots, uv, suv)
    dh_got = swap_core(dh_other)
    dh_own, hidden, *down_sent = lax.optimization_barrier((dh_own, hidden, *down_sent))
    do_own, through, ga_attn, dy_a, dy_b = first_back(
        place, dh_own, dh_got, base, h1, hA, start, stat, attn_gain, slots, chips, fast, cols
    )
    dy_b = exchange(dy_b)
    do_got = swap_core(do_own)
    y_mine = jnp.concatenate([y_one, y_two], axis=1)
    y_got = swap_core(lax.dynamic_slice_in_dim(after(y_mine, h_own), (1 - core) * hc, hc, 2))
    down_sent = [after(one, do_own) for one in down_sent]
    down_part, down_next = second(down_kept, down_sent)

    alphas = [relative(ga_attn[0:1]), relative(ga_mlp[0:1])]
    extra = []
    wide = 2 * half + hc
    fill = lambda r: jnp.pad(r, ((0, 0), (0, wide - r.shape[1])))
    for n in range(nz):
        at = ((z - n) % nz) * cols
        line = jnp.concatenate([lax.dynamic_slice_in_dim(g, at, cols, 1) for g in alphas], axis=1)
        first = gsuv[n, :2].reshape(1, 2 * half)
        extra.append(jnp.pad(jnp.concatenate([fill(first), fill(line)]), ((0, EXTRA - 2), (0, 0))))
    extra = jnp.stack(extra)
    h_own, *_ = lax.optimization_barrier((h_own, *down_next))
    up_made, up_kept = weight_grads(
        place, sent_at, kept_at, chips, (h_own, h_got), duv, (do_own, do_got), (y_mine, y_got), extra
    )
    down_keep, down_got = [p[0] for p in down_part], [p[1] for p in down_part]
    down_got = [after(one, *up_kept) for one in down_got]
    down_slots = slot_sums(list(zip(down_keep, down_got)))
    dy_b, dy_a, *both = lax.optimization_barrier((dy_b, dy_a, *up_made, *down_slots))
    up_made, down_slots = both[: len(up_made)], both[len(up_made) :]
    down_along = [onward(down_slots[n].astype(bf16), nz - n) for n in range(1, nz)]
    up_sent = [swap_chip(one, order[0]) for one, order in zip(up_made, orders)]

    dy_a = exchange(dy_a)
    common = lambda dy, y, logs: (
        is_long, q, k, v, dy.reshape(y.shape), y, logs, rho, cosine, sine, gain, ones
    )
    dqkv_b, dk_part, dv_part, sqk_b = attn_bwd(
        *common(dy_b, y_b, logs_b), middle, blocks - middle, None
    )

    if not fast:
        through = relative(through)
    through = through.astype(f32)

    def input_part(dqkv, side):
        part = dot_t(dqkv, qkv_full)
        mine_at = z * (own // 2)
        here = lax.dynamic_slice_in_dim(part, mine_at, own // 2, 0)
        here = here + through[side * (own // 2) : (side + 1) * (own // 2)]
        return lax.dynamic_update_slice_in_dim(part.astype(bf16), here.astype(bf16), mine_at, 0)

    dqkv_b, dk_part, dy_a = lax.optimization_barrier((dqkv_b, dk_part, dy_a))
    part_b = input_part(dqkv_b, 1)
    cut = lambda n: lax.dynamic_slice_in_dim(part_b, ((z + n) % nz) * cols, cols, 1)
    part_cuts = [cut(n) for n in range(nz)]
    down_along = [after(one, dqkv_b) for one in down_along]
    sum_down_t = down_slots[0] + sum(one.astype(f32) for one in down_along)
    up_part, up_next = second(up_kept, [after(one, dqkv_b) for one in up_sent])
    part_got = [onward(part_cuts[n], n) for n in range(1, nz)]
    dk_part, dy_a, *_ = lax.optimization_barrier((dk_part, dy_a, *up_next, *part_cuts, sum_down_t))
    dqkv_a, sqk_a = attn_bwd(*common(dy_a, y_a, logs_a), 0, middle, [dk_part, dv_part])
    part_got = [after(one, dqkv_a) for one in part_got]
    input_b = part_cuts[0].astype(f32) + sum(one.astype(f32) for one in part_got)
    up_part = [(keep, after(got, dqkv_a)) for keep, got in up_part]
    part_a = input_part(dqkv_a, 0)
    up_slots = slot_sums(up_part)
    passed = onward(up_slots[1].astype(bf16))
    for n in range(2, nz):
        passed = onward((up_slots[n] + passed.astype(f32)).astype(bf16))
    passed, part_a = lax.optimization_barrier((passed, part_a))
    sum_up_t = up_slots[0] + passed.astype(f32)
    input_a = lax.psum_scatter(part_a, "head", scatter_dimension=1, tiled=True)
    input_grad = jnp.concatenate([input_a.astype(f32), input_b], axis=0)
    hidden_t = hidden.reshape(nz, 2, own // 2, cols).transpose(1, 0, 2, 3).reshape(rows, cols)

    dqkv = jnp.concatenate([dqkv_a, dqkv_b], axis=0)
    grad_qkv = t_dot(tokens_full, dqkv).astype(bf16)
    sqk = jnp.pad((sqk_a + sqk_b), ((0, EXTRA - 8), (0, 2 * cols)))
    shard = [lax.dynamic_slice_in_dim(grad_qkv, (b ^ r) * span, span, 0) for r in range(nb)]
    shard = [jnp.concatenate([s, sqk.astype(bf16)], axis=0) for s in shard]
    qbits = [1 << n for n in range(int(math.log2(nb)))]
    held = {r: shard[r] for r in range(nb)}
    for bit in qbits:
        send_at = [r for r in held if r & bit]
        send = jnp.concatenate([held[r] for r in send_at], axis=0).astype(bf16)
        got = swap_batch(send, bit)
        size = span + EXTRA
        held = {
            r ^ bit: held[r ^ bit].astype(f32) + got[n * size : (n + 1) * size].astype(f32)
            for n, r in enumerate(send_at)
        }
    cell = width // (nz * nb)
    sum_sqk = lax.dynamic_slice_in_dim(held[0][span, :cols], b * cell, cell, 0)
    qkv_new = adam_wide(w_qkv, held[0][:span], moment_qkv, square_qkv)

    def both_halves(total):
        two = (total[:span], total[span : 2 * span])
        here = jnp.concatenate([pick(two, core), total[2 * span :]], axis=0)
        there = jnp.concatenate([pick(two, 1 - core), total[2 * span :]], axis=0)
        there = swap_core(there.astype(bf16)).astype(f32)
        return [pick((here, there), core), pick((there, here), core)]

    join = lambda halves, at, size: [p[:span, at : at + size] for p in halves]
    halves = both_halves(sum_down_t)
    down_new = adam_tall(w_down, jnp.concatenate(join(halves, 0, half), axis=1), moment_down, square_down)
    halves = both_halves(sum_up_t)
    grad_up = jnp.concatenate(join(halves, 0, half) + join(halves, half, half), axis=1)
    up_new = adam_wide(w_up, grad_up, moment_up, square_up)
    out_new = adam_tall(w_out, jnp.concatenate(join(halves, 2 * half, hc), axis=1), moment_out, square_out)
    suv_rows = jnp.stack(
        [jnp.concatenate([p[span, c * half : (c + 1) * half] for p in halves]) for c in range(2)]
    )
    sum_suv = lax.dynamic_slice_in_dim(suv_rows, b * (hid // nb), hid // nb, 1)
    alphas = halves[0][span + 1] + halves[1][span + 1]
    sum_attn = lax.dynamic_slice_in_dim(alphas[:cols], b * cell, cell, 0)
    sum_mlp = lax.dynamic_slice_in_dim(alphas[cols : 2 * cols], b * cell, cell, 0)

    hidden = hidden_t.astype(f32)

    squares = [qkv_new[4], out_new[4][:1], up_new[4], down_new[4][:1]]
    sizes = [t.size for t in squares]
    norms = jnp.concatenate([t.reshape(-1) for t in squares]).reshape(-1, 128)
    for bit in qbits:
        norms = norms + swap_batch(norms, bit)
    norms = norms.reshape(-1)
    ends = [0] + [sum(sizes[: n + 1]) for n in range(4)]
    back = lambda n, shape: norms[ends[n] : ends[n + 1]].reshape(shape)
    eight = lambda value: jnp.broadcast_to(value, (8, value.shape[1]))
    new_qkv, new_out, new_up, new_down = scale_weights(
        [back(0, (3, cols)), eight(back(1, (1, cols))), back(2, (2, hid)), eight(back(3, (1, hid)))],
        [qkv_new[3], out_new[3], up_new[3], down_new[3]],
        width,
    )
    sum_qkv, first_a, second_a = qkv_new[:3]
    sum_out, first_b, second_b = out_new[:3]
    sum_up, first_c, second_c = up_new[:3]
    sum_down, first_d, second_d = down_new[:3]
    return (
        hidden,
        input_grad,
        sum_qkv,
        sum_out,
        sum_up,
        sum_down,
        first_a,
        first_b,
        first_c,
        first_d,
        second_a,
        second_b,
        second_c,
        second_d,
        new_qkv,
        new_out,
        new_up,
        new_down,
        sum_sqk,
        sum_attn,
        sum_mlp,
        sum_suv,
    )


def solution(mesh):
    tokens = P("batch", "head")
    wide = P("batch", None, "head")
    tall = P("head", "batch")
    flat = P(("head", "batch"))
    weights = (wide, tall, wide, tall)
    return jax.shard_map(
        per_device,
        mesh=mesh,
        in_specs=(tokens, tokens, P("batch"))
        + weights * 3
        + (P("head"), P(), P(), P(None, "head")),
        out_specs=(tokens, tokens) + weights * 4 + (flat, flat, flat, P(None, ("head", "batch"))),
        check_vma=False,
    )
```

```python
import functools
import math

import jax
import jax.numpy as jnp
from jax import lax
from jax.experimental import pallas as pl
from jax.experimental.pallas import tpu as pltpu
from jax.sharding import PartitionSpec as P

HEAD_DIM = 64
SHORT = 1024

layer_eps = 1e-06
learn_rate = 0.008
beta_one = 0.9
beta_two = 0.95
adam_eps = 1e-08
bias_one = 1.0 - math.exp(100.0 * math.log(0.9))
bias_two = 1.0 - math.exp(100.0 * math.log(0.95))
score_scale = 8.0
LOG2E = math.log2(math.e)
LN2 = math.log(2.0)

bf16 = jnp.bfloat16
f32 = jnp.float32
VMEM_LIMIT = 56 * 1024 * 1024


def dot(a, b):
    return jnp.dot(a, b, preferred_element_type=f32)


def dot_t(a, b):
    return lax.dot_general(a, b, (((1,), (1,)), ((), ())), preferred_element_type=f32)


def t_dot(a, b):
    return lax.dot_general(a, b, (((0,), (0,)), ((), ())), preferred_element_type=f32)


def params():
    return pltpu.CompilerParams(vmem_limit_bytes=VMEM_LIMIT)


def full_spec(shape):
    return pl.BlockSpec(shape, lambda *_: (0,) * len(shape))


def head_sum(value, ones):
    high = value.astype(bf16)
    low = (value - high.astype(f32)).astype(bf16)
    return dot(high, ones) + dot(low, ones)


def widen(value, cols):
    return jnp.concatenate([value] * (cols // value.shape[1]), axis=1)


def swap_halves(value):
    cols = value.shape[-1]
    half = HEAD_DIM // 2
    lane = lax.broadcasted_iota(jnp.int32, value.shape, 1)
    first = (lane % HEAD_DIM) < half
    up = pltpu.roll(value, cols - half, 1)
    down = pltpu.roll(value, half, 1)
    return jnp.where(first, up, down)


def qkv_kernel(place_ref, *refs, parts):
    tokens = refs[:parts]
    w_ref, cos_ref, sin_ref, gain_ref, ones_ref, x_ref, q_ref, k_ref, v_ref, rho_ref = refs[parts:]
    cols = v_ref.shape[1]
    z = place_ref[0]
    for n in range(parts):
        at = pl.multiple_of(lax.rem(z + parts - n, parts) * cols, cols)
        x_ref[:, pl.ds(at, cols)] = tokens[n][...]
    proj = dot(x_ref[...], w_ref[...])
    cosine = widen(cos_ref[...], cols)
    sine = widen(sin_ref[...], cols)
    ones = ones_ref[...]
    gain = gain_ref[...]
    heads = cols // HEAD_DIM
    lane = lax.broadcasted_iota(jnp.int32, rho_ref.shape, 1)
    stats = jnp.zeros(rho_ref.shape, f32)
    for c, (out, scale) in enumerate(((q_ref, score_scale * LOG2E), (k_ref, 1.0))):
        part = proj[:, c * cols : (c + 1) * cols]
        rho = lax.rsqrt(head_sum(part * part, ones) + layer_eps)
        rot = part * cosine + swap_halves(part) * sine
        out[...] = (rot * rho * (gain * scale)).astype(bf16)
        for h in range(heads):
            stats = jnp.where(lane == c * heads + h, rho[:, h * HEAD_DIM : h * HEAD_DIM + 1], stats)
    rho_ref[...] = stats
    v_ref[...] = proj[:, 2 * cols :].astype(bf16)


def qkv_project(place, tokens, w, cosine, sine, gain, ones):
    rows, cols = tokens[0].shape
    parts = len(tokens)
    width = parts * cols
    blk = 512
    row = lambda n: pl.BlockSpec((blk, n), lambda i, s: (i, 0))
    return pl.pallas_call(
        functools.partial(qkv_kernel, parts=parts),
        grid_spec=pltpu.PrefetchScalarGridSpec(
            num_scalar_prefetch=1,
            grid=(rows // blk,),
            in_specs=[row(cols)] * parts
            + [full_spec((width, 3 * cols)), row(128), row(128)]
            + [full_spec((1, cols)), full_spec((cols, cols))],
            out_specs=[row(width)] + [row(cols)] * 3 + [row(128)],
        ),
        out_shape=[jax.ShapeDtypeStruct((rows, width), bf16)]
        + [jax.ShapeDtypeStruct((rows, cols), bf16)] * 3
        + [jax.ShapeDtypeStruct((rows, 128), f32)],
        compiler_params=params(),
    )(place, *tokens, w, cosine, sine, gain, ones)


def head_masks(cols, heads):
    lane = lax.broadcasted_iota(jnp.int32, (1, cols), 1) // HEAD_DIM
    return [(lane == h) for h in range(heads)]


def masked(value, mask):
    return jnp.where(mask, value, jnp.zeros_like(value))


def attn_fwd_kernel(long_ref, q_ref, k_ref, v_ref, y_ref, l_ref, acc, mass, *, heads, blk, sub, first):
    i = first + pl.program_id(0)
    cols = q_ref.shape[1]
    masks = head_masks(cols, heads)
    per = SHORT // blk
    low = jnp.where(long_ref[0] != 0, 0, (i // per) * per)
    acc[...] = jnp.zeros_like(acc)
    mass[...] = jnp.zeros_like(mass)

    def lanes(p):
        total = p[:, 0:128]
        for n in range(1, p.shape[1] // 128):
            total = total + p[:, n * 128 : (n + 1) * 128]
        return total

    def body(j, carry):
        start = pl.multiple_of(j * blk, blk)
        keys = k_ref[pl.ds(start, blk), :]
        vals = v_ref[pl.ds(start, blk), :]
        q = q_ref[...]
        total = jnp.zeros(acc.shape, f32)
        for h in range(heads):
            p = jnp.exp2(dot_t(masked(q, masks[h]), keys))
            mass[h] += lanes(p)
            total += dot(p.astype(bf16), masked(vals, masks[h]))
        acc[...] += total
        return carry

    lax.fori_loop(low, i, body, 0)
    start = pl.multiple_of(i * blk, blk)
    causal = lax.broadcasted_iota(jnp.int32, (sub, sub), 0) >= lax.broadcasted_iota(
        jnp.int32, (sub, sub), 1
    )
    for a in range(blk // sub):
        rows = slice(a * sub, (a + 1) * sub)
        q = q_ref[rows, :]
        for b in range(a + 1):
            at = pl.multiple_of(start + b * sub, sub)
            keys = k_ref[pl.ds(at, sub), :]
            vals = v_ref[pl.ds(at, sub), :]
            total = jnp.zeros((sub, cols), f32)
            for h in range(heads):
                p = jnp.exp2(dot_t(masked(q, masks[h]), keys))
                if a == b:
                    p = jnp.where(causal, p, 0.0)
                mass[h, rows, :] += lanes(p)
                total += dot(p.astype(bf16), masked(vals, masks[h]))
            acc[rows, :] += total
    inverse = jnp.zeros(acc.shape, f32)
    logs = jnp.zeros(l_ref.shape, f32)
    lane = lax.broadcasted_iota(jnp.int32, l_ref.shape, 1)
    for h in range(heads):
        column = jnp.sum(mass[h], axis=1, keepdims=True)
        inverse = jnp.where(masks[h], 1.0 / column, inverse)
        logs = jnp.where(lane == h, jnp.log2(column), logs)
    y_ref[...] = (acc[...] * inverse).astype(bf16)
    l_ref[...] = logs


def attn_fwd(is_long, q, k, v, first, count):
    rows, cols = q.shape
    heads = cols // HEAD_DIM
    blk, sub = 512, 256
    row = lambda n: pl.BlockSpec((blk, n), lambda i, s: (i, 0))
    whole = pl.BlockSpec(((first + count) * blk, cols), lambda i, s: (0, 0))
    return pl.pallas_call(
        functools.partial(attn_fwd_kernel, heads=heads, blk=blk, sub=sub, first=first),
        grid_spec=pltpu.PrefetchScalarGridSpec(
            num_scalar_prefetch=1,
            grid=(count,),
            in_specs=[pl.BlockSpec((blk, cols), lambda i, s: (first + i, 0)), whole, whole],
            out_specs=[row(cols), row(128)],
            scratch_shapes=[pltpu.VMEM((blk, cols), f32), pltpu.VMEM((heads, blk, 128), f32)],
        ),
        out_shape=[
            jax.ShapeDtypeStruct((count * blk, cols), bf16),
            jax.ShapeDtypeStruct((count * blk, 128), f32),
        ],
        compiler_params=params(),
    )(is_long, q, k, v)


def attn_bwd_kernel(
    long_ref, q_ref, qk_ref, dy_ref, y_ref, l_ref, k_ref, v_ref, rho_ref, cos_ref, sin_ref, gain_ref,
    ones_ref, dk_in, dv_in, out_ref, dk_out, dv_out, s_ref, acc, dk_acc, dv_acc, stats, *, heads, blk, sub, first, count
):
    step = pl.program_id(0)
    local = count - 1 - step
    i = first + local
    cols = q_ref.shape[1]
    masks = head_masks(cols, heads)
    per = SHORT // blk
    low = jnp.where(long_ref[0] != 0, 0, (i // per) * per)
    ones = ones_ref[...]
    gain = gain_ref[...]

    @pl.when(step == 0)
    def _():
        dk_acc[...] = jnp.zeros_like(dk_acc)
        dv_acc[...] = jnp.zeros_like(dv_acc)
        s_ref[...] = jnp.zeros_like(s_ref)
        if dk_in is not None:
            dk_acc[...] = dk_in[...]
            dv_acc[...] = dv_in[...]

    acc[...] = jnp.zeros_like(acc)
    prod = dy_ref[...].astype(f32) * y_ref[...].astype(f32)
    high = prod.astype(bf16)
    rest = (prod - high.astype(f32)).astype(bf16)
    pickers = (
        lax.broadcasted_iota(jnp.int32, (8, cols), 1) // HEAD_DIM
        == lax.broadcasted_iota(jnp.int32, (8, cols), 0)
    ).astype(bf16)
    stats[0:8, :] = dot_t(pickers, high) + dot_t(pickers, rest)
    stats[8:16, :] = l_ref[...].T[0:8, :]

    def piece(at, size, rows, causal):
        keys = k_ref[pl.ds(at, size), :]
        vals = v_ref[pl.ds(at, size), :]
        q = q_ref[rows, :]
        dy = dy_ref[rows, :]
        total_q = jnp.zeros(q.shape, f32)
        total_k = jnp.zeros(keys.shape, f32)
        total_v = jnp.zeros(keys.shape, f32)
        for h in range(heads):
            qm = masked(q, masks[h])
            dym = masked(dy, masks[h])
            p = jnp.exp2(dot_t(keys, qm) - stats[8 + h : 9 + h, rows])
            if causal is not None:
                p = jnp.where(causal, p, 0.0)
            ds = (p * (dot_t(vals, dym) - stats[h : h + 1, rows])).astype(bf16)
            total_v += dot(p.astype(bf16), dym)
            total_k += dot(ds, qm)
            total_q += t_dot(ds, masked(keys, masks[h]))
        acc[rows, :] += total_q
        dk_acc[pl.ds(at, size), :] += total_k
        dv_acc[pl.ds(at, size), :] += total_v

    def body(j, carry):
        piece(pl.multiple_of(j * blk, blk), blk, slice(0, blk), None)
        return carry

    lax.fori_loop(low, i, body, 0)
    start = pl.multiple_of(i * blk, blk)
    causal = lax.broadcasted_iota(jnp.int32, (sub, sub), 0) <= lax.broadcasted_iota(
        jnp.int32, (sub, sub), 1
    )
    for a in range(blk // sub):
        for b in range(a + 1):
            piece(
                pl.multiple_of(start + b * sub, sub),
                sub,
                slice(a * sub, (a + 1) * sub),
                causal if a == b else None,
            )
    cosine = widen(cos_ref[...], cols)
    sine = widen(sin_ref[...], cols)
    total = jnp.zeros((1, cols), f32)
    here = pl.ds(start, blk)
    for c, (value, unit, up, scale) in enumerate(
        (
            (acc[...], q_ref[...], score_scale, score_scale * LOG2E),
            (dk_acc[here, :], k_ref[here, :], LN2, 1.0),
        )
    ):
        rho = jnp.zeros(value.shape, f32)
        for h in range(heads):
            at = c * heads + h
            rho = jnp.where(masks[h], rho_ref[:, at : at + 1], rho)
        grad = value * up
        unit = unit.astype(f32) * (1.0 / (gain * scale))
        total += jnp.sum(grad * unit, axis=0, keepdims=True)
        grad = grad * gain
        back = rho * (grad - unit * head_sum(grad * unit, ones))
        turned = back * cosine - swap_halves(back) * sine
        out_ref[:, c * cols : (c + 1) * cols] = turned.astype(bf16)
    out_ref[:, 2 * cols :] = dv_acc[here, :].astype(bf16)
    s_ref[0:1, :] += total
    if dk_out is not None:
        @pl.when(step == count - 1)
        def _():
            dk_out[...] = dk_acc[0 : first * blk, :]
            dv_out[...] = dv_acc[0 : first * blk, :]


def attn_bwd(is_long, q, k, v, dy, y, logs, rho, cosine, sine, gain, ones, first, count, carry):
    rows, cols = q.shape
    heads = cols // HEAD_DIM
    blk, sub = 512, 256
    top = (first + count) * blk
    at = lambda s: first + count - 1 - s
    row = lambda n: pl.BlockSpec((blk, n), lambda s, m: (at(s), 0))
    whole = pl.BlockSpec((top, cols), lambda s, m: (0, 0))
    ins = [q, k, dy, y, logs, k, v, rho, cosine, sine, gain, ones]
    mine = lambda n: pl.BlockSpec((blk, n), lambda s, m: (count - 1 - s, 0))
    in_specs = [row(cols)] * 2 + [mine(cols)] * 2 + [mine(128), whole, whole] + [row(128)] * 3
    in_specs += [full_spec((1, cols)), full_spec((cols, cols))]
    body = functools.partial(
        attn_bwd_kernel, heads=heads, blk=blk, sub=sub, first=first, count=count
    )
    outs = [jax.ShapeDtypeStruct((count * blk, 3 * cols), bf16)]
    out_specs = [pl.BlockSpec((blk, 3 * cols), lambda s, m: (count - 1 - s, 0))]
    if first:
        outs += [jax.ShapeDtypeStruct((first * blk, cols), f32)] * 2
        out_specs += [full_spec((first * blk, cols))] * 2
        inner = lambda *r: body(*r[:13], None, None, *r[13:])
    else:
        ins += carry
        in_specs += [full_spec((top, cols))] * 2
        inner = lambda *r: body(*r[:16], None, None, *r[16:])
    outs.append(jax.ShapeDtypeStruct((8, cols), f32))
    out_specs.append(full_spec((8, cols)))
    return pl.pallas_call(
        inner,
        grid_spec=pltpu.PrefetchScalarGridSpec(
            num_scalar_prefetch=1,
            grid=(count,),
            in_specs=in_specs,
            out_specs=out_specs,
            scratch_shapes=[
                pltpu.VMEM((blk, cols), f32),
                pltpu.VMEM((top, cols), f32),
                pltpu.VMEM((top, cols), f32),
                pltpu.VMEM((16, blk), f32),
            ],
        ),
        out_shape=outs,
        compiler_params=params(),
    )(is_long, *ins)


def row_norm(value):
    return lax.rsqrt(jnp.mean(value * value, axis=1, keepdims=True) + layer_eps)


def norm_back(scale, result, grad):
    return scale * (grad - result * jnp.mean(grad * result, axis=1, keepdims=True))


def pack_kernel(core_ref, up_ref, down_ref, out_ref, mine_ref, theirs_ref):
    half = up_ref.shape[2] // 2
    low = core_ref[0] == 0
    down = down_ref[...].astype(bf16).T
    out = out_ref[...].astype(bf16).T
    for ref, first in ((mine_ref, low), (theirs_ref, jnp.logical_not(low))):
        for c in range(2):
            ref[:, c * half : (c + 1) * half] = jnp.where(
                first, up_ref[:, c, :half], up_ref[:, c, half:]
            ).astype(bf16)
        ref[:, 2 * half : 3 * half] = jnp.where(first, down[:, :half], down[:, half:])
        ref[:, 3 * half :] = out


def pack(core, w_up, w_down, w_out):
    span, _, hid = w_up.shape
    cols = w_out.shape[0]
    vmem = pl.BlockSpec(memory_space=pltpu.VMEM)
    return pl.pallas_call(
        pack_kernel,
        in_specs=[pl.BlockSpec(memory_space=pltpu.SMEM)] + [vmem] * 3,
        out_specs=[vmem] * 2,
        out_shape=[jax.ShapeDtypeStruct((span, 3 * hid // 2 + cols), bf16)] * 2,
        compiler_params=params(),
    )(core, w_up, w_down, w_out)


def place_of(r, chip, chunk):
    return pl.ds(pl.multiple_of((r ^ chip) * chunk, chunk), chunk)


def put_relative(ref, chip, chips, fast):
    if not fast:
        return ref[...]
    if len(ref.shape) == 3:
        return jnp.concatenate([ref[r ^ chip] for r in range(chips)], axis=1)
    chunk = ref.shape[1] // chips
    return jnp.concatenate([ref[:, place_of(r, chip, chunk)] for r in range(chips)], axis=1)


def put_natural(ref, value, chip, chips, fast):
    if not fast:
        ref[...] = value
        return
    chunk = value.shape[1] // chips
    for r in range(chips):
        part = value[:, r * chunk : (r + 1) * chunk]
        if len(ref.shape) == 3:
            ref[r ^ chip] = part
        else:
            ref[:, place_of(r, chip, chunk)] = part


def attn_out_kernel(place_ref, *refs, counts, chips, fast):
    total = sum(counts)
    flat, refs = refs[:total], refs[total:]
    ya_ref, yb_ref, x_ref, alpha_ref, ha_ref, h1_ref, hb_ref, stat_ref, acc = refs
    z, chip = place_ref[0], place_ref[1]
    parts = len(counts)
    early = pl.program_id(0) == 0
    index = 0
    for n in range(parts):
        at = lax.rem(z + parts - n, parts)
        y = jnp.where(early, ya_ref[at], yb_ref[at])
        column = 0
        for piece in flat[index : index + counts[n]]:
            part = slice(column, column + piece.shape[0])
            if n == 0:
                acc[:, part] = dot_t(y, piece[...])
            else:
                acc[:, part] += dot_t(y, piece[...])
            column += piece.shape[0]
        index += counts[n]
    total = acc[...]
    norm = row_norm(total)
    hidden = total * norm
    start = put_relative(x_ref, chip, chips, fast).astype(f32)
    mixed = start + alpha_ref[...] * (hidden - start)
    first_norm = row_norm(mixed)
    out = mixed * first_norm
    ha_ref[...] = hidden
    h1_ref[...] = out
    hb_ref[...] = out.astype(bf16)
    lane = lax.broadcasted_iota(jnp.int32, stat_ref.shape, 1)
    stat_ref[...] = jnp.where(lane == 0, norm, first_norm)


def own_rows(blk, parts, width, fast):
    if fast:
        return pl.BlockSpec((blk, width), lambda i, s: (i * parts + s[0], 0))
    return pl.BlockSpec((blk, width), lambda i, s: (i, 0))


def out_weights(slots, cols):
    flat = [p for slot in slots for p in slot]
    last = flat[0].shape[1] // cols - 1
    return flat, [pl.BlockSpec((p.shape[0], cols), lambda i, s: (0, last)) for p in flat]


def attn_out(place, ya, yb, slots, x, alpha, chips, fast):
    parts, blk, cols = ya.shape
    width = x.shape[1]
    rows = 2 * blk
    row = lambda n: pl.BlockSpec((blk, n), lambda i, s: (i, 0))
    flat, specs = out_weights(slots, cols)
    return pl.pallas_call(
        functools.partial(attn_out_kernel, counts=[len(t) for t in slots], chips=chips, fast=fast),
        grid_spec=pltpu.PrefetchScalarGridSpec(
            num_scalar_prefetch=1,
            grid=(2,),
            in_specs=specs
            + [full_spec(ya.shape)] * 2
            + [own_rows(blk, parts, width, fast), full_spec((1, width))],
            out_specs=[row(width)] * 3 + [row(128)],
            scratch_shapes=[pltpu.VMEM((blk, width), f32)],
        ),
        out_shape=[jax.ShapeDtypeStruct((rows, width), d) for d in (f32, f32, bf16)]
        + [jax.ShapeDtypeStruct((rows, 128), f32)],
        compiler_params=params(),
    )(place, *flat, ya, yb, x, alpha)


def loss_kernel(place_ref, own_ref, got_ref, h1_ref, cot_ref, alpha_ref, hidden_ref, dmo_ref, base_ref, ga_ref, *, chips, fast):
    chip = place_ref[1]
    total = own_ref[...] + got_ref[...].astype(f32)
    alpha = alpha_ref[...]
    norm = row_norm(total)
    inner = total * norm
    h1 = h1_ref[...]
    mixed = h1 + alpha * (inner - h1)
    last = row_norm(mixed)
    hidden = mixed * last
    grad = norm_back(last, hidden, put_relative(cot_ref, chip, chips, fast).astype(f32))
    put_natural(hidden_ref, hidden.astype(bf16), chip, chips, fast)
    base_ref[...] = (1.0 - alpha) * grad
    dmo_ref[...] = norm_back(norm, inner, alpha * grad).astype(bf16)

    @pl.when(pl.program_id(0) == 0)
    def _():
        ga_ref[...] = jnp.zeros_like(ga_ref)

    ga_ref[0:1, :] += jnp.sum(grad * (inner - h1), axis=0, keepdims=True)


def loss(place, own, got, h1, cot, alpha, chips, fast):
    rows, width = own.shape
    blk = rows // 2
    row = pl.BlockSpec((blk, width), lambda i, s: (i, 0))
    part = row
    if fast:
        part = pl.BlockSpec((chips, blk, width // chips), lambda i, s: (0, i, 0))
    return pl.pallas_call(
        functools.partial(loss_kernel, chips=chips, fast=fast),
        grid_spec=pltpu.PrefetchScalarGridSpec(
            num_scalar_prefetch=1,
            grid=(rows // blk,),
            in_specs=[row] * 3 + [part, full_spec((1, width))],
            out_specs=[part] + [row] * 2 + [full_spec((8, width))],
        ),
        out_shape=[jax.ShapeDtypeStruct(cot.shape, bf16)]
        + [jax.ShapeDtypeStruct((rows, width), d) for d in (bf16, f32)]
        + [jax.ShapeDtypeStruct((8, width), f32)],
        compiler_params=params(),
    )(place, own, got, h1, cot, alpha)


def first_back_kernel(place_ref, *refs, counts, chips, fast):
    total = sum(counts)
    flat, refs = refs[:total], refs[total:]
    own_ref, got_ref, base_ref, h1_ref, ha_ref, x_ref, stat_ref, alpha_ref = refs[:8]
    do_ref, through_ref, ga_ref, dya_ref, dyb_ref = refs[8:]
    z, chip = place_ref[0], place_ref[1]
    alpha = alpha_ref[...]
    grad = base_ref[...] + own_ref[...] + got_ref[...].astype(f32)
    grad = norm_back(stat_ref[:, 1:2], h1_ref[...], grad)
    ha = ha_ref[...]
    put_natural(through_ref, ((1.0 - alpha) * grad).astype(bf16), chip, chips, fast)
    back = norm_back(stat_ref[:, 0:1], ha, alpha * grad).astype(bf16)
    do_ref[...] = back
    parts = len(counts)
    step = pl.program_id(0)
    index = 0
    for n in range(parts):
        at = lax.rem(z + parts - n, parts)
        part = jnp.zeros(dya_ref.shape[1:], f32)
        column = 0
        for piece in flat[index : index + counts[n]]:
            part += dot(do_ref[:, column : column + piece.shape[0]], piece[...])
            column += piece.shape[0]
        index += counts[n]
        part = part.astype(bf16)
        for side, ref in enumerate((dya_ref, dyb_ref)):

            @pl.when(step == side)
            def _(ref=ref, part=part, at=at):
                ref[at] = part

    @pl.when(step == 0)
    def _():
        ga_ref[...] = jnp.zeros_like(ga_ref)

    start = put_relative(x_ref, chip, chips, fast).astype(f32)
    ga_ref[0:1, :] += jnp.sum(grad * (ha - start), axis=0, keepdims=True)


def first_back(place, own, got, base, h1, ha, x, stat, alpha, slots, chips, fast, cols):
    rows, width = own.shape
    parts = len(slots)
    blk = rows // 2
    row = lambda n: pl.BlockSpec((blk, n), lambda i, s: (i, 0))
    flat, specs = out_weights(slots, cols)
    return pl.pallas_call(
        functools.partial(first_back_kernel, counts=[len(t) for t in slots], chips=chips, fast=fast),
        grid_spec=pltpu.PrefetchScalarGridSpec(
            num_scalar_prefetch=1,
            grid=(2,),
            in_specs=specs
            + [row(width)] * 5
            + [own_rows(blk, parts, width, fast), row(128), full_spec((1, width))],
            out_specs=[row(width)] * 2
            + [full_spec((8, width))]
            + [full_spec((parts, blk, cols))] * 2,
        ),
        out_shape=[jax.ShapeDtypeStruct((rows, width), bf16)] * 2
        + [jax.ShapeDtypeStruct((8, width), f32)]
        + [jax.ShapeDtypeStruct((parts, blk, cols), bf16)] * 2,
        compiler_params=params(),
    )(place, *flat, own, got, base, h1, ha, x, stat, alpha)


def fetch_weights(q, slots, wbuf, sems):
    def copies(j):
        at = 0
        found = []
        for p, piece in enumerate(slots[j]):
            size = piece.shape[0]
            found.append(
                pltpu.make_async_copy(
                    piece.at[:, : wbuf.shape[2]], wbuf.at[j % 2, at : at + size, :], sems.at[j % 2, p]
                )
            )
            at += size
        return found

    for j in range(len(slots)):

        @pl.when(q == j)
        def _(j=j):
            if j == 0:
                for copy in copies(0):
                    copy.start()
            if j + 1 < len(slots):
                for copy in copies(j + 1):
                    copy.start()
            for copy in copies(j):
                copy.wait()


def mlp_fwd_kernel(*refs, half, counts):
    total = sum(counts)
    flat, refs = refs[:total], refs[total:]
    slots, at = [], 0
    for n in counts:
        slots.append(flat[at : at + n])
        at += n
    ha_ref, hb_ref, suv_ref, act_ref, uv_ref, own_ref, got_ref, acc, wbuf, sems = refs
    rows = ha_ref.shape[0]
    q = pl.program_id(0)

    @pl.when(q == 0)
    def _():
        own_ref[...] = jnp.zeros_like(own_ref)
        acc[...] = jnp.zeros_like(acc)

    fetch_weights(q, slots, wbuf, sems)
    w = wbuf.at[lax.rem(q, 2)]
    for base, h_ref, sum_ref in ((0, ha_ref, own_ref), (rows, hb_ref, acc)):
        at = slice(base, base + rows)
        pair = dot(h_ref[...], w[:, : 2 * half])
        lifted = pair[:, :half] * suv_ref[0:1, :]
        gated = pair[:, half:] * suv_ref[1:2, :]
        act = (lifted * gated * jax.nn.sigmoid(gated)).astype(bf16)
        uv_ref[at, :] = pair.astype(bf16)
        act_ref[at, :] = act
        sum_ref[...] += dot_t(act, w[:, 2 * half : 3 * half])

    @pl.when(q == pl.num_programs(0) - 1)
    def _():
        got_ref[...] = acc[...].astype(bf16)


def mlp_fwd(ha, hb, slots, suv):
    rows, width = ha.shape
    parts, _, half = suv.shape
    take = lambda n: pl.BlockSpec((None, 2 * rows, n), lambda q: (q, 0, 0))
    whole = full_spec((rows, width))
    anywhere = pl.BlockSpec(memory_space=pl.ANY)
    flat = [p for slot in slots for p in slot]
    return pl.pallas_call(
        functools.partial(mlp_fwd_kernel, half=half, counts=[len(s) for s in slots]),
        grid=(parts,),
        in_specs=[anywhere] * len(flat)
        + [whole, whole, pl.BlockSpec((None, 2, half), lambda q: (q, 0, 0))],
        out_specs=[take(half), take(2 * half), whole, whole],
        out_shape=[
            jax.ShapeDtypeStruct((parts, 2 * rows, half), bf16),
            jax.ShapeDtypeStruct((parts, 2 * rows, 2 * half), bf16),
            jax.ShapeDtypeStruct((rows, width), f32),
            jax.ShapeDtypeStruct((rows, width), bf16),
        ],
        scratch_shapes=[
            pltpu.VMEM((rows, width), f32),
            pltpu.VMEM((2, width, 3 * half), bf16),
            pltpu.SemaphoreType.DMA((2, max(len(s) for s in slots))),
        ],
        compiler_params=params(),
    )(*flat, ha, hb, suv)


def mlp_bwd_kernel(*refs, half, counts):
    total = sum(counts)
    flat, refs = refs[:total], refs[total:]
    slots, at = [], 0
    for n in counts:
        slots.append(flat[at : at + n])
        at += n
    da_ref, db_ref, uv_ref, suv_ref, duv_ref, own_ref, got_ref, gs_ref, acc, wbuf, sems = refs
    rows = da_ref.shape[0]
    q = pl.program_id(0)

    @pl.when(q == 0)
    def _():
        own_ref[...] = jnp.zeros_like(own_ref)
        acc[...] = jnp.zeros_like(acc)

    gs_ref[...] = jnp.zeros_like(gs_ref)
    fetch_weights(q, slots, wbuf, sems)
    w = wbuf.at[lax.rem(q, 2)]
    for base, d_ref, sum_ref in ((0, da_ref, own_ref), (rows, db_ref, acc)):
        at = slice(base, base + rows)
        grad = dot(d_ref[...], w[:, 2 * half : 3 * half])
        up = uv_ref[at, :half].astype(f32)
        gate = uv_ref[at, half:].astype(f32)
        su = suv_ref[0:1, :]
        sv = suv_ref[1:2, :]
        lifted = up * su
        gated = gate * sv
        sigma = jax.nn.sigmoid(gated)
        da = grad * gated * sigma
        db = grad * lifted * sigma * (1.0 + gated * (1.0 - sigma))
        gs_ref[0:1, :] += jnp.sum(da * up, axis=0, keepdims=True)
        gs_ref[1:2, :] += jnp.sum(db * gate, axis=0, keepdims=True)
        duv_ref[at, :half] = (da * su).astype(bf16)
        duv_ref[at, half:] = (db * sv).astype(bf16)
        sum_ref[...] += dot_t(duv_ref[at, :], w[:, : 2 * half])

    @pl.when(q == pl.num_programs(0) - 1)
    def _():
        got_ref[...] = acc[...].astype(bf16)


def mlp_bwd(da, db, slots, uv, suv):
    rows, width = da.shape
    parts, _, half = suv.shape
    take = lambda n: pl.BlockSpec((None, 2 * rows, n), lambda q: (q, 0, 0))
    whole = full_spec((rows, width))
    anywhere = pl.BlockSpec(memory_space=pl.ANY)
    flat = [p for slot in slots for p in slot]
    return pl.pallas_call(
        functools.partial(mlp_bwd_kernel, half=half, counts=[len(s) for s in slots]),
        grid=(parts,),
        in_specs=[anywhere] * len(flat)
        + [
            whole,
            whole,
            take(2 * half),
            pl.BlockSpec((None, 2, half), lambda q: (q, 0, 0)),
        ],
        out_specs=[
            take(2 * half),
            whole,
            whole,
            pl.BlockSpec((None, 8, half), lambda q: (q, 0, 0)),
        ],
        out_shape=[
            jax.ShapeDtypeStruct((parts, 2 * rows, 2 * half), bf16),
            jax.ShapeDtypeStruct((rows, width), f32),
            jax.ShapeDtypeStruct((rows, width), bf16),
            jax.ShapeDtypeStruct((parts, 8, half), f32),
        ],
        scratch_shapes=[
            pltpu.VMEM((rows, width), f32),
            pltpu.VMEM((2, width, 3 * half), bf16),
            pltpu.SemaphoreType.DMA((2, max(len(s) for s in slots))),
        ],
        compiler_params=params(),
    )(*flat, da, db, uv, suv)


EXTRA = 16


def grad_kernel(place_ref, *refs, orders, parts, chunk, more):
    ha_ref, hb_ref = refs[:2]
    refs = refs[2:]
    if more:
        oa_ref, ob_ref, ya_ref, yb_ref, gs_ref, g1_ref, g2_ref = refs[:7]
        refs = refs[7:]
    val_ref, *outs = refs[:5]
    turned = refs[5]
    rows = ha_ref.shape[0]
    k = pl.program_id(0)

    @pl.when(k == 0)
    def _():
        turned[:, :rows] = ha_ref[...].T
        turned[:, rows:] = hb_ref[...].T
        if more:
            refs[6][:, :rows] = oa_ref[...].T
            refs[6][:, rows:] = ob_ref[...].T

    if more:
        size = outs[0].shape[2]
        fill = lambda row: jnp.concatenate([row, jnp.zeros((1, size - row.shape[1]), f32)], axis=1)
        line = lax.broadcasted_iota(jnp.int32, (EXTRA, size), 0)
        units = fill(jnp.concatenate([gs_ref[0:1, :], gs_ref[1:2, :]], axis=1))
        steps = fill(jnp.concatenate([g1_ref[0:1, :], g2_ref[0:1, :]], axis=1))
        extra = jnp.where(line == 0, units, jnp.where(line == 1, steps, 0.0)).astype(bf16)

    for side in range(2):

        @pl.when((k < parts // 2) == (side == 0))
        def _(side=side):
            for which, ref in zip(orders[side], outs[2 * side : 2 * side + 2]):
                for j, r in enumerate(which):
                    at = slice(r * chunk, (r + 1) * chunk)
                    value = dot(turned[at, :], val_ref[...]).astype(bf16)
                    size = value.shape[1]
                    ref[j, :chunk, :size] = value
                    if more:
                        ref[j, :chunk, size:] = (
                            dot(refs[6][at, :rows], ya_ref[...]) + dot(refs[6][at, rows:], yb_ref[...])
                        ).astype(bf16)
                        ref[j, chunk:, :] = extra


def weight_grads(place, sends, keeps, chips, hs, value, os=None, ys=None, extra=None):
    rows, width = hs[0].shape
    chunk = width // chips
    parts, _, size = value.shape
    more = os is not None
    hc = ys[1].shape[2] if more else 0
    tall = chunk + (EXTRA if more else 0)
    middle = parts // 2
    if chunk % 128:
        result = []
        for which, lo in ((sends[0], 0), (keeps[0], 0), (sends[1], middle), (keeps[1], middle)):
            cut = lambda pair: jnp.concatenate(
                [jnp.concatenate(pair, axis=0)[:, r * chunk : (r + 1) * chunk] for r in which], axis=1
            )
            found = []
            for k in range(lo, lo + middle):
                one = t_dot(cut(hs), value[k])
                if more:
                    at = (place[0] - k) % parts
                    y = lax.dynamic_index_in_dim(ys[0], at, 0, keepdims=False)
                    y = lax.dynamic_slice_in_dim(y, place[2] * hc, hc, 1)
                    y = jnp.concatenate([y, lax.dynamic_index_in_dim(ys[1], at, 0, keepdims=False)])
                    one = jnp.concatenate([one, t_dot(cut(os), y)], axis=1)
                one = one.reshape(len(which), chunk, size + hc)
                if more:
                    wide = jnp.broadcast_to(extra[k][None], (len(which), EXTRA, size + hc))
                    one = jnp.concatenate([one, wide], axis=1)
                found.append(one.astype(bf16))
            result.append(jnp.stack(found, axis=1))
        return [result[0], result[2]], [result[1], result[3]]
    whole = full_spec((rows, width))
    ins = list(hs)
    in_specs = [whole] * 2
    scratch = [pltpu.VMEM((width, 2 * rows), bf16)]
    if more:
        slot = lambda k, p: lax.rem(p[0] + parts - k, parts)
        cols = ys[0].shape[2]
        part = pl.BlockSpec((8, cols), lambda k, p: (0, slot(k, p) ^ p[1]))
        ins += [*os, ys[0], ys[1], *extra]
        in_specs += [whole] * 2
        in_specs += [
            pl.BlockSpec((None, rows, hc), lambda k, p: (slot(k, p), 0, p[2])),
            pl.BlockSpec((None, rows, hc), lambda k, p: (slot(k, p), 0, 0)),
            pl.BlockSpec((None, 8, size // 2), lambda k, p: (k, 0, 0)),
            part,
            part,
        ]
        scratch = scratch * 2
    ins.append(value)
    in_specs.append(pl.BlockSpec((None, 2 * rows, size), lambda k, p: (k, 0, 0)))
    lists = [sends[0], keeps[0], sends[1], keeps[1]]
    block = lambda one: (len(one), None, tall, size + hc)
    early = lambda k, p: (0, jnp.minimum(k, middle - 1), 0, 0)
    late = lambda k, p: (0, jnp.maximum(k - middle, 0), 0, 0)
    out = pl.pallas_call(
        functools.partial(
            grad_kernel, orders=(lists[:2], lists[2:]), parts=parts, chunk=chunk, more=more
        ),
        grid_spec=pltpu.PrefetchScalarGridSpec(
            num_scalar_prefetch=1,
            grid=(parts,),
            in_specs=in_specs,
            out_specs=[
                pl.BlockSpec(block(one), early if n < 2 else late) for n, one in enumerate(lists)
            ],
            scratch_shapes=scratch,
        ),
        out_shape=[
            jax.ShapeDtypeStruct((len(one), middle, tall, size + hc), bf16) for one in lists
        ],
        compiler_params=params(),
    )(place, *ins)
    return [out[0], out[2]], [out[1], out[3]]


def adam_values(weight, grad, first, second):
    first_new = beta_one * first + (1.0 - beta_one) * grad
    second_new = beta_two * second + (1.0 - beta_two) * grad * grad
    moved = weight - learn_rate * (first_new / bias_one) / (
        jnp.sqrt(second_new / bias_two) + adam_eps
    )
    return first_new, second_new, moved


def lane_sums(value):
    ones = jnp.ones((8, value.shape[1]), bf16)
    high = value.astype(bf16)
    low = (value - high.astype(f32)).astype(bf16)
    return dot_t(ones, high) + dot_t(ones, low)


def adam_wide_kernel(w_ref, g_ref, m_ref, v_ref, g_out, m_out, v_out, n_out, s_out):
    cols = w_ref.shape[2]
    for c in range(w_ref.shape[1]):
        grad = g_ref[:, c * cols : (c + 1) * cols]
        first, second, moved = adam_values(w_ref[:, c, :], grad, m_ref[:, c, :], v_ref[:, c, :])
        g_out[:, c, :] = grad
        m_out[:, c, :] = first
        v_out[:, c, :] = second
        n_out[:, c, :] = moved
        s_out[c : c + 1, :] = jnp.sum(moved * moved, axis=0, keepdims=True)


def adam_wide(w, g, m, v):
    vmem = pl.BlockSpec(memory_space=pltpu.VMEM)
    return pl.pallas_call(
        adam_wide_kernel,
        in_specs=[vmem] * 4,
        out_specs=[vmem] * 5,
        out_shape=[jax.ShapeDtypeStruct(w.shape, f32)] * 4
        + [jax.ShapeDtypeStruct(w.shape[1:], f32)],
        compiler_params=params(),
    )(w, g, m, v)


def adam_tall_kernel(w_ref, g_ref, m_ref, v_ref, g_out, m_out, v_out, n_out, s_out):
    grad = g_ref[...].T
    first, second, moved = adam_values(w_ref[...], grad, m_ref[...], v_ref[...])
    g_out[...] = grad
    m_out[...] = first
    v_out[...] = second
    n_out[...] = moved
    s_out[...] = lane_sums(moved * moved)


def adam_tall(w, g, m, v):
    vmem = pl.BlockSpec(memory_space=pltpu.VMEM)
    return pl.pallas_call(
        adam_tall_kernel,
        in_specs=[vmem] * 4,
        out_specs=[vmem] * 5,
        out_shape=[jax.ShapeDtypeStruct(w.shape, f32)] * 4
        + [jax.ShapeDtypeStruct((8, w.shape[0]), f32)],
        compiler_params=params(),
    )(w, g, m, v)


def scale_kernel(na_ref, nb_ref, nc_ref, nd_ref, a_ref, b_ref, c_ref, d_ref, ao_ref, bo_ref, co_ref, do_ref, *, width):
    factor = lambda value: lax.rsqrt(value / width + layer_eps)
    for norm, ref, out in ((na_ref, a_ref, ao_ref), (nc_ref, c_ref, co_ref)):
        for c in range(ref.shape[1]):
            out[:, c, :] = ref[:, c, :] * factor(norm[c : c + 1, :])
    for norm, ref, out in ((nb_ref, b_ref, bo_ref), (nd_ref, d_ref, do_ref)):
        out[...] = ref[...] * factor(norm[...]).T[:, 0:1]


def scale_weights(norms, weights, width):
    vmem = pl.BlockSpec(memory_space=pltpu.VMEM)
    return pl.pallas_call(
        functools.partial(scale_kernel, width=width),
        in_specs=[vmem] * 8,
        out_specs=[vmem] * 4,
        out_shape=[jax.ShapeDtypeStruct(w.shape, f32) for w in weights],
        compiler_params=params(),
    )(*norms, *weights)


def after(value, *others):
    return lax.optimization_barrier((value, *others))[0]


def per_device(
    layer_input,
    cotangent,
    positions,
    w_qkv,
    w_out,
    w_up,
    w_down,
    moment_qkv,
    moment_out,
    moment_up,
    moment_down,
    square_qkv,
    square_out,
    square_up,
    square_down,
    s_qk,
    alpha_attn,
    alpha_mlp,
    s_uv,
):
    nz = lax.axis_size("head")
    nb = lax.axis_size("batch")
    z = lax.axis_index("head")
    b = lax.axis_index("batch")
    core = b % 2
    chip = b // 2
    chips = nb // 2
    bits = [1 << n for n in range(int(math.log2(chips)))]
    rows, cols = layer_input.shape
    width = cols * nz
    own = rows // nz
    hid = w_down.shape[0]
    half = hid // 2
    hc = cols // 2
    heads = cols // HEAD_DIM
    span = w_qkv.shape[0]
    chunk = width // chips
    core_s = core.reshape(1).astype(jnp.int32)
    place = jnp.stack([z, chip, core]).astype(jnp.int32)
    fast = chunk == cols and chunk % 128 == 0

    def swap_batch(value, bit):
        return lax.ppermute(value, "batch", [(i, i ^ bit) for i in range(nb)])

    def swap_core(value):
        return swap_batch(value, 1)

    def swap_chip(value, bit):
        return swap_batch(value, 2 * bit)

    def onward(value, k=1):
        return lax.ppermute(value, "head", [(i, (i + k) % nz) for i in range(nz)])

    def exchange(value):
        return lax.all_to_all(value, "head", split_axis=0, concat_axis=0)

    def pick(pair, index):
        return jnp.where(index == 0, pair[0], pair[1])

    def relative(value):
        return jnp.concatenate(
            [
                lax.dynamic_slice_in_dim(value, (chip ^ r) * chunk, chunk, value.ndim - 1)
                for r in range(chips)
            ],
            axis=-1,
        )

    def spread(value):
        if chips <= 4:
            return [value] + [swap_chip(value, r) for r in range(1, chips)]
        for bit in bits:
            value = jnp.concatenate([value, swap_chip(value, bit)], axis=0)
        return [value]

    tokens = [layer_input, onward(layer_input)]
    mine, theirs = pack(core_s, w_up, w_down, w_out)
    qkv_own = after(w_qkv, mine).reshape(span, 3 * cols).astype(bf16)
    qkv_full = lax.all_gather(qkv_own, "batch", axis=0, tiled=True)
    theirs = swap_core(theirs)
    packet = jnp.concatenate([pick((mine, theirs), core), pick((theirs, mine), core)], axis=0)
    hops = [packet, onward(packet)]
    slots = [spread(packet)]
    suv_own = after(pick((s_uv[:, :half], s_uv[:, half:]), core), tokens[1])
    suv = jnp.stack([suv_own] + [onward(suv_own, n) for n in range(1, nz)])
    tokens[1], hops[1], places, suv, alpha_attn, alpha_mlp, *last = lax.optimization_barrier(
        (tokens[1], hops[1], positions, suv, alpha_attn, alpha_mlp, *slots[0])
    )
    slots[0] = list(last)

    freqs = jnp.exp(
        (jnp.arange(128) % (HEAD_DIM // 2)).astype(f32) * (-2.0 * math.log(10000.0) / HEAD_DIM)
    )
    phase = places.astype(f32)[:, None] * freqs[None, :]
    side = jnp.where(jnp.arange(128) % HEAD_DIM < HEAD_DIM // 2, -1.0, 1.0).astype(f32)
    cosine, sine = jnp.cos(phase), jnp.sin(phase) * side[None, :]
    lane = jnp.arange(cols) // HEAD_DIM
    ones = (lane[:, None] == lane[None, :]).astype(bf16)
    gain = s_qk.reshape(1, cols)
    is_long = (places[SHORT : SHORT + 1] != 0).astype(jnp.int32)
    attn_gain = relative(alpha_attn[None])
    mlp_gain = relative(alpha_mlp[None])

    for n in range(2, nz):
        slots.append(spread(hops[-1]))
        tokens.append(onward(tokens[-1]))
        if n < nz - 1:
            hops.append(onward(hops[-1]))
            tokens[-1], hops[-1], cosine, sine, ones, attn_gain, mlp_gain, *last = (
                lax.optimization_barrier(
                    (tokens[-1], hops[-1], cosine, sine, ones, attn_gain, mlp_gain, *slots[-1])
                )
            )
            slots[-1] = list(last)
    last_hop, tokens[-1] = lax.optimization_barrier((hops[-1], tokens[-1]))
    hops.append(onward(last_hop))

    blocks = rows // 512
    middle = blocks // 2
    tokens_full, q, k, v, rho = qkv_project(place, tokens, qkv_full, cosine, sine, gain, ones)
    y_a, logs_a = attn_fwd(is_long, q, k, v, 0, middle)
    q_b, hops[-1], *last = lax.optimization_barrier((after(q, y_a), hops[-1], *slots[-1]))
    slots[-1] = list(last)
    slots.append(spread(hops[-1]))
    y_b, logs_b = attn_fwd(is_long, q_b, k, v, middle, blocks - middle)
    y_one = exchange(y_a.reshape(nz, own // 2, cols))
    y_in, y_one = lax.optimization_barrier((y_b, y_one))
    y_two = exchange(y_in.reshape(nz, own // 2, cols))
    flat = lambda value: value.transpose(1, 0, 2).reshape(own, width)
    start = tokens_full
    if not fast:
        start = jnp.concatenate(
            [
                lax.dynamic_slice_in_dim(tokens_full, h * (rows // 2) + z * (own // 2), own // 2, 0)
                for h in range(2)
            ]
        )
        start = relative(start)
    y_mine = jnp.concatenate([y_one, y_two], axis=1)
    y_got = swap_core(lax.dynamic_slice_in_dim(y_mine, (1 - core) * hc, hc, 2))
    y_one, y_two, y_mine, y_got = lax.optimization_barrier((y_one, y_two, y_mine, y_got))
    hA, h1, h_own, stat = attn_out(place, y_one, y_two, slots, start, attn_gain, chips, fast)
    h_got = swap_core(h_own)
    cot = after(cotangent, h_own).reshape(2, nz, own // 2, cols).transpose(1, 0, 2, 3)
    cot = exchange(cot.reshape(nz, own, cols))

    act, uv, mo_own, mo_other = mlp_fwd(h_own, h_got, slots, suv)
    mo_got = swap_core(mo_other)
    if not fast:
        cot = relative(flat(cot))
    hidden, d_own, base, ga_mlp = loss(place, mo_own, mo_got, h1, cot, mlp_gain, chips, fast)
    d_got = swap_core(d_own)
    if not fast:
        hidden = relative(hidden).reshape(own, nz, cols).transpose(1, 0, 2)
    hidden = exchange(hidden)

    orders = [bits, bits[::-1]]
    sent_at = [[r for r in range(chips) if r & order[0]] for order in orders]
    kept_at = [[r for r in range(chips) if not r & order[0]] for order in orders]

    def second(kept, sent):
        found, sends = [], []
        for order, left, got, keep in zip(orders, kept_at, sent, kept):
            terms = [keep, got]
            for bit in order[1:]:
                send_at = [n for n, r in enumerate(left) if r & bit]
                keep_at = [n for n, r in enumerate(left) if not r & bit]
                left = [left[n] for n in keep_at]
                cut = lambda v, at: jnp.concatenate([v[n : n + 1] for n in at], axis=0)
                send = sum(cut(t, send_at).astype(f32) for t in terms).astype(bf16)
                terms = [cut(t, keep_at) for t in terms] + [swap_chip(send, bit)]
                sends.append(send)
            found.append(terms)
        return found, sends

    def slot_sums(found):
        return [sum(t[0, n].astype(f32) for t in terms) for terms in found for n in range(nz // 2)]

    def wait_last(found, *others):
        return [terms[:-1] + [after(terms[-1], *others)] for terms in found]

    down_made, down_kept = weight_grads(place, sent_at, kept_at, chips, (d_own, d_got), act)
    down_sent = [swap_chip(one, order[0]) for one, order in zip(down_made, orders)]
    d_own, d_got, *_ = lax.optimization_barrier((d_own, d_got, *down_made))
    duv, dh_own, dh_other, gsuv = mlp_bwd(d_own, d_got, slots, uv, suv)
    dh_got = swap_core(dh_other)
    down_sent = [after(one, dh_other) for one in down_sent]
    down_part, down_next = second(down_kept, down_sent)
    dh_own, hidden, *_ = lax.optimization_barrier((dh_own, hidden, *down_next))
    do_own, through, ga_attn, dy_a, dy_b = first_back(
        place, dh_own, dh_got, base, h1, hA, start, stat, attn_gain, slots, chips, fast, cols
    )
    dy_b = exchange(dy_b)
    do_got = swap_core(do_own)

    extra = (gsuv, ga_attn, ga_mlp)
    if not fast:
        alphas = [relative(ga_attn[0:1]), relative(ga_mlp[0:1])]
        extra = []
        wide = 2 * half + hc
        fill = lambda r: jnp.pad(r, ((0, 0), (0, wide - r.shape[1])))
        for n in range(nz):
            at = ((z - n) % nz) * cols
            line = [lax.dynamic_slice_in_dim(g, at, cols, 1) for g in alphas]
            lines = [gsuv[n, :2].reshape(1, 2 * half), jnp.concatenate(line, axis=1)]
            lines = jnp.concatenate([fill(r) for r in lines])
            extra.append(jnp.pad(lines, ((0, EXTRA - 2), (0, 0))))
        extra = jnp.stack(extra)
    up_made, up_kept = weight_grads(
        place, sent_at, kept_at, chips, (h_own, h_got), duv, (do_own, do_got), (y_mine, y_got), extra
    )
    down_part = wait_last(down_part, *up_kept)
    down_last = [terms[-1] for terms in down_part]
    dy_b, dy_a, *both = lax.optimization_barrier((dy_b, dy_a, *up_made, *down_last))
    up_made, down_last = both[: len(up_made)], both[len(up_made) :]
    down_slots = slot_sums([t[:-1] + [last] for t, last in zip(down_part, down_last)])
    down_along = [onward(down_slots[n].astype(bf16), nz - n) for n in range(1, nz)]
    up_sent = [swap_chip(one, order[0]) for one, order in zip(up_made, orders)]

    dy_a = exchange(dy_a)
    common = lambda dy, y, logs: (
        is_long, q, k, v, dy.reshape(y.shape), y, logs, rho, cosine, sine, gain, ones
    )
    dqkv_b, dk_part, dv_part, sqk_b = attn_bwd(
        *common(dy_b, y_b, logs_b), middle, blocks - middle, None
    )

    if not fast:
        through = relative(through)
    through = through.astype(f32)

    def input_part(dqkv, side):
        part = dot_t(dqkv, qkv_full)
        mine_at = z * (own // 2)
        here = lax.dynamic_slice_in_dim(part, mine_at, own // 2, 0)
        here = here + through[side * (own // 2) : (side + 1) * (own // 2)]
        return lax.dynamic_update_slice_in_dim(part.astype(bf16), here.astype(bf16), mine_at, 0)

    dqkv_b, dk_part, dy_a = lax.optimization_barrier((dqkv_b, dk_part, dy_a))
    part_b = jnp.einsum(
        "tn,zcn->ztc", dqkv_b, qkv_full.reshape(nz, cols, 3 * cols), preferred_element_type=f32
    )
    mine_at = z * (own // 2)
    here = lax.dynamic_slice_in_dim(part_b, mine_at, own // 2, 1)
    here = here + through[own // 2 :].reshape(own // 2, nz, cols).transpose(1, 0, 2)
    part_b = lax.dynamic_update_slice_in_dim(part_b.astype(bf16), here.astype(bf16), mine_at, 1)
    down_along = [after(one, dqkv_b) for one in down_along]
    sum_down_t = down_slots[0] + sum(one.astype(f32) for one in down_along)
    up_part, up_next = second(up_kept, [after(one, dqkv_b) for one in up_sent])
    part_got = exchange(part_b)
    dk_part, dy_a, *_ = lax.optimization_barrier((dk_part, dy_a, *up_next, part_b, sum_down_t))
    dqkv_a, sqk_a = attn_bwd(*common(dy_a, y_a, logs_a), 0, middle, [dk_part, dv_part])
    input_b = jnp.sum(after(part_got, dqkv_a).astype(f32), axis=0)
    up_part = wait_last(up_part, dqkv_a)
    part_a = input_part(dqkv_a, 0)
    up_slots = slot_sums(up_part)
    passed = onward(up_slots[1].astype(bf16))
    for n in range(2, nz):
        if n == nz - 1:
            passed, part_a = lax.optimization_barrier((passed, part_a))
        passed = onward((up_slots[n] + passed.astype(f32)).astype(bf16))
    sum_up_t = up_slots[0] + passed.astype(f32)
    input_a = lax.psum_scatter(part_a, "head", scatter_dimension=1, tiled=True)
    input_grad = jnp.concatenate([input_a.astype(f32), input_b], axis=0)
    hidden_t = hidden.reshape(nz, 2, own // 2, cols).transpose(1, 0, 2, 3).reshape(rows, cols)

    dqkv = jnp.concatenate([dqkv_a, dqkv_b], axis=0)
    grad_qkv = t_dot(tokens_full, dqkv).astype(bf16)
    sqk = jnp.pad((sqk_a + sqk_b), ((0, EXTRA - 8), (0, 2 * cols)))
    shard = [lax.dynamic_slice_in_dim(grad_qkv, (b ^ r) * span, span, 0) for r in range(nb)]
    shard = [jnp.concatenate([s, sqk.astype(bf16)], axis=0) for s in shard]
    qbits = [1 << n for n in range(int(math.log2(nb)))]
    held = {r: shard[r] for r in range(nb)}
    for bit in qbits:
        send_at = [r for r in held if r & bit]
        send = jnp.concatenate([held[r] for r in send_at], axis=0).astype(bf16)
        got = swap_batch(send, bit)
        size = span + EXTRA
        held = {
            r ^ bit: held[r ^ bit].astype(f32) + got[n * size : (n + 1) * size].astype(f32)
            for n, r in enumerate(send_at)
        }
    cell = width // (nz * nb)
    sum_sqk = lax.dynamic_slice_in_dim(held[0][span, :cols], b * cell, cell, 0)
    qkv_new = adam_wide(w_qkv, held[0][:span], moment_qkv, square_qkv)

    def both_halves(total):
        two = (total[:span], total[span : 2 * span])
        here = jnp.concatenate([pick(two, core), total[2 * span :]], axis=0)
        there = jnp.concatenate([pick(two, 1 - core), total[2 * span :]], axis=0)
        there = swap_core(there.astype(bf16)).astype(f32)
        return [pick((here, there), core), pick((there, here), core)]

    join = lambda halves, at, size: [p[:span, at : at + size] for p in halves]
    halves = both_halves(after(sum_down_t, part_a))
    down_new = adam_tall(w_down, jnp.concatenate(join(halves, 0, half), axis=1), moment_down, square_down)
    halves = both_halves(sum_up_t)
    grad_up = jnp.concatenate(join(halves, 0, half) + join(halves, half, half), axis=1)
    up_new = adam_wide(w_up, grad_up, moment_up, square_up)
    out_new = adam_tall(w_out, jnp.concatenate(join(halves, 2 * half, hc), axis=1), moment_out, square_out)
    suv_rows = jnp.stack(
        [jnp.concatenate([p[span, c * half : (c + 1) * half] for p in halves]) for c in range(2)]
    )
    sum_suv = lax.dynamic_slice_in_dim(suv_rows, b * (hid // nb), hid // nb, 1)
    alphas = halves[0][span + 1] + halves[1][span + 1]
    sum_attn = lax.dynamic_slice_in_dim(alphas[:cols], b * cell, cell, 0)
    sum_mlp = lax.dynamic_slice_in_dim(alphas[cols : 2 * cols], b * cell, cell, 0)

    hidden = hidden_t.astype(f32)

    squares = [qkv_new[4], out_new[4][:1], up_new[4], down_new[4][:1]]
    sizes = [t.size for t in squares]
    norms = jnp.concatenate([t.reshape(-1) for t in squares]).reshape(-1, 128)
    for bit in qbits:
        norms = norms + swap_batch(norms, bit)
    norms = norms.reshape(-1)
    ends = [0] + [sum(sizes[: n + 1]) for n in range(4)]
    back = lambda n, shape: norms[ends[n] : ends[n + 1]].reshape(shape)
    eight = lambda value: jnp.broadcast_to(value, (8, value.shape[1]))
    new_qkv, new_out, new_up, new_down = scale_weights(
        [back(0, (3, cols)), eight(back(1, (1, cols))), back(2, (2, hid)), eight(back(3, (1, hid)))],
        [qkv_new[3], out_new[3], up_new[3], down_new[3]],
        width,
    )
    sum_qkv, first_a, second_a = qkv_new[:3]
    sum_out, first_b, second_b = out_new[:3]
    sum_up, first_c, second_c = up_new[:3]
    sum_down, first_d, second_d = down_new[:3]
    return (
        hidden,
        input_grad,
        sum_qkv,
        sum_out,
        sum_up,
        sum_down,
        first_a,
        first_b,
        first_c,
        first_d,
        second_a,
        second_b,
        second_c,
        second_d,
        new_qkv,
        new_out,
        new_up,
        new_down,
        sum_sqk,
        sum_attn,
        sum_mlp,
        sum_suv,
    )


def solution(mesh):
    tokens = P("batch", "head")
    wide = P("batch", None, "head")
    tall = P("head", "batch")
    flat = P(("head", "batch"))
    weights = (wide, tall, wide, tall)
    return jax.shard_map(
        per_device,
        mesh=mesh,
        in_specs=(tokens, tokens, P("batch"))
        + weights * 3
        + (P("head"), P(), P(), P(None, "head")),
        out_specs=(tokens, tokens) + weights * 4 + (flat, flat, flat, P(None, ("head", "batch"))),
        check_vma=False,
    )
```

```python
import functools
import math

import jax
import jax.numpy as jnp
from jax import lax
from jax.experimental import pallas as pl
from jax.experimental.pallas import tpu as pltpu
from jax.sharding import PartitionSpec as P

HEAD_DIM = 64
SHORT = 1024

layer_eps = 1e-06
learn_rate = 0.008
beta_one = 0.9
beta_two = 0.95
adam_eps = 1e-08
bias_one = 1.0 - math.exp(100.0 * math.log(0.9))
bias_two = 1.0 - math.exp(100.0 * math.log(0.95))
score_scale = 8.0
LOG2E = math.log2(math.e)
LN2 = math.log(2.0)

bf16 = jnp.bfloat16
f32 = jnp.float32


def dot(a, b):
    return jnp.dot(a, b, preferred_element_type=f32)


def dot_t(a, b):
    return lax.dot_general(a, b, (((1,), (1,)), ((), ())), preferred_element_type=f32)


def t_dot(a, b):
    return lax.dot_general(a, b, (((0,), (0,)), ((), ())), preferred_element_type=f32)


def params(mib):
    return pltpu.CompilerParams(vmem_limit_bytes=mib * 1024 * 1024)


def full_spec(shape):
    return pl.BlockSpec(shape, lambda *_: (0,) * len(shape))


def head_sum(value, ones):
    high = value.astype(bf16)
    low = (value - high.astype(f32)).astype(bf16)
    return dot(high, ones) + dot(low, ones)


def widen(value, cols):
    return jnp.concatenate([value] * (cols // value.shape[1]), axis=1)


def swap_halves(value):
    cols = value.shape[-1]
    half = HEAD_DIM // 2
    lane = lax.broadcasted_iota(jnp.int32, value.shape, 1)
    first = (lane % HEAD_DIM) < half
    up = pltpu.roll(value, cols - half, 1)
    down = pltpu.roll(value, half, 1)
    return jnp.where(first, up, down)


def qkv_kernel(place_ref, *refs, parts):
    tokens = refs[:parts]
    w_ref, cos_ref, sin_ref, gain_ref, ones_ref, x_ref, q_ref, k_ref, v_ref, rho_ref = refs[parts:]
    cols = v_ref.shape[1]
    z = place_ref[0]
    for n in range(parts):
        at = pl.multiple_of(lax.rem(z + parts - n, parts) * cols, cols)
        x_ref[:, pl.ds(at, cols)] = tokens[n][...]
    proj = dot(x_ref[...], w_ref[...])
    cosine = widen(cos_ref[...], cols)
    sine = widen(sin_ref[...], cols)
    ones = ones_ref[...]
    gain = gain_ref[...]
    heads = cols // HEAD_DIM
    lane = lax.broadcasted_iota(jnp.int32, rho_ref.shape, 1)
    stats = jnp.zeros(rho_ref.shape, f32)
    for c, (out, scale) in enumerate(((q_ref, score_scale * LOG2E), (k_ref, 1.0))):
        part = proj[:, c * cols : (c + 1) * cols]
        rho = lax.rsqrt(head_sum(part * part, ones) + layer_eps)
        rot = part * cosine + swap_halves(part) * sine
        out[...] = (rot * rho * (gain * scale)).astype(bf16)
        for h in range(heads):
            stats = jnp.where(lane == c * heads + h, rho[:, h * HEAD_DIM : h * HEAD_DIM + 1], stats)
    rho_ref[...] = stats
    v_ref[...] = proj[:, 2 * cols :].astype(bf16)


def qkv_project(place, tokens, w, cosine, sine, gain, ones):
    rows, cols = tokens[0].shape
    parts = len(tokens)
    width = parts * cols
    blk = 512
    row = lambda n: pl.BlockSpec((blk, n), lambda i, s: (i, 0))
    return pl.pallas_call(
        functools.partial(qkv_kernel, parts=parts),
        grid_spec=pltpu.PrefetchScalarGridSpec(
            num_scalar_prefetch=1,
            grid=(rows // blk,),
            in_specs=[row(cols)] * parts
            + [full_spec((width, 3 * cols)), row(128), row(128)]
            + [full_spec((1, cols)), full_spec((cols, cols))],
            out_specs=[row(width)] + [row(cols)] * 3 + [row(128)],
        ),
        out_shape=[jax.ShapeDtypeStruct((rows, width), bf16)]
        + [jax.ShapeDtypeStruct((rows, cols), bf16)] * 3
        + [jax.ShapeDtypeStruct((rows, 128), f32)],
        compiler_params=params(24),
    )(place, *tokens, w, cosine, sine, gain, ones)


def head_masks(cols, heads):
    lane = lax.broadcasted_iota(jnp.int32, (1, cols), 1) // HEAD_DIM
    return [(lane == h) for h in range(heads)]


def masked(value, mask):
    return jnp.where(mask, value, jnp.zeros_like(value))


def attn_fwd_kernel(long_ref, q_ref, k_ref, v_ref, y_ref, l_ref, acc, mass, *, heads, blk, sub, first):
    i = first + pl.program_id(0)
    cols = q_ref.shape[1]
    masks = head_masks(cols, heads)
    per = SHORT // blk
    low = jnp.where(long_ref[0] != 0, 0, (i // per) * per)
    acc[...] = jnp.zeros_like(acc)
    mass[...] = jnp.zeros_like(mass)

    def lanes(p):
        total = p[:, 0:128]
        for n in range(1, p.shape[1] // 128):
            total = total + p[:, n * 128 : (n + 1) * 128]
        return total

    def body(j, carry):
        start = pl.multiple_of(j * blk, blk)
        keys = k_ref[pl.ds(start, blk), :]
        vals = v_ref[pl.ds(start, blk), :]
        q = q_ref[...]
        total = jnp.zeros(acc.shape, f32)
        for h in range(heads):
            p = jnp.exp2(dot_t(masked(q, masks[h]), keys))
            mass[h] += lanes(p)
            total += dot(p.astype(bf16), masked(vals, masks[h]))
        acc[...] += total
        return carry

    lax.fori_loop(low, i, body, 0)
    start = pl.multiple_of(i * blk, blk)
    causal = lax.broadcasted_iota(jnp.int32, (sub, sub), 0) >= lax.broadcasted_iota(
        jnp.int32, (sub, sub), 1
    )
    for a in range(blk // sub):
        rows = slice(a * sub, (a + 1) * sub)
        q = q_ref[rows, :]
        for b in range(a + 1):
            at = pl.multiple_of(start + b * sub, sub)
            keys = k_ref[pl.ds(at, sub), :]
            vals = v_ref[pl.ds(at, sub), :]
            total = jnp.zeros((sub, cols), f32)
            for h in range(heads):
                p = jnp.exp2(dot_t(masked(q, masks[h]), keys))
                if a == b:
                    p = jnp.where(causal, p, 0.0)
                mass[h, rows, :] += lanes(p)
                total += dot(p.astype(bf16), masked(vals, masks[h]))
            acc[rows, :] += total
    inverse = jnp.zeros(acc.shape, f32)
    logs = jnp.zeros(l_ref.shape, f32)
    lane = lax.broadcasted_iota(jnp.int32, l_ref.shape, 1)
    for h in range(heads):
        column = jnp.sum(mass[h], axis=1, keepdims=True)
        inverse = jnp.where(masks[h], 1.0 / column, inverse)
        logs = jnp.where(lane == h, jnp.log2(column), logs)
    y_ref[...] = (acc[...] * inverse).astype(bf16)
    l_ref[...] = logs


def attn_fwd(is_long, q, k, v, first, count):
    rows, cols = q.shape
    heads = cols // HEAD_DIM
    blk, sub = 512, 256
    row = lambda n: pl.BlockSpec((blk, n), lambda i, s: (i, 0))
    whole = pl.BlockSpec(((first + count) * blk, cols), lambda i, s: (0, 0))
    return pl.pallas_call(
        functools.partial(attn_fwd_kernel, heads=heads, blk=blk, sub=sub, first=first),
        grid_spec=pltpu.PrefetchScalarGridSpec(
            num_scalar_prefetch=1,
            grid=(count,),
            in_specs=[pl.BlockSpec((blk, cols), lambda i, s: (first + i, 0)), whole, whole],
            out_specs=[row(cols), row(128)],
            scratch_shapes=[pltpu.VMEM((blk, cols), f32), pltpu.VMEM((heads, blk, 128), f32)],
        ),
        out_shape=[
            jax.ShapeDtypeStruct((count * blk, cols), bf16),
            jax.ShapeDtypeStruct((count * blk, 128), f32),
        ],
        compiler_params=params(20),
    )(is_long, q, k, v)


def attn_bwd_kernel(
    long_ref, q_ref, qk_ref, dy_ref, y_ref, l_ref, k_ref, v_ref, rho_ref, cos_ref, sin_ref, gain_ref,
    ones_ref, dk_in, dv_in, out_ref, dk_out, dv_out, s_ref, acc, dk_acc, dv_acc, stats, *, heads, blk, sub, first, count
):
    step = pl.program_id(0)
    local = count - 1 - step
    i = first + local
    cols = q_ref.shape[1]
    masks = head_masks(cols, heads)
    per = SHORT // blk
    low = jnp.where(long_ref[0] != 0, 0, (i // per) * per)
    ones = ones_ref[...]
    gain = gain_ref[...]

    @pl.when(step == 0)
    def _():
        dk_acc[...] = jnp.zeros_like(dk_acc)
        dv_acc[...] = jnp.zeros_like(dv_acc)
        s_ref[...] = jnp.zeros_like(s_ref)
        if dk_in is not None:
            dk_acc[...] = dk_in[...]
            dv_acc[...] = dv_in[...]

    acc[...] = jnp.zeros_like(acc)
    prod = dy_ref[...].astype(f32) * y_ref[...].astype(f32)
    high = prod.astype(bf16)
    rest = (prod - high.astype(f32)).astype(bf16)
    pickers = (
        lax.broadcasted_iota(jnp.int32, (8, cols), 1) // HEAD_DIM
        == lax.broadcasted_iota(jnp.int32, (8, cols), 0)
    ).astype(bf16)
    stats[0:8, :] = dot_t(pickers, high) + dot_t(pickers, rest)
    stats[8:16, :] = l_ref[...].T[0:8, :]

    def piece(at, size, rows, causal):
        keys = k_ref[pl.ds(at, size), :]
        vals = v_ref[pl.ds(at, size), :]
        q = q_ref[rows, :]
        dy = dy_ref[rows, :]
        total_q = jnp.zeros(q.shape, f32)
        total_k = jnp.zeros(keys.shape, f32)
        total_v = jnp.zeros(keys.shape, f32)
        for h in range(heads):
            qm = masked(q, masks[h])
            dym = masked(dy, masks[h])
            p = jnp.exp2(dot_t(keys, qm) - stats[8 + h : 9 + h, rows])
            if causal is not None:
                p = jnp.where(causal, p, 0.0)
            ds = (p * (dot_t(vals, dym) - stats[h : h + 1, rows])).astype(bf16)
            total_v += dot(p.astype(bf16), dym)
            total_k += dot(ds, qm)
            total_q += t_dot(ds, masked(keys, masks[h]))
        acc[rows, :] += total_q
        dk_acc[pl.ds(at, size), :] += total_k
        dv_acc[pl.ds(at, size), :] += total_v

    def body(j, carry):
        piece(pl.multiple_of(j * blk, blk), blk, slice(0, blk), None)
        return carry

    lax.fori_loop(low, i, body, 0)
    start = pl.multiple_of(i * blk, blk)
    causal = lax.broadcasted_iota(jnp.int32, (sub, sub), 0) <= lax.broadcasted_iota(
        jnp.int32, (sub, sub), 1
    )
    for a in range(blk // sub):
        for b in range(a + 1):
            piece(
                pl.multiple_of(start + b * sub, sub),
                sub,
                slice(a * sub, (a + 1) * sub),
                causal if a == b else None,
            )
    cosine = widen(cos_ref[...], cols)
    sine = widen(sin_ref[...], cols)
    total = jnp.zeros((1, cols), f32)
    here = pl.ds(start, blk)
    for c, (value, unit, up, scale) in enumerate(
        (
            (acc[...], q_ref[...], score_scale, score_scale * LOG2E),
            (dk_acc[here, :], k_ref[here, :], LN2, 1.0),
        )
    ):
        rho = jnp.zeros(value.shape, f32)
        for h in range(heads):
            at = c * heads + h
            rho = jnp.where(masks[h], rho_ref[:, at : at + 1], rho)
        grad = value * up
        unit = unit.astype(f32) * (1.0 / (gain * scale))
        total += jnp.sum(grad * unit, axis=0, keepdims=True)
        grad = grad * gain
        back = rho * (grad - unit * head_sum(grad * unit, ones))
        turned = back * cosine - swap_halves(back) * sine
        out_ref[:, c * cols : (c + 1) * cols] = turned.astype(bf16)
    out_ref[:, 2 * cols :] = dv_acc[here, :].astype(bf16)
    s_ref[0:1, :] += total
    if dk_out is not None:
        @pl.when(step == count - 1)
        def _():
            dk_out[...] = dk_acc[0 : first * blk, :]
            dv_out[...] = dv_acc[0 : first * blk, :]


def attn_bwd(is_long, q, k, v, dy, y, logs, rho, cosine, sine, gain, ones, first, count, carry):
    rows, cols = q.shape
    heads = cols // HEAD_DIM
    blk, sub = 512, 256
    top = (first + count) * blk
    at = lambda s: first + count - 1 - s
    row = lambda n: pl.BlockSpec((blk, n), lambda s, m: (at(s), 0))
    whole = pl.BlockSpec((top, cols), lambda s, m: (0, 0))
    ins = [q, k, dy, y, logs, k, v, rho, cosine, sine, gain, ones]
    mine = lambda n: pl.BlockSpec((blk, n), lambda s, m: (count - 1 - s, 0))
    in_specs = [row(cols)] * 2 + [mine(cols)] * 2 + [mine(128), whole, whole] + [row(128)] * 3
    in_specs += [full_spec((1, cols)), full_spec((cols, cols))]
    body = functools.partial(
        attn_bwd_kernel, heads=heads, blk=blk, sub=sub, first=first, count=count
    )
    outs = [jax.ShapeDtypeStruct((count * blk, 3 * cols), bf16)]
    out_specs = [pl.BlockSpec((blk, 3 * cols), lambda s, m: (count - 1 - s, 0))]
    if first:
        outs += [jax.ShapeDtypeStruct((first * blk, cols), f32)] * 2
        out_specs += [full_spec((first * blk, cols))] * 2
        inner = lambda *r: body(*r[:13], None, None, *r[13:])
    else:
        ins += carry
        in_specs += [full_spec((top, cols))] * 2
        inner = lambda *r: body(*r[:16], None, None, *r[16:])
    outs.append(jax.ShapeDtypeStruct((8, cols), f32))
    out_specs.append(full_spec((8, cols)))
    return pl.pallas_call(
        inner,
        grid_spec=pltpu.PrefetchScalarGridSpec(
            num_scalar_prefetch=1,
            grid=(count,),
            in_specs=in_specs,
            out_specs=out_specs,
            scratch_shapes=[
                pltpu.VMEM((blk, cols), f32),
                pltpu.VMEM((top, cols), f32),
                pltpu.VMEM((top, cols), f32),
                pltpu.VMEM((16, blk), f32),
            ],
        ),
        out_shape=outs,
        compiler_params=params(28),
    )(is_long, *ins)


def row_norm(value):
    return lax.rsqrt(jnp.mean(value * value, axis=1, keepdims=True) + layer_eps)


def norm_back(scale, result, grad):
    return scale * (grad - result * jnp.mean(grad * result, axis=1, keepdims=True))


def pack_kernel(core_ref, up_ref, gain_ref, down_ref, out_ref, mine_ref, theirs_ref):
    half = up_ref.shape[2] // 2
    low = core_ref[0] == 0
    down = down_ref[...].astype(bf16).T
    out = out_ref[...].astype(bf16).T
    for ref, first in ((mine_ref, low), (theirs_ref, jnp.logical_not(low))):
        for c in range(2):
            gain = gain_ref[c : c + 1, :]
            ref[:, c * half : (c + 1) * half] = jnp.where(
                first, up_ref[:, c, :half] * gain[:, :half], up_ref[:, c, half:] * gain[:, half:]
            ).astype(bf16)
        ref[:, 2 * half : 3 * half] = jnp.where(first, down[:, :half], down[:, half:])
        ref[:, 3 * half :] = out


def pack(core, w_up, gain, w_down, w_out):
    span, _, hid = w_up.shape
    cols = w_out.shape[0]
    vmem = pl.BlockSpec(memory_space=pltpu.VMEM)
    return pl.pallas_call(
        pack_kernel,
        in_specs=[pl.BlockSpec(memory_space=pltpu.SMEM)] + [vmem] * 4,
        out_specs=[vmem] * 2,
        out_shape=[jax.ShapeDtypeStruct((span, 3 * hid // 2 + cols), bf16)] * 2,
        compiler_params=params(16),
    )(core, w_up, gain, w_down, w_out)


def place_of(r, chip, chunk):
    return pl.ds(pl.multiple_of((r ^ chip) * chunk, chunk), chunk)


def put_relative(ref, chip, chips, fast):
    if not fast:
        return ref[...]
    if len(ref.shape) == 3:
        return jnp.concatenate([ref[r ^ chip] for r in range(chips)], axis=1)
    chunk = ref.shape[1] // chips
    return jnp.concatenate([ref[:, place_of(r, chip, chunk)] for r in range(chips)], axis=1)


def put_natural(ref, value, chip, chips, fast):
    if not fast:
        ref[...] = value
        return
    chunk = value.shape[1] // chips
    for r in range(chips):
        part = value[:, r * chunk : (r + 1) * chunk]
        if len(ref.shape) == 3:
            ref[r ^ chip] = part
        else:
            ref[:, place_of(r, chip, chunk)] = part


def attn_out_kernel(place_ref, *refs, counts, chips, fast):
    total = sum(counts)
    flat, refs = refs[:total], refs[total:]
    ya_ref, yb_ref, x_ref, alpha_ref, ha_ref, h1_ref, hb_ref, stat_ref, all_ref, half_ref, acc = refs
    z, chip, low = place_ref[0], place_ref[1], place_ref[2] == 0
    parts = len(counts)
    early = pl.program_id(0) == 0
    index = 0
    for n in range(parts):
        at = lax.rem(z + parts - n, parts)
        y = jnp.where(early, ya_ref[at], yb_ref[at])
        hc = y.shape[1] // 2
        all_ref[at] = y
        half_ref[at] = jnp.where(low, y[:, hc:], y[:, :hc])
        column = 0
        for piece in flat[index : index + counts[n]]:
            part = slice(column, column + piece.shape[0])
            if n == 0:
                acc[:, part] = dot_t(y, piece[...])
            else:
                acc[:, part] += dot_t(y, piece[...])
            column += piece.shape[0]
        index += counts[n]
    total = acc[...]
    norm = row_norm(total)
    hidden = total * norm
    start = put_relative(x_ref, chip, chips, fast).astype(f32)
    mixed = start + alpha_ref[...] * (hidden - start)
    first_norm = row_norm(mixed)
    out = mixed * first_norm
    ha_ref[...] = hidden
    h1_ref[...] = out
    hb_ref[...] = out.astype(bf16)
    lane = lax.broadcasted_iota(jnp.int32, stat_ref.shape, 1)
    stat_ref[...] = jnp.where(lane == 0, norm, first_norm)


def own_rows(blk, parts, width, fast):
    if fast:
        return pl.BlockSpec((blk, width), lambda i, s: (i * parts + s[0], 0))
    return pl.BlockSpec((blk, width), lambda i, s: (i, 0))


def out_weights(slots, cols):
    flat = [p for slot in slots for p in slot]
    last = flat[0].shape[1] // cols - 1
    return flat, [pl.BlockSpec((p.shape[0], cols), lambda i, s: (0, last)) for p in flat]


def attn_out(place, ya, yb, slots, x, alpha, chips, fast):
    parts, blk, cols = ya.shape
    width = x.shape[1]
    rows = 2 * blk
    row = lambda n: pl.BlockSpec((blk, n), lambda i, s: (i, 0))
    flat, specs = out_weights(slots, cols)
    return pl.pallas_call(
        functools.partial(attn_out_kernel, counts=[len(t) for t in slots], chips=chips, fast=fast),
        grid_spec=pltpu.PrefetchScalarGridSpec(
            num_scalar_prefetch=1,
            grid=(2,),
            in_specs=specs
            + [full_spec(ya.shape)] * 2
            + [own_rows(blk, parts, width, fast), full_spec((1, width))],
            out_specs=[row(width)] * 3
            + [row(128)]
            + [pl.BlockSpec((parts, blk, n), lambda i, s: (0, i, 0)) for n in (cols, cols // 2)],
            scratch_shapes=[pltpu.VMEM((blk, width), f32)],
        ),
        out_shape=[jax.ShapeDtypeStruct((rows, width), d) for d in (f32, f32, bf16)]
        + [jax.ShapeDtypeStruct((rows, 128), f32)]
        + [jax.ShapeDtypeStruct((parts, rows, n), bf16) for n in (cols, cols // 2)],
        compiler_params=params(24),
    )(place, *flat, ya, yb, x, alpha)


def loss_kernel(place_ref, own_ref, got_ref, h1_ref, cot_ref, alpha_ref, hidden_ref, dmo_ref, base_ref, ga_ref, *, chips, fast):
    chip = place_ref[1]
    total = own_ref[...] + got_ref[...].astype(f32)
    alpha = alpha_ref[...]
    norm = row_norm(total)
    inner = total * norm
    h1 = h1_ref[...]
    mixed = h1 + alpha * (inner - h1)
    last = row_norm(mixed)
    hidden = mixed * last
    grad = norm_back(last, hidden, put_relative(cot_ref, chip, chips, fast).astype(f32))
    put_natural(hidden_ref, hidden.astype(bf16), chip, chips, fast)
    base_ref[...] = (1.0 - alpha) * grad
    dmo_ref[...] = norm_back(norm, inner, alpha * grad).astype(bf16)

    @pl.when(pl.program_id(0) == 0)
    def _():
        ga_ref[...] = jnp.zeros_like(ga_ref)

    ga_ref[0:1, :] += jnp.sum(grad * (inner - h1), axis=0, keepdims=True)


def loss(place, own, got, h1, cot, alpha, chips, fast):
    rows, width = own.shape
    blk = rows // 2
    row = pl.BlockSpec((blk, width), lambda i, s: (i, 0))
    part = row
    if fast:
        part = pl.BlockSpec((chips, blk, width // chips), lambda i, s: (0, i, 0))
    return pl.pallas_call(
        functools.partial(loss_kernel, chips=chips, fast=fast),
        grid_spec=pltpu.PrefetchScalarGridSpec(
            num_scalar_prefetch=1,
            grid=(rows // blk,),
            in_specs=[row] * 3 + [part, full_spec((1, width))],
            out_specs=[part] + [row] * 2 + [full_spec((8, width))],
        ),
        out_shape=[jax.ShapeDtypeStruct(cot.shape, bf16)]
        + [jax.ShapeDtypeStruct((rows, width), d) for d in (bf16, f32)]
        + [jax.ShapeDtypeStruct((8, width), f32)],
        compiler_params=params(24),
    )(place, own, got, h1, cot, alpha)


def first_back_kernel(place_ref, *refs, counts, chips, fast):
    total = sum(counts)
    flat, refs = refs[:total], refs[total:]
    own_ref, got_ref, base_ref, h1_ref, ha_ref, x_ref, stat_ref, alpha_ref = refs[:8]
    do_ref, through_ref, ga_ref, dya_ref, dyb_ref = refs[8:]
    z, chip = place_ref[0], place_ref[1]
    alpha = alpha_ref[...]
    grad = base_ref[...] + own_ref[...] + got_ref[...].astype(f32)
    grad = norm_back(stat_ref[:, 1:2], h1_ref[...], grad)
    ha = ha_ref[...]
    put_natural(through_ref, ((1.0 - alpha) * grad).astype(bf16), chip, chips, fast)
    back = norm_back(stat_ref[:, 0:1], ha, alpha * grad).astype(bf16)
    do_ref[...] = back
    parts = len(counts)
    step = pl.program_id(0)
    index = 0
    for n in range(parts):
        at = lax.rem(z + parts - n, parts)
        part = jnp.zeros(dya_ref.shape[1:], f32)
        column = 0
        for piece in flat[index : index + counts[n]]:
            part += dot(do_ref[:, column : column + piece.shape[0]], piece[...])
            column += piece.shape[0]
        index += counts[n]
        part = part.astype(bf16)
        for side, ref in enumerate((dya_ref, dyb_ref)):

            @pl.when(step == side)
            def _(ref=ref, part=part, at=at):
                ref[at] = part

    @pl.when(step == 0)
    def _():
        ga_ref[...] = jnp.zeros_like(ga_ref)

    start = put_relative(x_ref, chip, chips, fast).astype(f32)
    ga_ref[0:1, :] += jnp.sum(grad * (ha - start), axis=0, keepdims=True)


def first_back(place, own, got, base, h1, ha, x, stat, alpha, slots, chips, fast, cols):
    rows, width = own.shape
    parts = len(slots)
    blk = rows // 2
    row = lambda n: pl.BlockSpec((blk, n), lambda i, s: (i, 0))
    flat, specs = out_weights(slots, cols)
    return pl.pallas_call(
        functools.partial(first_back_kernel, counts=[len(t) for t in slots], chips=chips, fast=fast),
        grid_spec=pltpu.PrefetchScalarGridSpec(
            num_scalar_prefetch=1,
            grid=(2,),
            in_specs=specs
            + [row(width)] * 5
            + [own_rows(blk, parts, width, fast), row(128), full_spec((1, width))],
            out_specs=[row(width)] * 2
            + [full_spec((8, width))]
            + [full_spec((parts, blk, cols))] * 2,
        ),
        out_shape=[jax.ShapeDtypeStruct((rows, width), bf16)] * 2
        + [jax.ShapeDtypeStruct((8, width), f32)]
        + [jax.ShapeDtypeStruct((parts, blk, cols), bf16)] * 2,
        compiler_params=params(30),
    )(place, *flat, own, got, base, h1, ha, x, stat, alpha)


def fetch_weights(q, slots, wbuf, sems):
    def copies(j):
        at = 0
        found = []
        for p, piece in enumerate(slots[j]):
            size = piece.shape[0]
            found.append(
                pltpu.make_async_copy(
                    piece.at[:, : wbuf.shape[2]], wbuf.at[j % 2, at : at + size, :], sems.at[j % 2, p]
                )
            )
            at += size
        return found

    for j in range(len(slots)):

        @pl.when(q == j)
        def _(j=j):
            if j == 0:
                for copy in copies(0):
                    copy.start()
            if j + 1 < len(slots):
                for copy in copies(j + 1):
                    copy.start()
            for copy in copies(j):
                copy.wait()


def mlp_fwd_kernel(*refs, half, counts):
    total = sum(counts)
    flat, refs = refs[:total], refs[total:]
    slots, at = [], 0
    for n in counts:
        slots.append(flat[at : at + n])
        at += n
    ha_ref, hb_ref, act_ref, uv_ref, own_ref, got_ref, acc, wbuf, sems = refs
    rows = ha_ref.shape[0]
    q = pl.program_id(0)

    @pl.when(q == 0)
    def _():
        own_ref[...] = jnp.zeros_like(own_ref)
        acc[...] = jnp.zeros_like(acc)

    fetch_weights(q, slots, wbuf, sems)
    w = wbuf.at[lax.rem(q, 2)]
    for base, h_ref, sum_ref in ((0, ha_ref, own_ref), (rows, hb_ref, acc)):
        at = slice(base, base + rows)
        pair = dot(h_ref[...], w[:, : 2 * half])
        lifted = pair[:, :half]
        gated = pair[:, half:]
        act = (lifted * gated * jax.nn.sigmoid(gated)).astype(bf16)
        uv_ref[at, :] = pair.astype(bf16)
        act_ref[at, :] = act
        sum_ref[...] += dot_t(act, w[:, 2 * half : 3 * half])

    @pl.when(q == pl.num_programs(0) - 1)
    def _():
        got_ref[...] = acc[...].astype(bf16)


def mlp_fwd(ha, hb, slots, half):
    rows, width = ha.shape
    parts = len(slots)
    take = lambda n: pl.BlockSpec((None, 2 * rows, n), lambda q: (q, 0, 0))
    whole = full_spec((rows, width))
    anywhere = pl.BlockSpec(memory_space=pl.ANY)
    flat = [p for slot in slots for p in slot]
    return pl.pallas_call(
        functools.partial(mlp_fwd_kernel, half=half, counts=[len(s) for s in slots]),
        grid=(parts,),
        in_specs=[anywhere] * len(flat)
        + [whole, whole],
        out_specs=[take(half), take(2 * half), whole, whole],
        out_shape=[
            jax.ShapeDtypeStruct((parts, 2 * rows, half), bf16),
            jax.ShapeDtypeStruct((parts, 2 * rows, 2 * half), bf16),
            jax.ShapeDtypeStruct((rows, width), f32),
            jax.ShapeDtypeStruct((rows, width), bf16),
        ],
        scratch_shapes=[
            pltpu.VMEM((rows, width), f32),
            pltpu.VMEM((2, width, 3 * half), bf16),
            pltpu.SemaphoreType.DMA((2, max(len(s) for s in slots))),
        ],
        compiler_params=params(32),
    )(*flat, ha, hb)


def mlp_bwd_kernel(*refs, half, counts):
    total = sum(counts)
    flat, refs = refs[:total], refs[total:]
    slots, at = [], 0
    for n in counts:
        slots.append(flat[at : at + n])
        at += n
    da_ref, db_ref, uv_ref, duv_ref, own_ref, got_ref, gs_ref, acc, wbuf, sems = refs
    rows = da_ref.shape[0]
    q = pl.program_id(0)

    @pl.when(q == 0)
    def _():
        own_ref[...] = jnp.zeros_like(own_ref)
        acc[...] = jnp.zeros_like(acc)

    gs_ref[...] = jnp.zeros_like(gs_ref)
    fetch_weights(q, slots, wbuf, sems)
    w = wbuf.at[lax.rem(q, 2)]
    for base, d_ref, sum_ref in ((0, da_ref, own_ref), (rows, db_ref, acc)):
        at = slice(base, base + rows)
        grad = dot(d_ref[...], w[:, 2 * half : 3 * half])
        lifted = uv_ref[at, :half].astype(f32)
        gated = uv_ref[at, half:].astype(f32)
        sigma = jax.nn.sigmoid(gated)
        da = grad * gated * sigma
        db = grad * lifted * sigma * (1.0 + gated * (1.0 - sigma))
        gs_ref[0:1, :] += jnp.sum(da * lifted, axis=0, keepdims=True)
        gs_ref[1:2, :] += jnp.sum(db * gated, axis=0, keepdims=True)
        duv_ref[at, :half] = da.astype(bf16)
        duv_ref[at, half:] = db.astype(bf16)
        sum_ref[...] += dot_t(duv_ref[at, :], w[:, : 2 * half])

    @pl.when(q == pl.num_programs(0) - 1)
    def _():
        got_ref[...] = acc[...].astype(bf16)


def mlp_bwd(da, db, slots, uv, half):
    rows, width = da.shape
    parts = len(slots)
    take = lambda n: pl.BlockSpec((None, 2 * rows, n), lambda q: (q, 0, 0))
    whole = full_spec((rows, width))
    anywhere = pl.BlockSpec(memory_space=pl.ANY)
    flat = [p for slot in slots for p in slot]
    return pl.pallas_call(
        functools.partial(mlp_bwd_kernel, half=half, counts=[len(s) for s in slots]),
        grid=(parts,),
        in_specs=[anywhere] * len(flat)
        + [
            whole,
            whole,
            take(2 * half),
        ],
        out_specs=[
            take(2 * half),
            whole,
            whole,
            pl.BlockSpec((None, 8, half), lambda q: (q, 0, 0)),
        ],
        out_shape=[
            jax.ShapeDtypeStruct((parts, 2 * rows, 2 * half), bf16),
            jax.ShapeDtypeStruct((rows, width), f32),
            jax.ShapeDtypeStruct((rows, width), bf16),
            jax.ShapeDtypeStruct((parts, 8, half), f32),
        ],
        scratch_shapes=[
            pltpu.VMEM((rows, width), f32),
            pltpu.VMEM((2, width, 3 * half), bf16),
            pltpu.SemaphoreType.DMA((2, max(len(s) for s in slots))),
        ],
        compiler_params=params(36),
    )(*flat, da, db, uv)


EXTRA = 16


def grad_kernel(place_ref, *refs, orders, parts, chunk, more):
    ha_ref, hb_ref = refs[:2]
    refs = refs[2:]
    if more:
        oa_ref, ob_ref, ya_ref, yb_ref, gs_ref, g1_ref, g2_ref = refs[:7]
        refs = refs[7:]
    val_ref, *outs = refs[:5]
    turned = refs[5]
    rows = ha_ref.shape[0]
    k = pl.program_id(0)

    @pl.when(k == 0)
    def _():
        turned[:, :rows] = ha_ref[...].T
        turned[:, rows:] = hb_ref[...].T
        if more:
            refs[6][:, :rows] = oa_ref[...].T
            refs[6][:, rows:] = ob_ref[...].T

    if more:
        size = outs[0].shape[2]
        fill = lambda row: jnp.concatenate([row, jnp.zeros((1, size - row.shape[1]), f32)], axis=1)
        line = lax.broadcasted_iota(jnp.int32, (EXTRA, size), 0)
        units = fill(jnp.concatenate([gs_ref[0:1, :], gs_ref[1:2, :]], axis=1))
        steps = fill(jnp.concatenate([g1_ref[0:1, :], g2_ref[0:1, :]], axis=1))
        extra = jnp.where(line == 0, units, jnp.where(line == 1, steps, 0.0)).astype(bf16)

    for side in range(2):

        @pl.when((k < parts // 2) == (side == 0))
        def _(side=side):
            for which, ref in zip(orders[side], outs[2 * side : 2 * side + 2]):
                for j, r in enumerate(which):
                    at = slice(r * chunk, (r + 1) * chunk)
                    value = dot(turned[at, :], val_ref[...]).astype(bf16)
                    size = value.shape[1]
                    ref[j, :chunk, :size] = value
                    if more:
                        ref[j, :chunk, size:] = (
                            dot(refs[6][at, :rows], ya_ref[...]) + dot(refs[6][at, rows:], yb_ref[...])
                        ).astype(bf16)
                        ref[j, chunk:, :] = extra


def weight_grads(place, sends, keeps, chips, hs, value, os=None, ys=None, extra=None):
    rows, width = hs[0].shape
    chunk = width // chips
    parts, _, size = value.shape
    more = os is not None
    hc = ys[1].shape[2] if more else 0
    tall = chunk + (EXTRA if more else 0)
    middle = parts // 2
    if chunk % 128:
        result = []
        for which, lo in ((sends[0], 0), (keeps[0], 0), (sends[1], middle), (keeps[1], middle)):
            cut = lambda pair: jnp.concatenate(
                [jnp.concatenate(pair, axis=0)[:, r * chunk : (r + 1) * chunk] for r in which], axis=1
            )
            found = []
            for k in range(lo, lo + middle):
                one = t_dot(cut(hs), value[k])
                if more:
                    at = (place[0] - k) % parts
                    y = lax.dynamic_index_in_dim(ys[0], at, 0, keepdims=False)
                    y = lax.dynamic_slice_in_dim(y, place[2] * hc, hc, 1)
                    y = jnp.concatenate([y, lax.dynamic_index_in_dim(ys[1], at, 0, keepdims=False)])
                    one = jnp.concatenate([one, t_dot(cut(os), y)], axis=1)
                one = one.reshape(len(which), chunk, size + hc)
                if more:
                    wide = jnp.broadcast_to(extra[k][None], (len(which), EXTRA, size + hc))
                    one = jnp.concatenate([one, wide], axis=1)
                found.append(one.astype(bf16))
            result.append(jnp.stack(found, axis=1))
        return [result[0], result[2]], [result[1], result[3]]
    whole = full_spec((rows, width))
    ins = list(hs)
    in_specs = [whole] * 2
    scratch = [pltpu.VMEM((width, 2 * rows), bf16)]
    if more:
        slot = lambda k, p: lax.rem(p[0] + parts - k, parts)
        cols = ys[0].shape[2]
        part = pl.BlockSpec((8, cols), lambda k, p: (0, slot(k, p) ^ p[1]))
        ins += [*os, ys[0], ys[1], *extra]
        in_specs += [whole] * 2
        in_specs += [
            pl.BlockSpec((None, rows, hc), lambda k, p: (slot(k, p), 0, p[2])),
            pl.BlockSpec((None, rows, hc), lambda k, p: (slot(k, p), 0, 0)),
            pl.BlockSpec((None, 8, size // 2), lambda k, p: (k, 0, 0)),
            part,
            part,
        ]
        scratch = scratch * 2
    ins.append(value)
    in_specs.append(pl.BlockSpec((None, 2 * rows, size), lambda k, p: (k, 0, 0)))
    lists = [sends[0], keeps[0], sends[1], keeps[1]]
    block = lambda one: (len(one), None, tall, size + hc)
    early = lambda k, p: (0, jnp.minimum(k, middle - 1), 0, 0)
    late = lambda k, p: (0, jnp.maximum(k - middle, 0), 0, 0)
    out = pl.pallas_call(
        functools.partial(
            grad_kernel, orders=(lists[:2], lists[2:]), parts=parts, chunk=chunk, more=more
        ),
        grid_spec=pltpu.PrefetchScalarGridSpec(
            num_scalar_prefetch=1,
            grid=(parts,),
            in_specs=in_specs,
            out_specs=[
                pl.BlockSpec(block(one), early if n < 2 else late) for n, one in enumerate(lists)
            ],
            scratch_shapes=scratch,
        ),
        out_shape=[
            jax.ShapeDtypeStruct((len(one), middle, tall, size + hc), bf16) for one in lists
        ],
        compiler_params=params(36),
    )(place, *ins)
    return [out[0], out[2]], [out[1], out[3]]


def adam_values(weight, grad, first, second):
    first_new = beta_one * first + (1.0 - beta_one) * grad
    second_new = beta_two * second + (1.0 - beta_two) * grad * grad
    moved = weight - learn_rate * (first_new / bias_one) / (
        jnp.sqrt(second_new / bias_two) + adam_eps
    )
    return first_new, second_new, moved


def lane_sums(value):
    ones = jnp.ones((8, value.shape[1]), bf16)
    high = value.astype(bf16)
    low = (value - high.astype(f32)).astype(bf16)
    return dot_t(ones, high) + dot_t(ones, low)


def adam_wide_kernel(w_ref, g_ref, m_ref, v_ref, g_out, m_out, v_out, n_out, s_out):
    cols = w_ref.shape[2]
    for c in range(w_ref.shape[1]):
        grad = g_ref[:, c * cols : (c + 1) * cols]
        first, second, moved = adam_values(w_ref[:, c, :], grad, m_ref[:, c, :], v_ref[:, c, :])
        g_out[:, c, :] = grad
        m_out[:, c, :] = first
        v_out[:, c, :] = second
        n_out[:, c, :] = moved
        s_out[c : c + 1, :] = jnp.sum(moved * moved, axis=0, keepdims=True)


def adam_wide(w, g, m, v):
    vmem = pl.BlockSpec(memory_space=pltpu.VMEM)
    return pl.pallas_call(
        adam_wide_kernel,
        in_specs=[vmem] * 4,
        out_specs=[vmem] * 5,
        out_shape=[jax.ShapeDtypeStruct(w.shape, f32)] * 4
        + [jax.ShapeDtypeStruct(w.shape[1:], f32)],
        compiler_params=params(16),
    )(w, g, m, v)


def adam_tall_kernel(w_ref, g_ref, m_ref, v_ref, g_out, m_out, v_out, n_out, s_out):
    grad = g_ref[...].T
    first, second, moved = adam_values(w_ref[...], grad, m_ref[...], v_ref[...])
    g_out[...] = grad
    m_out[...] = first
    v_out[...] = second
    n_out[...] = moved
    s_out[...] = lane_sums(moved * moved)


def adam_tall(w, g, m, v):
    vmem = pl.BlockSpec(memory_space=pltpu.VMEM)
    return pl.pallas_call(
        adam_tall_kernel,
        in_specs=[vmem] * 4,
        out_specs=[vmem] * 5,
        out_shape=[jax.ShapeDtypeStruct(w.shape, f32)] * 4
        + [jax.ShapeDtypeStruct((8, w.shape[0]), f32)],
        compiler_params=params(16),
    )(w, g, m, v)


def scale_kernel(na_ref, nb_ref, nc_ref, nd_ref, a_ref, b_ref, c_ref, d_ref, ao_ref, bo_ref, co_ref, do_ref, *, width):
    factor = lambda value: lax.rsqrt(value / width + layer_eps)
    for norm, ref, out in ((na_ref, a_ref, ao_ref), (nc_ref, c_ref, co_ref)):
        for c in range(ref.shape[1]):
            out[:, c, :] = ref[:, c, :] * factor(norm[c : c + 1, :])
    for norm, ref, out in ((nb_ref, b_ref, bo_ref), (nd_ref, d_ref, do_ref)):
        out[...] = ref[...] * factor(norm[...]).T[:, 0:1]


def scale_weights(norms, weights, width):
    vmem = pl.BlockSpec(memory_space=pltpu.VMEM)
    return pl.pallas_call(
        functools.partial(scale_kernel, width=width),
        in_specs=[vmem] * 8,
        out_specs=[vmem] * 4,
        out_shape=[jax.ShapeDtypeStruct(w.shape, f32) for w in weights],
        compiler_params=params(16),
    )(*norms, *weights)


def after(value, *others):
    return lax.optimization_barrier((value, *others))[0]


def per_device(
    layer_input,
    cotangent,
    positions,
    w_qkv,
    w_out,
    w_up,
    w_down,
    moment_qkv,
    moment_out,
    moment_up,
    moment_down,
    square_qkv,
    square_out,
    square_up,
    square_down,
    s_qk,
    alpha_attn,
    alpha_mlp,
    s_uv,
):
    nz = lax.axis_size("head")
    nb = lax.axis_size("batch")
    z = lax.axis_index("head")
    b = lax.axis_index("batch")
    core = b % 2
    chip = b // 2
    chips = nb // 2
    bits = [1 << n for n in range(int(math.log2(chips)))]
    rows, cols = layer_input.shape
    width = cols * nz
    own = rows // nz
    hid = w_down.shape[0]
    half = hid // 2
    hc = cols // 2
    heads = cols // HEAD_DIM
    span = w_qkv.shape[0]
    chunk = width // chips
    core_s = core.reshape(1).astype(jnp.int32)
    place = jnp.stack([z, chip, core]).astype(jnp.int32)
    fast = chunk == cols and chunk % 128 == 0

    def swap_batch(value, bit):
        return lax.ppermute(value, "batch", [(i, i ^ bit) for i in range(nb)])

    def swap_core(value):
        return swap_batch(value, 1)

    def swap_chip(value, bit):
        return swap_batch(value, 2 * bit)

    def onward(value, k=1):
        return lax.ppermute(value, "head", [(i, (i + k) % nz) for i in range(nz)])

    def exchange(value):
        return lax.all_to_all(value, "head", split_axis=0, concat_axis=0)

    def pick(pair, index):
        return jnp.where(index == 0, pair[0], pair[1])

    def relative(value):
        return jnp.concatenate(
            [
                lax.dynamic_slice_in_dim(value, (chip ^ r) * chunk, chunk, value.ndim - 1)
                for r in range(chips)
            ],
            axis=-1,
        )

    def spread(value):
        if chips <= 4:
            return [value] + [swap_chip(value, r) for r in range(1, chips)]
        for bit in bits:
            value = jnp.concatenate([value, swap_chip(value, bit)], axis=0)
        return [value]

    tokens = [layer_input, onward(layer_input)]
    mine, theirs = pack(core_s, w_up, s_uv, w_down, w_out)
    qkv_own = after(w_qkv, mine).reshape(span, 3 * cols).astype(bf16)
    qkv_full = lax.all_gather(qkv_own, "batch", axis=0, tiled=True)
    theirs = swap_core(theirs)
    packet = jnp.concatenate([pick((mine, theirs), core), pick((theirs, mine), core)], axis=0)
    hops = [packet, onward(packet)]
    slots = [spread(packet)]
    tokens[1], hops[1], places, alpha_attn, alpha_mlp, *last = lax.optimization_barrier(
        (tokens[1], hops[1], positions, alpha_attn, alpha_mlp, *slots[0])
    )
    slots[0] = list(last)

    freqs = jnp.exp(
        (jnp.arange(128) % (HEAD_DIM // 2)).astype(f32) * (-2.0 * math.log(10000.0) / HEAD_DIM)
    )
    phase = places.astype(f32)[:, None] * freqs[None, :]
    side = jnp.where(jnp.arange(128) % HEAD_DIM < HEAD_DIM // 2, -1.0, 1.0).astype(f32)
    cosine, sine = jnp.cos(phase), jnp.sin(phase) * side[None, :]
    lane = jnp.arange(cols) // HEAD_DIM
    ones = (lane[:, None] == lane[None, :]).astype(bf16)
    gain = s_qk.reshape(1, cols)
    is_long = (places[SHORT : SHORT + 1] != 0).astype(jnp.int32)
    attn_gain = relative(alpha_attn[None])
    mlp_gain = relative(alpha_mlp[None])

    for n in range(2, nz):
        slots.append(spread(hops[-1]))
        tokens.append(onward(tokens[-1]))
        if n < nz - 1:
            hops.append(onward(hops[-1]))
            tokens[-1], hops[-1], cosine, sine, ones, attn_gain, mlp_gain, *last = (
                lax.optimization_barrier(
                    (tokens[-1], hops[-1], cosine, sine, ones, attn_gain, mlp_gain, *slots[-1])
                )
            )
            slots[-1] = list(last)
    last_hop, tokens[-1] = lax.optimization_barrier((hops[-1], tokens[-1]))
    hops.append(onward(last_hop))

    blocks = rows // 512
    middle = blocks // 2
    tokens_full, q, k, v, rho = qkv_project(place, tokens, qkv_full, cosine, sine, gain, ones)
    y_a, logs_a = attn_fwd(is_long, q, k, v, 0, middle)
    q_b, hops[-1], *last = lax.optimization_barrier((after(q, y_a), hops[-1], *slots[-1]))
    slots[-1] = list(last)
    slots.append(spread(hops[-1]))
    y_b, logs_b = attn_fwd(is_long, q_b, k, v, middle, blocks - middle)
    y_one = exchange(y_a.reshape(nz, own // 2, cols))
    y_in, y_one = lax.optimization_barrier((y_b, y_one))
    y_two = exchange(y_in.reshape(nz, own // 2, cols))
    flat = lambda value: value.transpose(1, 0, 2).reshape(own, width)
    start = tokens_full
    if not fast:
        start = jnp.concatenate(
            [
                lax.dynamic_slice_in_dim(tokens_full, h * (rows // 2) + z * (own // 2), own // 2, 0)
                for h in range(2)
            ]
        )
        start = relative(start)
    y_one, y_two, *last = lax.optimization_barrier((y_one, y_two, *slots[-1]))
    slots[-1] = list(last)
    hA, h1, h_own, stat, y_mine, y_other = attn_out(place, y_one, y_two, slots, start, attn_gain, chips, fast)
    h_got = swap_core(h_own)
    y_got = swap_core(y_other)
    h_got, y_got = lax.optimization_barrier((h_got, y_got))
    cot = after(cotangent, h_own).reshape(2, nz, own // 2, cols).transpose(1, 0, 2, 3)
    cot = exchange(cot.reshape(nz, own, cols))

    act, uv, mo_own, mo_other = mlp_fwd(h_own, h_got, slots, half)
    mo_got = swap_core(mo_other)
    if not fast:
        cot = relative(flat(cot))
    hidden, d_own, base, ga_mlp = loss(place, mo_own, mo_got, h1, cot, mlp_gain, chips, fast)
    d_got = swap_core(d_own)
    if not fast:
        hidden = relative(hidden).reshape(own, nz, cols).transpose(1, 0, 2)
    hidden = exchange(hidden)

    orders = [bits, bits[::-1]]
    sent_at = [[r for r in range(chips) if r & order[0]] for order in orders]
    kept_at = [[r for r in range(chips) if not r & order[0]] for order in orders]

    def second(kept, sent):
        found, sends = [], []
        for order, left, got, keep in zip(orders, kept_at, sent, kept):
            terms = [keep, got]
            for bit in order[1:]:
                send_at = [n for n, r in enumerate(left) if r & bit]
                keep_at = [n for n, r in enumerate(left) if not r & bit]
                left = [left[n] for n in keep_at]
                cut = lambda v, at: jnp.concatenate([v[n : n + 1] for n in at], axis=0)
                send = sum(cut(t, send_at).astype(f32) for t in terms).astype(bf16)
                terms = [cut(t, keep_at) for t in terms] + [swap_chip(send, bit)]
                sends.append(send)
            found.append(terms)
        return found, sends

    def slot_sums(found):
        return [sum(t[0, n].astype(f32) for t in terms) for terms in found for n in range(nz // 2)]

    def wait_last(found, *others):
        return [terms[:-1] + [after(terms[-1], *others)] for terms in found]

    down_made, down_kept = weight_grads(place, sent_at, kept_at, chips, (d_own, d_got), act)
    down_sent = [swap_chip(one, order[0]) for one, order in zip(down_made, orders)]
    d_own, d_got, *_ = lax.optimization_barrier((d_own, d_got, *down_made))
    duv, dh_own, dh_other, gsuv = mlp_bwd(d_own, d_got, slots, uv, half)
    dh_got = swap_core(dh_other)
    down_sent = [after(one, dh_other) for one in down_sent]
    down_part, down_next = second(down_kept, down_sent)
    dh_own, hidden, *_ = lax.optimization_barrier((dh_own, hidden, *down_next))
    do_own, through, ga_attn, dy_a, dy_b = first_back(
        place, dh_own, dh_got, base, h1, hA, start, stat, attn_gain, slots, chips, fast, cols
    )
    dy_b = exchange(dy_b)
    do_got = swap_core(do_own)

    extra = (gsuv, ga_attn, ga_mlp)
    if not fast:
        alphas = [relative(ga_attn[0:1]), relative(ga_mlp[0:1])]
        extra = []
        wide = 2 * half + hc
        fill = lambda r: jnp.pad(r, ((0, 0), (0, wide - r.shape[1])))
        for n in range(nz):
            at = ((z - n) % nz) * cols
            line = [lax.dynamic_slice_in_dim(g, at, cols, 1) for g in alphas]
            lines = [gsuv[n, :2].reshape(1, 2 * half), jnp.concatenate(line, axis=1)]
            lines = jnp.concatenate([fill(r) for r in lines])
            extra.append(jnp.pad(lines, ((0, EXTRA - 2), (0, 0))))
        extra = jnp.stack(extra)
    up_made, up_kept = weight_grads(
        place, sent_at, kept_at, chips, (h_own, h_got), duv, (do_own, do_got), (y_mine, y_got), extra
    )
    down_part = wait_last(down_part, *up_kept)
    down_last = [terms[-1] for terms in down_part]
    dy_b, dy_a, *both = lax.optimization_barrier((dy_b, dy_a, *up_made, *down_last))
    up_made, down_last = both[: len(up_made)], both[len(up_made) :]
    down_slots = slot_sums([t[:-1] + [last] for t, last in zip(down_part, down_last)])
    down_along = [onward(down_slots[n].astype(bf16), nz - n) for n in range(1, nz)]
    up_sent = [swap_chip(one, order[0]) for one, order in zip(up_made, orders)]

    dy_a = exchange(dy_a)
    common = lambda dy, y, logs: (
        is_long, q, k, v, dy.reshape(y.shape), y, logs, rho, cosine, sine, gain, ones
    )
    dqkv_b, dk_part, dv_part, sqk_b = attn_bwd(
        *common(dy_b, y_b, logs_b), middle, blocks - middle, None
    )

    if not fast:
        through = relative(through)
    through = through.astype(f32)

    def input_part(dqkv, side):
        part = dot_t(dqkv, qkv_full)
        mine_at = z * (own // 2)
        here = lax.dynamic_slice_in_dim(part, mine_at, own // 2, 0)
        here = here + through[side * (own // 2) : (side + 1) * (own // 2)]
        return lax.dynamic_update_slice_in_dim(part.astype(bf16), here.astype(bf16), mine_at, 0)

    dqkv_b, dk_part, dy_a = lax.optimization_barrier((dqkv_b, dk_part, dy_a))
    part_b = jnp.einsum(
        "tn,zcn->ztc", dqkv_b, qkv_full.reshape(nz, cols, 3 * cols), preferred_element_type=f32
    )
    mine_at = z * (own // 2)
    here = lax.dynamic_slice_in_dim(part_b, mine_at, own // 2, 1)
    here = here + through[own // 2 :].reshape(own // 2, nz, cols).transpose(1, 0, 2)
    part_b = lax.dynamic_update_slice_in_dim(part_b.astype(bf16), here.astype(bf16), mine_at, 1)
    down_along = [after(one, dqkv_b) for one in down_along]
    sum_down_t = down_slots[0] + sum(one.astype(f32) for one in down_along)
    up_part, up_next = second(up_kept, [after(one, dqkv_b) for one in up_sent])
    part_got = exchange(part_b)
    dk_part, dy_a, *_ = lax.optimization_barrier((dk_part, dy_a, *up_next, part_b, sum_down_t))
    dqkv_a, sqk_a = attn_bwd(*common(dy_a, y_a, logs_a), 0, middle, [dk_part, dv_part])
    input_b = jnp.sum(after(part_got, dqkv_a).astype(f32), axis=0)
    up_part = wait_last(up_part, dqkv_a)
    part_a = input_part(dqkv_a, 0)
    up_slots = slot_sums(up_part)
    passed = onward(up_slots[1].astype(bf16))
    for n in range(2, nz):
        if n == nz - 1:
            passed, part_a = lax.optimization_barrier((passed, part_a))
        passed = onward((up_slots[n] + passed.astype(f32)).astype(bf16))
    sum_up_t = up_slots[0] + passed.astype(f32)
    input_a = lax.psum_scatter(part_a, "head", scatter_dimension=1, tiled=True)
    input_grad = jnp.concatenate([input_a.astype(f32), input_b], axis=0)
    hidden_t = hidden.reshape(nz, 2, own // 2, cols).transpose(1, 0, 2, 3).reshape(rows, cols)

    dqkv = jnp.concatenate([dqkv_a, dqkv_b], axis=0)
    grad_qkv = t_dot(tokens_full, dqkv).astype(bf16)
    sqk = jnp.pad((sqk_a + sqk_b), ((0, EXTRA - 8), (0, 2 * cols)))
    shard = [lax.dynamic_slice_in_dim(grad_qkv, (b ^ r) * span, span, 0) for r in range(nb)]
    shard = [jnp.concatenate([s, sqk.astype(bf16)], axis=0) for s in shard]
    qbits = [1 << n for n in range(int(math.log2(nb)))]
    held = {r: shard[r] for r in range(nb)}
    for bit in qbits:
        send_at = [r for r in held if r & bit]
        send = jnp.concatenate([held[r] for r in send_at], axis=0).astype(bf16)
        got = swap_batch(send, bit)
        size = span + EXTRA
        held = {
            r ^ bit: held[r ^ bit].astype(f32) + got[n * size : (n + 1) * size].astype(f32)
            for n, r in enumerate(send_at)
        }
    cell = width // (nz * nb)
    sum_sqk = lax.dynamic_slice_in_dim(held[0][span, :cols], b * cell, cell, 0)
    qkv_new = adam_wide(w_qkv, held[0][:span], moment_qkv, square_qkv)

    def both_halves(total):
        two = (total[:span], total[span : 2 * span])
        here = jnp.concatenate([pick(two, core), total[2 * span :]], axis=0)
        there = jnp.concatenate([pick(two, 1 - core), total[2 * span :]], axis=0)
        there = swap_core(there.astype(bf16)).astype(f32)
        return [pick((here, there), core), pick((there, here), core)]

    join = lambda halves, at, size: [p[:span, at : at + size] for p in halves]
    halves = both_halves(after(sum_down_t, part_a))
    down_new = adam_tall(w_down, jnp.concatenate(join(halves, 0, half), axis=1), moment_down, square_down)
    halves = both_halves(sum_up_t)
    grad_up = jnp.concatenate(join(halves, 0, half) + join(halves, half, half), axis=1)
    grad_up = grad_up * s_uv.reshape(1, 2 * hid)
    up_new = adam_wide(w_up, grad_up, moment_up, square_up)
    out_new = adam_tall(w_out, jnp.concatenate(join(halves, 2 * half, hc), axis=1), moment_out, square_out)
    suv_rows = jnp.stack(
        [jnp.concatenate([p[span, c * half : (c + 1) * half] for p in halves]) for c in range(2)]
    )
    suv_rows = suv_rows / s_uv
    sum_suv = lax.dynamic_slice_in_dim(suv_rows, b * (hid // nb), hid // nb, 1)
    alphas = halves[0][span + 1] + halves[1][span + 1]
    sum_attn = lax.dynamic_slice_in_dim(alphas[:cols], b * cell, cell, 0)
    sum_mlp = lax.dynamic_slice_in_dim(alphas[cols : 2 * cols], b * cell, cell, 0)

    hidden = hidden_t.astype(f32)

    squares = [qkv_new[4], out_new[4][:1], up_new[4], down_new[4][:1]]
    sizes = [t.size for t in squares]
    norms = jnp.concatenate([t.reshape(-1) for t in squares]).reshape(-1, 128)
    for bit in qbits:
        norms = norms + swap_batch(norms, bit)
    norms = norms.reshape(-1)
    ends = [0] + [sum(sizes[: n + 1]) for n in range(4)]
    back = lambda n, shape: norms[ends[n] : ends[n + 1]].reshape(shape)
    eight = lambda value: jnp.broadcast_to(value, (8, value.shape[1]))
    new_qkv, new_out, new_up, new_down = scale_weights(
        [back(0, (3, cols)), eight(back(1, (1, cols))), back(2, (2, hid)), eight(back(3, (1, hid)))],
        [qkv_new[3], out_new[3], up_new[3], down_new[3]],
        width,
    )
    sum_qkv, first_a, second_a = qkv_new[:3]
    sum_out, first_b, second_b = out_new[:3]
    sum_up, first_c, second_c = up_new[:3]
    sum_down, first_d, second_d = down_new[:3]
    return (
        hidden,
        input_grad,
        sum_qkv,
        sum_out,
        sum_up,
        sum_down,
        first_a,
        first_b,
        first_c,
        first_d,
        second_a,
        second_b,
        second_c,
        second_d,
        new_qkv,
        new_out,
        new_up,
        new_down,
        sum_sqk,
        sum_attn,
        sum_mlp,
        sum_suv,
    )


def solution(mesh):
    tokens = P("batch", "head")
    wide = P("batch", None, "head")
    tall = P("head", "batch")
    flat = P(("head", "batch"))
    weights = (wide, tall, wide, tall)
    return jax.shard_map(
        per_device,
        mesh=mesh,
        in_specs=(tokens, tokens, P("batch"))
        + weights * 3
        + (P("head"), P(), P(), P(None, "head")),
        out_specs=(tokens, tokens) + weights * 4 + (flat, flat, flat, P(None, ("head", "batch"))),
        check_vma=False,
    )
```

```python
import functools
import math

import jax
import jax.numpy as jnp
from jax import lax
from jax.experimental import pallas as pl
from jax.experimental.pallas import tpu as pltpu
from jax.sharding import PartitionSpec as P

HEAD_DIM = 64
SHORT = 1024

layer_eps = 1e-06
learn_rate = 0.008
beta_one = 0.9
beta_two = 0.95
adam_eps = 1e-08
bias_one = 1.0 - math.exp(100.0 * math.log(0.9))
bias_two = 1.0 - math.exp(100.0 * math.log(0.95))
score_scale = 8.0
LOG2E = math.log2(math.e)
LN2 = math.log(2.0)

bf16 = jnp.bfloat16
f32 = jnp.float32


def dot(a, b):
    return jnp.dot(a, b, preferred_element_type=f32)


def dot_t(a, b):
    return lax.dot_general(a, b, (((1,), (1,)), ((), ())), preferred_element_type=f32)


def t_dot(a, b):
    return lax.dot_general(a, b, (((0,), (0,)), ((), ())), preferred_element_type=f32)


def params(mib):
    return pltpu.CompilerParams(vmem_limit_bytes=mib * 1024 * 1024)


def full_spec(shape):
    return pl.BlockSpec(shape, lambda *_: (0,) * len(shape))


def head_sum(value, ones):
    high = value.astype(bf16)
    low = (value - high.astype(f32)).astype(bf16)
    return dot(high, ones) + dot(low, ones)


def widen(value, cols):
    return jnp.concatenate([value] * (cols // value.shape[1]), axis=1)


def swap_halves(value):
    cols = value.shape[-1]
    half = HEAD_DIM // 2
    lane = lax.broadcasted_iota(jnp.int32, value.shape, 1)
    first = (lane % HEAD_DIM) < half
    up = pltpu.roll(value, cols - half, 1)
    down = pltpu.roll(value, half, 1)
    return jnp.where(first, up, down)


def qkv_kernel(place_ref, *refs, parts):
    tokens = refs[:parts]
    w_ref, cos_ref, sin_ref, gain_ref, ones_ref, x_ref, q_ref, k_ref, v_ref, rho_ref = refs[parts:]
    cols = v_ref.shape[1]
    z = place_ref[0]
    for n in range(parts):
        at = pl.multiple_of(lax.rem(z + parts - n, parts) * cols, cols)
        x_ref[:, pl.ds(at, cols)] = tokens[n][...]
    proj = dot(x_ref[...], w_ref[...])
    cosine = widen(cos_ref[...], cols)
    sine = widen(sin_ref[...], cols)
    ones = ones_ref[...]
    gain = gain_ref[...]
    heads = cols // HEAD_DIM
    lane = lax.broadcasted_iota(jnp.int32, rho_ref.shape, 1)
    stats = jnp.zeros(rho_ref.shape, f32)
    for c, (out, scale) in enumerate(((q_ref, score_scale * LOG2E), (k_ref, 1.0))):
        part = proj[:, c * cols : (c + 1) * cols]
        rho = lax.rsqrt(head_sum(part * part, ones) + layer_eps)
        rot = part * cosine + swap_halves(part) * sine
        out[...] = (rot * rho * (gain * scale)).astype(bf16)
        for h in range(heads):
            stats = jnp.where(lane == c * heads + h, rho[:, h * HEAD_DIM : h * HEAD_DIM + 1], stats)
    rho_ref[...] = stats
    v_ref[...] = proj[:, 2 * cols :].astype(bf16)


def qkv_project(place, tokens, w, cosine, sine, gain, ones):
    rows, cols = tokens[0].shape
    parts = len(tokens)
    width = parts * cols
    blk = 512
    row = lambda n: pl.BlockSpec((blk, n), lambda i, s: (i, 0))
    return pl.pallas_call(
        functools.partial(qkv_kernel, parts=parts),
        grid_spec=pltpu.PrefetchScalarGridSpec(
            num_scalar_prefetch=1,
            grid=(rows // blk,),
            in_specs=[row(cols)] * parts
            + [full_spec((width, 3 * cols)), row(128), row(128)]
            + [full_spec((1, cols)), full_spec((cols, cols))],
            out_specs=[row(width)] + [row(cols)] * 3 + [row(128)],
        ),
        out_shape=[jax.ShapeDtypeStruct((rows, width), bf16)]
        + [jax.ShapeDtypeStruct((rows, cols), bf16)] * 3
        + [jax.ShapeDtypeStruct((rows, 128), f32)],
        compiler_params=params(56),
    )(place, *tokens, w, cosine, sine, gain, ones)


def head_masks(cols, heads):
    lane = lax.broadcasted_iota(jnp.int32, (1, cols), 1) // HEAD_DIM
    return [(lane == h) for h in range(heads)]


def masked(value, mask):
    return jnp.where(mask, value, jnp.zeros_like(value))


def attn_fwd_kernel(long_ref, q_ref, k_ref, v_ref, y_ref, l_ref, acc, mass, *, heads, blk, sub, first):
    i = first + pl.program_id(0)
    cols = q_ref.shape[1]
    masks = head_masks(cols, heads)
    per = SHORT // blk
    low = jnp.where(long_ref[0] != 0, 0, (i // per) * per)
    acc[...] = jnp.zeros_like(acc)
    mass[...] = jnp.zeros_like(mass)

    def lanes(p):
        total = p[:, 0:128]
        for n in range(1, p.shape[1] // 128):
            total = total + p[:, n * 128 : (n + 1) * 128]
        return total

    def body(j, carry):
        start = pl.multiple_of(j * blk, blk)
        keys = k_ref[pl.ds(start, blk), :]
        vals = v_ref[pl.ds(start, blk), :]
        q = q_ref[...]
        total = jnp.zeros(acc.shape, f32)
        for h in range(heads):
            p = jnp.exp2(dot_t(masked(q, masks[h]), keys))
            mass[h] += lanes(p)
            total += dot(p.astype(bf16), masked(vals, masks[h]))
        acc[...] += total
        return carry

    lax.fori_loop(low, i, body, 0)
    start = pl.multiple_of(i * blk, blk)
    causal = lax.broadcasted_iota(jnp.int32, (sub, sub), 0) >= lax.broadcasted_iota(
        jnp.int32, (sub, sub), 1
    )
    for a in range(blk // sub):
        rows = slice(a * sub, (a + 1) * sub)
        q = q_ref[rows, :]
        for b in range(a + 1):
            at = pl.multiple_of(start + b * sub, sub)
            keys = k_ref[pl.ds(at, sub), :]
            vals = v_ref[pl.ds(at, sub), :]
            total = jnp.zeros((sub, cols), f32)
            for h in range(heads):
                p = jnp.exp2(dot_t(masked(q, masks[h]), keys))
                if a == b:
                    p = jnp.where(causal, p, 0.0)
                mass[h, rows, :] += lanes(p)
                total += dot(p.astype(bf16), masked(vals, masks[h]))
            acc[rows, :] += total
    inverse = jnp.zeros(acc.shape, f32)
    logs = jnp.zeros(l_ref.shape, f32)
    lane = lax.broadcasted_iota(jnp.int32, l_ref.shape, 1)
    for h in range(heads):
        column = jnp.sum(mass[h], axis=1, keepdims=True)
        inverse = jnp.where(masks[h], 1.0 / column, inverse)
        logs = jnp.where(lane == h, jnp.log2(column), logs)
    y_ref[...] = (acc[...] * inverse).astype(bf16)
    l_ref[...] = logs


def attn_fwd(is_long, q, k, v, first, count):
    rows, cols = q.shape
    heads = cols // HEAD_DIM
    blk, sub = 512, 256
    row = lambda n: pl.BlockSpec((blk, n), lambda i, s: (i, 0))
    whole = pl.BlockSpec(((first + count) * blk, cols), lambda i, s: (0, 0))
    return pl.pallas_call(
        functools.partial(attn_fwd_kernel, heads=heads, blk=blk, sub=sub, first=first),
        grid_spec=pltpu.PrefetchScalarGridSpec(
            num_scalar_prefetch=1,
            grid=(count,),
            in_specs=[pl.BlockSpec((blk, cols), lambda i, s: (first + i, 0)), whole, whole],
            out_specs=[row(cols), row(128)],
            scratch_shapes=[pltpu.VMEM((blk, cols), f32), pltpu.VMEM((heads, blk, 128), f32)],
        ),
        out_shape=[
            jax.ShapeDtypeStruct((count * blk, cols), bf16),
            jax.ShapeDtypeStruct((count * blk, 128), f32),
        ],
        compiler_params=params(56),
    )(is_long, q, k, v)


def attn_bwd_kernel(
    long_ref, q_ref, qk_ref, dy_ref, y_ref, l_ref, k_ref, v_ref, rho_ref, cos_ref, sin_ref, gain_ref,
    ones_ref, dk_in, dv_in, out_ref, dk_out, dv_out, s_ref, acc, dk_acc, dv_acc, stats, *, heads, blk, sub, first, count
):
    step = pl.program_id(0)
    local = count - 1 - step
    i = first + local
    cols = q_ref.shape[1]
    masks = head_masks(cols, heads)
    per = SHORT // blk
    low = jnp.where(long_ref[0] != 0, 0, (i // per) * per)
    ones = ones_ref[...]
    gain = gain_ref[...]

    @pl.when(step == 0)
    def _():
        dk_acc[...] = jnp.zeros_like(dk_acc)
        dv_acc[...] = jnp.zeros_like(dv_acc)
        s_ref[...] = jnp.zeros_like(s_ref)
        if dk_in is not None:
            dk_acc[...] = dk_in[...]
            dv_acc[...] = dv_in[...]

    acc[...] = jnp.zeros_like(acc)
    prod = dy_ref[...].astype(f32) * y_ref[...].astype(f32)
    high = prod.astype(bf16)
    rest = (prod - high.astype(f32)).astype(bf16)
    pickers = (
        lax.broadcasted_iota(jnp.int32, (8, cols), 1) // HEAD_DIM
        == lax.broadcasted_iota(jnp.int32, (8, cols), 0)
    ).astype(bf16)
    stats[0:8, :] = dot_t(pickers, high) + dot_t(pickers, rest)
    stats[8:16, :] = l_ref[...].T[0:8, :]

    def piece(at, size, rows, causal):
        keys = k_ref[pl.ds(at, size), :]
        vals = v_ref[pl.ds(at, size), :]
        q = q_ref[rows, :]
        dy = dy_ref[rows, :]
        total_q = jnp.zeros(q.shape, f32)
        total_k = jnp.zeros(keys.shape, f32)
        total_v = jnp.zeros(keys.shape, f32)
        for h in range(heads):
            qm = masked(q, masks[h])
            dym = masked(dy, masks[h])
            p = jnp.exp2(dot_t(keys, qm) - stats[8 + h : 9 + h, rows])
            if causal is not None:
                p = jnp.where(causal, p, 0.0)
            ds = (p * (dot_t(vals, dym) - stats[h : h + 1, rows])).astype(bf16)
            total_v += dot(p.astype(bf16), dym)
            total_k += dot(ds, qm)
            total_q += t_dot(ds, masked(keys, masks[h]))
        acc[rows, :] += total_q
        dk_acc[pl.ds(at, size), :] += total_k
        dv_acc[pl.ds(at, size), :] += total_v

    def body(j, carry):
        piece(pl.multiple_of(j * blk, blk), blk, slice(0, blk), None)
        return carry

    lax.fori_loop(low, i, body, 0)
    start = pl.multiple_of(i * blk, blk)
    causal = lax.broadcasted_iota(jnp.int32, (sub, sub), 0) <= lax.broadcasted_iota(
        jnp.int32, (sub, sub), 1
    )
    for a in range(blk // sub):
        for b in range(a + 1):
            piece(
                pl.multiple_of(start + b * sub, sub),
                sub,
                slice(a * sub, (a + 1) * sub),
                causal if a == b else None,
            )
    cosine = widen(cos_ref[...], cols)
    sine = widen(sin_ref[...], cols)
    total = jnp.zeros((1, cols), f32)
    here = pl.ds(start, blk)
    for c, (value, unit, up, scale) in enumerate(
        (
            (acc[...], q_ref[...], score_scale, score_scale * LOG2E),
            (dk_acc[here, :], k_ref[here, :], LN2, 1.0),
        )
    ):
        rho = jnp.zeros(value.shape, f32)
        for h in range(heads):
            at = c * heads + h
            rho = jnp.where(masks[h], rho_ref[:, at : at + 1], rho)
        grad = value * up
        unit = unit.astype(f32) * (1.0 / (gain * scale))
        total += jnp.sum(grad * unit, axis=0, keepdims=True)
        grad = grad * gain
        back = rho * (grad - unit * head_sum(grad * unit, ones))
        turned = back * cosine - swap_halves(back) * sine
        out_ref[:, c * cols : (c + 1) * cols] = turned.astype(bf16)
    out_ref[:, 2 * cols :] = dv_acc[here, :].astype(bf16)
    s_ref[0:1, :] += total
    if dk_out is not None:
        @pl.when(step == count - 1)
        def _():
            dk_out[...] = dk_acc[0 : first * blk, :]
            dv_out[...] = dv_acc[0 : first * blk, :]


def attn_bwd(is_long, q, k, v, dy, y, logs, rho, cosine, sine, gain, ones, first, count, carry):
    rows, cols = q.shape
    heads = cols // HEAD_DIM
    blk, sub = 512, 256
    top = (first + count) * blk
    at = lambda s: first + count - 1 - s
    row = lambda n: pl.BlockSpec((blk, n), lambda s, m: (at(s), 0))
    whole = pl.BlockSpec((top, cols), lambda s, m: (0, 0))
    ins = [q, k, dy, y, logs, k, v, rho, cosine, sine, gain, ones]
    mine = lambda n: pl.BlockSpec((blk, n), lambda s, m: (count - 1 - s, 0))
    in_specs = [row(cols)] * 2 + [mine(cols)] * 2 + [mine(128), whole, whole] + [row(128)] * 3
    in_specs += [full_spec((1, cols)), full_spec((cols, cols))]
    body = functools.partial(
        attn_bwd_kernel, heads=heads, blk=blk, sub=sub, first=first, count=count
    )
    outs = [jax.ShapeDtypeStruct((count * blk, 3 * cols), bf16)]
    out_specs = [pl.BlockSpec((blk, 3 * cols), lambda s, m: (count - 1 - s, 0))]
    if first:
        outs += [jax.ShapeDtypeStruct((first * blk, cols), f32)] * 2
        out_specs += [full_spec((first * blk, cols))] * 2
        inner = lambda *r: body(*r[:13], None, None, *r[13:])
    else:
        ins += carry
        in_specs += [full_spec((top, cols))] * 2
        inner = lambda *r: body(*r[:16], None, None, *r[16:])
    outs.append(jax.ShapeDtypeStruct((8, cols), f32))
    out_specs.append(full_spec((8, cols)))
    return pl.pallas_call(
        inner,
        grid_spec=pltpu.PrefetchScalarGridSpec(
            num_scalar_prefetch=1,
            grid=(count,),
            in_specs=in_specs,
            out_specs=out_specs,
            scratch_shapes=[
                pltpu.VMEM((blk, cols), f32),
                pltpu.VMEM((top, cols), f32),
                pltpu.VMEM((top, cols), f32),
                pltpu.VMEM((16, blk), f32),
            ],
        ),
        out_shape=outs,
        compiler_params=params(56),
    )(is_long, *ins)


def row_norm(value):
    return lax.rsqrt(jnp.mean(value * value, axis=1, keepdims=True) + layer_eps)


def norm_back(scale, result, grad):
    return scale * (grad - result * jnp.mean(grad * result, axis=1, keepdims=True))


def pack_kernel(core_ref, up_ref, gain_ref, down_ref, out_ref, mine_ref, theirs_ref):
    half = up_ref.shape[2] // 2
    low = core_ref[0] == 0
    down = down_ref[...].astype(bf16).T
    out = out_ref[...].astype(bf16).T
    for ref, first in ((mine_ref, low), (theirs_ref, jnp.logical_not(low))):
        for c in range(2):
            gain = gain_ref[c : c + 1, :]
            ref[:, c * half : (c + 1) * half] = jnp.where(
                first, up_ref[:, c, :half] * gain[:, :half], up_ref[:, c, half:] * gain[:, half:]
            ).astype(bf16)
        ref[:, 2 * half : 3 * half] = jnp.where(first, down[:, :half], down[:, half:])
        ref[:, 3 * half :] = out


def pack(core, w_up, gain, w_down, w_out):
    span, _, hid = w_up.shape
    cols = w_out.shape[0]
    vmem = pl.BlockSpec(memory_space=pltpu.VMEM)
    return pl.pallas_call(
        pack_kernel,
        in_specs=[pl.BlockSpec(memory_space=pltpu.SMEM)] + [vmem] * 4,
        out_specs=[vmem] * 2,
        out_shape=[jax.ShapeDtypeStruct((span, 3 * hid // 2 + cols), bf16)] * 2,
        compiler_params=params(16),
    )(core, w_up, gain, w_down, w_out)


def place_of(r, chip, chunk):
    return pl.ds(pl.multiple_of((r ^ chip) * chunk, chunk), chunk)


def put_relative(ref, chip, chips, fast):
    if not fast:
        return ref[...]
    if len(ref.shape) == 3:
        return jnp.concatenate([ref[r ^ chip] for r in range(chips)], axis=1)
    chunk = ref.shape[1] // chips
    return jnp.concatenate([ref[:, place_of(r, chip, chunk)] for r in range(chips)], axis=1)


def put_natural(ref, value, chip, chips, fast):
    if not fast:
        ref[...] = value
        return
    chunk = value.shape[1] // chips
    for r in range(chips):
        part = value[:, r * chunk : (r + 1) * chunk]
        if len(ref.shape) == 3:
            ref[r ^ chip] = part
        else:
            ref[:, place_of(r, chip, chunk)] = part


def attn_out_kernel(place_ref, *refs, counts, chips, fast):
    total = sum(counts)
    flat, refs = refs[:total], refs[total:]
    ya_ref, yb_ref, x_ref, alpha_ref, ha_ref, h1_ref, hb_ref, stat_ref, all_ref, half_ref, acc = refs
    z, chip, low = place_ref[0], place_ref[1], place_ref[2] == 0
    parts = len(counts)
    early = pl.program_id(0) == 0
    index = 0
    for n in range(parts):
        at = lax.rem(z + parts - n, parts)
        y = jnp.where(early, ya_ref[at], yb_ref[at])
        hc = y.shape[1] // 2
        all_ref[at] = y
        half_ref[at] = jnp.where(low, y[:, hc:], y[:, :hc])
        column = 0
        for piece in flat[index : index + counts[n]]:
            part = slice(column, column + piece.shape[0])
            if n == 0:
                acc[:, part] = dot_t(y, piece[...])
            else:
                acc[:, part] += dot_t(y, piece[...])
            column += piece.shape[0]
        index += counts[n]
    total = acc[...]
    norm = row_norm(total)
    hidden = total * norm
    start = put_relative(x_ref, chip, chips, fast).astype(f32)
    mixed = start + alpha_ref[...] * (hidden - start)
    first_norm = row_norm(mixed)
    out = mixed * first_norm
    ha_ref[...] = hidden
    h1_ref[...] = out
    hb_ref[...] = out.astype(bf16)
    lane = lax.broadcasted_iota(jnp.int32, stat_ref.shape, 1)
    stat_ref[...] = jnp.where(lane == 0, norm, first_norm)


def own_rows(blk, parts, width, fast):
    if fast:
        return pl.BlockSpec((blk, width), lambda i, s: (i * parts + s[0], 0))
    return pl.BlockSpec((blk, width), lambda i, s: (i, 0))


def out_weights(slots, cols):
    flat = [p for slot in slots for p in slot]
    last = flat[0].shape[1] // cols - 1
    return flat, [pl.BlockSpec((p.shape[0], cols), lambda i, s: (0, last)) for p in flat]


def attn_out(place, ya, yb, slots, x, alpha, chips, fast):
    parts, blk, cols = ya.shape
    width = x.shape[1]
    rows = 2 * blk
    row = lambda n: pl.BlockSpec((blk, n), lambda i, s: (i, 0))
    flat, specs = out_weights(slots, cols)
    return pl.pallas_call(
        functools.partial(attn_out_kernel, counts=[len(t) for t in slots], chips=chips, fast=fast),
        grid_spec=pltpu.PrefetchScalarGridSpec(
            num_scalar_prefetch=1,
            grid=(2,),
            in_specs=specs
            + [full_spec(ya.shape)] * 2
            + [own_rows(blk, parts, width, fast), full_spec((1, width))],
            out_specs=[row(width)] * 3
            + [row(128)]
            + [pl.BlockSpec((parts, blk, n), lambda i, s: (0, i, 0)) for n in (cols, cols // 2)],
            scratch_shapes=[pltpu.VMEM((blk, width), f32)],
        ),
        out_shape=[jax.ShapeDtypeStruct((rows, width), d) for d in (f32, f32, bf16)]
        + [jax.ShapeDtypeStruct((rows, 128), f32)]
        + [jax.ShapeDtypeStruct((parts, rows, n), bf16) for n in (cols, cols // 2)],
        compiler_params=params(56),
    )(place, *flat, ya, yb, x, alpha)


def loss_kernel(place_ref, own_ref, got_ref, h1_ref, cot_ref, alpha_ref, hidden_ref, dmo_ref, base_ref, ga_ref, *, chips, fast):
    chip = place_ref[1]
    total = own_ref[...] + got_ref[...].astype(f32)
    alpha = alpha_ref[...]
    norm = row_norm(total)
    inner = total * norm
    h1 = h1_ref[...]
    mixed = h1 + alpha * (inner - h1)
    last = row_norm(mixed)
    hidden = mixed * last
    grad = norm_back(last, hidden, put_relative(cot_ref, chip, chips, fast).astype(f32))
    put_natural(hidden_ref, hidden.astype(bf16), chip, chips, fast)
    base_ref[...] = (1.0 - alpha) * grad
    dmo_ref[...] = norm_back(norm, inner, alpha * grad).astype(bf16)

    @pl.when(pl.program_id(0) == 0)
    def _():
        ga_ref[...] = jnp.zeros_like(ga_ref)

    ga_ref[0:1, :] += jnp.sum(grad * (inner - h1), axis=0, keepdims=True)


def loss(place, own, got, h1, cot, alpha, chips, fast):
    rows, width = own.shape
    blk = rows // 2
    row = pl.BlockSpec((blk, width), lambda i, s: (i, 0))
    part = row
    if fast:
        part = pl.BlockSpec((chips, blk, width // chips), lambda i, s: (0, i, 0))
    return pl.pallas_call(
        functools.partial(loss_kernel, chips=chips, fast=fast),
        grid_spec=pltpu.PrefetchScalarGridSpec(
            num_scalar_prefetch=1,
            grid=(rows // blk,),
            in_specs=[row] * 3 + [part, full_spec((1, width))],
            out_specs=[part] + [row] * 2 + [full_spec((8, width))],
        ),
        out_shape=[jax.ShapeDtypeStruct(cot.shape, bf16)]
        + [jax.ShapeDtypeStruct((rows, width), d) for d in (bf16, f32)]
        + [jax.ShapeDtypeStruct((8, width), f32)],
        compiler_params=params(56),
    )(place, own, got, h1, cot, alpha)


def first_back_kernel(place_ref, *refs, counts, chips, fast):
    total = sum(counts)
    flat, refs = refs[:total], refs[total:]
    own_ref, got_ref, base_ref, h1_ref, ha_ref, x_ref, stat_ref, alpha_ref = refs[:8]
    do_ref, through_ref, ga_ref, dya_ref, dyb_ref = refs[8:]
    z, chip = place_ref[0], place_ref[1]
    alpha = alpha_ref[...]
    grad = base_ref[...] + own_ref[...] + got_ref[...].astype(f32)
    grad = norm_back(stat_ref[:, 1:2], h1_ref[...], grad)
    ha = ha_ref[...]
    put_natural(through_ref, ((1.0 - alpha) * grad).astype(bf16), chip, chips, fast)
    back = norm_back(stat_ref[:, 0:1], ha, alpha * grad).astype(bf16)
    do_ref[...] = back
    parts = len(counts)
    step = pl.program_id(0)
    index = 0
    for n in range(parts):
        at = lax.rem(z + parts - n, parts)
        part = jnp.zeros(dya_ref.shape[1:], f32)
        column = 0
        for piece in flat[index : index + counts[n]]:
            part += dot(do_ref[:, column : column + piece.shape[0]], piece[...])
            column += piece.shape[0]
        index += counts[n]
        part = part.astype(bf16)
        for side, ref in enumerate((dya_ref, dyb_ref)):

            @pl.when(step == side)
            def _(ref=ref, part=part, at=at):
                ref[at] = part

    @pl.when(step == 0)
    def _():
        ga_ref[...] = jnp.zeros_like(ga_ref)

    start = put_relative(x_ref, chip, chips, fast).astype(f32)
    ga_ref[0:1, :] += jnp.sum(grad * (ha - start), axis=0, keepdims=True)


def first_back(place, own, got, base, h1, ha, x, stat, alpha, slots, chips, fast, cols):
    rows, width = own.shape
    parts = len(slots)
    blk = rows // 2
    row = lambda n: pl.BlockSpec((blk, n), lambda i, s: (i, 0))
    flat, specs = out_weights(slots, cols)
    return pl.pallas_call(
        functools.partial(first_back_kernel, counts=[len(t) for t in slots], chips=chips, fast=fast),
        grid_spec=pltpu.PrefetchScalarGridSpec(
            num_scalar_prefetch=1,
            grid=(2,),
            in_specs=specs
            + [row(width)] * 5
            + [own_rows(blk, parts, width, fast), row(128), full_spec((1, width))],
            out_specs=[row(width)] * 2
            + [full_spec((8, width))]
            + [full_spec((parts, blk, cols))] * 2,
        ),
        out_shape=[jax.ShapeDtypeStruct((rows, width), bf16)] * 2
        + [jax.ShapeDtypeStruct((8, width), f32)]
        + [jax.ShapeDtypeStruct((parts, blk, cols), bf16)] * 2,
        compiler_params=params(56),
    )(place, *flat, own, got, base, h1, ha, x, stat, alpha)


def fetch_weights(q, slots, wbuf, sems):
    def copies(j):
        at = 0
        found = []
        for p, piece in enumerate(slots[j]):
            size = piece.shape[0]
            found.append(
                pltpu.make_async_copy(
                    piece.at[:, : wbuf.shape[2]], wbuf.at[j % 2, at : at + size, :], sems.at[j % 2, p]
                )
            )
            at += size
        return found

    for j in range(len(slots)):

        @pl.when(q == j)
        def _(j=j):
            if j == 0:
                for copy in copies(0):
                    copy.start()
            if j + 1 < len(slots):
                for copy in copies(j + 1):
                    copy.start()
            for copy in copies(j):
                copy.wait()


def mlp_fwd_kernel(*refs, half, counts):
    total = sum(counts)
    flat, refs = refs[:total], refs[total:]
    slots, at = [], 0
    for n in counts:
        slots.append(flat[at : at + n])
        at += n
    ha_ref, hb_ref, act_ref, uv_ref, own_ref, got_ref, acc, wbuf, sems = refs
    rows = ha_ref.shape[0]
    q = pl.program_id(0)

    @pl.when(q == 0)
    def _():
        own_ref[...] = jnp.zeros_like(own_ref)
        acc[...] = jnp.zeros_like(acc)

    fetch_weights(q, slots, wbuf, sems)
    w = wbuf.at[lax.rem(q, 2)]
    for base, h_ref, sum_ref in ((0, ha_ref, own_ref), (rows, hb_ref, acc)):
        at = slice(base, base + rows)
        pair = dot(h_ref[...], w[:, : 2 * half])
        lifted = pair[:, :half]
        gated = pair[:, half:]
        act = (lifted * gated * jax.nn.sigmoid(gated)).astype(bf16)
        uv_ref[at, :] = pair.astype(bf16)
        act_ref[at, :] = act
        sum_ref[...] += dot_t(act, w[:, 2 * half : 3 * half])

    @pl.when(q == pl.num_programs(0) - 1)
    def _():
        got_ref[...] = acc[...].astype(bf16)


def mlp_fwd(ha, hb, slots, half):
    rows, width = ha.shape
    parts = len(slots)
    take = lambda n: pl.BlockSpec((None, 2 * rows, n), lambda q: (q, 0, 0))
    whole = full_spec((rows, width))
    anywhere = pl.BlockSpec(memory_space=pl.ANY)
    flat = [p for slot in slots for p in slot]
    return pl.pallas_call(
        functools.partial(mlp_fwd_kernel, half=half, counts=[len(s) for s in slots]),
        grid=(parts,),
        in_specs=[anywhere] * len(flat)
        + [whole, whole],
        out_specs=[take(half), take(2 * half), whole, whole],
        out_shape=[
            jax.ShapeDtypeStruct((parts, 2 * rows, half), bf16),
            jax.ShapeDtypeStruct((parts, 2 * rows, 2 * half), bf16),
            jax.ShapeDtypeStruct((rows, width), f32),
            jax.ShapeDtypeStruct((rows, width), bf16),
        ],
        scratch_shapes=[
            pltpu.VMEM((rows, width), f32),
            pltpu.VMEM((2, width, 3 * half), bf16),
            pltpu.SemaphoreType.DMA((2, max(len(s) for s in slots))),
        ],
        compiler_params=params(56),
    )(*flat, ha, hb)


def mlp_bwd_kernel(*refs, half, counts):
    total = sum(counts)
    flat, refs = refs[:total], refs[total:]
    slots, at = [], 0
    for n in counts:
        slots.append(flat[at : at + n])
        at += n
    da_ref, db_ref, uv_ref, duv_ref, own_ref, got_ref, gs_ref, acc, wbuf, sems = refs
    rows = da_ref.shape[0]
    q = pl.program_id(0)

    @pl.when(q == 0)
    def _():
        own_ref[...] = jnp.zeros_like(own_ref)
        acc[...] = jnp.zeros_like(acc)

    gs_ref[...] = jnp.zeros_like(gs_ref)
    fetch_weights(q, slots, wbuf, sems)
    w = wbuf.at[lax.rem(q, 2)]
    for base, d_ref, sum_ref in ((0, da_ref, own_ref), (rows, db_ref, acc)):
        at = slice(base, base + rows)
        grad = dot(d_ref[...], w[:, 2 * half : 3 * half])
        lifted = uv_ref[at, :half].astype(f32)
        gated = uv_ref[at, half:].astype(f32)
        sigma = jax.nn.sigmoid(gated)
        da = grad * gated * sigma
        db = grad * lifted * sigma * (1.0 + gated * (1.0 - sigma))
        gs_ref[0:1, :] += jnp.sum(da * lifted, axis=0, keepdims=True)
        gs_ref[1:2, :] += jnp.sum(db * gated, axis=0, keepdims=True)
        duv_ref[at, :half] = da.astype(bf16)
        duv_ref[at, half:] = db.astype(bf16)
        sum_ref[...] += dot_t(duv_ref[at, :], w[:, : 2 * half])

    @pl.when(q == pl.num_programs(0) - 1)
    def _():
        got_ref[...] = acc[...].astype(bf16)


def mlp_bwd(da, db, slots, uv, half):
    rows, width = da.shape
    parts = len(slots)
    take = lambda n: pl.BlockSpec((None, 2 * rows, n), lambda q: (q, 0, 0))
    whole = full_spec((rows, width))
    anywhere = pl.BlockSpec(memory_space=pl.ANY)
    flat = [p for slot in slots for p in slot]
    return pl.pallas_call(
        functools.partial(mlp_bwd_kernel, half=half, counts=[len(s) for s in slots]),
        grid=(parts,),
        in_specs=[anywhere] * len(flat)
        + [
            whole,
            whole,
            take(2 * half),
        ],
        out_specs=[
            take(2 * half),
            whole,
            whole,
            pl.BlockSpec((None, 8, half), lambda q: (q, 0, 0)),
        ],
        out_shape=[
            jax.ShapeDtypeStruct((parts, 2 * rows, 2 * half), bf16),
            jax.ShapeDtypeStruct((rows, width), f32),
            jax.ShapeDtypeStruct((rows, width), bf16),
            jax.ShapeDtypeStruct((parts, 8, half), f32),
        ],
        scratch_shapes=[
            pltpu.VMEM((rows, width), f32),
            pltpu.VMEM((2, width, 3 * half), bf16),
            pltpu.SemaphoreType.DMA((2, max(len(s) for s in slots))),
        ],
        compiler_params=params(56),
    )(*flat, da, db, uv)


EXTRA = 16


def grad_kernel(place_ref, *refs, orders, parts, chunk, more):
    ha_ref, hb_ref = refs[:2]
    refs = refs[2:]
    if more:
        oa_ref, ob_ref, ya_ref, yb_ref, gs_ref, g1_ref, g2_ref = refs[:7]
        refs = refs[7:]
    val_ref, *outs = refs[:5]
    turned = refs[5]
    rows = ha_ref.shape[0]
    k = pl.program_id(0)

    @pl.when(k == 0)
    def _():
        turned[:, :rows] = ha_ref[...].T
        turned[:, rows:] = hb_ref[...].T
        if more:
            refs[6][:, :rows] = oa_ref[...].T
            refs[6][:, rows:] = ob_ref[...].T

    if more:
        size = outs[0].shape[2]
        fill = lambda row: jnp.concatenate([row, jnp.zeros((1, size - row.shape[1]), f32)], axis=1)
        line = lax.broadcasted_iota(jnp.int32, (EXTRA, size), 0)
        units = fill(jnp.concatenate([gs_ref[0:1, :], gs_ref[1:2, :]], axis=1))
        steps = fill(jnp.concatenate([g1_ref[0:1, :], g2_ref[0:1, :]], axis=1))
        extra = jnp.where(line == 0, units, jnp.where(line == 1, steps, 0.0)).astype(bf16)

    for side in range(2):

        @pl.when((k < parts // 2) == (side == 0))
        def _(side=side):
            for which, ref in zip(orders[side], outs[2 * side : 2 * side + 2]):
                for j, r in enumerate(which):
                    at = slice(r * chunk, (r + 1) * chunk)
                    value = dot(turned[at, :], val_ref[...]).astype(bf16)
                    size = value.shape[1]
                    ref[j, :chunk, :size] = value
                    if more:
                        ref[j, :chunk, size:] = (
                            dot(refs[6][at, :rows], ya_ref[...]) + dot(refs[6][at, rows:], yb_ref[...])
                        ).astype(bf16)
                        ref[j, chunk:, :] = extra


def weight_grads(place, sends, keeps, chips, hs, value, os=None, ys=None, extra=None):
    rows, width = hs[0].shape
    chunk = width // chips
    parts, _, size = value.shape
    more = os is not None
    hc = ys[1].shape[2] if more else 0
    tall = chunk + (EXTRA if more else 0)
    middle = parts // 2
    if chunk % 128:
        result = []
        for which, lo in ((sends[0], 0), (keeps[0], 0), (sends[1], middle), (keeps[1], middle)):
            cut = lambda pair: jnp.concatenate(
                [jnp.concatenate(pair, axis=0)[:, r * chunk : (r + 1) * chunk] for r in which], axis=1
            )
            found = []
            for k in range(lo, lo + middle):
                one = t_dot(cut(hs), value[k])
                if more:
                    at = (place[0] - k) % parts
                    y = lax.dynamic_index_in_dim(ys[0], at, 0, keepdims=False)
                    y = lax.dynamic_slice_in_dim(y, place[2] * hc, hc, 1)
                    y = jnp.concatenate([y, lax.dynamic_index_in_dim(ys[1], at, 0, keepdims=False)])
                    one = jnp.concatenate([one, t_dot(cut(os), y)], axis=1)
                one = one.reshape(len(which), chunk, size + hc)
                if more:
                    wide = jnp.broadcast_to(extra[k][None], (len(which), EXTRA, size + hc))
                    one = jnp.concatenate([one, wide], axis=1)
                found.append(one.astype(bf16))
            result.append(jnp.stack(found, axis=1))
        return [result[0], result[2]], [result[1], result[3]]
    whole = full_spec((rows, width))
    ins = list(hs)
    in_specs = [whole] * 2
    scratch = [pltpu.VMEM((width, 2 * rows), bf16)]
    if more:
        slot = lambda k, p: lax.rem(p[0] + parts - k, parts)
        cols = ys[0].shape[2]
        part = pl.BlockSpec((8, cols), lambda k, p: (0, slot(k, p) ^ p[1]))
        ins += [*os, ys[0], ys[1], *extra]
        in_specs += [whole] * 2
        in_specs += [
            pl.BlockSpec((None, rows, hc), lambda k, p: (slot(k, p), 0, p[2])),
            pl.BlockSpec((None, rows, hc), lambda k, p: (slot(k, p), 0, 0)),
            pl.BlockSpec((None, 8, size // 2), lambda k, p: (k, 0, 0)),
            part,
            part,
        ]
        scratch = scratch * 2
    ins.append(value)
    in_specs.append(pl.BlockSpec((None, 2 * rows, size), lambda k, p: (k, 0, 0)))
    lists = [sends[0], keeps[0], sends[1], keeps[1]]
    block = lambda one: (len(one), None, tall, size + hc)
    early = lambda k, p: (0, jnp.minimum(k, middle - 1), 0, 0)
    late = lambda k, p: (0, jnp.maximum(k - middle, 0), 0, 0)
    out = pl.pallas_call(
        functools.partial(
            grad_kernel, orders=(lists[:2], lists[2:]), parts=parts, chunk=chunk, more=more
        ),
        grid_spec=pltpu.PrefetchScalarGridSpec(
            num_scalar_prefetch=1,
            grid=(parts,),
            in_specs=in_specs,
            out_specs=[
                pl.BlockSpec(block(one), early if n < 2 else late) for n, one in enumerate(lists)
            ],
            scratch_shapes=scratch,
        ),
        out_shape=[
            jax.ShapeDtypeStruct((len(one), middle, tall, size + hc), bf16) for one in lists
        ],
        compiler_params=params(56),
    )(place, *ins)
    return [out[0], out[2]], [out[1], out[3]]


def adam_values(weight, grad, first, second):
    first_new = beta_one * first + (1.0 - beta_one) * grad
    second_new = beta_two * second + (1.0 - beta_two) * grad * grad
    moved = weight - learn_rate * (first_new / bias_one) / (
        jnp.sqrt(second_new / bias_two) + adam_eps
    )
    return first_new, second_new, moved


def lane_sums(value):
    ones = jnp.ones((8, value.shape[1]), bf16)
    high = value.astype(bf16)
    low = (value - high.astype(f32)).astype(bf16)
    return dot_t(ones, high) + dot_t(ones, low)


def adam_wide_kernel(w_ref, g_ref, m_ref, v_ref, g_out, m_out, v_out, n_out, s_out):
    cols = w_ref.shape[2]
    for c in range(w_ref.shape[1]):
        grad = g_ref[:, c * cols : (c + 1) * cols]
        first, second, moved = adam_values(w_ref[:, c, :], grad, m_ref[:, c, :], v_ref[:, c, :])
        g_out[:, c, :] = grad
        m_out[:, c, :] = first
        v_out[:, c, :] = second
        n_out[:, c, :] = moved
        s_out[c : c + 1, :] = jnp.sum(moved * moved, axis=0, keepdims=True)


def adam_wide(w, g, m, v):
    vmem = pl.BlockSpec(memory_space=pltpu.VMEM)
    return pl.pallas_call(
        adam_wide_kernel,
        in_specs=[vmem] * 4,
        out_specs=[vmem] * 5,
        out_shape=[jax.ShapeDtypeStruct(w.shape, f32)] * 4
        + [jax.ShapeDtypeStruct(w.shape[1:], f32)],
        compiler_params=params(16),
    )(w, g, m, v)


def adam_tall_kernel(w_ref, g_ref, m_ref, v_ref, g_out, m_out, v_out, n_out, s_out):
    grad = g_ref[...].T
    first, second, moved = adam_values(w_ref[...], grad, m_ref[...], v_ref[...])
    g_out[...] = grad
    m_out[...] = first
    v_out[...] = second
    n_out[...] = moved
    s_out[...] = lane_sums(moved * moved)


def adam_tall(w, g, m, v):
    vmem = pl.BlockSpec(memory_space=pltpu.VMEM)
    return pl.pallas_call(
        adam_tall_kernel,
        in_specs=[vmem] * 4,
        out_specs=[vmem] * 5,
        out_shape=[jax.ShapeDtypeStruct(w.shape, f32)] * 4
        + [jax.ShapeDtypeStruct((8, w.shape[0]), f32)],
        compiler_params=params(16),
    )(w, g, m, v)


def scale_kernel(na_ref, nb_ref, nc_ref, nd_ref, a_ref, b_ref, c_ref, d_ref, ao_ref, bo_ref, co_ref, do_ref, *, width):
    factor = lambda value: lax.rsqrt(value / width + layer_eps)
    for norm, ref, out in ((na_ref, a_ref, ao_ref), (nc_ref, c_ref, co_ref)):
        for c in range(ref.shape[1]):
            out[:, c, :] = ref[:, c, :] * factor(norm[c : c + 1, :])
    for norm, ref, out in ((nb_ref, b_ref, bo_ref), (nd_ref, d_ref, do_ref)):
        out[...] = ref[...] * factor(norm[...]).T[:, 0:1]


def scale_weights(norms, weights, width):
    vmem = pl.BlockSpec(memory_space=pltpu.VMEM)
    return pl.pallas_call(
        functools.partial(scale_kernel, width=width),
        in_specs=[vmem] * 8,
        out_specs=[vmem] * 4,
        out_shape=[jax.ShapeDtypeStruct(w.shape, f32) for w in weights],
        compiler_params=params(16),
    )(*norms, *weights)


def after(value, *others):
    return lax.optimization_barrier((value, *others))[0]


def per_device(
    layer_input,
    cotangent,
    positions,
    w_qkv,
    w_out,
    w_up,
    w_down,
    moment_qkv,
    moment_out,
    moment_up,
    moment_down,
    square_qkv,
    square_out,
    square_up,
    square_down,
    s_qk,
    alpha_attn,
    alpha_mlp,
    s_uv,
):
    nz = lax.axis_size("head")
    nb = lax.axis_size("batch")
    z = lax.axis_index("head")
    b = lax.axis_index("batch")
    core = b % 2
    chip = b // 2
    chips = nb // 2
    bits = [1 << n for n in range(int(math.log2(chips)))]
    rows, cols = layer_input.shape
    width = cols * nz
    own = rows // nz
    hid = w_down.shape[0]
    half = hid // 2
    hc = cols // 2
    heads = cols // HEAD_DIM
    span = w_qkv.shape[0]
    chunk = width // chips
    core_s = core.reshape(1).astype(jnp.int32)
    place = jnp.stack([z, chip, core]).astype(jnp.int32)
    fast = chunk == cols and chunk % 128 == 0

    def swap_batch(value, bit):
        return lax.ppermute(value, "batch", [(i, i ^ bit) for i in range(nb)])

    def swap_core(value):
        return swap_batch(value, 1)

    def swap_chip(value, bit):
        return swap_batch(value, 2 * bit)

    def onward(value, k=1):
        return lax.ppermute(value, "head", [(i, (i + k) % nz) for i in range(nz)])

    def exchange(value):
        return lax.all_to_all(value, "head", split_axis=0, concat_axis=0)

    def pick(pair, index):
        return jnp.where(index == 0, pair[0], pair[1])

    def relative(value):
        return jnp.concatenate(
            [
                lax.dynamic_slice_in_dim(value, (chip ^ r) * chunk, chunk, value.ndim - 1)
                for r in range(chips)
            ],
            axis=-1,
        )

    def spread(value):
        if chips <= 4:
            return [value] + [swap_chip(value, r) for r in range(1, chips)]
        for bit in bits:
            value = jnp.concatenate([value, swap_chip(value, bit)], axis=0)
        return [value]

    tokens = [layer_input, onward(layer_input)]
    mine, theirs = pack(core_s, w_up, s_uv, w_down, w_out)
    qkv_own = after(w_qkv, mine).reshape(span, 3 * cols).astype(bf16)
    qkv_full = lax.all_gather(qkv_own, "batch", axis=0, tiled=True)
    theirs = swap_core(theirs)
    packet = jnp.concatenate([pick((mine, theirs), core), pick((theirs, mine), core)], axis=0)
    hops = [packet, onward(packet)]
    slots = [spread(packet)]
    tokens[1], hops[1], places, alpha_attn, alpha_mlp, *last = lax.optimization_barrier(
        (tokens[1], hops[1], positions, alpha_attn, alpha_mlp, *slots[0])
    )
    slots[0] = list(last)

    freqs = jnp.exp(
        (jnp.arange(128) % (HEAD_DIM // 2)).astype(f32) * (-2.0 * math.log(10000.0) / HEAD_DIM)
    )
    phase = places.astype(f32)[:, None] * freqs[None, :]
    side = jnp.where(jnp.arange(128) % HEAD_DIM < HEAD_DIM // 2, -1.0, 1.0).astype(f32)
    cosine, sine = jnp.cos(phase), jnp.sin(phase) * side[None, :]
    lane = jnp.arange(cols) // HEAD_DIM
    ones = (lane[:, None] == lane[None, :]).astype(bf16)
    gain = s_qk.reshape(1, cols)
    is_long = (places[SHORT : SHORT + 1] != 0).astype(jnp.int32)
    attn_gain = relative(alpha_attn[None])
    mlp_gain = relative(alpha_mlp[None])

    for n in range(2, nz):
        slots.append(spread(hops[-1]))
        tokens.append(onward(tokens[-1]))
        if n < nz - 1:
            hops.append(onward(hops[-1]))
            tokens[-1], hops[-1], cosine, sine, ones, attn_gain, mlp_gain, *last = (
                lax.optimization_barrier(
                    (tokens[-1], hops[-1], cosine, sine, ones, attn_gain, mlp_gain, *slots[-1])
                )
            )
            slots[-1] = list(last)
    last_hop, tokens[-1] = lax.optimization_barrier((hops[-1], tokens[-1]))
    hops.append(onward(last_hop))

    blocks = rows // 512
    middle = blocks // 2
    tokens_full, q, k, v, rho = qkv_project(place, tokens, qkv_full, cosine, sine, gain, ones)
    y_a, logs_a = attn_fwd(is_long, q, k, v, 0, middle)
    q_b, hops[-1], *last = lax.optimization_barrier((after(q, y_a), hops[-1], *slots[-1]))
    slots[-1] = list(last)
    slots.append(spread(hops[-1]))
    y_b, logs_b = attn_fwd(is_long, q_b, k, v, middle, blocks - middle)
    y_one = exchange(y_a.reshape(nz, own // 2, cols))
    y_in, y_one = lax.optimization_barrier((y_b, y_one))
    y_two = exchange(y_in.reshape(nz, own // 2, cols))
    flat = lambda value: value.transpose(1, 0, 2).reshape(own, width)
    start = tokens_full
    if not fast:
        start = jnp.concatenate(
            [
                lax.dynamic_slice_in_dim(tokens_full, h * (rows // 2) + z * (own // 2), own // 2, 0)
                for h in range(2)
            ]
        )
        start = relative(start)
    y_one, y_two, *last = lax.optimization_barrier((y_one, y_two, *slots[-1]))
    slots[-1] = list(last)
    hA, h1, h_own, stat, y_mine, y_other = attn_out(place, y_one, y_two, slots, start, attn_gain, chips, fast)
    h_got = swap_core(h_own)
    y_got = swap_core(y_other)
    h_got, y_got = lax.optimization_barrier((h_got, y_got))
    cot = after(cotangent, h_own).reshape(2, nz, own // 2, cols).transpose(1, 0, 2, 3)
    cot = exchange(cot.reshape(nz, own, cols))

    act, uv, mo_own, mo_other = mlp_fwd(h_own, h_got, slots, half)
    mo_got = swap_core(mo_other)
    if not fast:
        cot = relative(flat(cot))
    hidden, d_own, base, ga_mlp = loss(place, mo_own, mo_got, h1, cot, mlp_gain, chips, fast)
    d_got = swap_core(d_own)
    if not fast:
        hidden = relative(hidden).reshape(own, nz, cols).transpose(1, 0, 2)
    hidden = exchange(hidden)

    orders = [bits, bits[::-1]]
    sent_at = [[r for r in range(chips) if r & order[0]] for order in orders]
    kept_at = [[r for r in range(chips) if not r & order[0]] for order in orders]

    def second(kept, sent):
        found, sends = [], []
        for order, left, got, keep in zip(orders, kept_at, sent, kept):
            terms = [keep, got]
            for bit in order[1:]:
                send_at = [n for n, r in enumerate(left) if r & bit]
                keep_at = [n for n, r in enumerate(left) if not r & bit]
                left = [left[n] for n in keep_at]
                cut = lambda v, at: jnp.concatenate([v[n : n + 1] for n in at], axis=0)
                send = sum(cut(t, send_at).astype(f32) for t in terms).astype(bf16)
                terms = [cut(t, keep_at) for t in terms] + [swap_chip(send, bit)]
                sends.append(send)
            found.append(terms)
        return found, sends

    def slot_sums(found):
        return [sum(t[0, n].astype(f32) for t in terms) for terms in found for n in range(nz // 2)]

    def wait_last(found, *others):
        return [terms[:-1] + [after(terms[-1], *others)] for terms in found]

    down_made, down_kept = weight_grads(place, sent_at, kept_at, chips, (d_own, d_got), act)
    down_sent = [swap_chip(one, order[0]) for one, order in zip(down_made, orders)]
    d_own, d_got, *_ = lax.optimization_barrier((d_own, d_got, *down_made))
    duv, dh_own, dh_other, gsuv = mlp_bwd(d_own, d_got, slots, uv, half)
    dh_got = swap_core(dh_other)
    down_sent = [after(one, dh_other) for one in down_sent]
    down_part, down_next = second(down_kept, down_sent)
    dh_own, hidden, *_ = lax.optimization_barrier((dh_own, hidden, *down_next))
    do_own, through, ga_attn, dy_a, dy_b = first_back(
        place, dh_own, dh_got, base, h1, hA, start, stat, attn_gain, slots, chips, fast, cols
    )
    dy_b = exchange(dy_b)
    do_got = swap_core(do_own)

    extra = (gsuv, ga_attn, ga_mlp)
    if not fast:
        alphas = [relative(ga_attn[0:1]), relative(ga_mlp[0:1])]
        extra = []
        wide = 2 * half + hc
        fill = lambda r: jnp.pad(r, ((0, 0), (0, wide - r.shape[1])))
        for n in range(nz):
            at = ((z - n) % nz) * cols
            line = [lax.dynamic_slice_in_dim(g, at, cols, 1) for g in alphas]
            lines = [gsuv[n, :2].reshape(1, 2 * half), jnp.concatenate(line, axis=1)]
            lines = jnp.concatenate([fill(r) for r in lines])
            extra.append(jnp.pad(lines, ((0, EXTRA - 2), (0, 0))))
        extra = jnp.stack(extra)
    up_made, up_kept = weight_grads(
        place, sent_at, kept_at, chips, (h_own, h_got), duv, (do_own, do_got), (y_mine, y_got), extra
    )
    down_part = wait_last(down_part, *up_kept)
    down_last = [terms[-1] for terms in down_part]
    dy_b, dy_a, *both = lax.optimization_barrier((dy_b, dy_a, *up_made, *down_last))
    up_made, down_last = both[: len(up_made)], both[len(up_made) :]
    down_slots = slot_sums([t[:-1] + [last] for t, last in zip(down_part, down_last)])
    down_along = [onward(down_slots[n].astype(bf16), nz - n) for n in range(1, nz)]
    up_sent = [swap_chip(one, order[0]) for one, order in zip(up_made, orders)]

    dy_a = exchange(dy_a)
    common = lambda dy, y, logs: (
        is_long, q, k, v, dy.reshape(y.shape), y, logs, rho, cosine, sine, gain, ones
    )
    dqkv_b, dk_part, dv_part, sqk_b = attn_bwd(
        *common(dy_b, y_b, logs_b), middle, blocks - middle, None
    )

    if not fast:
        through = relative(through)

    mine_at = z * (own // 2)

    def input_part(dqkv, side):
        part = dot_t(dqkv, qkv_full).astype(bf16)
        here = lax.dynamic_slice_in_dim(part, mine_at, own // 2, 0).astype(f32)
        here = here + through[side * (own // 2) : (side + 1) * (own // 2)].astype(f32)
        return lax.dynamic_update_slice_in_dim(part, here.astype(bf16), mine_at, 0)

    dqkv_b, dk_part, dy_a = lax.optimization_barrier((dqkv_b, dk_part, dy_a))
    part_b = jnp.einsum(
        "tn,zcn->ztc", dqkv_b, qkv_full.reshape(nz, cols, 3 * cols), preferred_element_type=f32
    ).astype(bf16)
    here = lax.dynamic_slice_in_dim(part_b, mine_at, own // 2, 1).astype(f32)
    here = here + through[own // 2 :].reshape(own // 2, nz, cols).transpose(1, 0, 2).astype(f32)
    part_b = lax.dynamic_update_slice_in_dim(part_b, here.astype(bf16), mine_at, 1)
    down_along = [after(one, dqkv_b) for one in down_along]
    up_part, up_next = second(up_kept, [after(one, dqkv_b) for one in up_sent])
    part_got = exchange(part_b)
    dk_part, dy_a, *_ = lax.optimization_barrier((dk_part, dy_a, *up_next, part_b, *down_along))
    dqkv_a, sqk_a = attn_bwd(*common(dy_a, y_a, logs_a), 0, middle, [dk_part, dv_part])
    input_b = jnp.sum(after(part_got, dqkv_a).astype(f32), axis=0)
    up_part = wait_last(up_part, dqkv_a, *[terms[-1] for terms in up_part])
    part_a = input_part(dqkv_a, 0)
    up_slots = slot_sums(up_part)
    passed = onward(up_slots[1].astype(bf16))
    for n in range(2, nz):
        if n == nz - 2:
            passed, part_a = lax.optimization_barrier((passed, part_a))
        passed = onward((up_slots[n] + passed.astype(f32)).astype(bf16))
    sum_up_t = up_slots[0] + passed.astype(f32)
    input_a = lax.psum_scatter(part_a, "head", scatter_dimension=1, tiled=True)
    input_grad = jnp.concatenate([input_a.astype(f32), input_b], axis=0)
    hidden_t = after(hidden, part_a).reshape(nz, 2, own // 2, cols).transpose(1, 0, 2, 3).reshape(rows, cols)

    dqkv = jnp.concatenate([dqkv_a, dqkv_b], axis=0)
    grad_qkv = t_dot(tokens_full, dqkv).astype(bf16)
    sqk = jnp.pad((sqk_a + sqk_b), ((0, EXTRA - 8), (0, 2 * cols)))
    shard = [lax.dynamic_slice_in_dim(grad_qkv, (b ^ r) * span, span, 0) for r in range(nb)]
    shard = [jnp.concatenate([s, sqk.astype(bf16)], axis=0) for s in shard]
    qbits = [1 << n for n in range(int(math.log2(nb)))]
    held = {r: shard[r] for r in range(nb)}
    for bit in qbits:
        send_at = [r for r in held if r & bit]
        send = jnp.concatenate([held[r] for r in send_at], axis=0).astype(bf16)
        got = swap_batch(send, bit)
        size = span + EXTRA
        held = {
            r ^ bit: held[r ^ bit].astype(f32) + got[n * size : (n + 1) * size].astype(f32)
            for n, r in enumerate(send_at)
        }
    cell = width // (nz * nb)
    sum_sqk = lax.dynamic_slice_in_dim(held[0][span, :cols], b * cell, cell, 0)
    w_late, m_late, v_late, _ = lax.optimization_barrier((w_qkv, moment_qkv, square_qkv, part_a))
    qkv_new = adam_wide(w_late, held[0][:span], m_late, v_late)

    def both_halves(total):
        two = (total[:span], total[span : 2 * span])
        here = jnp.concatenate([pick(two, core), total[2 * span :]], axis=0)
        there = jnp.concatenate([pick(two, 1 - core), total[2 * span :]], axis=0)
        there = swap_core(there.astype(bf16)).astype(f32)
        return [pick((here, there), core), pick((there, here), core)]

    join = lambda halves, at, size: [p[:span, at : at + size] for p in halves]
    down_along = [after(one, part_a) for one in down_along]
    halves = both_halves(down_slots[0] + sum(one.astype(f32) for one in down_along))
    down_new = adam_tall(w_down, jnp.concatenate(join(halves, 0, half), axis=1), moment_down, square_down)
    halves = both_halves(sum_up_t)
    grad_up = jnp.concatenate(join(halves, 0, half) + join(halves, half, half), axis=1)
    grad_up = grad_up * s_uv.reshape(1, 2 * hid)
    up_new = adam_wide(w_up, grad_up, moment_up, square_up)
    out_new = adam_tall(w_out, jnp.concatenate(join(halves, 2 * half, hc), axis=1), moment_out, square_out)
    suv_rows = jnp.stack(
        [jnp.concatenate([p[span, c * half : (c + 1) * half] for p in halves]) for c in range(2)]
    )
    suv_rows = suv_rows / s_uv
    sum_suv = lax.dynamic_slice_in_dim(suv_rows, b * (hid // nb), hid // nb, 1)
    alphas = halves[0][span + 1] + halves[1][span + 1]
    sum_attn = lax.dynamic_slice_in_dim(alphas[:cols], b * cell, cell, 0)
    sum_mlp = lax.dynamic_slice_in_dim(alphas[cols : 2 * cols], b * cell, cell, 0)

    hidden = hidden_t.astype(f32)

    squares = [qkv_new[4], out_new[4][:1], up_new[4], down_new[4][:1]]
    sizes = [t.size for t in squares]
    norms = jnp.concatenate([t.reshape(-1) for t in squares]).reshape(-1, 128)
    for bit in qbits:
        norms = norms + swap_batch(norms, bit)
    norms = norms.reshape(-1)
    ends = [0] + [sum(sizes[: n + 1]) for n in range(4)]
    back = lambda n, shape: norms[ends[n] : ends[n + 1]].reshape(shape)
    eight = lambda value: jnp.broadcast_to(value, (8, value.shape[1]))
    new_qkv, new_out, new_up, new_down = scale_weights(
        [back(0, (3, cols)), eight(back(1, (1, cols))), back(2, (2, hid)), eight(back(3, (1, hid)))],
        [qkv_new[3], out_new[3], up_new[3], down_new[3]],
        width,
    )
    sum_qkv, first_a, second_a = qkv_new[:3]
    sum_out, first_b, second_b = out_new[:3]
    sum_up, first_c, second_c = up_new[:3]
    sum_down, first_d, second_d = down_new[:3]
    return (
        hidden,
        input_grad,
        sum_qkv,
        sum_out,
        sum_up,
        sum_down,
        first_a,
        first_b,
        first_c,
        first_d,
        second_a,
        second_b,
        second_c,
        second_d,
        new_qkv,
        new_out,
        new_up,
        new_down,
        sum_sqk,
        sum_attn,
        sum_mlp,
        sum_suv,
    )


def solution(mesh):
    tokens = P("batch", "head")
    wide = P("batch", None, "head")
    tall = P("head", "batch")
    flat = P(("head", "batch"))
    weights = (wide, tall, wide, tall)
    return jax.shard_map(
        per_device,
        mesh=mesh,
        in_specs=(tokens, tokens, P("batch"))
        + weights * 3
        + (P("head"), P(), P(), P(None, "head")),
        out_specs=(tokens, tokens) + weights * 4 + (flat, flat, flat, P(None, ("head", "batch"))),
        check_vma=False,
    )
```

```python
import functools
import math

import jax
import jax.numpy as jnp
from jax import lax
from jax.experimental import pallas as pl
from jax.experimental.pallas import tpu as pltpu
from jax.sharding import PartitionSpec as P

HEAD_DIM = 64
SHORT = 1024

layer_eps = 1e-06
learn_rate = 0.008
beta_one = 0.9
beta_two = 0.95
adam_eps = 1e-08
bias_one = 1.0 - math.exp(100.0 * math.log(0.9))
bias_two = 1.0 - math.exp(100.0 * math.log(0.95))
score_scale = 8.0
LOG2E = math.log2(math.e)
LN2 = math.log(2.0)

bf16 = jnp.bfloat16
f32 = jnp.float32


def dot(a, b):
    return jnp.dot(a, b, preferred_element_type=f32)


def dot_t(a, b):
    return lax.dot_general(a, b, (((1,), (1,)), ((), ())), preferred_element_type=f32)


def t_dot(a, b):
    return lax.dot_general(a, b, (((0,), (0,)), ((), ())), preferred_element_type=f32)


def params(mib):
    return pltpu.CompilerParams(vmem_limit_bytes=mib * 1024 * 1024)


def full_spec(shape):
    return pl.BlockSpec(shape, lambda *_: (0,) * len(shape))


def head_sum(value, ones):
    high = value.astype(bf16)
    low = (value - high.astype(f32)).astype(bf16)
    return dot(high, ones) + dot(low, ones)


def widen(value, cols):
    return jnp.concatenate([value] * (cols // value.shape[1]), axis=1)


def swap_halves(value):
    cols = value.shape[-1]
    half = HEAD_DIM // 2
    lane = lax.broadcasted_iota(jnp.int32, value.shape, 1)
    first = (lane % HEAD_DIM) < half
    up = pltpu.roll(value, cols - half, 1)
    down = pltpu.roll(value, half, 1)
    return jnp.where(first, up, down)


def qkv_kernel(place_ref, *refs, parts):
    tokens = refs[:parts]
    w_ref, cos_ref, sin_ref, gain_ref, ones_ref, x_ref, q_ref, k_ref, v_ref, rho_ref = refs[parts:]
    cols = v_ref.shape[1]
    z = place_ref[0]
    for n in range(parts):
        at = pl.multiple_of(lax.rem(z + parts - n, parts) * cols, cols)
        x_ref[:, pl.ds(at, cols)] = tokens[n][...]
    proj = dot(x_ref[...], w_ref[...])
    cosine = widen(cos_ref[...], cols)
    sine = widen(sin_ref[...], cols)
    ones = ones_ref[...]
    gain = gain_ref[...]
    heads = cols // HEAD_DIM
    lane = lax.broadcasted_iota(jnp.int32, rho_ref.shape, 1)
    stats = jnp.zeros(rho_ref.shape, f32)
    for c, (out, scale) in enumerate(((q_ref, score_scale * LOG2E), (k_ref, 1.0))):
        part = proj[:, c * cols : (c + 1) * cols]
        rho = lax.rsqrt(head_sum(part * part, ones) + layer_eps)
        rot = part * cosine + swap_halves(part) * sine
        out[...] = (rot * rho * (gain * scale)).astype(bf16)
        for h in range(heads):
            stats = jnp.where(lane == c * heads + h, rho[:, h * HEAD_DIM : h * HEAD_DIM + 1], stats)
    rho_ref[...] = stats
    v_ref[...] = proj[:, 2 * cols :].astype(bf16)


def qkv_project(place, tokens, w, cosine, sine, gain, ones):
    rows, cols = tokens[0].shape
    parts = len(tokens)
    width = parts * cols
    blk = 512
    row = lambda n: pl.BlockSpec((blk, n), lambda i, s: (i, 0))
    return pl.pallas_call(
        functools.partial(qkv_kernel, parts=parts),
        grid_spec=pltpu.PrefetchScalarGridSpec(
            num_scalar_prefetch=1,
            grid=(rows // blk,),
            in_specs=[row(cols)] * parts
            + [full_spec((width, 3 * cols)), row(128), row(128)]
            + [full_spec((1, cols)), full_spec((cols, cols))],
            out_specs=[row(width)] + [row(cols)] * 3 + [row(128)],
        ),
        out_shape=[jax.ShapeDtypeStruct((rows, width), bf16)]
        + [jax.ShapeDtypeStruct((rows, cols), bf16)] * 3
        + [jax.ShapeDtypeStruct((rows, 128), f32)],
        compiler_params=params(56),
    )(place, *tokens, w, cosine, sine, gain, ones)


def head_masks(cols, heads):
    lane = lax.broadcasted_iota(jnp.int32, (1, cols), 1) // HEAD_DIM
    return [(lane == h) for h in range(heads)]


def masked(value, mask):
    return jnp.where(mask, value, jnp.zeros_like(value))


def attn_fwd_kernel(long_ref, q_ref, k_ref, v_ref, y_ref, l_ref, acc, mass, *, heads, blk, sub, first):
    i = first + pl.program_id(0)
    cols = q_ref.shape[1]
    masks = head_masks(cols, heads)
    per = SHORT // blk
    low = jnp.where(long_ref[0] != 0, 0, (i // per) * per)
    acc[...] = jnp.zeros_like(acc)
    mass[...] = jnp.zeros_like(mass)

    def lanes(p):
        total = p[:, 0:128]
        for n in range(1, p.shape[1] // 128):
            total = total + p[:, n * 128 : (n + 1) * 128]
        return total

    def body(j, carry):
        start = pl.multiple_of(j * blk, blk)
        keys = k_ref[pl.ds(start, blk), :]
        vals = v_ref[pl.ds(start, blk), :]
        q = q_ref[...]
        total = jnp.zeros(acc.shape, f32)
        for h in range(heads):
            p = jnp.exp2(dot_t(masked(q, masks[h]), keys))
            mass[h] += lanes(p)
            total += dot(p.astype(bf16), masked(vals, masks[h]))
        acc[...] += total
        return carry

    lax.fori_loop(low, i, body, 0)
    start = pl.multiple_of(i * blk, blk)
    causal = lax.broadcasted_iota(jnp.int32, (sub, sub), 0) >= lax.broadcasted_iota(
        jnp.int32, (sub, sub), 1
    )
    for a in range(blk // sub):
        rows = slice(a * sub, (a + 1) * sub)
        q = q_ref[rows, :]
        for b in range(a + 1):
            at = pl.multiple_of(start + b * sub, sub)
            keys = k_ref[pl.ds(at, sub), :]
            vals = v_ref[pl.ds(at, sub), :]
            total = jnp.zeros((sub, cols), f32)
            for h in range(heads):
                p = jnp.exp2(dot_t(masked(q, masks[h]), keys))
                if a == b:
                    p = jnp.where(causal, p, 0.0)
                mass[h, rows, :] += lanes(p)
                total += dot(p.astype(bf16), masked(vals, masks[h]))
            acc[rows, :] += total
    inverse = jnp.zeros(acc.shape, f32)
    logs = jnp.zeros(l_ref.shape, f32)
    lane = lax.broadcasted_iota(jnp.int32, l_ref.shape, 1)
    for h in range(heads):
        column = jnp.sum(mass[h], axis=1, keepdims=True)
        inverse = jnp.where(masks[h], 1.0 / column, inverse)
        logs = jnp.where(lane == h, jnp.log2(column), logs)
    y_ref[...] = (acc[...] * inverse).astype(bf16)
    l_ref[...] = logs


def attn_fwd(is_long, q, k, v, first, count):
    rows, cols = q.shape
    heads = cols // HEAD_DIM
    blk, sub = 512, 256
    row = lambda n: pl.BlockSpec((blk, n), lambda i, s: (i, 0))
    whole = pl.BlockSpec(((first + count) * blk, cols), lambda i, s: (0, 0))
    return pl.pallas_call(
        functools.partial(attn_fwd_kernel, heads=heads, blk=blk, sub=sub, first=first),
        grid_spec=pltpu.PrefetchScalarGridSpec(
            num_scalar_prefetch=1,
            grid=(count,),
            in_specs=[pl.BlockSpec((blk, cols), lambda i, s: (first + i, 0)), whole, whole],
            out_specs=[row(cols), row(128)],
            scratch_shapes=[pltpu.VMEM((blk, cols), f32), pltpu.VMEM((heads, blk, 128), f32)],
        ),
        out_shape=[
            jax.ShapeDtypeStruct((count * blk, cols), bf16),
            jax.ShapeDtypeStruct((count * blk, 128), f32),
        ],
        compiler_params=params(56),
    )(is_long, q, k, v)


def attn_bwd_kernel(
    long_ref, q_ref, qk_ref, dy_ref, y_ref, l_ref, k_ref, v_ref, rho_ref, cos_ref, sin_ref, gain_ref,
    ones_ref, dk_in, dv_in, out_ref, dk_out, dv_out, s_ref, acc, dk_acc, dv_acc, stats, dys, *, heads, blk, sub, first, count
):
    step = pl.program_id(0)
    local = count - 1 - step
    i = first + local
    cols = q_ref.shape[1]
    masks = head_masks(cols, heads)
    per = SHORT // blk
    low = jnp.where(long_ref[0] != 0, 0, (i // per) * per)
    ones = ones_ref[...]
    gain = gain_ref[...]

    @pl.when(step == 0)
    def _():
        dk_acc[...] = jnp.zeros_like(dk_acc)
        dv_acc[...] = jnp.zeros_like(dv_acc)
        s_ref[...] = jnp.zeros_like(s_ref)
        if dk_in is not None:
            dk_acc[...] = dk_in[...]
            dv_acc[...] = dv_in[...]

    acc[...] = jnp.zeros_like(acc)
    dys[...] = dy_ref[...].reshape(dys.shape)
    prod = dys[...].astype(f32) * y_ref[...].astype(f32)
    high = prod.astype(bf16)
    rest = (prod - high.astype(f32)).astype(bf16)
    pickers = (
        lax.broadcasted_iota(jnp.int32, (8, cols), 1) // HEAD_DIM
        == lax.broadcasted_iota(jnp.int32, (8, cols), 0)
    ).astype(bf16)
    stats[0:8, :] = dot_t(pickers, high) + dot_t(pickers, rest)
    stats[8:16, :] = l_ref[...].T[0:8, :]

    def piece(at, size, rows, causal):
        keys = k_ref[pl.ds(at, size), :]
        vals = v_ref[pl.ds(at, size), :]
        q = q_ref[rows, :]
        dy = dys[rows, :]
        total_q = jnp.zeros(q.shape, f32)
        total_k = jnp.zeros(keys.shape, f32)
        total_v = jnp.zeros(keys.shape, f32)
        for h in range(heads):
            qm = masked(q, masks[h])
            dym = masked(dy, masks[h])
            p = jnp.exp2(dot_t(keys, qm) - stats[8 + h : 9 + h, rows])
            if causal is not None:
                p = jnp.where(causal, p, 0.0)
            ds = (p * (dot_t(vals, dym) - stats[h : h + 1, rows])).astype(bf16)
            total_v += dot(p.astype(bf16), dym)
            total_k += dot(ds, qm)
            total_q += t_dot(ds, masked(keys, masks[h]))
        acc[rows, :] += total_q
        dk_acc[pl.ds(at, size), :] += total_k
        dv_acc[pl.ds(at, size), :] += total_v

    def body(j, carry):
        piece(pl.multiple_of(j * blk, blk), blk, slice(0, blk), None)
        return carry

    lax.fori_loop(low, i, body, 0)
    start = pl.multiple_of(i * blk, blk)
    causal = lax.broadcasted_iota(jnp.int32, (sub, sub), 0) <= lax.broadcasted_iota(
        jnp.int32, (sub, sub), 1
    )
    for a in range(blk // sub):
        for b in range(a + 1):
            piece(
                pl.multiple_of(start + b * sub, sub),
                sub,
                slice(a * sub, (a + 1) * sub),
                causal if a == b else None,
            )
    cosine = widen(cos_ref[...], cols)
    sine = widen(sin_ref[...], cols)
    total = jnp.zeros((1, cols), f32)
    here = pl.ds(start, blk)
    for c, (value, unit, up, scale) in enumerate(
        (
            (acc[...], q_ref[...], score_scale, score_scale * LOG2E),
            (dk_acc[here, :], k_ref[here, :], LN2, 1.0),
        )
    ):
        rho = jnp.zeros(value.shape, f32)
        for h in range(heads):
            at = c * heads + h
            rho = jnp.where(masks[h], rho_ref[:, at : at + 1], rho)
        grad = value * up
        unit = unit.astype(f32) * (1.0 / (gain * scale))
        total += jnp.sum(grad * unit, axis=0, keepdims=True)
        grad = grad * gain
        back = rho * (grad - unit * head_sum(grad * unit, ones))
        turned = back * cosine - swap_halves(back) * sine
        out_ref[:, c * cols : (c + 1) * cols] = turned.astype(bf16)
    out_ref[:, 2 * cols :] = dv_acc[here, :].astype(bf16)
    s_ref[0:1, :] += total
    if dk_out is not None:
        @pl.when(step == count - 1)
        def _():
            dk_out[...] = dk_acc[0 : first * blk, :]
            dv_out[...] = dv_acc[0 : first * blk, :]


def attn_bwd(is_long, q, k, v, dy, y, logs, rho, cosine, sine, gain, ones, first, count, carry):
    rows, cols = q.shape
    heads = cols // HEAD_DIM
    blk, sub = 512, 256
    top = (first + count) * blk
    at = lambda s: first + count - 1 - s
    row = lambda n: pl.BlockSpec((blk, n), lambda s, m: (at(s), 0))
    whole = pl.BlockSpec((top, cols), lambda s, m: (0, 0))
    ins = [q, k, dy, y, logs, k, v, rho, cosine, sine, gain, ones]
    mine = lambda n: pl.BlockSpec((blk, n), lambda s, m: (count - 1 - s, 0))
    share = dy.shape[2]
    half_at = 1 if first else 0
    in_specs = [row(cols)] * 2
    in_specs.append(
        pl.BlockSpec((blk // share, None, share, cols), lambda s, m: (count - 1 - s, half_at, 0, 0))
    )
    in_specs += [mine(cols), mine(128), whole, whole] + [row(128)] * 3
    in_specs += [full_spec((1, cols)), full_spec((cols, cols))]
    body = functools.partial(
        attn_bwd_kernel, heads=heads, blk=blk, sub=sub, first=first, count=count
    )
    outs = [jax.ShapeDtypeStruct((count * blk, 3 * cols), bf16)]
    out_specs = [pl.BlockSpec((blk, 3 * cols), lambda s, m: (count - 1 - s, 0))]
    if first:
        outs += [jax.ShapeDtypeStruct((first * blk, cols), f32)] * 2
        out_specs += [full_spec((first * blk, cols))] * 2
        inner = lambda *r: body(*r[:13], None, None, *r[13:])
    else:
        ins += carry
        in_specs += [full_spec((top, cols))] * 2
        inner = lambda *r: body(*r[:16], None, None, *r[16:])
    outs.append(jax.ShapeDtypeStruct((8, cols), f32))
    out_specs.append(full_spec((8, cols)))
    return pl.pallas_call(
        inner,
        grid_spec=pltpu.PrefetchScalarGridSpec(
            num_scalar_prefetch=1,
            grid=(count,),
            in_specs=in_specs,
            out_specs=out_specs,
            scratch_shapes=[
                pltpu.VMEM((blk, cols), f32),
                pltpu.VMEM((top, cols), f32),
                pltpu.VMEM((top, cols), f32),
                pltpu.VMEM((16, blk), f32),
                pltpu.VMEM((blk, cols), bf16),
            ],
        ),
        out_shape=outs,
        compiler_params=params(56),
    )(is_long, *ins)


def row_norm(value):
    return lax.rsqrt(jnp.mean(value * value, axis=1, keepdims=True) + layer_eps)


def norm_back(scale, result, grad):
    return scale * (grad - result * jnp.mean(grad * result, axis=1, keepdims=True))


def pack_kernel(core_ref, up_ref, gain_ref, down_ref, out_ref, mine_ref, theirs_ref):
    half = up_ref.shape[2] // 2
    low = core_ref[0] == 0
    down = down_ref[...].astype(bf16).T
    out = out_ref[...].astype(bf16).T
    for ref, first in ((mine_ref, low), (theirs_ref, jnp.logical_not(low))):
        for c in range(2):
            gain = gain_ref[c : c + 1, :]
            ref[:, c * half : (c + 1) * half] = jnp.where(
                first, up_ref[:, c, :half] * gain[:, :half], up_ref[:, c, half:] * gain[:, half:]
            ).astype(bf16)
        ref[:, 2 * half : 3 * half] = jnp.where(first, down[:, :half], down[:, half:])
        ref[:, 3 * half :] = out


def pack(core, w_up, gain, w_down, w_out):
    span, _, hid = w_up.shape
    cols = w_out.shape[0]
    vmem = pl.BlockSpec(memory_space=pltpu.VMEM)
    return pl.pallas_call(
        pack_kernel,
        in_specs=[pl.BlockSpec(memory_space=pltpu.SMEM)] + [vmem] * 4,
        out_specs=[vmem] * 2,
        out_shape=[jax.ShapeDtypeStruct((span, 3 * hid // 2 + cols), bf16)] * 2,
        compiler_params=params(16),
    )(core, w_up, gain, w_down, w_out)


def place_of(r, chip, chunk):
    return pl.ds(pl.multiple_of((r ^ chip) * chunk, chunk), chunk)


def put_relative(ref, chip, chips, fast):
    if not fast:
        return ref[...]
    if len(ref.shape) == 3:
        return jnp.concatenate([ref[r ^ chip] for r in range(chips)], axis=1)
    chunk = ref.shape[1] // chips
    return jnp.concatenate([ref[:, place_of(r, chip, chunk)] for r in range(chips)], axis=1)


def put_natural(ref, value, chip, chips, fast):
    if not fast:
        ref[...] = value
        return
    chunk = value.shape[1] // chips
    for r in range(chips):
        part = value[:, r * chunk : (r + 1) * chunk]
        if len(ref.shape) == 3:
            ref[r ^ chip] = part
        else:
            ref[:, place_of(r, chip, chunk)] = part


def attn_out_kernel(place_ref, *refs, counts, chips, fast):
    total = sum(counts)
    flat, refs = refs[:total], refs[total:]
    ya_ref, yb_ref, x_ref, alpha_ref, ha_ref, h1_ref, hb_ref, stat_ref, all_ref, half_ref, acc = refs
    z, chip, low = place_ref[0], place_ref[1], place_ref[2] == 0
    parts = len(counts)
    early = pl.program_id(0) == 0
    index = 0
    for n in range(parts):
        at = lax.rem(z + parts - n, parts)
        y = jnp.where(early, ya_ref[at], yb_ref[at])
        hc = y.shape[1] // 2
        all_ref[at] = y
        half_ref[at] = jnp.where(low, y[:, hc:], y[:, :hc])
        column = 0
        for piece in flat[index : index + counts[n]]:
            part = slice(column, column + piece.shape[0])
            if n == 0:
                acc[:, part] = dot_t(y, piece[...])
            else:
                acc[:, part] += dot_t(y, piece[...])
            column += piece.shape[0]
        index += counts[n]
    total = acc[...]
    norm = row_norm(total)
    hidden = total * norm
    start = put_relative(x_ref, chip, chips, fast).astype(f32)
    mixed = start + alpha_ref[...] * (hidden - start)
    first_norm = row_norm(mixed)
    out = mixed * first_norm
    ha_ref[...] = hidden
    h1_ref[...] = out
    hb_ref[...] = out.astype(bf16)
    lane = lax.broadcasted_iota(jnp.int32, stat_ref.shape, 1)
    stat_ref[...] = jnp.where(lane == 0, norm, first_norm)


def own_rows(blk, parts, width, fast):
    if fast:
        return pl.BlockSpec((blk, width), lambda i, s: (i * parts + s[0], 0))
    return pl.BlockSpec((blk, width), lambda i, s: (i, 0))


def out_weights(slots, cols):
    flat = [p for slot in slots for p in slot]
    last = flat[0].shape[1] // cols - 1
    return flat, [pl.BlockSpec((p.shape[0], cols), lambda i, s: (0, last)) for p in flat]


def attn_out(place, ya, yb, slots, x, alpha, chips, fast):
    parts, blk, cols = ya.shape
    width = x.shape[1]
    rows = 2 * blk
    row = lambda n: pl.BlockSpec((blk, n), lambda i, s: (i, 0))
    flat, specs = out_weights(slots, cols)
    return pl.pallas_call(
        functools.partial(attn_out_kernel, counts=[len(t) for t in slots], chips=chips, fast=fast),
        grid_spec=pltpu.PrefetchScalarGridSpec(
            num_scalar_prefetch=1,
            grid=(2,),
            in_specs=specs
            + [full_spec(ya.shape)] * 2
            + [own_rows(blk, parts, width, fast), full_spec((1, width))],
            out_specs=[row(width)] * 3
            + [row(128)]
            + [pl.BlockSpec((parts, blk, n), lambda i, s: (0, i, 0)) for n in (cols, cols // 2)],
            scratch_shapes=[pltpu.VMEM((blk, width), f32)],
        ),
        out_shape=[jax.ShapeDtypeStruct((rows, width), d) for d in (f32, f32, bf16)]
        + [jax.ShapeDtypeStruct((rows, 128), f32)]
        + [jax.ShapeDtypeStruct((parts, rows, n), bf16) for n in (cols, cols // 2)],
        compiler_params=params(56),
    )(place, *flat, ya, yb, x, alpha)


def loss_kernel(place_ref, own_ref, got_ref, h1_ref, cot_ref, alpha_ref, hidden_ref, dmo_ref, base_ref, ga_ref, *, chips, fast):
    chip = place_ref[1]
    total = own_ref[...] + got_ref[...].astype(f32)
    alpha = alpha_ref[...]
    norm = row_norm(total)
    inner = total * norm
    h1 = h1_ref[...]
    mixed = h1 + alpha * (inner - h1)
    last = row_norm(mixed)
    hidden = mixed * last
    grad = norm_back(last, hidden, put_relative(cot_ref, chip, chips, fast).astype(f32))
    put_natural(hidden_ref, hidden.astype(bf16), chip, chips, fast)
    base_ref[...] = (1.0 - alpha) * grad
    dmo_ref[...] = norm_back(norm, inner, alpha * grad).astype(bf16)

    @pl.when(pl.program_id(0) == 0)
    def _():
        ga_ref[...] = jnp.zeros_like(ga_ref)

    ga_ref[0:1, :] += jnp.sum(grad * (inner - h1), axis=0, keepdims=True)


def loss(place, own, got, h1, cot, alpha, chips, fast):
    rows, width = own.shape
    blk = rows // 2
    row = pl.BlockSpec((blk, width), lambda i, s: (i, 0))
    part = row
    if fast:
        part = pl.BlockSpec((chips, blk, width // chips), lambda i, s: (0, i, 0))
    return pl.pallas_call(
        functools.partial(loss_kernel, chips=chips, fast=fast),
        grid_spec=pltpu.PrefetchScalarGridSpec(
            num_scalar_prefetch=1,
            grid=(rows // blk,),
            in_specs=[row] * 3 + [part, full_spec((1, width))],
            out_specs=[part] + [row] * 2 + [full_spec((8, width))],
        ),
        out_shape=[jax.ShapeDtypeStruct(cot.shape, bf16)]
        + [jax.ShapeDtypeStruct((rows, width), d) for d in (bf16, f32)]
        + [jax.ShapeDtypeStruct((8, width), f32)],
        compiler_params=params(56),
    )(place, own, got, h1, cot, alpha)


def first_back_kernel(place_ref, *refs, counts, chips, fast):
    total = sum(counts)
    flat, refs = refs[:total], refs[total:]
    own_ref, got_ref, base_ref, h1_ref, ha_ref, x_ref, stat_ref, alpha_ref = refs[:8]
    do_ref, through_ref, ga_ref, dy_ref = refs[8:]
    z, chip = place_ref[0], place_ref[1]
    alpha = alpha_ref[...]
    grad = base_ref[...] + own_ref[...] + got_ref[...].astype(f32)
    grad = norm_back(stat_ref[:, 1:2], h1_ref[...], grad)
    ha = ha_ref[...]
    put_natural(through_ref, ((1.0 - alpha) * grad).astype(bf16), chip, chips, fast)
    back = norm_back(stat_ref[:, 0:1], ha, alpha * grad).astype(bf16)
    do_ref[...] = back
    parts = len(counts)
    step = pl.program_id(0)
    index = 0
    for n in range(parts):
        at = lax.rem(z + parts - n, parts)
        part = jnp.zeros(dy_ref.shape[1:], f32)
        column = 0
        for piece in flat[index : index + counts[n]]:
            part += dot(back[:, column : column + piece.shape[0]], piece[...])
            column += piece.shape[0]
        index += counts[n]
        dy_ref[at] = part.astype(bf16)

    @pl.when(step == 0)
    def _():
        ga_ref[...] = jnp.zeros_like(ga_ref)

    start = put_relative(x_ref, chip, chips, fast).astype(f32)
    ga_ref[0:1, :] += jnp.sum(grad * (ha - start), axis=0, keepdims=True)


def first_back(place, own, got, base, h1, ha, x, stat, alpha, slots, chips, fast, cols):
    rows, width = own.shape
    parts = len(slots)
    blk = rows // 2
    row = lambda n: pl.BlockSpec((blk, n), lambda i, s: (i, 0))
    flat, specs = out_weights(slots, cols)
    return pl.pallas_call(
        functools.partial(first_back_kernel, counts=[len(t) for t in slots], chips=chips, fast=fast),
        grid_spec=pltpu.PrefetchScalarGridSpec(
            num_scalar_prefetch=1,
            grid=(2,),
            in_specs=specs
            + [row(width)] * 5
            + [own_rows(blk, parts, width, fast), row(128), full_spec((1, width))],
            out_specs=[row(width)] * 2
            + [full_spec((8, width)), pl.BlockSpec((parts, blk, cols), lambda i, s: (0, i, 0))],
        ),
        out_shape=[jax.ShapeDtypeStruct((rows, width), bf16)] * 2
        + [
            jax.ShapeDtypeStruct((8, width), f32),
            jax.ShapeDtypeStruct((parts, rows, cols), bf16),
        ],
        compiler_params=params(56),
    )(place, *flat, own, got, base, h1, ha, x, stat, alpha)


def fetch_weights(q, slots, wbuf, sems):
    def copies(j):
        at = 0
        found = []
        for p, piece in enumerate(slots[j]):
            size = piece.shape[0]
            found.append(
                pltpu.make_async_copy(
                    piece.at[:, : wbuf.shape[2]], wbuf.at[j % 2, at : at + size, :], sems.at[j % 2, p]
                )
            )
            at += size
        return found

    for j in range(len(slots)):

        @pl.when(q == j)
        def _(j=j):
            if j == 0:
                for copy in copies(0):
                    copy.start()
            if j + 1 < len(slots):
                for copy in copies(j + 1):
                    copy.start()
            for copy in copies(j):
                copy.wait()


def mlp_fwd_kernel(*refs, half, counts):
    total = sum(counts)
    flat, refs = refs[:total], refs[total:]
    slots, at = [], 0
    for n in counts:
        slots.append(flat[at : at + n])
        at += n
    ha_ref, hb_ref, act_ref, uv_ref, own_ref, got_ref, acc, wbuf, sems = refs
    rows = ha_ref.shape[0]
    q = pl.program_id(0)

    @pl.when(q == 0)
    def _():
        own_ref[...] = jnp.zeros_like(own_ref)
        acc[...] = jnp.zeros_like(acc)

    fetch_weights(q, slots, wbuf, sems)
    w = wbuf.at[lax.rem(q, 2)]
    for base, h_ref, sum_ref in ((0, ha_ref, own_ref), (rows, hb_ref, acc)):
        at = slice(base, base + rows)
        pair = dot(h_ref[...], w[:, : 2 * half])
        lifted = pair[:, :half]
        gated = pair[:, half:]
        act = (lifted * gated * jax.nn.sigmoid(gated)).astype(bf16)
        uv_ref[at, :] = pair.astype(bf16)
        act_ref[at, :] = act
        sum_ref[...] += dot_t(act, w[:, 2 * half : 3 * half])

    @pl.when(q == pl.num_programs(0) - 1)
    def _():
        got_ref[...] = acc[...].astype(bf16)


def mlp_fwd(ha, hb, slots, half):
    rows, width = ha.shape
    parts = len(slots)
    take = lambda n: pl.BlockSpec((None, 2 * rows, n), lambda q: (q, 0, 0))
    whole = full_spec((rows, width))
    anywhere = pl.BlockSpec(memory_space=pl.ANY)
    flat = [p for slot in slots for p in slot]
    return pl.pallas_call(
        functools.partial(mlp_fwd_kernel, half=half, counts=[len(s) for s in slots]),
        grid=(parts,),
        in_specs=[anywhere] * len(flat)
        + [whole, whole],
        out_specs=[take(half), take(2 * half), whole, whole],
        out_shape=[
            jax.ShapeDtypeStruct((parts, 2 * rows, half), bf16),
            jax.ShapeDtypeStruct((parts, 2 * rows, 2 * half), bf16),
            jax.ShapeDtypeStruct((rows, width), f32),
            jax.ShapeDtypeStruct((rows, width), bf16),
        ],
        scratch_shapes=[
            pltpu.VMEM((rows, width), f32),
            pltpu.VMEM((2, width, 3 * half), bf16),
            pltpu.SemaphoreType.DMA((2, max(len(s) for s in slots))),
        ],
        compiler_params=params(56),
    )(*flat, ha, hb)


def mlp_bwd_kernel(*refs, half, counts):
    total = sum(counts)
    flat, refs = refs[:total], refs[total:]
    slots, at = [], 0
    for n in counts:
        slots.append(flat[at : at + n])
        at += n
    da_ref, db_ref, uv_ref, duv_ref, own_ref, got_ref, gs_ref, acc, wbuf, sems = refs
    rows = da_ref.shape[0]
    q = pl.program_id(0)

    @pl.when(q == 0)
    def _():
        own_ref[...] = jnp.zeros_like(own_ref)
        acc[...] = jnp.zeros_like(acc)

    gs_ref[...] = jnp.zeros_like(gs_ref)
    fetch_weights(q, slots, wbuf, sems)
    w = wbuf.at[lax.rem(q, 2)]
    for base, d_ref, sum_ref in ((0, da_ref, own_ref), (rows, db_ref, acc)):
        at = slice(base, base + rows)
        grad = dot(d_ref[...], w[:, 2 * half : 3 * half])
        lifted = uv_ref[at, :half].astype(f32)
        gated = uv_ref[at, half:].astype(f32)
        sigma = jax.nn.sigmoid(gated)
        da = grad * gated * sigma
        db = grad * lifted * sigma * (1.0 + gated * (1.0 - sigma))
        gs_ref[0:1, :] += jnp.sum(da * lifted, axis=0, keepdims=True)
        gs_ref[1:2, :] += jnp.sum(db * gated, axis=0, keepdims=True)
        duv_ref[at, :half] = da.astype(bf16)
        duv_ref[at, half:] = db.astype(bf16)
        sum_ref[...] += dot_t(duv_ref[at, :], w[:, : 2 * half])

    @pl.when(q == pl.num_programs(0) - 1)
    def _():
        got_ref[...] = acc[...].astype(bf16)


def mlp_bwd(da, db, slots, uv, half):
    rows, width = da.shape
    parts = len(slots)
    take = lambda n: pl.BlockSpec((None, 2 * rows, n), lambda q: (q, 0, 0))
    whole = full_spec((rows, width))
    anywhere = pl.BlockSpec(memory_space=pl.ANY)
    flat = [p for slot in slots for p in slot]
    return pl.pallas_call(
        functools.partial(mlp_bwd_kernel, half=half, counts=[len(s) for s in slots]),
        grid=(parts,),
        in_specs=[anywhere] * len(flat)
        + [
            whole,
            whole,
            take(2 * half),
        ],
        out_specs=[
            take(2 * half),
            whole,
            whole,
            pl.BlockSpec((None, 8, half), lambda q: (q, 0, 0)),
        ],
        out_shape=[
            jax.ShapeDtypeStruct((parts, 2 * rows, 2 * half), bf16),
            jax.ShapeDtypeStruct((rows, width), f32),
            jax.ShapeDtypeStruct((rows, width), bf16),
            jax.ShapeDtypeStruct((parts, 8, half), f32),
        ],
        scratch_shapes=[
            pltpu.VMEM((rows, width), f32),
            pltpu.VMEM((2, width, 3 * half), bf16),
            pltpu.SemaphoreType.DMA((2, max(len(s) for s in slots))),
        ],
        compiler_params=params(56),
    )(*flat, da, db, uv)


EXTRA = 16


def grad_kernel(place_ref, *refs, orders, parts, chunk, more):
    ha_ref, hb_ref = refs[:2]
    refs = refs[2:]
    if more:
        oa_ref, ob_ref, ya_ref, yb_ref, gs_ref, g1_ref, g2_ref = refs[:7]
        refs = refs[7:]
    val_ref, *outs = refs[:5]
    turned = refs[5]
    rows = ha_ref.shape[0]
    k = pl.program_id(0)

    @pl.when(k == 0)
    def _():
        turned[:, :rows] = ha_ref[...].T
        turned[:, rows:] = hb_ref[...].T
        if more:
            refs[6][:, :rows] = oa_ref[...].T
            refs[6][:, rows:] = ob_ref[...].T

    if more:
        size = outs[0].shape[2]
        fill = lambda row: jnp.concatenate([row, jnp.zeros((1, size - row.shape[1]), f32)], axis=1)
        line = lax.broadcasted_iota(jnp.int32, (EXTRA, size), 0)
        units = fill(jnp.concatenate([gs_ref[0:1, :], gs_ref[1:2, :]], axis=1))
        steps = fill(jnp.concatenate([g1_ref[0:1, :], g2_ref[0:1, :]], axis=1))
        extra = jnp.where(line == 0, units, jnp.where(line == 1, steps, 0.0)).astype(bf16)

    for side in range(2):

        @pl.when((k < parts // 2) == (side == 0))
        def _(side=side):
            for which, ref in zip(orders[side], outs[2 * side : 2 * side + 2]):
                for j, r in enumerate(which):
                    at = slice(r * chunk, (r + 1) * chunk)
                    value = dot(turned[at, :], val_ref[...]).astype(bf16)
                    size = value.shape[1]
                    ref[j, :chunk, :size] = value
                    if more:
                        ref[j, :chunk, size:] = (
                            dot(refs[6][at, :rows], ya_ref[...]) + dot(refs[6][at, rows:], yb_ref[...])
                        ).astype(bf16)
                        ref[j, chunk:, :] = extra


def weight_grads(place, sends, keeps, chips, hs, value, os=None, ys=None, extra=None):
    rows, width = hs[0].shape
    chunk = width // chips
    parts, _, size = value.shape
    more = os is not None
    hc = ys[1].shape[2] if more else 0
    tall = chunk + (EXTRA if more else 0)
    middle = parts // 2
    if chunk % 128:
        result = []
        for which, lo in ((sends[0], 0), (keeps[0], 0), (sends[1], middle), (keeps[1], middle)):
            cut = lambda pair: jnp.concatenate(
                [jnp.concatenate(pair, axis=0)[:, r * chunk : (r + 1) * chunk] for r in which], axis=1
            )
            found = []
            for k in range(lo, lo + middle):
                one = t_dot(cut(hs), value[k])
                if more:
                    at = (place[0] - k) % parts
                    y = lax.dynamic_index_in_dim(ys[0], at, 0, keepdims=False)
                    y = lax.dynamic_slice_in_dim(y, place[2] * hc, hc, 1)
                    y = jnp.concatenate([y, lax.dynamic_index_in_dim(ys[1], at, 0, keepdims=False)])
                    one = jnp.concatenate([one, t_dot(cut(os), y)], axis=1)
                one = one.reshape(len(which), chunk, size + hc)
                if more:
                    wide = jnp.broadcast_to(extra[k][None], (len(which), EXTRA, size + hc))
                    one = jnp.concatenate([one, wide], axis=1)
                found.append(one.astype(bf16))
            result.append(jnp.stack(found, axis=1))
        return [result[0], result[2]], [result[1], result[3]]
    whole = full_spec((rows, width))
    ins = list(hs)
    in_specs = [whole] * 2
    scratch = [pltpu.VMEM((width, 2 * rows), bf16)]
    if more:
        slot = lambda k, p: lax.rem(p[0] + parts - k, parts)
        cols = ys[0].shape[2]
        part = pl.BlockSpec((8, cols), lambda k, p: (0, slot(k, p) ^ p[1]))
        ins += [*os, ys[0], ys[1], *extra]
        in_specs += [whole] * 2
        in_specs += [
            pl.BlockSpec((None, rows, hc), lambda k, p: (slot(k, p), 0, p[2])),
            pl.BlockSpec((None, rows, hc), lambda k, p: (slot(k, p), 0, 0)),
            pl.BlockSpec((None, 8, size // 2), lambda k, p: (k, 0, 0)),
            part,
            part,
        ]
        scratch = scratch * 2
    ins.append(value)
    in_specs.append(pl.BlockSpec((None, 2 * rows, size), lambda k, p: (k, 0, 0)))
    lists = [sends[0], keeps[0], sends[1], keeps[1]]
    block = lambda one: (len(one), None, tall, size + hc)
    early = lambda k, p: (0, jnp.minimum(k, middle - 1), 0, 0)
    late = lambda k, p: (0, jnp.maximum(k - middle, 0), 0, 0)
    out = pl.pallas_call(
        functools.partial(
            grad_kernel, orders=(lists[:2], lists[2:]), parts=parts, chunk=chunk, more=more
        ),
        grid_spec=pltpu.PrefetchScalarGridSpec(
            num_scalar_prefetch=1,
            grid=(parts,),
            in_specs=in_specs,
            out_specs=[
                pl.BlockSpec(block(one), early if n < 2 else late) for n, one in enumerate(lists)
            ],
            scratch_shapes=scratch,
        ),
        out_shape=[
            jax.ShapeDtypeStruct((len(one), middle, tall, size + hc), bf16) for one in lists
        ],
        compiler_params=params(56),
    )(place, *ins)
    return [out[0], out[2]], [out[1], out[3]]


def pair_sum_kernel(ka_ref, ga_ref, kb_ref, gb_ref, a_ref, b_ref):
    a_ref[...] = (ka_ref[...].astype(f32) + ga_ref[...].astype(f32)).astype(bf16)
    b_ref[...] = (kb_ref[...].astype(f32) + gb_ref[...].astype(f32)).astype(bf16)


def pair_sums(kept, got, at):
    _, slots, tall, wide = kept[0].shape
    spec = lambda n: pl.BlockSpec((None, None, tall, wide), lambda k, n=n: (n, k, 0, 0))
    return pl.pallas_call(
        pair_sum_kernel,
        grid=(slots,),
        in_specs=[spec(at[0]), spec(at[0]), spec(at[1]), spec(at[1])],
        out_specs=[spec(0)] * 2,
        out_shape=[jax.ShapeDtypeStruct((1, slots, tall, wide), bf16)] * 2,
        compiler_params=params(56),
    )(kept[0], got[0], kept[1], got[1])


def adam_values(weight, grad, first, second):
    first_new = beta_one * first + (1.0 - beta_one) * grad
    second_new = beta_two * second + (1.0 - beta_two) * grad * grad
    moved = weight - learn_rate * (first_new / bias_one) / (
        jnp.sqrt(second_new / bias_two) + adam_eps
    )
    return first_new, second_new, moved


def lane_sums(value):
    ones = jnp.ones((8, value.shape[1]), bf16)
    high = value.astype(bf16)
    low = (value - high.astype(f32)).astype(bf16)
    return dot_t(ones, high) + dot_t(ones, low)


def adam_wide_kernel(w_ref, g_ref, m_ref, v_ref, g_out, m_out, v_out, n_out, s_out):
    cols = w_ref.shape[2]
    for c in range(w_ref.shape[1]):
        grad = g_ref[:, c * cols : (c + 1) * cols]
        first, second, moved = adam_values(w_ref[:, c, :], grad, m_ref[:, c, :], v_ref[:, c, :])
        g_out[:, c, :] = grad
        m_out[:, c, :] = first
        v_out[:, c, :] = second
        n_out[:, c, :] = moved
        s_out[c : c + 1, :] = jnp.sum(moved * moved, axis=0, keepdims=True)


def adam_wide(w, g, m, v):
    vmem = pl.BlockSpec(memory_space=pltpu.VMEM)
    return pl.pallas_call(
        adam_wide_kernel,
        in_specs=[vmem] * 4,
        out_specs=[vmem] * 5,
        out_shape=[jax.ShapeDtypeStruct(w.shape, f32)] * 4
        + [jax.ShapeDtypeStruct(w.shape[1:], f32)],
        compiler_params=params(16),
    )(w, g, m, v)


def adam_tall_kernel(w_ref, g_ref, m_ref, v_ref, g_out, m_out, v_out, n_out, s_out):
    grad = g_ref[...].T
    first, second, moved = adam_values(w_ref[...], grad, m_ref[...], v_ref[...])
    g_out[...] = grad
    m_out[...] = first
    v_out[...] = second
    n_out[...] = moved
    s_out[...] = lane_sums(moved * moved)


def adam_tall(w, g, m, v):
    vmem = pl.BlockSpec(memory_space=pltpu.VMEM)
    return pl.pallas_call(
        adam_tall_kernel,
        in_specs=[vmem] * 4,
        out_specs=[vmem] * 5,
        out_shape=[jax.ShapeDtypeStruct(w.shape, f32)] * 4
        + [jax.ShapeDtypeStruct((8, w.shape[0]), f32)],
        compiler_params=params(16),
    )(w, g, m, v)


def scale_kernel(na_ref, nb_ref, nc_ref, nd_ref, a_ref, b_ref, c_ref, d_ref, ao_ref, bo_ref, co_ref, do_ref, *, width):
    factor = lambda value: lax.rsqrt(value / width + layer_eps)
    for norm, ref, out in ((na_ref, a_ref, ao_ref), (nc_ref, c_ref, co_ref)):
        for c in range(ref.shape[1]):
            out[:, c, :] = ref[:, c, :] * factor(norm[c : c + 1, :])
    for norm, ref, out in ((nb_ref, b_ref, bo_ref), (nd_ref, d_ref, do_ref)):
        out[...] = ref[...] * factor(norm[...]).T[:, 0:1]


def scale_weights(norms, weights, width):
    vmem = pl.BlockSpec(memory_space=pltpu.VMEM)
    return pl.pallas_call(
        functools.partial(scale_kernel, width=width),
        in_specs=[vmem] * 8,
        out_specs=[vmem] * 4,
        out_shape=[jax.ShapeDtypeStruct(w.shape, f32) for w in weights],
        compiler_params=params(16),
    )(*norms, *weights)


def after(value, *others):
    return lax.optimization_barrier((value, *others))[0]


def per_device(
    layer_input,
    cotangent,
    positions,
    w_qkv,
    w_out,
    w_up,
    w_down,
    moment_qkv,
    moment_out,
    moment_up,
    moment_down,
    square_qkv,
    square_out,
    square_up,
    square_down,
    s_qk,
    alpha_attn,
    alpha_mlp,
    s_uv,
):
    nz = lax.axis_size("head")
    nb = lax.axis_size("batch")
    z = lax.axis_index("head")
    b = lax.axis_index("batch")
    core = b % 2
    chip = b // 2
    chips = nb // 2
    bits = [1 << n for n in range(int(math.log2(chips)))]
    rows, cols = layer_input.shape
    width = cols * nz
    own = rows // nz
    hid = w_down.shape[0]
    half = hid // 2
    hc = cols // 2
    heads = cols // HEAD_DIM
    span = w_qkv.shape[0]
    chunk = width // chips
    core_s = core.reshape(1).astype(jnp.int32)
    place = jnp.stack([z, chip, core]).astype(jnp.int32)
    fast = chunk == cols and chunk % 128 == 0

    def swap_batch(value, bit):
        return lax.ppermute(value, "batch", [(i, i ^ bit) for i in range(nb)])

    def swap_core(value):
        return swap_batch(value, 1)

    def swap_chip(value, bit):
        return swap_batch(value, 2 * bit)

    def onward(value, k=1):
        return lax.ppermute(value, "head", [(i, (i + k) % nz) for i in range(nz)])

    def exchange(value):
        return lax.all_to_all(value, "head", split_axis=0, concat_axis=0)

    def pick(pair, index):
        return jnp.where(index == 0, pair[0], pair[1])

    def relative(value):
        return jnp.concatenate(
            [
                lax.dynamic_slice_in_dim(value, (chip ^ r) * chunk, chunk, value.ndim - 1)
                for r in range(chips)
            ],
            axis=-1,
        )

    def spread(value):
        if chips <= 4:
            return [value] + [swap_chip(value, r) for r in range(1, chips)]
        for bit in bits:
            value = jnp.concatenate([value, swap_chip(value, bit)], axis=0)
        return [value]

    tokens = [layer_input, onward(layer_input)]
    mine, theirs = pack(core_s, w_up, s_uv, w_down, w_out)
    qkv_own = after(w_qkv, mine).reshape(span, 3 * cols).astype(bf16)
    qkv_full = lax.all_gather(qkv_own, "batch", axis=0, tiled=True)
    theirs = swap_core(theirs)
    packet = jnp.concatenate([pick((mine, theirs), core), pick((theirs, mine), core)], axis=0)
    hops = [packet, onward(packet)]
    slots = [spread(packet)]
    tokens[1], hops[1], places, alpha_attn, alpha_mlp, *last = lax.optimization_barrier(
        (tokens[1], hops[1], positions, alpha_attn, alpha_mlp, *slots[0])
    )
    slots[0] = list(last)

    freqs = jnp.exp(
        (jnp.arange(128) % (HEAD_DIM // 2)).astype(f32) * (-2.0 * math.log(10000.0) / HEAD_DIM)
    )
    phase = places.astype(f32)[:, None] * freqs[None, :]
    side = jnp.where(jnp.arange(128) % HEAD_DIM < HEAD_DIM // 2, -1.0, 1.0).astype(f32)
    cosine, sine = jnp.cos(phase), jnp.sin(phase) * side[None, :]
    lane = jnp.arange(cols) // HEAD_DIM
    ones = (lane[:, None] == lane[None, :]).astype(bf16)
    gain = s_qk.reshape(1, cols)
    is_long = (places[SHORT : SHORT + 1] != 0).astype(jnp.int32)
    attn_gain = relative(alpha_attn[None])
    mlp_gain = relative(alpha_mlp[None])

    for n in range(2, nz):
        slots.append(spread(hops[-1]))
        tokens.append(onward(tokens[-1]))
        if n < nz - 1:
            hops.append(onward(hops[-1]))
            tokens[-1], hops[-1], cosine, sine, ones, attn_gain, mlp_gain, *last = (
                lax.optimization_barrier(
                    (tokens[-1], hops[-1], cosine, sine, ones, attn_gain, mlp_gain, *slots[-1])
                )
            )
            slots[-1] = list(last)
    last_hop, tokens[-1] = lax.optimization_barrier((hops[-1], tokens[-1]))
    hops.append(onward(last_hop))

    blocks = rows // 512
    middle = blocks // 2
    tokens_full, q, k, v, rho = qkv_project(place, tokens, qkv_full, cosine, sine, gain, ones)
    y_a, logs_a = attn_fwd(is_long, q, k, v, 0, middle)
    q_b, hops[-1], *last = lax.optimization_barrier((after(q, y_a), hops[-1], *slots[-1]))
    slots[-1] = list(last)
    slots.append(spread(hops[-1]))
    y_b, logs_b = attn_fwd(is_long, q_b, k, v, middle, blocks - middle)
    y_one = exchange(y_a.reshape(nz, own // 2, cols))
    y_in, y_one = lax.optimization_barrier((y_b, y_one))
    y_two = exchange(y_in.reshape(nz, own // 2, cols))
    flat = lambda value: value.transpose(1, 0, 2).reshape(own, width)
    start = tokens_full
    if not fast:
        start = jnp.concatenate(
            [
                lax.dynamic_slice_in_dim(tokens_full, h * (rows // 2) + z * (own // 2), own // 2, 0)
                for h in range(2)
            ]
        )
        start = relative(start)
    y_one, y_two, *last = lax.optimization_barrier((y_one, y_two, *slots[-1]))
    slots[-1] = list(last)
    hA, h1, h_own, stat, y_mine, y_other = attn_out(place, y_one, y_two, slots, start, attn_gain, chips, fast)
    h_got = swap_core(h_own)
    y_got = swap_core(y_other)
    h_got, y_got = lax.optimization_barrier((h_got, y_got))
    cot = after(cotangent, h_own).reshape(2, nz, own // 2, cols).transpose(1, 0, 2, 3)
    cot = exchange(cot.reshape(nz, own, cols))

    act, uv, mo_own, mo_other = mlp_fwd(h_own, h_got, slots, half)
    mo_got = swap_core(mo_other)
    if not fast:
        cot = relative(flat(cot))
    hidden, d_own, base, ga_mlp = loss(place, mo_own, mo_got, h1, cot, mlp_gain, chips, fast)
    d_got = swap_core(d_own)
    if not fast:
        hidden = relative(hidden).reshape(own, nz, cols).transpose(1, 0, 2)
    hidden = exchange(hidden)

    orders = [bits, bits[::-1]]
    sent_at = [[r for r in range(chips) if r & order[0]] for order in orders]
    kept_at = [[r for r in range(chips) if not r & order[0]] for order in orders]

    def second(kept, sent):
        found, sends = [], []
        if chips == 4:
            at = [[n for n, r in enumerate(left) if r & order[1]] for order, left in zip(orders, kept_at)]
            sends = pair_sums(kept, sent, [one[0] for one in at])
            for order, one, keep, got, send in zip(orders, at, kept, sent, sends):
                cut = lambda t, n=1 - one[0]: t[n : n + 1]
                found.append([cut(keep), cut(got), swap_chip(send, order[1])])
            return found, sends
        for order, left, got, keep in zip(orders, kept_at, sent, kept):
            terms = [keep, got]
            for bit in order[1:]:
                send_at = [n for n, r in enumerate(left) if r & bit]
                keep_at = [n for n, r in enumerate(left) if not r & bit]
                left = [left[n] for n in keep_at]
                cut = lambda v, at: jnp.concatenate([v[n : n + 1] for n in at], axis=0)
                send = sum(cut(t, send_at).astype(f32) for t in terms).astype(bf16)
                terms = [cut(t, keep_at) for t in terms] + [swap_chip(send, bit)]
                sends.append(send)
            found.append(terms)
        return found, sends

    def slot_sums(found):
        return [sum(t[0, n].astype(f32) for t in terms) for terms in found for n in range(nz // 2)]

    def wait_last(found, *others):
        return [terms[:-1] + [after(terms[-1], *others)] for terms in found]

    down_made, down_kept = weight_grads(place, sent_at, kept_at, chips, (d_own, d_got), act)
    down_sent = [swap_chip(one, order[0]) for one, order in zip(down_made, orders)]
    d_own, d_got, *_ = lax.optimization_barrier((d_own, d_got, *down_made))
    duv, dh_own, dh_other, gsuv = mlp_bwd(d_own, d_got, slots, uv, half)
    dh_got = swap_core(dh_other)
    down_sent = [after(one, dh_other) for one in down_sent]
    down_part, down_next = second(down_kept, down_sent)
    dh_own, hidden, *_ = lax.optimization_barrier((dh_own, hidden, *down_next))
    do_own, through, ga_attn, dy = first_back(
        place, dh_own, dh_got, base, h1, hA, start, stat, attn_gain, slots, chips, fast, cols
    )
    dy = exchange(dy)
    do_got = swap_core(do_own)

    extra = (gsuv, ga_attn, ga_mlp)
    if not fast:
        alphas = [relative(ga_attn[0:1]), relative(ga_mlp[0:1])]
        extra = []
        wide = 2 * half + hc
        fill = lambda r: jnp.pad(r, ((0, 0), (0, wide - r.shape[1])))
        for n in range(nz):
            at = ((z - n) % nz) * cols
            line = [lax.dynamic_slice_in_dim(g, at, cols, 1) for g in alphas]
            lines = [gsuv[n, :2].reshape(1, 2 * half), jnp.concatenate(line, axis=1)]
            lines = jnp.concatenate([fill(r) for r in lines])
            extra.append(jnp.pad(lines, ((0, EXTRA - 2), (0, 0))))
        extra = jnp.stack(extra)
    up_made, up_kept = weight_grads(
        place, sent_at, kept_at, chips, (h_own, h_got), duv, (do_own, do_got), (y_mine, y_got), extra
    )
    down_part = wait_last(down_part, *up_kept)
    down_last = [terms[-1] for terms in down_part]
    dy, *both = lax.optimization_barrier((dy, *up_made, *down_last))
    up_made, down_last = both[: len(up_made)], both[len(up_made) :]
    down_slots = slot_sums([t[:-1] + [last] for t, last in zip(down_part, down_last)])
    down_along = [onward(down_slots[n].astype(bf16), nz - n) for n in range(1, nz)]
    up_sent = [swap_chip(one, order[0]) for one, order in zip(up_made, orders)]

    dy = dy.reshape(nz, 2, own // 2, cols)
    common = lambda y, logs: (
        is_long, q, k, v, dy, y, logs, rho, cosine, sine, gain, ones
    )
    dqkv_b, dk_part, dv_part, sqk_b = attn_bwd(
        *common(y_b, logs_b), middle, blocks - middle, None
    )

    if not fast:
        through = relative(through)

    mine_at = z * (own // 2)

    def input_part(dqkv, side):
        part = dot_t(dqkv, qkv_full).astype(bf16)
        here = lax.dynamic_slice_in_dim(part, mine_at, own // 2, 0).astype(f32)
        here = here + through[side * (own // 2) : (side + 1) * (own // 2)].astype(f32)
        return lax.dynamic_update_slice_in_dim(part, here.astype(bf16), mine_at, 0)

    part_b = jnp.einsum(
        "tn,zcn->ztc", dqkv_b, qkv_full.reshape(nz, cols, 3 * cols), preferred_element_type=f32
    ).astype(bf16)
    here = lax.dynamic_slice_in_dim(part_b, mine_at, own // 2, 1).astype(f32)
    here = here + through[own // 2 :].reshape(own // 2, nz, cols).transpose(1, 0, 2).astype(f32)
    part_b = lax.dynamic_update_slice_in_dim(part_b, here.astype(bf16), mine_at, 1)
    down_along = [after(one, dqkv_b) for one in down_along]
    up_part, up_next = second(up_kept, [after(one, dqkv_b) for one in up_sent])
    part_got = exchange(part_b)
    dk_part, *_ = lax.optimization_barrier((dk_part, *up_next, part_b, *down_along))
    dqkv_a, sqk_a = attn_bwd(*common(y_a, logs_a), 0, middle, [dk_part, dv_part])
    input_b = jnp.sum(after(part_got, dqkv_a).astype(f32), axis=0)
    up_part = wait_last(up_part, dqkv_a, *[terms[-1] for terms in up_part])
    part_a = input_part(dqkv_a, 0)
    up_slots = slot_sums(up_part)
    passed = up_slots[1].astype(bf16)
    part_a, passed = lax.optimization_barrier((part_a, passed))
    dqkv_late = after(dqkv_a, passed)
    passed = onward(passed)
    for n in range(2, nz):
        if n == nz - 1:
            passed, part_a = lax.optimization_barrier((passed, part_a))
        passed = onward((up_slots[n] + passed.astype(f32)).astype(bf16))
    sum_up_t = up_slots[0] + passed.astype(f32)
    input_a = lax.psum_scatter(part_a, "head", scatter_dimension=1, tiled=True)
    input_grad = jnp.concatenate([input_a.astype(f32), input_b], axis=0)
    hidden_t = after(hidden, part_a).reshape(nz, 2, own // 2, cols).transpose(1, 0, 2, 3).reshape(rows, cols)

    dqkv = jnp.concatenate([dqkv_late, dqkv_b], axis=0)
    grad_qkv = t_dot(tokens_full, dqkv).astype(bf16)
    sqk = jnp.pad((sqk_a + sqk_b), ((0, EXTRA - 8), (0, 2 * cols)))
    shard = [lax.dynamic_slice_in_dim(grad_qkv, (b ^ r) * span, span, 0) for r in range(nb)]
    shard = [jnp.concatenate([s, sqk.astype(bf16)], axis=0) for s in shard]
    qbits = [1 << n for n in range(int(math.log2(nb)))]
    held = {r: shard[r] for r in range(nb)}
    for bit in qbits:
        send_at = [r for r in held if r & bit]
        send = jnp.concatenate([held[r] for r in send_at], axis=0).astype(bf16)
        got = swap_batch(send, bit)
        size = span + EXTRA
        held = {
            r ^ bit: held[r ^ bit].astype(f32) + got[n * size : (n + 1) * size].astype(f32)
            for n, r in enumerate(send_at)
        }
    cell = width // (nz * nb)
    sum_sqk = lax.dynamic_slice_in_dim(held[0][span, :cols], b * cell, cell, 0)
    w_late, m_late, v_late, _ = lax.optimization_barrier((w_qkv, moment_qkv, square_qkv, part_a))
    qkv_new = adam_wide(w_late, held[0][:span], m_late, v_late)

    def both_halves(total):
        two = (total[:span], total[span : 2 * span])
        here = jnp.concatenate([pick(two, core), total[2 * span :]], axis=0)
        there = jnp.concatenate([pick(two, 1 - core), total[2 * span :]], axis=0)
        there = swap_core(there.astype(bf16)).astype(f32)
        return [pick((here, there), core), pick((there, here), core)]

    join = lambda halves, at, size: [p[:span, at : at + size] for p in halves]
    down_along = [after(one, part_a) for one in down_along]
    halves = both_halves(down_slots[0] + sum(one.astype(f32) for one in down_along))
    down_new = adam_tall(w_down, jnp.concatenate(join(halves, 0, half), axis=1), moment_down, square_down)
    halves = both_halves(sum_up_t)
    grad_up = jnp.concatenate(join(halves, 0, half) + join(halves, half, half), axis=1)
    grad_up = grad_up * s_uv.reshape(1, 2 * hid)
    up_new = adam_wide(w_up, grad_up, moment_up, square_up)
    out_new = adam_tall(w_out, jnp.concatenate(join(halves, 2 * half, hc), axis=1), moment_out, square_out)
    suv_rows = jnp.stack(
        [jnp.concatenate([p[span, c * half : (c + 1) * half] for p in halves]) for c in range(2)]
    )
    suv_rows = suv_rows / s_uv
    sum_suv = lax.dynamic_slice_in_dim(suv_rows, b * (hid // nb), hid // nb, 1)
    alphas = halves[0][span + 1] + halves[1][span + 1]
    sum_attn = lax.dynamic_slice_in_dim(alphas[:cols], b * cell, cell, 0)
    sum_mlp = lax.dynamic_slice_in_dim(alphas[cols : 2 * cols], b * cell, cell, 0)

    hidden = hidden_t.astype(f32)

    squares = [qkv_new[4], out_new[4][:1], up_new[4], down_new[4][:1]]
    sizes = [t.size for t in squares]
    norms = jnp.concatenate([t.reshape(-1) for t in squares]).reshape(-1, 128)
    for bit in qbits:
        norms = norms + swap_batch(norms, bit)
    norms = norms.reshape(-1)
    ends = [0] + [sum(sizes[: n + 1]) for n in range(4)]
    back = lambda n, shape: norms[ends[n] : ends[n + 1]].reshape(shape)
    eight = lambda value: jnp.broadcast_to(value, (8, value.shape[1]))
    new_qkv, new_out, new_up, new_down = scale_weights(
        [back(0, (3, cols)), eight(back(1, (1, cols))), back(2, (2, hid)), eight(back(3, (1, hid)))],
        [qkv_new[3], out_new[3], up_new[3], down_new[3]],
        width,
    )
    sum_qkv, first_a, second_a = qkv_new[:3]
    sum_out, first_b, second_b = out_new[:3]
    sum_up, first_c, second_c = up_new[:3]
    sum_down, first_d, second_d = down_new[:3]
    return (
        hidden,
        input_grad,
        sum_qkv,
        sum_out,
        sum_up,
        sum_down,
        first_a,
        first_b,
        first_c,
        first_d,
        second_a,
        second_b,
        second_c,
        second_d,
        new_qkv,
        new_out,
        new_up,
        new_down,
        sum_sqk,
        sum_attn,
        sum_mlp,
        sum_suv,
    )


def solution(mesh):
    tokens = P("batch", "head")
    wide = P("batch", None, "head")
    tall = P("head", "batch")
    flat = P(("head", "batch"))
    weights = (wide, tall, wide, tall)
    return jax.shard_map(
        per_device,
        mesh=mesh,
        in_specs=(tokens, tokens, P("batch"))
        + weights * 3
        + (P("head"), P(), P(), P(None, "head")),
        out_specs=(tokens, tokens) + weights * 4 + (flat, flat, flat, P(None, ("head", "batch"))),
        check_vma=False,
    )
```

```python
import functools
import math

import jax
import jax.numpy as jnp
from jax import lax
from jax.experimental import pallas as pl
from jax.experimental.pallas import tpu as pltpu
from jax.sharding import PartitionSpec as P

HEAD_DIM = 64
SHORT = 1024

layer_eps = 1e-06
learn_rate = 0.008
beta_one = 0.9
beta_two = 0.95
adam_eps = 1e-08
bias_one = 1.0 - math.exp(100.0 * math.log(0.9))
bias_two = 1.0 - math.exp(100.0 * math.log(0.95))
score_scale = 8.0
LOG2E = math.log2(math.e)
LN2 = math.log(2.0)

bf16 = jnp.bfloat16
f32 = jnp.float32


def dot(a, b):
    return jnp.dot(a, b, preferred_element_type=f32)


def dot_t(a, b):
    return lax.dot_general(a, b, (((1,), (1,)), ((), ())), preferred_element_type=f32)


def t_dot(a, b):
    return lax.dot_general(a, b, (((0,), (0,)), ((), ())), preferred_element_type=f32)


def params(mib):
    return pltpu.CompilerParams(vmem_limit_bytes=mib * 1024 * 1024)


def full_spec(shape):
    return pl.BlockSpec(shape, lambda *_: (0,) * len(shape))


def head_sum(value, ones):
    high = value.astype(bf16)
    low = (value - high.astype(f32)).astype(bf16)
    return dot(high, ones) + dot(low, ones)


def widen(value, cols):
    return jnp.concatenate([value] * (cols // value.shape[1]), axis=1)


def swap_halves(value):
    cols = value.shape[-1]
    half = HEAD_DIM // 2
    lane = lax.broadcasted_iota(jnp.int32, value.shape, 1)
    first = (lane % HEAD_DIM) < half
    up = pltpu.roll(value, cols - half, 1)
    down = pltpu.roll(value, half, 1)
    return jnp.where(first, up, down)


def qkv_kernel(place_ref, *refs, parts):
    tokens = refs[:parts]
    w_ref, cos_ref, sin_ref, gain_ref, ones_ref, x_ref, q_ref, k_ref, v_ref, rho_ref = refs[parts:]
    cols = v_ref.shape[1]
    z = place_ref[0]
    for n in range(parts):
        at = pl.multiple_of(lax.rem(z + parts - n, parts) * cols, cols)
        x_ref[:, pl.ds(at, cols)] = tokens[n][...]
    proj = dot(x_ref[...], w_ref[...])
    cosine = widen(cos_ref[...], cols)
    sine = widen(sin_ref[...], cols)
    ones = ones_ref[...]
    gain = gain_ref[...]
    heads = cols // HEAD_DIM
    lane = lax.broadcasted_iota(jnp.int32, rho_ref.shape, 1)
    stats = jnp.zeros(rho_ref.shape, f32)
    for c, (out, scale) in enumerate(((q_ref, score_scale * LOG2E), (k_ref, 1.0))):
        part = proj[:, c * cols : (c + 1) * cols]
        rho = lax.rsqrt(head_sum(part * part, ones) + layer_eps)
        rot = part * cosine + swap_halves(part) * sine
        out[...] = (rot * rho * (gain * scale)).astype(bf16)
        for h in range(heads):
            stats = jnp.where(lane == c * heads + h, rho[:, h * HEAD_DIM : h * HEAD_DIM + 1], stats)
    rho_ref[...] = stats
    v_ref[...] = proj[:, 2 * cols :].astype(bf16)


def qkv_project(place, tokens, w, cosine, sine, gain, ones):
    rows, cols = tokens[0].shape
    parts = len(tokens)
    width = parts * cols
    blk = 512
    row = lambda n: pl.BlockSpec((blk, n), lambda i, s: (i, 0))
    return pl.pallas_call(
        functools.partial(qkv_kernel, parts=parts),
        grid_spec=pltpu.PrefetchScalarGridSpec(
            num_scalar_prefetch=1,
            grid=(rows // blk,),
            in_specs=[row(cols)] * parts
            + [full_spec((width, 3 * cols)), row(128), row(128)]
            + [full_spec((1, cols)), full_spec((cols, cols))],
            out_specs=[row(width)] + [row(cols)] * 3 + [row(128)],
        ),
        out_shape=[jax.ShapeDtypeStruct((rows, width), bf16)]
        + [jax.ShapeDtypeStruct((rows, cols), bf16)] * 3
        + [jax.ShapeDtypeStruct((rows, 128), f32)],
        compiler_params=params(56),
    )(place, *tokens, w, cosine, sine, gain, ones)


def head_masks(cols, heads):
    lane = lax.broadcasted_iota(jnp.int32, (1, cols), 1) // HEAD_DIM
    return [(lane == h) for h in range(heads)]


def masked(value, mask):
    return jnp.where(mask, value, jnp.zeros_like(value))


def attn_fwd_kernel(long_ref, q_ref, k_ref, v_ref, y_ref, l_ref, acc, mass, *, heads, blk, sub, first):
    i = first + pl.program_id(0)
    cols = q_ref.shape[1]
    masks = head_masks(cols, heads)
    per = SHORT // blk
    low = jnp.where(long_ref[0] != 0, 0, (i // per) * per)
    acc[...] = jnp.zeros_like(acc)
    mass[...] = jnp.zeros_like(mass)

    def lanes(p):
        total = p[:, 0:128]
        for n in range(1, p.shape[1] // 128):
            total = total + p[:, n * 128 : (n + 1) * 128]
        return total

    def body(j, carry):
        start = pl.multiple_of(j * blk, blk)
        keys = k_ref[pl.ds(start, blk), :]
        vals = v_ref[pl.ds(start, blk), :]
        q = q_ref[...]
        total = jnp.zeros(acc.shape, f32)
        for h in range(heads):
            p = jnp.exp2(dot_t(masked(q, masks[h]), keys))
            mass[h] += lanes(p)
            total += dot(p.astype(bf16), masked(vals, masks[h]))
        acc[...] += total
        return carry

    lax.fori_loop(low, i, body, 0)
    start = pl.multiple_of(i * blk, blk)
    causal = lax.broadcasted_iota(jnp.int32, (sub, sub), 0) >= lax.broadcasted_iota(
        jnp.int32, (sub, sub), 1
    )
    for a in range(blk // sub):
        rows = slice(a * sub, (a + 1) * sub)
        q = q_ref[rows, :]
        for b in range(a + 1):
            at = pl.multiple_of(start + b * sub, sub)
            keys = k_ref[pl.ds(at, sub), :]
            vals = v_ref[pl.ds(at, sub), :]
            total = jnp.zeros((sub, cols), f32)
            for h in range(heads):
                p = jnp.exp2(dot_t(masked(q, masks[h]), keys))
                if a == b:
                    p = jnp.where(causal, p, 0.0)
                mass[h, rows, :] += lanes(p)
                total += dot(p.astype(bf16), masked(vals, masks[h]))
            acc[rows, :] += total
    inverse = jnp.zeros(acc.shape, f32)
    logs = jnp.zeros(l_ref.shape, f32)
    lane = lax.broadcasted_iota(jnp.int32, l_ref.shape, 1)
    for h in range(heads):
        column = jnp.sum(mass[h], axis=1, keepdims=True)
        inverse = jnp.where(masks[h], 1.0 / column, inverse)
        logs = jnp.where(lane == h, jnp.log2(column), logs)
    y_ref[...] = (acc[...] * inverse).astype(bf16)
    l_ref[...] = logs


def attn_fwd(is_long, q, k, v, first, count):
    rows, cols = q.shape
    heads = cols // HEAD_DIM
    blk, sub = 512, 256
    row = lambda n: pl.BlockSpec((blk, n), lambda i, s: (i, 0))
    whole = pl.BlockSpec(((first + count) * blk, cols), lambda i, s: (0, 0))
    return pl.pallas_call(
        functools.partial(attn_fwd_kernel, heads=heads, blk=blk, sub=sub, first=first),
        grid_spec=pltpu.PrefetchScalarGridSpec(
            num_scalar_prefetch=1,
            grid=(count,),
            in_specs=[pl.BlockSpec((blk, cols), lambda i, s: (first + i, 0)), whole, whole],
            out_specs=[row(cols), row(128)],
            scratch_shapes=[pltpu.VMEM((blk, cols), f32), pltpu.VMEM((heads, blk, 128), f32)],
        ),
        out_shape=[
            jax.ShapeDtypeStruct((count * blk, cols), bf16),
            jax.ShapeDtypeStruct((count * blk, 128), f32),
        ],
        compiler_params=params(56),
    )(is_long, q, k, v)


def attn_bwd_kernel(
    long_ref, q_ref, qk_ref, dy_ref, y_ref, l_ref, k_ref, v_ref, rho_ref, cos_ref, sin_ref, gain_ref,
    ones_ref, dk_in, dv_in, out_ref, dk_out, dv_out, s_ref, acc, dk_acc, dv_acc, stats, dys, *, heads, blk, sub, first, count
):
    step = pl.program_id(0)
    local = count - 1 - step
    i = first + local
    cols = q_ref.shape[1]
    masks = head_masks(cols, heads)
    per = SHORT // blk
    low = jnp.where(long_ref[0] != 0, 0, (i // per) * per)
    ones = ones_ref[...]
    gain = gain_ref[...]

    @pl.when(step == 0)
    def _():
        dk_acc[...] = jnp.zeros_like(dk_acc)
        dv_acc[...] = jnp.zeros_like(dv_acc)
        s_ref[...] = jnp.zeros_like(s_ref)
        if dk_in is not None:
            dk_acc[...] = dk_in[...]
            dv_acc[...] = dv_in[...]

    acc[...] = jnp.zeros_like(acc)
    dys[...] = dy_ref[...].reshape(dys.shape)
    prod = dys[...].astype(f32) * y_ref[...].astype(f32)
    high = prod.astype(bf16)
    rest = (prod - high.astype(f32)).astype(bf16)
    pickers = (
        lax.broadcasted_iota(jnp.int32, (8, cols), 1) // HEAD_DIM
        == lax.broadcasted_iota(jnp.int32, (8, cols), 0)
    ).astype(bf16)
    stats[0:8, :] = dot_t(pickers, high) + dot_t(pickers, rest)
    stats[8:16, :] = l_ref[...].T[0:8, :]

    def piece(at, size, rows, causal):
        keys = k_ref[pl.ds(at, size), :]
        vals = v_ref[pl.ds(at, size), :]
        q = q_ref[rows, :]
        dy = dys[rows, :]
        total_q = jnp.zeros(q.shape, f32)
        total_k = jnp.zeros(keys.shape, f32)
        total_v = jnp.zeros(keys.shape, f32)
        for h in range(heads):
            qm = masked(q, masks[h])
            dym = masked(dy, masks[h])
            p = jnp.exp2(dot_t(keys, qm) - stats[8 + h : 9 + h, rows])
            if causal is not None:
                p = jnp.where(causal, p, 0.0)
            ds = (p * (dot_t(vals, dym) - stats[h : h + 1, rows])).astype(bf16)
            total_v += dot(p.astype(bf16), dym)
            total_k += dot(ds, qm)
            total_q += t_dot(ds, masked(keys, masks[h]))
        acc[rows, :] += total_q
        dk_acc[pl.ds(at, size), :] += total_k
        dv_acc[pl.ds(at, size), :] += total_v

    def body(j, carry):
        piece(pl.multiple_of(j * blk, blk), blk, slice(0, blk), None)
        return carry

    lax.fori_loop(low, i, body, 0)
    start = pl.multiple_of(i * blk, blk)
    causal = lax.broadcasted_iota(jnp.int32, (sub, sub), 0) <= lax.broadcasted_iota(
        jnp.int32, (sub, sub), 1
    )
    for a in range(blk // sub):
        for b in range(a + 1):
            piece(
                pl.multiple_of(start + b * sub, sub),
                sub,
                slice(a * sub, (a + 1) * sub),
                causal if a == b else None,
            )
    cosine = widen(cos_ref[...], cols)
    sine = widen(sin_ref[...], cols)
    total = jnp.zeros((1, cols), f32)
    here = pl.ds(start, blk)
    for c, (value, unit, up, scale) in enumerate(
        (
            (acc[...], q_ref[...], score_scale, score_scale * LOG2E),
            (dk_acc[here, :], k_ref[here, :], LN2, 1.0),
        )
    ):
        rho = jnp.zeros(value.shape, f32)
        for h in range(heads):
            at = c * heads + h
            rho = jnp.where(masks[h], rho_ref[:, at : at + 1], rho)
        grad = value * up
        unit = unit.astype(f32) * (1.0 / (gain * scale))
        total += jnp.sum(grad * unit, axis=0, keepdims=True)
        grad = grad * gain
        back = rho * (grad - unit * head_sum(grad * unit, ones))
        turned = back * cosine - swap_halves(back) * sine
        out_ref[:, c * cols : (c + 1) * cols] = turned.astype(bf16)
    out_ref[:, 2 * cols :] = dv_acc[here, :].astype(bf16)
    s_ref[0:1, :] += total
    if dk_out is not None:
        @pl.when(step == count - 1)
        def _():
            dk_out[...] = dk_acc[0 : first * blk, :]
            dv_out[...] = dv_acc[0 : first * blk, :]


def attn_bwd(is_long, q, k, v, dy, y, logs, rho, cosine, sine, gain, ones, first, count, carry):
    rows, cols = q.shape
    heads = cols // HEAD_DIM
    blk, sub = 512, 256
    top = (first + count) * blk
    at = lambda s: first + count - 1 - s
    row = lambda n: pl.BlockSpec((blk, n), lambda s, m: (at(s), 0))
    whole = pl.BlockSpec((top, cols), lambda s, m: (0, 0))
    ins = [q, k, dy, y, logs, k, v, rho, cosine, sine, gain, ones]
    mine = lambda n: pl.BlockSpec((blk, n), lambda s, m: (count - 1 - s, 0))
    share = dy.shape[2]
    half_at = 1 if first else 0
    in_specs = [row(cols)] * 2
    in_specs.append(
        pl.BlockSpec((blk // share, None, share, cols), lambda s, m: (count - 1 - s, half_at, 0, 0))
    )
    in_specs += [mine(cols), mine(128), whole, whole] + [row(128)] * 3
    in_specs += [full_spec((1, cols)), full_spec((cols, cols))]
    body = functools.partial(
        attn_bwd_kernel, heads=heads, blk=blk, sub=sub, first=first, count=count
    )
    outs = [jax.ShapeDtypeStruct((count * blk, 3 * cols), bf16)]
    out_specs = [pl.BlockSpec((blk, 3 * cols), lambda s, m: (count - 1 - s, 0))]
    if first:
        outs += [jax.ShapeDtypeStruct((first * blk, cols), f32)] * 2
        out_specs += [full_spec((first * blk, cols))] * 2
        inner = lambda *r: body(*r[:13], None, None, *r[13:])
    else:
        ins += carry
        in_specs += [full_spec((top, cols))] * 2
        inner = lambda *r: body(*r[:16], None, None, *r[16:])
    outs.append(jax.ShapeDtypeStruct((8, cols), f32))
    out_specs.append(full_spec((8, cols)))
    return pl.pallas_call(
        inner,
        grid_spec=pltpu.PrefetchScalarGridSpec(
            num_scalar_prefetch=1,
            grid=(count,),
            in_specs=in_specs,
            out_specs=out_specs,
            scratch_shapes=[
                pltpu.VMEM((blk, cols), f32),
                pltpu.VMEM((top, cols), f32),
                pltpu.VMEM((top, cols), f32),
                pltpu.VMEM((16, blk), f32),
                pltpu.VMEM((blk, cols), bf16),
            ],
        ),
        out_shape=outs,
        compiler_params=params(56),
    )(is_long, *ins)


def row_norm(value):
    return lax.rsqrt(jnp.mean(value * value, axis=1, keepdims=True) + layer_eps)


def norm_back(scale, result, grad):
    return scale * (grad - result * jnp.mean(grad * result, axis=1, keepdims=True))


def pack_kernel(core_ref, up_ref, gain_ref, down_ref, out_ref, mine_ref, theirs_ref):
    half = up_ref.shape[2] // 2
    low = core_ref[0] == 0
    down = down_ref[...].astype(bf16).T
    out = out_ref[...].astype(bf16).T
    for ref, first in ((mine_ref, low), (theirs_ref, jnp.logical_not(low))):
        for c in range(2):
            gain = gain_ref[c : c + 1, :]
            ref[:, c * half : (c + 1) * half] = jnp.where(
                first, up_ref[:, c, :half] * gain[:, :half], up_ref[:, c, half:] * gain[:, half:]
            ).astype(bf16)
        ref[:, 2 * half : 3 * half] = jnp.where(first, down[:, :half], down[:, half:])
        ref[:, 3 * half :] = out


def pack(core, w_up, gain, w_down, w_out):
    span, _, hid = w_up.shape
    cols = w_out.shape[0]
    vmem = pl.BlockSpec(memory_space=pltpu.VMEM)
    return pl.pallas_call(
        pack_kernel,
        in_specs=[pl.BlockSpec(memory_space=pltpu.SMEM)] + [vmem] * 4,
        out_specs=[vmem] * 2,
        out_shape=[jax.ShapeDtypeStruct((span, 3 * hid // 2 + cols), bf16)] * 2,
        compiler_params=params(16),
    )(core, w_up, gain, w_down, w_out)


def place_of(r, chip, chunk):
    return pl.ds(pl.multiple_of((r ^ chip) * chunk, chunk), chunk)


def put_relative(ref, chip, chips, fast):
    if not fast:
        return ref[...]
    if len(ref.shape) == 3:
        return jnp.concatenate([ref[r ^ chip] for r in range(chips)], axis=1)
    chunk = ref.shape[1] // chips
    return jnp.concatenate([ref[:, place_of(r, chip, chunk)] for r in range(chips)], axis=1)


def put_natural(ref, value, chip, chips, fast):
    if not fast:
        ref[...] = value
        return
    chunk = value.shape[1] // chips
    for r in range(chips):
        part = value[:, r * chunk : (r + 1) * chunk]
        if len(ref.shape) == 3:
            ref[r ^ chip] = part
        else:
            ref[:, place_of(r, chip, chunk)] = part


def attn_out_kernel(place_ref, *refs, counts, chips, fast):
    total = sum(counts)
    flat, refs = refs[:total], refs[total:]
    ya_ref, yb_ref, x_ref, alpha_ref, ha_ref, h1_ref, hb_ref, stat_ref, all_ref, half_ref, acc = refs
    z, chip, low = place_ref[0], place_ref[1], place_ref[2] == 0
    parts = len(counts)
    early = pl.program_id(0) == 0
    index = 0
    for n in range(parts):
        at = lax.rem(z + parts - n, parts)
        y = jnp.where(early, ya_ref[at], yb_ref[at])
        hc = y.shape[1] // 2
        all_ref[at] = y
        half_ref[at] = jnp.where(low, y[:, hc:], y[:, :hc])
        column = 0
        for piece in flat[index : index + counts[n]]:
            part = slice(column, column + piece.shape[0])
            if n == 0:
                acc[:, part] = dot_t(y, piece[...])
            else:
                acc[:, part] += dot_t(y, piece[...])
            column += piece.shape[0]
        index += counts[n]
    total = acc[...]
    norm = row_norm(total)
    hidden = total * norm
    start = put_relative(x_ref, chip, chips, fast).astype(f32)
    mixed = start + alpha_ref[...] * (hidden - start)
    first_norm = row_norm(mixed)
    out = mixed * first_norm
    ha_ref[...] = hidden
    h1_ref[...] = out
    hb_ref[...] = out.astype(bf16)
    lane = lax.broadcasted_iota(jnp.int32, stat_ref.shape, 1)
    stat_ref[...] = jnp.where(lane == 0, norm, first_norm)


def own_rows(blk, parts, width, fast):
    if fast:
        return pl.BlockSpec((blk, width), lambda i, s: (i * parts + s[0], 0))
    return pl.BlockSpec((blk, width), lambda i, s: (i, 0))


def out_weights(slots, cols):
    flat = [p for slot in slots for p in slot]
    last = flat[0].shape[1] // cols - 1
    return flat, [pl.BlockSpec((p.shape[0], cols), lambda i, s: (0, last)) for p in flat]


def attn_out(place, ya, yb, slots, x, alpha, chips, fast):
    parts, blk, cols = ya.shape
    width = x.shape[1]
    rows = 2 * blk
    row = lambda n: pl.BlockSpec((blk, n), lambda i, s: (i, 0))
    flat, specs = out_weights(slots, cols)
    return pl.pallas_call(
        functools.partial(attn_out_kernel, counts=[len(t) for t in slots], chips=chips, fast=fast),
        grid_spec=pltpu.PrefetchScalarGridSpec(
            num_scalar_prefetch=1,
            grid=(2,),
            in_specs=specs
            + [full_spec(ya.shape)] * 2
            + [own_rows(blk, parts, width, fast), full_spec((1, width))],
            out_specs=[row(width)] * 3
            + [row(128)]
            + [pl.BlockSpec((parts, blk, n), lambda i, s: (0, i, 0)) for n in (cols, cols // 2)],
            scratch_shapes=[pltpu.VMEM((blk, width), f32)],
        ),
        out_shape=[jax.ShapeDtypeStruct((rows, width), d) for d in (f32, f32, bf16)]
        + [jax.ShapeDtypeStruct((rows, 128), f32)]
        + [jax.ShapeDtypeStruct((parts, rows, n), bf16) for n in (cols, cols // 2)],
        compiler_params=params(56),
    )(place, *flat, ya, yb, x, alpha)


def loss_kernel(place_ref, own_ref, got_ref, h1_ref, cot_ref, alpha_ref, hidden_ref, dmo_ref, base_ref, ga_ref, *, chips, fast):
    chip = place_ref[1]
    total = own_ref[...] + got_ref[...].astype(f32)
    alpha = alpha_ref[...]
    norm = row_norm(total)
    inner = total * norm
    h1 = h1_ref[...]
    mixed = h1 + alpha * (inner - h1)
    last = row_norm(mixed)
    hidden = mixed * last
    grad = norm_back(last, hidden, put_relative(cot_ref, chip, chips, fast).astype(f32))
    put_natural(hidden_ref, hidden.astype(bf16), chip, chips, fast)
    base_ref[...] = (1.0 - alpha) * grad
    dmo_ref[...] = norm_back(norm, inner, alpha * grad).astype(bf16)

    @pl.when(pl.program_id(0) == 0)
    def _():
        ga_ref[...] = jnp.zeros_like(ga_ref)

    ga_ref[0:1, :] += jnp.sum(grad * (inner - h1), axis=0, keepdims=True)


def loss(place, own, got, h1, cot, alpha, chips, fast):
    rows, width = own.shape
    blk = rows // 2
    row = pl.BlockSpec((blk, width), lambda i, s: (i, 0))
    part = row
    if fast:
        part = pl.BlockSpec((chips, blk, width // chips), lambda i, s: (0, i, 0))
    return pl.pallas_call(
        functools.partial(loss_kernel, chips=chips, fast=fast),
        grid_spec=pltpu.PrefetchScalarGridSpec(
            num_scalar_prefetch=1,
            grid=(rows // blk,),
            in_specs=[row] * 3 + [part, full_spec((1, width))],
            out_specs=[part] + [row] * 2 + [full_spec((8, width))],
        ),
        out_shape=[jax.ShapeDtypeStruct(cot.shape, bf16)]
        + [jax.ShapeDtypeStruct((rows, width), d) for d in (bf16, f32)]
        + [jax.ShapeDtypeStruct((8, width), f32)],
        compiler_params=params(56),
    )(place, own, got, h1, cot, alpha)


def first_back_kernel(place_ref, *refs, counts, chips, fast):
    total = sum(counts)
    flat, refs = refs[:total], refs[total:]
    own_ref, got_ref, base_ref, h1_ref, ha_ref, x_ref, stat_ref, alpha_ref = refs[:8]
    do_ref, through_ref, ga_ref, dy_ref = refs[8:]
    z, chip = place_ref[0], place_ref[1]
    alpha = alpha_ref[...]
    grad = base_ref[...] + own_ref[...] + got_ref[...].astype(f32)
    grad = norm_back(stat_ref[:, 1:2], h1_ref[...], grad)
    ha = ha_ref[...]
    put_natural(through_ref, ((1.0 - alpha) * grad).astype(bf16), chip, chips, fast)
    back = norm_back(stat_ref[:, 0:1], ha, alpha * grad).astype(bf16)
    do_ref[...] = back
    parts = len(counts)
    step = pl.program_id(0)
    index = 0
    for n in range(parts):
        at = lax.rem(z + parts - n, parts)
        part = jnp.zeros(dy_ref.shape[1:], f32)
        column = 0
        for piece in flat[index : index + counts[n]]:
            part += dot(back[:, column : column + piece.shape[0]], piece[...])
            column += piece.shape[0]
        index += counts[n]
        dy_ref[at] = part.astype(bf16)

    @pl.when(step == 0)
    def _():
        ga_ref[...] = jnp.zeros_like(ga_ref)

    start = put_relative(x_ref, chip, chips, fast).astype(f32)
    ga_ref[0:1, :] += jnp.sum(grad * (ha - start), axis=0, keepdims=True)


def first_back(place, own, got, base, h1, ha, x, stat, alpha, slots, chips, fast, cols):
    rows, width = own.shape
    parts = len(slots)
    blk = rows // 2
    row = lambda n: pl.BlockSpec((blk, n), lambda i, s: (i, 0))
    flat, specs = out_weights(slots, cols)
    through, shape = row(width), (rows, width)
    if fast:
        through = pl.BlockSpec((parts, blk, cols), lambda i, s: (0, i, 0))
        shape = (parts, rows, cols)
    return pl.pallas_call(
        functools.partial(first_back_kernel, counts=[len(t) for t in slots], chips=chips, fast=fast),
        grid_spec=pltpu.PrefetchScalarGridSpec(
            num_scalar_prefetch=1,
            grid=(2,),
            in_specs=specs
            + [row(width)] * 5
            + [own_rows(blk, parts, width, fast), row(128), full_spec((1, width))],
            out_specs=[row(width), through]
            + [full_spec((8, width)), pl.BlockSpec((parts, blk, cols), lambda i, s: (0, i, 0))],
        ),
        out_shape=[jax.ShapeDtypeStruct((rows, width), bf16), jax.ShapeDtypeStruct(shape, bf16)]
        + [
            jax.ShapeDtypeStruct((8, width), f32),
            jax.ShapeDtypeStruct((parts, rows, cols), bf16),
        ],
        compiler_params=params(56),
    )(place, *flat, own, got, base, h1, ha, x, stat, alpha)


def fetch_weights(q, slots, wbuf, sems):
    def copies(j):
        at = 0
        found = []
        for p, piece in enumerate(slots[j]):
            size = piece.shape[0]
            found.append(
                pltpu.make_async_copy(
                    piece.at[:, : wbuf.shape[2]], wbuf.at[j % 2, at : at + size, :], sems.at[j % 2, p]
                )
            )
            at += size
        return found

    for j in range(len(slots)):

        @pl.when(q == j)
        def _(j=j):
            if j == 0:
                for copy in copies(0):
                    copy.start()
            if j + 1 < len(slots):
                for copy in copies(j + 1):
                    copy.start()
            for copy in copies(j):
                copy.wait()


def mlp_fwd_kernel(*refs, half, counts):
    total = sum(counts)
    flat, refs = refs[:total], refs[total:]
    slots, at = [], 0
    for n in counts:
        slots.append(flat[at : at + n])
        at += n
    ha_ref, hb_ref, act_ref, uv_ref, own_ref, got_ref, acc, wbuf, sems = refs
    rows = ha_ref.shape[0]
    q = pl.program_id(0)

    @pl.when(q == 0)
    def _():
        own_ref[...] = jnp.zeros_like(own_ref)
        acc[...] = jnp.zeros_like(acc)

    fetch_weights(q, slots, wbuf, sems)
    w = wbuf.at[lax.rem(q, 2)]
    for base, h_ref, sum_ref in ((0, ha_ref, own_ref), (rows, hb_ref, acc)):
        at = slice(base, base + rows)
        pair = dot(h_ref[...], w[:, : 2 * half])
        lifted = pair[:, :half]
        gated = pair[:, half:]
        act = (lifted * gated * jax.nn.sigmoid(gated)).astype(bf16)
        uv_ref[at, :] = pair.astype(bf16)
        act_ref[at, :] = act
        sum_ref[...] += dot_t(act, w[:, 2 * half : 3 * half])

    @pl.when(q == pl.num_programs(0) - 1)
    def _():
        got_ref[...] = acc[...].astype(bf16)


def mlp_fwd(ha, hb, slots, half):
    rows, width = ha.shape
    parts = len(slots)
    take = lambda n: pl.BlockSpec((None, 2 * rows, n), lambda q: (q, 0, 0))
    whole = full_spec((rows, width))
    anywhere = pl.BlockSpec(memory_space=pl.ANY)
    flat = [p for slot in slots for p in slot]
    return pl.pallas_call(
        functools.partial(mlp_fwd_kernel, half=half, counts=[len(s) for s in slots]),
        grid=(parts,),
        in_specs=[anywhere] * len(flat)
        + [whole, whole],
        out_specs=[take(half), take(2 * half), whole, whole],
        out_shape=[
            jax.ShapeDtypeStruct((parts, 2 * rows, half), bf16),
            jax.ShapeDtypeStruct((parts, 2 * rows, 2 * half), bf16),
            jax.ShapeDtypeStruct((rows, width), f32),
            jax.ShapeDtypeStruct((rows, width), bf16),
        ],
        scratch_shapes=[
            pltpu.VMEM((rows, width), f32),
            pltpu.VMEM((2, width, 3 * half), bf16),
            pltpu.SemaphoreType.DMA((2, max(len(s) for s in slots))),
        ],
        compiler_params=params(56),
    )(*flat, ha, hb)


def mlp_bwd_kernel(*refs, half, counts):
    total = sum(counts)
    flat, refs = refs[:total], refs[total:]
    slots, at = [], 0
    for n in counts:
        slots.append(flat[at : at + n])
        at += n
    da_ref, db_ref, uv_ref, duv_ref, own_ref, got_ref, gs_ref, acc, wbuf, sems = refs
    rows = da_ref.shape[0]
    q = pl.program_id(0)

    @pl.when(q == 0)
    def _():
        own_ref[...] = jnp.zeros_like(own_ref)
        acc[...] = jnp.zeros_like(acc)

    gs_ref[...] = jnp.zeros_like(gs_ref)
    fetch_weights(q, slots, wbuf, sems)
    w = wbuf.at[lax.rem(q, 2)]
    for base, d_ref, sum_ref in ((0, da_ref, own_ref), (rows, db_ref, acc)):
        at = slice(base, base + rows)
        grad = dot(d_ref[...], w[:, 2 * half : 3 * half])
        lifted = uv_ref[at, :half].astype(f32)
        gated = uv_ref[at, half:].astype(f32)
        sigma = jax.nn.sigmoid(gated)
        da = grad * gated * sigma
        db = grad * lifted * sigma * (1.0 + gated * (1.0 - sigma))
        gs_ref[0:1, :] += jnp.sum(da * lifted, axis=0, keepdims=True)
        gs_ref[1:2, :] += jnp.sum(db * gated, axis=0, keepdims=True)
        duv_ref[at, :half] = da.astype(bf16)
        duv_ref[at, half:] = db.astype(bf16)
        sum_ref[...] += dot_t(duv_ref[at, :], w[:, : 2 * half])

    @pl.when(q == pl.num_programs(0) - 1)
    def _():
        got_ref[...] = acc[...].astype(bf16)


def mlp_bwd(da, db, slots, uv, half):
    rows, width = da.shape
    parts = len(slots)
    take = lambda n: pl.BlockSpec((None, 2 * rows, n), lambda q: (q, 0, 0))
    whole = full_spec((rows, width))
    anywhere = pl.BlockSpec(memory_space=pl.ANY)
    flat = [p for slot in slots for p in slot]
    return pl.pallas_call(
        functools.partial(mlp_bwd_kernel, half=half, counts=[len(s) for s in slots]),
        grid=(parts,),
        in_specs=[anywhere] * len(flat)
        + [
            whole,
            whole,
            take(2 * half),
        ],
        out_specs=[
            take(2 * half),
            whole,
            whole,
            pl.BlockSpec((None, 8, half), lambda q: (q, 0, 0)),
        ],
        out_shape=[
            jax.ShapeDtypeStruct((parts, 2 * rows, 2 * half), bf16),
            jax.ShapeDtypeStruct((rows, width), f32),
            jax.ShapeDtypeStruct((rows, width), bf16),
            jax.ShapeDtypeStruct((parts, 8, half), f32),
        ],
        scratch_shapes=[
            pltpu.VMEM((rows, width), f32),
            pltpu.VMEM((2, width, 3 * half), bf16),
            pltpu.SemaphoreType.DMA((2, max(len(s) for s in slots))),
        ],
        compiler_params=params(56),
    )(*flat, da, db, uv)


EXTRA = 16


def grad_kernel(place_ref, *refs, orders, parts, chunk, more):
    ha_ref, hb_ref = refs[:2]
    refs = refs[2:]
    if more:
        oa_ref, ob_ref, ya_ref, yb_ref, gs_ref, g1_ref, g2_ref = refs[:7]
        refs = refs[7:]
    val_ref, *outs = refs[:5]
    turned = refs[5]
    rows = ha_ref.shape[0]
    k = pl.program_id(0)

    @pl.when(k == 0)
    def _():
        turned[:, :rows] = ha_ref[...].T
        turned[:, rows:] = hb_ref[...].T
        if more:
            refs[6][:, :rows] = oa_ref[...].T
            refs[6][:, rows:] = ob_ref[...].T

    if more:
        size = outs[0].shape[2]
        fill = lambda row: jnp.concatenate([row, jnp.zeros((1, size - row.shape[1]), f32)], axis=1)
        line = lax.broadcasted_iota(jnp.int32, (EXTRA, size), 0)
        units = fill(jnp.concatenate([gs_ref[0:1, :], gs_ref[1:2, :]], axis=1))
        steps = fill(jnp.concatenate([g1_ref[0:1, :], g2_ref[0:1, :]], axis=1))
        extra = jnp.where(line == 0, units, jnp.where(line == 1, steps, 0.0)).astype(bf16)

    for side in range(2):

        @pl.when((k < parts // 2) == (side == 0))
        def _(side=side):
            for which, ref in zip(orders[side], outs[2 * side : 2 * side + 2]):
                for j, r in enumerate(which):
                    at = slice(r * chunk, (r + 1) * chunk)
                    value = dot(turned[at, :], val_ref[...]).astype(bf16)
                    size = value.shape[1]
                    ref[j, :chunk, :size] = value
                    if more:
                        ref[j, :chunk, size:] = (
                            dot(refs[6][at, :rows], ya_ref[...]) + dot(refs[6][at, rows:], yb_ref[...])
                        ).astype(bf16)
                        ref[j, chunk:, :] = extra


def weight_grads(place, sends, keeps, chips, hs, value, os=None, ys=None, extra=None):
    rows, width = hs[0].shape
    chunk = width // chips
    parts, _, size = value.shape
    more = os is not None
    hc = ys[1].shape[2] if more else 0
    tall = chunk + (EXTRA if more else 0)
    middle = parts // 2
    if chunk % 128:
        result = []
        for which, lo in ((sends[0], 0), (keeps[0], 0), (sends[1], middle), (keeps[1], middle)):
            cut = lambda pair: jnp.concatenate(
                [jnp.concatenate(pair, axis=0)[:, r * chunk : (r + 1) * chunk] for r in which], axis=1
            )
            found = []
            for k in range(lo, lo + middle):
                one = t_dot(cut(hs), value[k])
                if more:
                    at = (place[0] - k) % parts
                    y = lax.dynamic_index_in_dim(ys[0], at, 0, keepdims=False)
                    y = lax.dynamic_slice_in_dim(y, place[2] * hc, hc, 1)
                    y = jnp.concatenate([y, lax.dynamic_index_in_dim(ys[1], at, 0, keepdims=False)])
                    one = jnp.concatenate([one, t_dot(cut(os), y)], axis=1)
                one = one.reshape(len(which), chunk, size + hc)
                if more:
                    wide = jnp.broadcast_to(extra[k][None], (len(which), EXTRA, size + hc))
                    one = jnp.concatenate([one, wide], axis=1)
                found.append(one.astype(bf16))
            result.append(jnp.stack(found, axis=1))
        return [result[0], result[2]], [result[1], result[3]]
    whole = full_spec((rows, width))
    ins = list(hs)
    in_specs = [whole] * 2
    scratch = [pltpu.VMEM((width, 2 * rows), bf16)]
    if more:
        slot = lambda k, p: lax.rem(p[0] + parts - k, parts)
        cols = ys[0].shape[2]
        part = pl.BlockSpec((8, cols), lambda k, p: (0, slot(k, p) ^ p[1]))
        ins += [*os, ys[0], ys[1], *extra]
        in_specs += [whole] * 2
        in_specs += [
            pl.BlockSpec((None, rows, hc), lambda k, p: (slot(k, p), 0, p[2])),
            pl.BlockSpec((None, rows, hc), lambda k, p: (slot(k, p), 0, 0)),
            pl.BlockSpec((None, 8, size // 2), lambda k, p: (k, 0, 0)),
            part,
            part,
        ]
        scratch = scratch * 2
    ins.append(value)
    in_specs.append(pl.BlockSpec((None, 2 * rows, size), lambda k, p: (k, 0, 0)))
    lists = [sends[0], keeps[0], sends[1], keeps[1]]
    block = lambda one: (len(one), None, tall, size + hc)
    early = lambda k, p: (0, jnp.minimum(k, middle - 1), 0, 0)
    late = lambda k, p: (0, jnp.maximum(k - middle, 0), 0, 0)
    out = pl.pallas_call(
        functools.partial(
            grad_kernel, orders=(lists[:2], lists[2:]), parts=parts, chunk=chunk, more=more
        ),
        grid_spec=pltpu.PrefetchScalarGridSpec(
            num_scalar_prefetch=1,
            grid=(parts,),
            in_specs=in_specs,
            out_specs=[
                pl.BlockSpec(block(one), early if n < 2 else late) for n, one in enumerate(lists)
            ],
            scratch_shapes=scratch,
        ),
        out_shape=[
            jax.ShapeDtypeStruct((len(one), middle, tall, size + hc), bf16) for one in lists
        ],
        compiler_params=params(56),
    )(place, *ins)
    return [out[0], out[2]], [out[1], out[3]]


def pair_sum_kernel(ka_ref, ga_ref, kb_ref, gb_ref, a_ref, b_ref):
    a_ref[...] = (ka_ref[...].astype(f32) + ga_ref[...].astype(f32)).astype(bf16)
    b_ref[...] = (kb_ref[...].astype(f32) + gb_ref[...].astype(f32)).astype(bf16)


def pair_sums(kept, got, at):
    _, slots, tall, wide = kept[0].shape
    spec = lambda n: pl.BlockSpec((None, None, tall, wide), lambda k, n=n: (n, k, 0, 0))
    return pl.pallas_call(
        pair_sum_kernel,
        grid=(slots,),
        in_specs=[spec(at[0]), spec(at[0]), spec(at[1]), spec(at[1])],
        out_specs=[spec(0)] * 2,
        out_shape=[jax.ShapeDtypeStruct((1, slots, tall, wide), bf16)] * 2,
        compiler_params=params(56),
    )(kept[0], got[0], kept[1], got[1])


def adam_values(weight, grad, first, second):
    first_new = beta_one * first + (1.0 - beta_one) * grad
    second_new = beta_two * second + (1.0 - beta_two) * grad * grad
    moved = weight - learn_rate * (first_new / bias_one) / (
        jnp.sqrt(second_new / bias_two) + adam_eps
    )
    return first_new, second_new, moved


def lane_sums(value):
    ones = jnp.ones((8, value.shape[1]), bf16)
    high = value.astype(bf16)
    low = (value - high.astype(f32)).astype(bf16)
    return dot_t(ones, high) + dot_t(ones, low)


def adam_wide_kernel(w_ref, g_ref, m_ref, v_ref, g_out, m_out, v_out, n_out, s_out):
    cols = w_ref.shape[2]
    for c in range(w_ref.shape[1]):
        grad = g_ref[:, c * cols : (c + 1) * cols]
        first, second, moved = adam_values(w_ref[:, c, :], grad, m_ref[:, c, :], v_ref[:, c, :])
        g_out[:, c, :] = grad
        m_out[:, c, :] = first
        v_out[:, c, :] = second
        n_out[:, c, :] = moved
        s_out[c : c + 1, :] = jnp.sum(moved * moved, axis=0, keepdims=True)


def adam_wide(w, g, m, v):
    vmem = pl.BlockSpec(memory_space=pltpu.VMEM)
    return pl.pallas_call(
        adam_wide_kernel,
        in_specs=[vmem] * 4,
        out_specs=[vmem] * 5,
        out_shape=[jax.ShapeDtypeStruct(w.shape, f32)] * 4
        + [jax.ShapeDtypeStruct(w.shape[1:], f32)],
        compiler_params=params(16),
    )(w, g, m, v)


def adam_tall_kernel(w_ref, g_ref, m_ref, v_ref, g_out, m_out, v_out, n_out, s_out):
    grad = g_ref[...].T
    first, second, moved = adam_values(w_ref[...], grad, m_ref[...], v_ref[...])
    g_out[...] = grad
    m_out[...] = first
    v_out[...] = second
    n_out[...] = moved
    s_out[...] = lane_sums(moved * moved)


def adam_tall(w, g, m, v):
    vmem = pl.BlockSpec(memory_space=pltpu.VMEM)
    return pl.pallas_call(
        adam_tall_kernel,
        in_specs=[vmem] * 4,
        out_specs=[vmem] * 5,
        out_shape=[jax.ShapeDtypeStruct(w.shape, f32)] * 4
        + [jax.ShapeDtypeStruct((8, w.shape[0]), f32)],
        compiler_params=params(16),
    )(w, g, m, v)


def scale_kernel(na_ref, nb_ref, nc_ref, nd_ref, a_ref, b_ref, c_ref, d_ref, ao_ref, bo_ref, co_ref, do_ref, *, width):
    factor = lambda value: lax.rsqrt(value / width + layer_eps)
    for norm, ref, out in ((na_ref, a_ref, ao_ref), (nc_ref, c_ref, co_ref)):
        for c in range(ref.shape[1]):
            out[:, c, :] = ref[:, c, :] * factor(norm[c : c + 1, :])
    for norm, ref, out in ((nb_ref, b_ref, bo_ref), (nd_ref, d_ref, do_ref)):
        out[...] = ref[...] * factor(norm[...]).T[:, 0:1]


def scale_weights(norms, weights, width):
    vmem = pl.BlockSpec(memory_space=pltpu.VMEM)
    return pl.pallas_call(
        functools.partial(scale_kernel, width=width),
        in_specs=[vmem] * 8,
        out_specs=[vmem] * 4,
        out_shape=[jax.ShapeDtypeStruct(w.shape, f32) for w in weights],
        compiler_params=params(16),
    )(*norms, *weights)


def after(value, *others):
    return lax.optimization_barrier((value, *others))[0]


def per_device(
    layer_input,
    cotangent,
    positions,
    w_qkv,
    w_out,
    w_up,
    w_down,
    moment_qkv,
    moment_out,
    moment_up,
    moment_down,
    square_qkv,
    square_out,
    square_up,
    square_down,
    s_qk,
    alpha_attn,
    alpha_mlp,
    s_uv,
):
    nz = lax.axis_size("head")
    nb = lax.axis_size("batch")
    z = lax.axis_index("head")
    b = lax.axis_index("batch")
    core = b % 2
    chip = b // 2
    chips = nb // 2
    bits = [1 << n for n in range(int(math.log2(chips)))]
    rows, cols = layer_input.shape
    width = cols * nz
    own = rows // nz
    hid = w_down.shape[0]
    half = hid // 2
    hc = cols // 2
    heads = cols // HEAD_DIM
    span = w_qkv.shape[0]
    chunk = width // chips
    core_s = core.reshape(1).astype(jnp.int32)
    place = jnp.stack([z, chip, core]).astype(jnp.int32)
    fast = chunk == cols and chunk % 128 == 0

    def swap_batch(value, bit):
        return lax.ppermute(value, "batch", [(i, i ^ bit) for i in range(nb)])

    def swap_core(value):
        return swap_batch(value, 1)

    def swap_chip(value, bit):
        return swap_batch(value, 2 * bit)

    def onward(value, k=1):
        return lax.ppermute(value, "head", [(i, (i + k) % nz) for i in range(nz)])

    def exchange(value):
        return lax.all_to_all(value, "head", split_axis=0, concat_axis=0)

    def pick(pair, index):
        return jnp.where(index == 0, pair[0], pair[1])

    def relative(value):
        return jnp.concatenate(
            [
                lax.dynamic_slice_in_dim(value, (chip ^ r) * chunk, chunk, value.ndim - 1)
                for r in range(chips)
            ],
            axis=-1,
        )

    def spread(value):
        if chips <= 4:
            return [value] + [swap_chip(value, r) for r in range(1, chips)]
        for bit in bits:
            value = jnp.concatenate([value, swap_chip(value, bit)], axis=0)
        return [value]

    tokens = [layer_input, onward(layer_input)]
    mine, theirs = pack(core_s, w_up, s_uv, w_down, w_out)
    qkv_own = after(w_qkv, mine).reshape(span, 3 * cols).astype(bf16)
    qkv_full = lax.all_gather(qkv_own, "batch", axis=0, tiled=True)
    theirs = swap_core(theirs)
    packet = jnp.concatenate([pick((mine, theirs), core), pick((theirs, mine), core)], axis=0)
    hops = [packet, onward(packet)]
    slots = [spread(packet)]
    tokens[1], hops[1], places, alpha_attn, alpha_mlp, *last = lax.optimization_barrier(
        (tokens[1], hops[1], positions, alpha_attn, alpha_mlp, *slots[0])
    )
    slots[0] = list(last)

    freqs = jnp.exp(
        (jnp.arange(128) % (HEAD_DIM // 2)).astype(f32) * (-2.0 * math.log(10000.0) / HEAD_DIM)
    )
    phase = places.astype(f32)[:, None] * freqs[None, :]
    side = jnp.where(jnp.arange(128) % HEAD_DIM < HEAD_DIM // 2, -1.0, 1.0).astype(f32)
    cosine, sine = jnp.cos(phase), jnp.sin(phase) * side[None, :]
    lane = jnp.arange(cols) // HEAD_DIM
    ones = (lane[:, None] == lane[None, :]).astype(bf16)
    gain = s_qk.reshape(1, cols)
    is_long = (places[SHORT : SHORT + 1] != 0).astype(jnp.int32)
    attn_gain = relative(alpha_attn[None])
    mlp_gain = relative(alpha_mlp[None])

    for n in range(2, nz):
        slots.append(spread(hops[-1]))
        tokens.append(onward(tokens[-1]))
        if n < nz - 1:
            hops.append(onward(hops[-1]))
            tokens[-1], hops[-1], cosine, sine, ones, attn_gain, mlp_gain, *last = (
                lax.optimization_barrier(
                    (tokens[-1], hops[-1], cosine, sine, ones, attn_gain, mlp_gain, *slots[-1])
                )
            )
            slots[-1] = list(last)
    last_hop, tokens[-1] = lax.optimization_barrier((hops[-1], tokens[-1]))
    hops.append(onward(last_hop))

    blocks = rows // 512
    middle = blocks // 2
    tokens_full, q, k, v, rho = qkv_project(place, tokens, qkv_full, cosine, sine, gain, ones)
    y_a, logs_a = attn_fwd(is_long, q, k, v, 0, middle)
    q_b, hops[-1], *last = lax.optimization_barrier((after(q, y_a), hops[-1], *slots[-1]))
    slots[-1] = list(last)
    slots.append(spread(hops[-1]))
    y_b, logs_b = attn_fwd(is_long, q_b, k, v, middle, blocks - middle)
    y_one = exchange(y_a.reshape(nz, own // 2, cols))
    y_in, y_one = lax.optimization_barrier((y_b, y_one))
    y_two = exchange(y_in.reshape(nz, own // 2, cols))
    flat = lambda value: value.transpose(1, 0, 2).reshape(own, width)
    start = tokens_full
    if not fast:
        start = jnp.concatenate(
            [
                lax.dynamic_slice_in_dim(tokens_full, h * (rows // 2) + z * (own // 2), own // 2, 0)
                for h in range(2)
            ]
        )
        start = relative(start)
    y_one, y_two, *last = lax.optimization_barrier((y_one, y_two, *slots[-1]))
    slots[-1] = list(last)
    hA, h1, h_own, stat, y_mine, y_other = attn_out(place, y_one, y_two, slots, start, attn_gain, chips, fast)
    h_got = swap_core(h_own)
    y_got = swap_core(y_other)
    h_got, y_got = lax.optimization_barrier((h_got, y_got))
    cot = after(cotangent, h_own).reshape(2, nz, own // 2, cols).transpose(1, 0, 2, 3)
    cot = exchange(cot.reshape(nz, own, cols))

    act, uv, mo_own, mo_other = mlp_fwd(h_own, h_got, slots, half)
    mo_got = swap_core(mo_other)
    if not fast:
        cot = relative(flat(cot))
    hidden, d_own, base, ga_mlp = loss(place, mo_own, mo_got, h1, cot, mlp_gain, chips, fast)
    d_got = swap_core(d_own)
    if not fast:
        hidden = relative(hidden).reshape(own, nz, cols).transpose(1, 0, 2)
    hidden = exchange(hidden)

    orders = [bits, bits[::-1]]
    sent_at = [[r for r in range(chips) if r & order[0]] for order in orders]
    kept_at = [[r for r in range(chips) if not r & order[0]] for order in orders]

    def second(kept, sent):
        found, sends = [], []
        if chips == 4:
            at = [[n for n, r in enumerate(left) if r & order[1]] for order, left in zip(orders, kept_at)]
            sends = pair_sums(kept, sent, [one[0] for one in at])
            for order, one, keep, got, send in zip(orders, at, kept, sent, sends):
                cut = lambda t, n=1 - one[0]: t[n : n + 1]
                found.append([cut(keep), cut(got), swap_chip(send, order[1])])
            return found, sends
        for order, left, got, keep in zip(orders, kept_at, sent, kept):
            terms = [keep, got]
            for bit in order[1:]:
                send_at = [n for n, r in enumerate(left) if r & bit]
                keep_at = [n for n, r in enumerate(left) if not r & bit]
                left = [left[n] for n in keep_at]
                cut = lambda v, at: jnp.concatenate([v[n : n + 1] for n in at], axis=0)
                send = sum(cut(t, send_at).astype(f32) for t in terms).astype(bf16)
                terms = [cut(t, keep_at) for t in terms] + [swap_chip(send, bit)]
                sends.append(send)
            found.append(terms)
        return found, sends

    def slot_sums(found):
        return [sum(t[0, n].astype(f32) for t in terms) for terms in found for n in range(nz // 2)]

    def wait_last(found, *others):
        return [terms[:-1] + [after(terms[-1], *others)] for terms in found]

    down_made, down_kept = weight_grads(place, sent_at, kept_at, chips, (d_own, d_got), act)
    down_sent = [swap_chip(one, order[0]) for one, order in zip(down_made, orders)]
    d_own, d_got, *_ = lax.optimization_barrier((d_own, d_got, *down_made))
    duv, dh_own, dh_other, gsuv = mlp_bwd(d_own, d_got, slots, uv, half)
    dh_got = swap_core(dh_other)
    down_sent = [after(one, dh_other) for one in down_sent]
    down_part, down_next = second(down_kept, down_sent)
    dh_own, hidden, *_ = lax.optimization_barrier((dh_own, hidden, *down_next))
    do_own, through, ga_attn, dy = first_back(
        place, dh_own, dh_got, base, h1, hA, start, stat, attn_gain, slots, chips, fast, cols
    )
    dy = exchange(dy)
    do_got = swap_core(do_own)

    extra = (gsuv, ga_attn, ga_mlp)
    if not fast:
        alphas = [relative(ga_attn[0:1]), relative(ga_mlp[0:1])]
        extra = []
        wide = 2 * half + hc
        fill = lambda r: jnp.pad(r, ((0, 0), (0, wide - r.shape[1])))
        for n in range(nz):
            at = ((z - n) % nz) * cols
            line = [lax.dynamic_slice_in_dim(g, at, cols, 1) for g in alphas]
            lines = [gsuv[n, :2].reshape(1, 2 * half), jnp.concatenate(line, axis=1)]
            lines = jnp.concatenate([fill(r) for r in lines])
            extra.append(jnp.pad(lines, ((0, EXTRA - 2), (0, 0))))
        extra = jnp.stack(extra)
    up_made, up_kept = weight_grads(
        place, sent_at, kept_at, chips, (h_own, h_got), duv, (do_own, do_got), (y_mine, y_got), extra
    )
    down_part = wait_last(down_part, *up_kept)
    down_last = [terms[-1] for terms in down_part]
    dy, *both = lax.optimization_barrier((dy, *up_made, *down_last))
    up_made, down_last = both[: len(up_made)], both[len(up_made) :]
    down_slots = slot_sums([t[:-1] + [last] for t, last in zip(down_part, down_last)])
    down_along = [onward(down_slots[n].astype(bf16), nz - n) for n in range(1, nz)]
    up_sent = [swap_chip(one, order[0]) for one, order in zip(up_made, orders)]

    dy = dy.reshape(nz, 2, own // 2, cols)
    common = lambda y, logs: (
        is_long, q, k, v, dy, y, logs, rho, cosine, sine, gain, ones
    )
    dqkv_b, dk_part, dv_part, sqk_b = attn_bwd(
        *common(y_b, logs_b), middle, blocks - middle, None
    )

    if not fast:
        through = relative(through).reshape(own, nz, cols).transpose(1, 0, 2)
    mine_at = z * (own // 2)
    qkv_parts = qkv_full.reshape(nz, cols, 3 * cols)

    def input_part(dqkv, side):
        part = jnp.einsum("tn,zcn->ztc", dqkv, qkv_parts, preferred_element_type=f32).astype(bf16)
        here = lax.dynamic_slice_in_dim(part, mine_at, own // 2, 1).astype(f32)
        more = after(through, dqkv)[:, side * (own // 2) : (side + 1) * (own // 2)]
        return lax.dynamic_update_slice_in_dim(part, (here + more.astype(f32)).astype(bf16), mine_at, 1)

    part_b = input_part(dqkv_b, 1)
    down_along = [after(one, dqkv_b) for one in down_along]
    part_got = exchange(part_b)
    dk_part, *_ = lax.optimization_barrier((dk_part, part_b, *down_along))
    dqkv_a, sqk_a = attn_bwd(*common(y_a, logs_a), 0, middle, [dk_part, dv_part])
    input_b = jnp.sum(after(part_got, dqkv_a).astype(f32), axis=0)
    up_part, up_next = second(up_kept, [after(one, dqkv_a) for one in up_sent])
    dqkv_a, *_ = lax.optimization_barrier((dqkv_a, *up_next))
    part_a = input_part(dqkv_a, 0)
    dqkv = jnp.concatenate([dqkv_a, dqkv_b], axis=0)
    grad_qkv = t_dot(tokens_full, dqkv).astype(bf16)
    up_part = wait_last(up_part, part_a, grad_qkv, *[terms[-1] for terms in up_part])
    up_slots = slot_sums(up_part)
    passed = up_slots[1].astype(bf16)
    part_a, grad_qkv, passed = lax.optimization_barrier((part_a, grad_qkv, passed))
    passed = onward(passed)
    for n in range(2, nz):
        if n == nz - 1:
            passed, part_a = lax.optimization_barrier((passed, part_a))
        passed = onward((up_slots[n] + passed.astype(f32)).astype(bf16))
    sum_up_t = up_slots[0] + passed.astype(f32)
    input_a = lax.psum_scatter(part_a.reshape(-1, cols), "head", scatter_dimension=0, tiled=True)
    input_grad = jnp.concatenate([input_a.astype(f32), input_b], axis=0)
    hidden_t = after(hidden, part_a).reshape(nz, 2, own // 2, cols).transpose(1, 0, 2, 3).reshape(rows, cols)

    sqk = jnp.pad((sqk_a + sqk_b), ((0, EXTRA - 8), (0, 2 * cols)))
    shard = [lax.dynamic_slice_in_dim(grad_qkv, (b ^ r) * span, span, 0) for r in range(nb)]
    shard = [jnp.concatenate([s, sqk.astype(bf16)], axis=0) for s in shard]
    qbits = [1 << n for n in range(int(math.log2(nb)))]
    held = {r: shard[r] for r in range(nb)}
    for bit in qbits:
        send_at = [r for r in held if r & bit]
        send = jnp.concatenate([held[r] for r in send_at], axis=0).astype(bf16)
        got = swap_batch(send, bit)
        size = span + EXTRA
        held = {
            r ^ bit: held[r ^ bit].astype(f32) + got[n * size : (n + 1) * size].astype(f32)
            for n, r in enumerate(send_at)
        }
    cell = width // (nz * nb)
    sum_sqk = lax.dynamic_slice_in_dim(held[0][span, :cols], b * cell, cell, 0)
    w_late, m_late, v_late, _ = lax.optimization_barrier((w_qkv, moment_qkv, square_qkv, part_a))
    qkv_new = adam_wide(w_late, held[0][:span], m_late, v_late)

    def both_halves(total):
        two = (total[:span], total[span : 2 * span])
        here = jnp.concatenate([pick(two, core), total[2 * span :]], axis=0)
        there = jnp.concatenate([pick(two, 1 - core), total[2 * span :]], axis=0)
        there = swap_core(there.astype(bf16)).astype(f32)
        return [pick((here, there), core), pick((there, here), core)]

    join = lambda halves, at, size: [p[:span, at : at + size] for p in halves]
    down_along = [after(one, part_a) for one in down_along]
    halves = both_halves(down_slots[0] + sum(one.astype(f32) for one in down_along))
    down_new = adam_tall(w_down, jnp.concatenate(join(halves, 0, half), axis=1), moment_down, square_down)
    halves = both_halves(sum_up_t)
    grad_up = jnp.concatenate(join(halves, 0, half) + join(halves, half, half), axis=1)
    grad_up = grad_up * s_uv.reshape(1, 2 * hid)
    up_new = adam_wide(w_up, grad_up, moment_up, square_up)
    out_new = adam_tall(w_out, jnp.concatenate(join(halves, 2 * half, hc), axis=1), moment_out, square_out)
    suv_rows = jnp.stack(
        [jnp.concatenate([p[span, c * half : (c + 1) * half] for p in halves]) for c in range(2)]
    )
    suv_rows = suv_rows / s_uv
    sum_suv = lax.dynamic_slice_in_dim(suv_rows, b * (hid // nb), hid // nb, 1)
    alphas = halves[0][span + 1] + halves[1][span + 1]
    sum_attn = lax.dynamic_slice_in_dim(alphas[:cols], b * cell, cell, 0)
    sum_mlp = lax.dynamic_slice_in_dim(alphas[cols : 2 * cols], b * cell, cell, 0)

    hidden = hidden_t.astype(f32)

    squares = [qkv_new[4], out_new[4][:1], up_new[4], down_new[4][:1]]
    sizes = [t.size for t in squares]
    norms = jnp.concatenate([t.reshape(-1) for t in squares]).reshape(-1, 128)
    for bit in qbits:
        norms = norms + swap_batch(norms, bit)
    norms = norms.reshape(-1)
    ends = [0] + [sum(sizes[: n + 1]) for n in range(4)]
    back = lambda n, shape: norms[ends[n] : ends[n + 1]].reshape(shape)
    eight = lambda value: jnp.broadcast_to(value, (8, value.shape[1]))
    new_qkv, new_out, new_up, new_down = scale_weights(
        [back(0, (3, cols)), eight(back(1, (1, cols))), back(2, (2, hid)), eight(back(3, (1, hid)))],
        [qkv_new[3], out_new[3], up_new[3], down_new[3]],
        width,
    )
    sum_qkv, first_a, second_a = qkv_new[:3]
    sum_out, first_b, second_b = out_new[:3]
    sum_up, first_c, second_c = up_new[:3]
    sum_down, first_d, second_d = down_new[:3]
    return (
        hidden,
        input_grad,
        sum_qkv,
        sum_out,
        sum_up,
        sum_down,
        first_a,
        first_b,
        first_c,
        first_d,
        second_a,
        second_b,
        second_c,
        second_d,
        new_qkv,
        new_out,
        new_up,
        new_down,
        sum_sqk,
        sum_attn,
        sum_mlp,
        sum_suv,
    )


def solution(mesh):
    tokens = P("batch", "head")
    wide = P("batch", None, "head")
    tall = P("head", "batch")
    flat = P(("head", "batch"))
    weights = (wide, tall, wide, tall)
    return jax.shard_map(
        per_device,
        mesh=mesh,
        in_specs=(tokens, tokens, P("batch"))
        + weights * 3
        + (P("head"), P(), P(), P(None, "head")),
        out_specs=(tokens, tokens) + weights * 4 + (flat, flat, flat, P(None, ("head", "batch"))),
        check_vma=False,
    )
```

```python
import functools
import math

import jax
import jax.numpy as jnp
from jax import lax
from jax.experimental import pallas as pl
from jax.experimental.pallas import tpu as pltpu
from jax.sharding import PartitionSpec as P

HEAD_DIM = 64
SHORT = 1024

layer_eps = 1e-06
learn_rate = 0.008
beta_one = 0.9
beta_two = 0.95
adam_eps = 1e-08
bias_one = 1.0 - math.exp(100.0 * math.log(0.9))
bias_two = 1.0 - math.exp(100.0 * math.log(0.95))
score_scale = 8.0
LOG2E = math.log2(math.e)
LN2 = math.log(2.0)

bf16 = jnp.bfloat16
f32 = jnp.float32


def dot(a, b):
    return jnp.dot(a, b, preferred_element_type=f32)


def dot_t(a, b):
    return lax.dot_general(a, b, (((1,), (1,)), ((), ())), preferred_element_type=f32)


def t_dot(a, b):
    return lax.dot_general(a, b, (((0,), (0,)), ((), ())), preferred_element_type=f32)


def params(mib):
    return pltpu.CompilerParams(vmem_limit_bytes=mib * 1024 * 1024)


def full_spec(shape):
    return pl.BlockSpec(shape, lambda *_: (0,) * len(shape))


def head_sum(value, ones):
    high = value.astype(bf16)
    low = (value - high.astype(f32)).astype(bf16)
    return dot(high, ones) + dot(low, ones)


def widen(value, cols):
    return jnp.concatenate([value] * (cols // value.shape[1]), axis=1)


def swap_halves(value):
    cols = value.shape[-1]
    half = HEAD_DIM // 2
    lane = lax.broadcasted_iota(jnp.int32, value.shape, 1)
    first = (lane % HEAD_DIM) < half
    up = pltpu.roll(value, cols - half, 1)
    down = pltpu.roll(value, half, 1)
    return jnp.where(first, up, down)


def qkv_kernel(place_ref, *refs, parts):
    tokens = refs[:parts]
    w_ref, cos_ref, sin_ref, gain_ref, ones_ref, x_ref, q_ref, k_ref, v_ref, rho_ref = refs[parts:]
    cols = v_ref.shape[1]
    z = place_ref[0]
    for n in range(parts):
        at = pl.multiple_of(lax.rem(z + parts - n, parts) * cols, cols)
        x_ref[:, pl.ds(at, cols)] = tokens[n][...]
    proj = dot(x_ref[...], w_ref[...])
    cosine = widen(cos_ref[...], cols)
    sine = widen(sin_ref[...], cols)
    ones = ones_ref[...]
    gain = gain_ref[...]
    heads = cols // HEAD_DIM
    lane = lax.broadcasted_iota(jnp.int32, rho_ref.shape, 1)
    stats = jnp.zeros(rho_ref.shape, f32)
    for c, (out, scale) in enumerate(((q_ref, score_scale * LOG2E), (k_ref, 1.0))):
        part = proj[:, c * cols : (c + 1) * cols]
        rho = lax.rsqrt(head_sum(part * part, ones) + layer_eps)
        rot = part * cosine + swap_halves(part) * sine
        out[...] = (rot * rho * (gain * scale)).astype(bf16)
        for h in range(heads):
            stats = jnp.where(lane == c * heads + h, rho[:, h * HEAD_DIM : h * HEAD_DIM + 1], stats)
    rho_ref[...] = stats
    v_ref[...] = proj[:, 2 * cols :].astype(bf16)


def qkv_project(place, tokens, w, cosine, sine, gain, ones):
    rows, cols = tokens[0].shape
    parts = len(tokens)
    width = parts * cols
    blk = 512
    row = lambda n: pl.BlockSpec((blk, n), lambda i, s: (i, 0))
    return pl.pallas_call(
        functools.partial(qkv_kernel, parts=parts),
        grid_spec=pltpu.PrefetchScalarGridSpec(
            num_scalar_prefetch=1,
            grid=(rows // blk,),
            in_specs=[row(cols)] * parts
            + [full_spec((width, 3 * cols)), row(128), row(128)]
            + [full_spec((1, cols)), full_spec((cols, cols))],
            out_specs=[row(width)] + [row(cols)] * 3 + [row(128)],
        ),
        out_shape=[jax.ShapeDtypeStruct((rows, width), bf16)]
        + [jax.ShapeDtypeStruct((rows, cols), bf16)] * 3
        + [jax.ShapeDtypeStruct((rows, 128), f32)],
        compiler_params=params(56),
    )(place, *tokens, w, cosine, sine, gain, ones)


def head_masks(cols, heads):
    lane = lax.broadcasted_iota(jnp.int32, (1, cols), 1) // HEAD_DIM
    return [(lane == h) for h in range(heads)]


def masked(value, mask):
    return jnp.where(mask, value, jnp.zeros_like(value))


def attn_fwd_kernel(long_ref, q_ref, k_ref, v_ref, y_ref, l_ref, acc, mass, *, heads, blk, sub, first):
    i = first + pl.program_id(0)
    cols = q_ref.shape[1]
    masks = head_masks(cols, heads)
    per = SHORT // blk
    low = jnp.where(long_ref[0] != 0, 0, (i // per) * per)
    acc[...] = jnp.zeros_like(acc)
    mass[...] = jnp.zeros_like(mass)

    def lanes(p):
        total = p[:, 0:128]
        for n in range(1, p.shape[1] // 128):
            total = total + p[:, n * 128 : (n + 1) * 128]
        return total

    def body(j, carry):
        start = pl.multiple_of(j * blk, blk)
        keys = k_ref[pl.ds(start, blk), :]
        vals = v_ref[pl.ds(start, blk), :]
        q = q_ref[...]
        total = jnp.zeros(acc.shape, f32)
        for h in range(heads):
            p = jnp.exp2(dot_t(masked(q, masks[h]), keys))
            mass[h] += lanes(p)
            total += dot(p.astype(bf16), masked(vals, masks[h]))
        acc[...] += total
        return carry

    lax.fori_loop(low, i, body, 0)
    start = pl.multiple_of(i * blk, blk)
    causal = lax.broadcasted_iota(jnp.int32, (sub, sub), 0) >= lax.broadcasted_iota(
        jnp.int32, (sub, sub), 1
    )
    for a in range(blk // sub):
        rows = slice(a * sub, (a + 1) * sub)
        q = q_ref[rows, :]
        for b in range(a + 1):
            at = pl.multiple_of(start + b * sub, sub)
            keys = k_ref[pl.ds(at, sub), :]
            vals = v_ref[pl.ds(at, sub), :]
            total = jnp.zeros((sub, cols), f32)
            for h in range(heads):
                p = jnp.exp2(dot_t(masked(q, masks[h]), keys))
                if a == b:
                    p = jnp.where(causal, p, 0.0)
                mass[h, rows, :] += lanes(p)
                total += dot(p.astype(bf16), masked(vals, masks[h]))
            acc[rows, :] += total
    inverse = jnp.zeros(acc.shape, f32)
    logs = jnp.zeros(l_ref.shape, f32)
    lane = lax.broadcasted_iota(jnp.int32, l_ref.shape, 1)
    for h in range(heads):
        column = jnp.sum(mass[h], axis=1, keepdims=True)
        inverse = jnp.where(masks[h], 1.0 / column, inverse)
        logs = jnp.where(lane == h, jnp.log2(column), logs)
    y_ref[...] = (acc[...] * inverse).astype(bf16)
    l_ref[...] = logs


def attn_fwd(is_long, q, k, v, first, count):
    rows, cols = q.shape
    heads = cols // HEAD_DIM
    blk, sub = 512, 256
    row = lambda n: pl.BlockSpec((blk, n), lambda i, s: (i, 0))
    whole = pl.BlockSpec(((first + count) * blk, cols), lambda i, s: (0, 0))
    return pl.pallas_call(
        functools.partial(attn_fwd_kernel, heads=heads, blk=blk, sub=sub, first=first),
        grid_spec=pltpu.PrefetchScalarGridSpec(
            num_scalar_prefetch=1,
            grid=(count,),
            in_specs=[pl.BlockSpec((blk, cols), lambda i, s: (first + i, 0)), whole, whole],
            out_specs=[row(cols), row(128)],
            scratch_shapes=[pltpu.VMEM((blk, cols), f32), pltpu.VMEM((heads, blk, 128), f32)],
        ),
        out_shape=[
            jax.ShapeDtypeStruct((count * blk, cols), bf16),
            jax.ShapeDtypeStruct((count * blk, 128), f32),
        ],
        compiler_params=params(56),
    )(is_long, q, k, v)


def attn_bwd_kernel(
    long_ref, q_ref, qk_ref, dy_ref, y_ref, l_ref, k_ref, v_ref, rho_ref, cos_ref, sin_ref, gain_ref,
    ones_ref, dk_in, dv_in, out_ref, dk_out, dv_out, s_ref, acc, dk_acc, dv_acc, stats, dys, *, heads, blk, sub, first, count
):
    step = pl.program_id(0)
    local = count - 1 - step
    i = first + local
    cols = q_ref.shape[1]
    masks = head_masks(cols, heads)
    per = SHORT // blk
    low = jnp.where(long_ref[0] != 0, 0, (i // per) * per)
    ones = ones_ref[...]
    gain = gain_ref[...]

    @pl.when(step == 0)
    def _():
        dk_acc[...] = jnp.zeros_like(dk_acc)
        dv_acc[...] = jnp.zeros_like(dv_acc)
        s_ref[...] = jnp.zeros_like(s_ref)
        if dk_in is not None:
            dk_acc[...] = dk_in[...]
            dv_acc[...] = dv_in[...]

    acc[...] = jnp.zeros_like(acc)
    dys[...] = dy_ref[...].reshape(dys.shape)
    prod = dys[...].astype(f32) * y_ref[...].astype(f32)
    high = prod.astype(bf16)
    rest = (prod - high.astype(f32)).astype(bf16)
    pickers = (
        lax.broadcasted_iota(jnp.int32, (8, cols), 1) // HEAD_DIM
        == lax.broadcasted_iota(jnp.int32, (8, cols), 0)
    ).astype(bf16)
    stats[0:8, :] = dot_t(pickers, high) + dot_t(pickers, rest)
    stats[8:16, :] = l_ref[...].T[0:8, :]

    def piece(at, size, rows, causal):
        keys = k_ref[pl.ds(at, size), :]
        vals = v_ref[pl.ds(at, size), :]
        q = q_ref[rows, :]
        dy = dys[rows, :]
        total_q = jnp.zeros(q.shape, f32)
        total_k = jnp.zeros(keys.shape, f32)
        total_v = jnp.zeros(keys.shape, f32)
        for h in range(heads):
            qm = masked(q, masks[h])
            dym = masked(dy, masks[h])
            p = jnp.exp2(dot_t(keys, qm) - stats[8 + h : 9 + h, rows])
            if causal is not None:
                p = jnp.where(causal, p, 0.0)
            ds = (p * (dot_t(vals, dym) - stats[h : h + 1, rows])).astype(bf16)
            total_v += dot(p.astype(bf16), dym)
            total_k += dot(ds, qm)
            total_q += t_dot(ds, masked(keys, masks[h]))
        acc[rows, :] += total_q
        dk_acc[pl.ds(at, size), :] += total_k
        dv_acc[pl.ds(at, size), :] += total_v

    def body(j, carry):
        piece(pl.multiple_of(j * blk, blk), blk, slice(0, blk), None)
        return carry

    lax.fori_loop(low, i, body, 0)
    start = pl.multiple_of(i * blk, blk)
    causal = lax.broadcasted_iota(jnp.int32, (sub, sub), 0) <= lax.broadcasted_iota(
        jnp.int32, (sub, sub), 1
    )
    for a in range(blk // sub):
        for b in range(a + 1):
            piece(
                pl.multiple_of(start + b * sub, sub),
                sub,
                slice(a * sub, (a + 1) * sub),
                causal if a == b else None,
            )
    cosine = widen(cos_ref[...], cols)
    sine = widen(sin_ref[...], cols)
    total = jnp.zeros((1, cols), f32)
    here = pl.ds(start, blk)
    for c, (value, unit, up, scale) in enumerate(
        (
            (acc[...], q_ref[...], score_scale, score_scale * LOG2E),
            (dk_acc[here, :], k_ref[here, :], LN2, 1.0),
        )
    ):
        rho = jnp.zeros(value.shape, f32)
        for h in range(heads):
            at = c * heads + h
            rho = jnp.where(masks[h], rho_ref[:, at : at + 1], rho)
        grad = value * up
        unit = unit.astype(f32) * (1.0 / (gain * scale))
        total += jnp.sum(grad * unit, axis=0, keepdims=True)
        grad = grad * gain
        back = rho * (grad - unit * head_sum(grad * unit, ones))
        turned = back * cosine - swap_halves(back) * sine
        out_ref[:, c * cols : (c + 1) * cols] = turned.astype(bf16)
    out_ref[:, 2 * cols :] = dv_acc[here, :].astype(bf16)
    s_ref[0:1, :] += total
    if dk_out is not None:
        @pl.when(step == count - 1)
        def _():
            dk_out[...] = dk_acc[0 : first * blk, :]
            dv_out[...] = dv_acc[0 : first * blk, :]


def attn_bwd(is_long, q, k, v, dy, y, logs, rho, cosine, sine, gain, ones, first, count, carry):
    rows, cols = q.shape
    heads = cols // HEAD_DIM
    blk, sub = 512, 256
    top = (first + count) * blk
    at = lambda s: first + count - 1 - s
    row = lambda n: pl.BlockSpec((blk, n), lambda s, m: (at(s), 0))
    whole = pl.BlockSpec((top, cols), lambda s, m: (0, 0))
    ins = [q, k, dy, y, logs, k, v, rho, cosine, sine, gain, ones]
    mine = lambda n: pl.BlockSpec((blk, n), lambda s, m: (count - 1 - s, 0))
    share = dy.shape[2]
    half_at = 1 if first else 0
    in_specs = [row(cols)] * 2
    in_specs.append(
        pl.BlockSpec((blk // share, None, share, cols), lambda s, m: (count - 1 - s, half_at, 0, 0))
    )
    in_specs += [mine(cols), mine(128), whole, whole] + [row(128)] * 3
    in_specs += [full_spec((1, cols)), full_spec((cols, cols))]
    body = functools.partial(
        attn_bwd_kernel, heads=heads, blk=blk, sub=sub, first=first, count=count
    )
    outs = [jax.ShapeDtypeStruct((count * blk, 3 * cols), bf16)]
    out_specs = [pl.BlockSpec((blk, 3 * cols), lambda s, m: (count - 1 - s, 0))]
    if first:
        outs += [jax.ShapeDtypeStruct((first * blk, cols), f32)] * 2
        out_specs += [full_spec((first * blk, cols))] * 2
        inner = lambda *r: body(*r[:13], None, None, *r[13:])
    else:
        ins += carry
        in_specs += [full_spec((top, cols))] * 2
        inner = lambda *r: body(*r[:16], None, None, *r[16:])
    outs.append(jax.ShapeDtypeStruct((8, cols), f32))
    out_specs.append(full_spec((8, cols)))
    return pl.pallas_call(
        inner,
        grid_spec=pltpu.PrefetchScalarGridSpec(
            num_scalar_prefetch=1,
            grid=(count,),
            in_specs=in_specs,
            out_specs=out_specs,
            scratch_shapes=[
                pltpu.VMEM((blk, cols), f32),
                pltpu.VMEM((top, cols), f32),
                pltpu.VMEM((top, cols), f32),
                pltpu.VMEM((16, blk), f32),
                pltpu.VMEM((blk, cols), bf16),
            ],
        ),
        out_shape=outs,
        compiler_params=params(56),
    )(is_long, *ins)


def row_norm(value):
    return lax.rsqrt(jnp.mean(value * value, axis=1, keepdims=True) + layer_eps)


def norm_back(scale, result, grad):
    return scale * (grad - result * jnp.mean(grad * result, axis=1, keepdims=True))


def pack_kernel(core_ref, up_ref, gain_ref, down_ref, out_ref, mine_ref, theirs_ref):
    half = up_ref.shape[2] // 2
    low = core_ref[0] == 0
    down = down_ref[...].astype(bf16).T
    out = out_ref[...].astype(bf16).T
    for ref, first in ((mine_ref, low), (theirs_ref, jnp.logical_not(low))):
        for c in range(2):
            gain = gain_ref[c : c + 1, :]
            ref[:, c * half : (c + 1) * half] = jnp.where(
                first, up_ref[:, c, :half] * gain[:, :half], up_ref[:, c, half:] * gain[:, half:]
            ).astype(bf16)
        ref[:, 2 * half : 3 * half] = jnp.where(first, down[:, :half], down[:, half:])
        ref[:, 3 * half :] = out


def pack(core, w_up, gain, w_down, w_out):
    span, _, hid = w_up.shape
    cols = w_out.shape[0]
    vmem = pl.BlockSpec(memory_space=pltpu.VMEM)
    return pl.pallas_call(
        pack_kernel,
        in_specs=[pl.BlockSpec(memory_space=pltpu.SMEM)] + [vmem] * 4,
        out_specs=[vmem] * 2,
        out_shape=[jax.ShapeDtypeStruct((span, 3 * hid // 2 + cols), bf16)] * 2,
        compiler_params=params(16),
    )(core, w_up, gain, w_down, w_out)


def place_of(r, chip, chunk):
    return pl.ds(pl.multiple_of((r ^ chip) * chunk, chunk), chunk)


def put_relative(ref, chip, chips, fast):
    if not fast:
        return ref[...]
    if len(ref.shape) == 3:
        return jnp.concatenate([ref[r ^ chip] for r in range(chips)], axis=1)
    chunk = ref.shape[1] // chips
    return jnp.concatenate([ref[:, place_of(r, chip, chunk)] for r in range(chips)], axis=1)


def put_natural(ref, value, chip, chips, fast):
    if not fast:
        ref[...] = value
        return
    chunk = value.shape[1] // chips
    for r in range(chips):
        part = value[:, r * chunk : (r + 1) * chunk]
        if len(ref.shape) == 3:
            ref[r ^ chip] = part
        else:
            ref[:, place_of(r, chip, chunk)] = part


def attn_out_kernel(place_ref, *refs, counts, chips, fast):
    total = sum(counts)
    flat, refs = refs[:total], refs[total:]
    ya_ref, yb_ref, x_ref, alpha_ref, ha_ref, h1_ref, hb_ref, stat_ref, all_ref, half_ref, acc = refs
    z, chip, low = place_ref[0], place_ref[1], place_ref[2] == 0
    parts = len(counts)
    early = pl.program_id(0) == 0
    index = 0
    for n in range(parts):
        at = lax.rem(z + parts - n, parts)
        y = jnp.where(early, ya_ref[at], yb_ref[at])
        hc = y.shape[1] // 2
        all_ref[at] = y
        half_ref[at] = jnp.where(low, y[:, hc:], y[:, :hc])
        column = 0
        for piece in flat[index : index + counts[n]]:
            part = slice(column, column + piece.shape[0])
            if n == 0:
                acc[:, part] = dot_t(y, piece[...])
            else:
                acc[:, part] += dot_t(y, piece[...])
            column += piece.shape[0]
        index += counts[n]
    total = acc[...]
    norm = row_norm(total)
    hidden = total * norm
    start = put_relative(x_ref, chip, chips, fast).astype(f32)
    mixed = start + alpha_ref[...] * (hidden - start)
    first_norm = row_norm(mixed)
    out = mixed * first_norm
    ha_ref[...] = hidden
    h1_ref[...] = out
    hb_ref[...] = out.astype(bf16)
    lane = lax.broadcasted_iota(jnp.int32, stat_ref.shape, 1)
    stat_ref[...] = jnp.where(lane == 0, norm, first_norm)


def own_rows(blk, parts, width, fast):
    if fast:
        return pl.BlockSpec((blk, width), lambda i, s: (i * parts + s[0], 0))
    return pl.BlockSpec((blk, width), lambda i, s: (i, 0))


def out_weights(slots, cols):
    flat = [p for slot in slots for p in slot]
    last = flat[0].shape[1] // cols - 1
    return flat, [pl.BlockSpec((p.shape[0], cols), lambda i, s: (0, last)) for p in flat]


def attn_out(place, ya, yb, slots, x, alpha, chips, fast):
    parts, blk, cols = ya.shape
    width = x.shape[1]
    rows = 2 * blk
    row = lambda n: pl.BlockSpec((blk, n), lambda i, s: (i, 0))
    flat, specs = out_weights(slots, cols)
    return pl.pallas_call(
        functools.partial(attn_out_kernel, counts=[len(t) for t in slots], chips=chips, fast=fast),
        grid_spec=pltpu.PrefetchScalarGridSpec(
            num_scalar_prefetch=1,
            grid=(2,),
            in_specs=specs
            + [full_spec(ya.shape)] * 2
            + [own_rows(blk, parts, width, fast), full_spec((1, width))],
            out_specs=[row(width)] * 3
            + [row(128)]
            + [pl.BlockSpec((parts, blk, n), lambda i, s: (0, i, 0)) for n in (cols, cols // 2)],
            scratch_shapes=[pltpu.VMEM((blk, width), f32)],
        ),
        out_shape=[jax.ShapeDtypeStruct((rows, width), d) for d in (f32, f32, bf16)]
        + [jax.ShapeDtypeStruct((rows, 128), f32)]
        + [jax.ShapeDtypeStruct((parts, rows, n), bf16) for n in (cols, cols // 2)],
        compiler_params=params(56),
    )(place, *flat, ya, yb, x, alpha)


def loss_kernel(place_ref, own_ref, got_ref, h1_ref, cot_ref, alpha_ref, hidden_ref, dmo_ref, base_ref, ga_ref, *, chips, fast):
    chip = place_ref[1]
    total = own_ref[...] + got_ref[...].astype(f32)
    alpha = alpha_ref[...]
    norm = row_norm(total)
    inner = total * norm
    h1 = h1_ref[...]
    mixed = h1 + alpha * (inner - h1)
    last = row_norm(mixed)
    hidden = mixed * last
    grad = norm_back(last, hidden, put_relative(cot_ref, chip, chips, fast).astype(f32))
    put_natural(hidden_ref, hidden.astype(bf16), chip, chips, fast)
    base_ref[...] = (1.0 - alpha) * grad
    dmo_ref[...] = norm_back(norm, inner, alpha * grad).astype(bf16)

    @pl.when(pl.program_id(0) == 0)
    def _():
        ga_ref[...] = jnp.zeros_like(ga_ref)

    ga_ref[0:1, :] += jnp.sum(grad * (inner - h1), axis=0, keepdims=True)


def loss(place, own, got, h1, cot, alpha, chips, fast):
    rows, width = own.shape
    blk = rows // 2
    row = pl.BlockSpec((blk, width), lambda i, s: (i, 0))
    part = row
    if fast:
        part = pl.BlockSpec((chips, blk, width // chips), lambda i, s: (0, i, 0))
    return pl.pallas_call(
        functools.partial(loss_kernel, chips=chips, fast=fast),
        grid_spec=pltpu.PrefetchScalarGridSpec(
            num_scalar_prefetch=1,
            grid=(rows // blk,),
            in_specs=[row] * 3 + [part, full_spec((1, width))],
            out_specs=[part] + [row] * 2 + [full_spec((8, width))],
        ),
        out_shape=[jax.ShapeDtypeStruct(cot.shape, bf16)]
        + [jax.ShapeDtypeStruct((rows, width), d) for d in (bf16, f32)]
        + [jax.ShapeDtypeStruct((8, width), f32)],
        compiler_params=params(56),
    )(place, own, got, h1, cot, alpha)


def first_back_kernel(place_ref, *refs, counts, chips, fast):
    total = sum(counts)
    flat, refs = refs[:total], refs[total:]
    own_ref, got_ref, base_ref, h1_ref, ha_ref, x_ref, stat_ref, alpha_ref = refs[:8]
    do_ref, through_ref, ga_ref, dy_ref = refs[8:]
    z, chip = place_ref[0], place_ref[1]
    alpha = alpha_ref[...]
    grad = base_ref[...] + own_ref[...] + got_ref[...].astype(f32)
    grad = norm_back(stat_ref[:, 1:2], h1_ref[...], grad)
    ha = ha_ref[...]
    put_natural(through_ref, ((1.0 - alpha) * grad).astype(bf16), chip, chips, fast)
    back = norm_back(stat_ref[:, 0:1], ha, alpha * grad).astype(bf16)
    do_ref[...] = back
    parts = len(counts)
    step = pl.program_id(0)
    index = 0
    for n in range(parts):
        at = lax.rem(z + parts - n, parts)
        part = jnp.zeros(dy_ref.shape[1:], f32)
        column = 0
        for piece in flat[index : index + counts[n]]:
            part += dot(back[:, column : column + piece.shape[0]], piece[...])
            column += piece.shape[0]
        index += counts[n]
        dy_ref[at] = part.astype(bf16)

    @pl.when(step == 0)
    def _():
        ga_ref[...] = jnp.zeros_like(ga_ref)

    start = put_relative(x_ref, chip, chips, fast).astype(f32)
    ga_ref[0:1, :] += jnp.sum(grad * (ha - start), axis=0, keepdims=True)


def first_back(place, own, got, base, h1, ha, x, stat, alpha, slots, chips, fast, cols):
    rows, width = own.shape
    parts = len(slots)
    blk = rows // 2
    row = lambda n: pl.BlockSpec((blk, n), lambda i, s: (i, 0))
    flat, specs = out_weights(slots, cols)
    through, shape = row(width), (rows, width)
    if fast:
        through = pl.BlockSpec((parts, blk, cols), lambda i, s: (0, i, 0))
        shape = (parts, rows, cols)
    return pl.pallas_call(
        functools.partial(first_back_kernel, counts=[len(t) for t in slots], chips=chips, fast=fast),
        grid_spec=pltpu.PrefetchScalarGridSpec(
            num_scalar_prefetch=1,
            grid=(2,),
            in_specs=specs
            + [row(width)] * 5
            + [own_rows(blk, parts, width, fast), row(128), full_spec((1, width))],
            out_specs=[row(width), through]
            + [full_spec((8, width)), pl.BlockSpec((parts, blk, cols), lambda i, s: (0, i, 0))],
        ),
        out_shape=[jax.ShapeDtypeStruct((rows, width), bf16), jax.ShapeDtypeStruct(shape, bf16)]
        + [
            jax.ShapeDtypeStruct((8, width), f32),
            jax.ShapeDtypeStruct((parts, rows, cols), bf16),
        ],
        compiler_params=params(56),
    )(place, *flat, own, got, base, h1, ha, x, stat, alpha)


def fetch_weights(q, slots, wbuf, sems):
    def copies(j):
        at = 0
        found = []
        for p, piece in enumerate(slots[j]):
            size = piece.shape[0]
            found.append(
                pltpu.make_async_copy(
                    piece.at[:, : wbuf.shape[2]], wbuf.at[j % 2, at : at + size, :], sems.at[j % 2, p]
                )
            )
            at += size
        return found

    for j in range(len(slots)):

        @pl.when(q == j)
        def _(j=j):
            if j == 0:
                for copy in copies(0):
                    copy.start()
            if j + 1 < len(slots):
                for copy in copies(j + 1):
                    copy.start()
            for copy in copies(j):
                copy.wait()


def mlp_fwd_kernel(*refs, half, counts):
    total = sum(counts)
    flat, refs = refs[:total], refs[total:]
    slots, at = [], 0
    for n in counts:
        slots.append(flat[at : at + n])
        at += n
    ha_ref, hb_ref, act_ref, uv_ref, own_ref, got_ref, acc, wbuf, sems = refs
    rows = ha_ref.shape[0]
    q = pl.program_id(0)

    @pl.when(q == 0)
    def _():
        own_ref[...] = jnp.zeros_like(own_ref)
        acc[...] = jnp.zeros_like(acc)

    fetch_weights(q, slots, wbuf, sems)
    w = wbuf.at[lax.rem(q, 2)]
    for base, h_ref, sum_ref in ((0, ha_ref, own_ref), (rows, hb_ref, acc)):
        at = slice(base, base + rows)
        pair = dot(h_ref[...], w[:, : 2 * half])
        lifted = pair[:, :half]
        gated = pair[:, half:]
        act = (lifted * gated * jax.nn.sigmoid(gated)).astype(bf16)
        uv_ref[at, :] = pair.astype(bf16)
        act_ref[at, :] = act
        sum_ref[...] += dot_t(act, w[:, 2 * half : 3 * half])

    @pl.when(q == pl.num_programs(0) - 1)
    def _():
        got_ref[...] = acc[...].astype(bf16)


def mlp_fwd(ha, hb, slots, half):
    rows, width = ha.shape
    parts = len(slots)
    take = lambda n: pl.BlockSpec((None, 2 * rows, n), lambda q: (q, 0, 0))
    whole = full_spec((rows, width))
    anywhere = pl.BlockSpec(memory_space=pl.ANY)
    flat = [p for slot in slots for p in slot]
    return pl.pallas_call(
        functools.partial(mlp_fwd_kernel, half=half, counts=[len(s) for s in slots]),
        grid=(parts,),
        in_specs=[anywhere] * len(flat)
        + [whole, whole],
        out_specs=[take(half), take(2 * half), whole, whole],
        out_shape=[
            jax.ShapeDtypeStruct((parts, 2 * rows, half), bf16),
            jax.ShapeDtypeStruct((parts, 2 * rows, 2 * half), bf16),
            jax.ShapeDtypeStruct((rows, width), f32),
            jax.ShapeDtypeStruct((rows, width), bf16),
        ],
        scratch_shapes=[
            pltpu.VMEM((rows, width), f32),
            pltpu.VMEM((2, width, 3 * half), bf16),
            pltpu.SemaphoreType.DMA((2, max(len(s) for s in slots))),
        ],
        compiler_params=params(56),
    )(*flat, ha, hb)


def mlp_bwd_kernel(*refs, half, counts):
    total = sum(counts)
    flat, refs = refs[:total], refs[total:]
    slots, at = [], 0
    for n in counts:
        slots.append(flat[at : at + n])
        at += n
    da_ref, db_ref, uv_ref, duv_ref, own_ref, got_ref, gs_ref, acc, wbuf, sems = refs
    rows = da_ref.shape[0]
    q = pl.program_id(0)

    @pl.when(q == 0)
    def _():
        own_ref[...] = jnp.zeros_like(own_ref)
        acc[...] = jnp.zeros_like(acc)

    gs_ref[...] = jnp.zeros_like(gs_ref)
    fetch_weights(q, slots, wbuf, sems)
    w = wbuf.at[lax.rem(q, 2)]
    for base, d_ref, sum_ref in ((0, da_ref, own_ref), (rows, db_ref, acc)):
        at = slice(base, base + rows)
        grad = dot(d_ref[...], w[:, 2 * half : 3 * half])
        lifted = uv_ref[at, :half].astype(f32)
        gated = uv_ref[at, half:].astype(f32)
        sigma = jax.nn.sigmoid(gated)
        da = grad * gated * sigma
        db = grad * lifted * sigma * (1.0 + gated * (1.0 - sigma))
        gs_ref[0:1, :] += jnp.sum(da * lifted, axis=0, keepdims=True)
        gs_ref[1:2, :] += jnp.sum(db * gated, axis=0, keepdims=True)
        duv_ref[at, :half] = da.astype(bf16)
        duv_ref[at, half:] = db.astype(bf16)
        sum_ref[...] += dot_t(duv_ref[at, :], w[:, : 2 * half])

    @pl.when(q == pl.num_programs(0) - 1)
    def _():
        got_ref[...] = acc[...].astype(bf16)


def mlp_bwd(da, db, slots, uv, half):
    rows, width = da.shape
    parts = len(slots)
    take = lambda n: pl.BlockSpec((None, 2 * rows, n), lambda q: (q, 0, 0))
    whole = full_spec((rows, width))
    anywhere = pl.BlockSpec(memory_space=pl.ANY)
    flat = [p for slot in slots for p in slot]
    return pl.pallas_call(
        functools.partial(mlp_bwd_kernel, half=half, counts=[len(s) for s in slots]),
        grid=(parts,),
        in_specs=[anywhere] * len(flat)
        + [
            whole,
            whole,
            take(2 * half),
        ],
        out_specs=[
            take(2 * half),
            whole,
            whole,
            pl.BlockSpec((None, 8, half), lambda q: (q, 0, 0)),
        ],
        out_shape=[
            jax.ShapeDtypeStruct((parts, 2 * rows, 2 * half), bf16),
            jax.ShapeDtypeStruct((rows, width), f32),
            jax.ShapeDtypeStruct((rows, width), bf16),
            jax.ShapeDtypeStruct((parts, 8, half), f32),
        ],
        scratch_shapes=[
            pltpu.VMEM((rows, width), f32),
            pltpu.VMEM((2, width, 3 * half), bf16),
            pltpu.SemaphoreType.DMA((2, max(len(s) for s in slots))),
        ],
        compiler_params=params(56),
    )(*flat, da, db, uv)


EXTRA = 16


def grad_kernel(place_ref, *refs, orders, parts, chunk, more):
    ha_ref, hb_ref = refs[:2]
    refs = refs[2:]
    if more:
        oa_ref, ob_ref, ya_ref, yb_ref, gs_ref, g1_ref, g2_ref = refs[:7]
        refs = refs[7:]
    val_ref, *outs = refs[:5]
    turned = refs[5]
    rows = ha_ref.shape[0]
    k = pl.program_id(0)

    @pl.when(k == 0)
    def _():
        turned[:, :rows] = ha_ref[...].T
        turned[:, rows:] = hb_ref[...].T
        if more:
            refs[6][:, :rows] = oa_ref[...].T
            refs[6][:, rows:] = ob_ref[...].T

    if more:
        size = outs[0].shape[2]
        fill = lambda row: jnp.concatenate([row, jnp.zeros((1, size - row.shape[1]), f32)], axis=1)
        line = lax.broadcasted_iota(jnp.int32, (EXTRA, size), 0)
        units = fill(jnp.concatenate([gs_ref[0:1, :], gs_ref[1:2, :]], axis=1))
        steps = fill(jnp.concatenate([g1_ref[0:1, :], g2_ref[0:1, :]], axis=1))
        extra = jnp.where(line == 0, units, jnp.where(line == 1, steps, 0.0)).astype(bf16)

    value = dot(turned[...], val_ref[...]).astype(bf16)
    size = value.shape[1]
    if more:
        other = (dot(refs[6][:, :rows], ya_ref[...]) + dot(refs[6][:, rows:], yb_ref[...])).astype(bf16)

    for side in range(2):

        @pl.when((k < parts // 2) == (side == 0))
        def _(side=side):
            for which, ref in zip(orders[side], outs[2 * side : 2 * side + 2]):
                for j, r in enumerate(which):
                    at = slice(r * chunk, (r + 1) * chunk)
                    ref[j, :chunk, :size] = value[at, :]
                    if more:
                        ref[j, :chunk, size:] = other[at, :]
                        ref[j, chunk:, :] = extra


def weight_grads(place, sends, keeps, chips, hs, value, os=None, ys=None, extra=None):
    rows, width = hs[0].shape
    chunk = width // chips
    parts, _, size = value.shape
    more = os is not None
    hc = ys[1].shape[2] if more else 0
    tall = chunk + (EXTRA if more else 0)
    middle = parts // 2
    if chunk % 128:
        result = []
        for which, lo in ((sends[0], 0), (keeps[0], 0), (sends[1], middle), (keeps[1], middle)):
            cut = lambda pair: jnp.concatenate(
                [jnp.concatenate(pair, axis=0)[:, r * chunk : (r + 1) * chunk] for r in which], axis=1
            )
            found = []
            for k in range(lo, lo + middle):
                one = t_dot(cut(hs), value[k])
                if more:
                    at = (place[0] - k) % parts
                    y = lax.dynamic_index_in_dim(ys[0], at, 0, keepdims=False)
                    y = lax.dynamic_slice_in_dim(y, place[2] * hc, hc, 1)
                    y = jnp.concatenate([y, lax.dynamic_index_in_dim(ys[1], at, 0, keepdims=False)])
                    one = jnp.concatenate([one, t_dot(cut(os), y)], axis=1)
                one = one.reshape(len(which), chunk, size + hc)
                if more:
                    wide = jnp.broadcast_to(extra[k][None], (len(which), EXTRA, size + hc))
                    one = jnp.concatenate([one, wide], axis=1)
                found.append(one.astype(bf16))
            result.append(jnp.stack(found, axis=1))
        return [result[0], result[2]], [result[1], result[3]]
    whole = full_spec((rows, width))
    ins = list(hs)
    in_specs = [whole] * 2
    scratch = [pltpu.VMEM((width, 2 * rows), bf16)]
    if more:
        slot = lambda k, p: lax.rem(p[0] + parts - k, parts)
        cols = ys[0].shape[2]
        part = pl.BlockSpec((8, cols), lambda k, p: (0, slot(k, p) ^ p[1]))
        ins += [*os, ys[0], ys[1], *extra]
        in_specs += [whole] * 2
        in_specs += [
            pl.BlockSpec((None, rows, hc), lambda k, p: (slot(k, p), 0, p[2])),
            pl.BlockSpec((None, rows, hc), lambda k, p: (slot(k, p), 0, 0)),
            pl.BlockSpec((None, 8, size // 2), lambda k, p: (k, 0, 0)),
            part,
            part,
        ]
        scratch = scratch * 2
    ins.append(value)
    in_specs.append(pl.BlockSpec((None, 2 * rows, size), lambda k, p: (k, 0, 0)))
    lists = [sends[0], keeps[0], sends[1], keeps[1]]
    block = lambda one: (len(one), None, tall, size + hc)
    early = lambda k, p: (0, jnp.minimum(k, middle - 1), 0, 0)
    late = lambda k, p: (0, jnp.maximum(k - middle, 0), 0, 0)
    out = pl.pallas_call(
        functools.partial(
            grad_kernel, orders=(lists[:2], lists[2:]), parts=parts, chunk=chunk, more=more
        ),
        grid_spec=pltpu.PrefetchScalarGridSpec(
            num_scalar_prefetch=1,
            grid=(parts,),
            in_specs=in_specs,
            out_specs=[
                pl.BlockSpec(block(one), early if n < 2 else late) for n, one in enumerate(lists)
            ],
            scratch_shapes=scratch,
        ),
        out_shape=[
            jax.ShapeDtypeStruct((len(one), middle, tall, size + hc), bf16) for one in lists
        ],
        compiler_params=params(56),
    )(place, *ins)
    return [out[0], out[2]], [out[1], out[3]]


def pair_sum_kernel(ka_ref, ga_ref, kb_ref, gb_ref, a_ref, b_ref):
    a_ref[...] = (ka_ref[...].astype(f32) + ga_ref[...].astype(f32)).astype(bf16)
    b_ref[...] = (kb_ref[...].astype(f32) + gb_ref[...].astype(f32)).astype(bf16)


def pair_sums(kept, got, at):
    _, slots, tall, wide = kept[0].shape
    spec = lambda n: pl.BlockSpec((None, None, tall, wide), lambda k, n=n: (n, k, 0, 0))
    return pl.pallas_call(
        pair_sum_kernel,
        grid=(slots,),
        in_specs=[spec(at[0]), spec(at[0]), spec(at[1]), spec(at[1])],
        out_specs=[spec(0)] * 2,
        out_shape=[jax.ShapeDtypeStruct((1, slots, tall, wide), bf16)] * 2,
        compiler_params=params(56),
    )(kept[0], got[0], kept[1], got[1])


def adam_values(weight, grad, first, second):
    first_new = beta_one * first + (1.0 - beta_one) * grad
    second_new = beta_two * second + (1.0 - beta_two) * grad * grad
    moved = weight - learn_rate * (first_new / bias_one) / (
        jnp.sqrt(second_new / bias_two) + adam_eps
    )
    return first_new, second_new, moved


def lane_sums(value):
    ones = jnp.ones((8, value.shape[1]), bf16)
    high = value.astype(bf16)
    low = (value - high.astype(f32)).astype(bf16)
    return dot_t(ones, high) + dot_t(ones, low)


def adam_wide_kernel(w_ref, g_ref, m_ref, v_ref, g_out, m_out, v_out, n_out, s_out):
    cols = w_ref.shape[2]
    for c in range(w_ref.shape[1]):
        grad = g_ref[:, c * cols : (c + 1) * cols]
        first, second, moved = adam_values(w_ref[:, c, :], grad, m_ref[:, c, :], v_ref[:, c, :])
        g_out[:, c, :] = grad
        m_out[:, c, :] = first
        v_out[:, c, :] = second
        n_out[:, c, :] = moved
        s_out[c : c + 1, :] = jnp.sum(moved * moved, axis=0, keepdims=True)


def adam_wide(w, g, m, v):
    vmem = pl.BlockSpec(memory_space=pltpu.VMEM)
    return pl.pallas_call(
        adam_wide_kernel,
        in_specs=[vmem] * 4,
        out_specs=[vmem] * 5,
        out_shape=[jax.ShapeDtypeStruct(w.shape, f32)] * 4
        + [jax.ShapeDtypeStruct(w.shape[1:], f32)],
        compiler_params=params(16),
    )(w, g, m, v)


def adam_tall_kernel(w_ref, g_ref, m_ref, v_ref, g_out, m_out, v_out, n_out, s_out):
    grad = g_ref[...].T
    first, second, moved = adam_values(w_ref[...], grad, m_ref[...], v_ref[...])
    g_out[...] = grad
    m_out[...] = first
    v_out[...] = second
    n_out[...] = moved
    s_out[...] = lane_sums(moved * moved)


def adam_tall(w, g, m, v):
    vmem = pl.BlockSpec(memory_space=pltpu.VMEM)
    return pl.pallas_call(
        adam_tall_kernel,
        in_specs=[vmem] * 4,
        out_specs=[vmem] * 5,
        out_shape=[jax.ShapeDtypeStruct(w.shape, f32)] * 4
        + [jax.ShapeDtypeStruct((8, w.shape[0]), f32)],
        compiler_params=params(16),
    )(w, g, m, v)


def scale_kernel(na_ref, nb_ref, nc_ref, nd_ref, a_ref, b_ref, c_ref, d_ref, ao_ref, bo_ref, co_ref, do_ref, *, width):
    factor = lambda value: lax.rsqrt(value / width + layer_eps)
    for norm, ref, out in ((na_ref, a_ref, ao_ref), (nc_ref, c_ref, co_ref)):
        for c in range(ref.shape[1]):
            out[:, c, :] = ref[:, c, :] * factor(norm[c : c + 1, :])
    for norm, ref, out in ((nb_ref, b_ref, bo_ref), (nd_ref, d_ref, do_ref)):
        out[...] = ref[...] * factor(norm[...]).T[:, 0:1]


def scale_weights(norms, weights, width):
    vmem = pl.BlockSpec(memory_space=pltpu.VMEM)
    return pl.pallas_call(
        functools.partial(scale_kernel, width=width),
        in_specs=[vmem] * 8,
        out_specs=[vmem] * 4,
        out_shape=[jax.ShapeDtypeStruct(w.shape, f32) for w in weights],
        compiler_params=params(16),
    )(*norms, *weights)


def after(value, *others):
    return lax.optimization_barrier((value, *others))[0]


def per_device(
    layer_input,
    cotangent,
    positions,
    w_qkv,
    w_out,
    w_up,
    w_down,
    moment_qkv,
    moment_out,
    moment_up,
    moment_down,
    square_qkv,
    square_out,
    square_up,
    square_down,
    s_qk,
    alpha_attn,
    alpha_mlp,
    s_uv,
):
    nz = lax.axis_size("head")
    nb = lax.axis_size("batch")
    z = lax.axis_index("head")
    b = lax.axis_index("batch")
    core = b % 2
    chip = b // 2
    chips = nb // 2
    bits = [1 << n for n in range(int(math.log2(chips)))]
    rows, cols = layer_input.shape
    width = cols * nz
    own = rows // nz
    hid = w_down.shape[0]
    half = hid // 2
    hc = cols // 2
    heads = cols // HEAD_DIM
    span = w_qkv.shape[0]
    chunk = width // chips
    core_s = core.reshape(1).astype(jnp.int32)
    place = jnp.stack([z, chip, core]).astype(jnp.int32)
    fast = chunk == cols and chunk % 128 == 0

    def swap_batch(value, bit):
        return lax.ppermute(value, "batch", [(i, i ^ bit) for i in range(nb)])

    def swap_core(value):
        return swap_batch(value, 1)

    def swap_chip(value, bit):
        return swap_batch(value, 2 * bit)

    def onward(value, k=1):
        return lax.ppermute(value, "head", [(i, (i + k) % nz) for i in range(nz)])

    def exchange(value):
        return lax.all_to_all(value, "head", split_axis=0, concat_axis=0)

    def pick(pair, index):
        return jnp.where(index == 0, pair[0], pair[1])

    def relative(value):
        return jnp.concatenate(
            [
                lax.dynamic_slice_in_dim(value, (chip ^ r) * chunk, chunk, value.ndim - 1)
                for r in range(chips)
            ],
            axis=-1,
        )

    def spread(value):
        if chips <= 4:
            return [value] + [swap_chip(value, r) for r in range(1, chips)]
        for bit in bits:
            value = jnp.concatenate([value, swap_chip(value, bit)], axis=0)
        return [value]

    tokens = [layer_input, onward(layer_input)]
    mine, theirs = pack(core_s, w_up, s_uv, w_down, w_out)
    qkv_own = after(w_qkv, mine).reshape(span, 3 * cols).astype(bf16)
    qkv_full = lax.all_gather(qkv_own, "batch", axis=0, tiled=True)
    theirs = swap_core(theirs)
    packet = jnp.concatenate([pick((mine, theirs), core), pick((theirs, mine), core)], axis=0)
    hops = [packet, onward(packet)]
    slots = [spread(packet)]
    tokens[1], hops[1], places, alpha_attn, alpha_mlp = lax.optimization_barrier(
        (tokens[1], hops[1], positions, alpha_attn, alpha_mlp)
    )
    come, *last = lax.optimization_barrier((hops[1], *slots[0]))
    slots[0] = list(last)

    freqs = jnp.exp(
        (jnp.arange(128) % (HEAD_DIM // 2)).astype(f32) * (-2.0 * math.log(10000.0) / HEAD_DIM)
    )
    phase = places.astype(f32)[:, None] * freqs[None, :]
    side = jnp.where(jnp.arange(128) % HEAD_DIM < HEAD_DIM // 2, -1.0, 1.0).astype(f32)
    cosine, sine = jnp.cos(phase), jnp.sin(phase) * side[None, :]
    lane = jnp.arange(cols) // HEAD_DIM
    ones = (lane[:, None] == lane[None, :]).astype(bf16)
    gain = s_qk.reshape(1, cols)
    is_long = (places[SHORT : SHORT + 1] != 0).astype(jnp.int32)
    attn_gain = relative(alpha_attn[None])
    mlp_gain = relative(alpha_mlp[None])

    for n in range(2, nz):
        slots.append(spread(come if n == 2 else hops[-1]))
        tokens.append(onward(tokens[-1]))
        if n < nz - 1:
            hops.append(onward(hops[-1]))
            tokens[-1], hops[-1], cosine, sine, ones, attn_gain, mlp_gain, *last = (
                lax.optimization_barrier(
                    (tokens[-1], hops[-1], cosine, sine, ones, attn_gain, mlp_gain, *slots[-1])
                )
            )
            slots[-1] = list(last)
    last_hop, tokens[-1] = lax.optimization_barrier((hops[-1], tokens[-1]))
    hops.append(onward(last_hop))

    blocks = rows // 512
    middle = blocks // 2
    tokens_full, q, k, v, rho = qkv_project(place, tokens, qkv_full, cosine, sine, gain, ones)
    y_a, logs_a = attn_fwd(is_long, q, k, v, 0, middle)
    q_b, hops[-1], *last = lax.optimization_barrier((after(q, y_a), hops[-1], *slots[-1]))
    slots[-1] = list(last)
    slots.append(spread(hops[-1]))
    y_b, logs_b = attn_fwd(is_long, q_b, k, v, middle, blocks - middle)
    y_one = exchange(y_a.reshape(nz, own // 2, cols))
    y_in, y_one = lax.optimization_barrier((y_b, y_one))
    y_two = exchange(y_in.reshape(nz, own // 2, cols))
    flat = lambda value: value.transpose(1, 0, 2).reshape(own, width)
    start = tokens_full
    if not fast:
        start = jnp.concatenate(
            [
                lax.dynamic_slice_in_dim(tokens_full, h * (rows // 2) + z * (own // 2), own // 2, 0)
                for h in range(2)
            ]
        )
        start = relative(start)
    y_one, y_two, *last = lax.optimization_barrier((y_one, y_two, *slots[-1]))
    slots[-1] = list(last)
    hA, h1, h_own, stat, y_mine, y_other = attn_out(place, y_one, y_two, slots, start, attn_gain, chips, fast)
    h_got = swap_core(h_own)
    y_got = swap_core(y_other)
    h_got, y_got = lax.optimization_barrier((h_got, y_got))
    cot = after(cotangent, h_own).reshape(2, nz, own // 2, cols).transpose(1, 0, 2, 3)
    cot = exchange(cot.reshape(nz, own, cols))

    act, uv, mo_own, mo_other = mlp_fwd(h_own, h_got, slots, half)
    mo_got = swap_core(mo_other)
    if not fast:
        cot = relative(flat(cot))
    hidden, d_own, base, ga_mlp = loss(place, mo_own, mo_got, h1, cot, mlp_gain, chips, fast)
    d_got = swap_core(d_own)
    if not fast:
        hidden = relative(hidden).reshape(own, nz, cols).transpose(1, 0, 2)
    hidden = exchange(hidden)

    orders = [bits, bits[::-1]]
    sent_at = [[r for r in range(chips) if r & order[0]] for order in orders]
    kept_at = [[r for r in range(chips) if not r & order[0]] for order in orders]

    def second(kept, sent):
        found, sends = [], []
        if chips == 4:
            at = [[n for n, r in enumerate(left) if r & order[1]] for order, left in zip(orders, kept_at)]
            sends = pair_sums(kept, sent, [one[0] for one in at])
            for order, one, keep, got, send in zip(orders, at, kept, sent, sends):
                cut = lambda t, n=1 - one[0]: t[n : n + 1]
                found.append([cut(keep), cut(got), swap_chip(send, order[1])])
            return found, sends
        for order, left, got, keep in zip(orders, kept_at, sent, kept):
            terms = [keep, got]
            for bit in order[1:]:
                send_at = [n for n, r in enumerate(left) if r & bit]
                keep_at = [n for n, r in enumerate(left) if not r & bit]
                left = [left[n] for n in keep_at]
                cut = lambda v, at: jnp.concatenate([v[n : n + 1] for n in at], axis=0)
                send = sum(cut(t, send_at).astype(f32) for t in terms).astype(bf16)
                terms = [cut(t, keep_at) for t in terms] + [swap_chip(send, bit)]
                sends.append(send)
            found.append(terms)
        return found, sends

    def slot_sums(found):
        return [sum(t[0, n].astype(f32) for t in terms) for terms in found for n in range(nz // 2)]

    def wait_last(found, *others):
        return [terms[:-1] + [after(terms[-1], *others)] for terms in found]

    down_made, down_kept = weight_grads(place, sent_at, kept_at, chips, (d_own, d_got), act)
    down_sent = [swap_chip(one, order[0]) for one, order in zip(down_made, orders)]
    d_own, d_got, *_ = lax.optimization_barrier((d_own, d_got, *down_made))
    duv, dh_own, dh_other, gsuv = mlp_bwd(d_own, d_got, slots, uv, half)
    dh_got = swap_core(dh_other)
    down_sent = [after(one, dh_other) for one in down_sent]
    down_part, down_next = second(down_kept, down_sent)
    dh_own, hidden, *_ = lax.optimization_barrier((dh_own, hidden, *down_next))
    do_own, through, ga_attn, dy = first_back(
        place, dh_own, dh_got, base, h1, hA, start, stat, attn_gain, slots, chips, fast, cols
    )
    dy = exchange(dy)
    do_got = swap_core(do_own)

    extra = (gsuv, ga_attn, ga_mlp)
    if not fast:
        alphas = [relative(ga_attn[0:1]), relative(ga_mlp[0:1])]
        extra = []
        wide = 2 * half + hc
        fill = lambda r: jnp.pad(r, ((0, 0), (0, wide - r.shape[1])))
        for n in range(nz):
            at = ((z - n) % nz) * cols
            line = [lax.dynamic_slice_in_dim(g, at, cols, 1) for g in alphas]
            lines = [gsuv[n, :2].reshape(1, 2 * half), jnp.concatenate(line, axis=1)]
            lines = jnp.concatenate([fill(r) for r in lines])
            extra.append(jnp.pad(lines, ((0, EXTRA - 2), (0, 0))))
        extra = jnp.stack(extra)
    up_made, up_kept = weight_grads(
        place, sent_at, kept_at, chips, (h_own, h_got), duv, (do_own, do_got), (y_mine, y_got), extra
    )
    down_part = wait_last(down_part, *up_kept)
    down_last = [terms[-1] for terms in down_part]
    dy, *both = lax.optimization_barrier((dy, *up_made, *down_last))
    up_made, down_last = both[: len(up_made)], both[len(up_made) :]
    down_slots = slot_sums([t[:-1] + [last] for t, last in zip(down_part, down_last)])
    down_along = [onward(down_slots[n].astype(bf16), nz - n) for n in range(1, nz)]
    up_sent = [swap_chip(one, order[0]) for one, order in zip(up_made, orders)]

    dy = dy.reshape(nz, 2, own // 2, cols)
    common = lambda y, logs: (
        is_long, q, k, v, dy, y, logs, rho, cosine, sine, gain, ones
    )
    dqkv_b, dk_part, dv_part, sqk_b = attn_bwd(
        *common(y_b, logs_b), middle, blocks - middle, None
    )

    if not fast:
        through = relative(through).reshape(own, nz, cols).transpose(1, 0, 2)
    mine_at = z * (own // 2)
    qkv_parts = qkv_full.reshape(nz, cols, 3 * cols)

    def input_part(dqkv, side):
        part = jnp.einsum("tn,zcn->ztc", dqkv, qkv_parts, preferred_element_type=f32).astype(bf16)
        here = lax.dynamic_slice_in_dim(part, mine_at, own // 2, 1).astype(f32)
        more = after(through, dqkv)[:, side * (own // 2) : (side + 1) * (own // 2)]
        return lax.dynamic_update_slice_in_dim(part, (here + more.astype(f32)).astype(bf16), mine_at, 1)

    part_b = input_part(dqkv_b, 1)
    down_along = [after(one, dqkv_b) for one in down_along]
    part_got = exchange(part_b)
    dk_part, *_ = lax.optimization_barrier((dk_part, part_b, *down_along))
    dqkv_a, sqk_a = attn_bwd(*common(y_a, logs_a), 0, middle, [dk_part, dv_part])
    input_b = jnp.sum(after(part_got, dqkv_a).astype(f32), axis=0)
    up_part, up_next = second(up_kept, [after(one, dqkv_a) for one in up_sent])
    dqkv_a, *_ = lax.optimization_barrier((dqkv_a, *up_next))
    part_a = input_part(dqkv_a, 0)
    dqkv = jnp.concatenate([dqkv_a, dqkv_b], axis=0)
    grad_qkv = t_dot(tokens_full, dqkv).astype(bf16)
    up_part = wait_last(up_part, part_a, grad_qkv, *[terms[-1] for terms in up_part])
    up_slots = slot_sums(up_part)
    passed = up_slots[1].astype(bf16)
    part_a, grad_qkv, passed = lax.optimization_barrier((part_a, grad_qkv, passed))
    passed = onward(passed)
    for n in range(2, nz):
        if n == nz - 1:
            passed, part_a = lax.optimization_barrier((passed, part_a))
        passed = onward((up_slots[n] + passed.astype(f32)).astype(bf16))
    sum_up_t = up_slots[0] + passed.astype(f32)
    input_a = lax.psum_scatter(part_a.reshape(-1, cols), "head", scatter_dimension=0, tiled=True)
    input_grad = jnp.concatenate([input_a.astype(f32), input_b], axis=0)
    hidden_t = after(hidden, part_a).reshape(nz, 2, own // 2, cols).transpose(1, 0, 2, 3).reshape(rows, cols)

    sqk = jnp.pad((sqk_a + sqk_b), ((0, EXTRA - 8), (0, 2 * cols)))
    shard = [lax.dynamic_slice_in_dim(grad_qkv, (b ^ r) * span, span, 0) for r in range(nb)]
    shard = [jnp.concatenate([s, sqk.astype(bf16)], axis=0) for s in shard]
    qbits = [1 << n for n in range(int(math.log2(nb)))]
    held = {r: shard[r] for r in range(nb)}
    for bit in qbits:
        send_at = [r for r in held if r & bit]
        send = jnp.concatenate([held[r] for r in send_at], axis=0).astype(bf16)
        got = swap_batch(send, bit)
        size = span + EXTRA
        held = {
            r ^ bit: held[r ^ bit].astype(f32) + got[n * size : (n + 1) * size].astype(f32)
            for n, r in enumerate(send_at)
        }
    cell = width // (nz * nb)
    sum_sqk = lax.dynamic_slice_in_dim(held[0][span, :cols], b * cell, cell, 0)
    w_late, m_late, v_late, _ = lax.optimization_barrier((w_qkv, moment_qkv, square_qkv, part_a))
    qkv_new = adam_wide(w_late, held[0][:span], m_late, v_late)

    def both_halves(total):
        two = (total[:span], total[span : 2 * span])
        here = jnp.concatenate([pick(two, core), total[2 * span :]], axis=0)
        there = jnp.concatenate([pick(two, 1 - core), total[2 * span :]], axis=0)
        there = swap_core(there.astype(bf16)).astype(f32)
        return [pick((here, there), core), pick((there, here), core)]

    join = lambda halves, at, size: [p[:span, at : at + size] for p in halves]
    down_along = [after(one, part_a) for one in down_along]
    halves = both_halves(down_slots[0] + sum(one.astype(f32) for one in down_along))
    down_new = adam_tall(w_down, jnp.concatenate(join(halves, 0, half), axis=1), moment_down, square_down)
    halves = both_halves(sum_up_t)
    grad_up = jnp.concatenate(join(halves, 0, half) + join(halves, half, half), axis=1)
    grad_up = grad_up * s_uv.reshape(1, 2 * hid)
    up_new = adam_wide(w_up, grad_up, moment_up, square_up)
    out_new = adam_tall(w_out, jnp.concatenate(join(halves, 2 * half, hc), axis=1), moment_out, square_out)
    suv_rows = jnp.stack(
        [jnp.concatenate([p[span, c * half : (c + 1) * half] for p in halves]) for c in range(2)]
    )
    suv_rows = suv_rows / s_uv
    sum_suv = lax.dynamic_slice_in_dim(suv_rows, b * (hid // nb), hid // nb, 1)
    alphas = halves[0][span + 1] + halves[1][span + 1]
    sum_attn = lax.dynamic_slice_in_dim(alphas[:cols], b * cell, cell, 0)
    sum_mlp = lax.dynamic_slice_in_dim(alphas[cols : 2 * cols], b * cell, cell, 0)

    hidden = hidden_t.astype(f32)

    squares = [qkv_new[4], out_new[4][:1], up_new[4], down_new[4][:1]]
    sizes = [t.size for t in squares]
    norms = jnp.concatenate([t.reshape(-1) for t in squares]).reshape(-1, 128)
    for bit in qbits:
        norms = norms + swap_batch(norms, bit)
    norms = norms.reshape(-1)
    ends = [0] + [sum(sizes[: n + 1]) for n in range(4)]
    back = lambda n, shape: norms[ends[n] : ends[n + 1]].reshape(shape)
    eight = lambda value: jnp.broadcast_to(value, (8, value.shape[1]))
    new_qkv, new_out, new_up, new_down = scale_weights(
        [back(0, (3, cols)), eight(back(1, (1, cols))), back(2, (2, hid)), eight(back(3, (1, hid)))],
        [qkv_new[3], out_new[3], up_new[3], down_new[3]],
        width,
    )
    sum_qkv, first_a, second_a = qkv_new[:3]
    sum_out, first_b, second_b = out_new[:3]
    sum_up, first_c, second_c = up_new[:3]
    sum_down, first_d, second_d = down_new[:3]
    return (
        hidden,
        input_grad,
        sum_qkv,
        sum_out,
        sum_up,
        sum_down,
        first_a,
        first_b,
        first_c,
        first_d,
        second_a,
        second_b,
        second_c,
        second_d,
        new_qkv,
        new_out,
        new_up,
        new_down,
        sum_sqk,
        sum_attn,
        sum_mlp,
        sum_suv,
    )


def solution(mesh):
    tokens = P("batch", "head")
    wide = P("batch", None, "head")
    tall = P("head", "batch")
    flat = P(("head", "batch"))
    weights = (wide, tall, wide, tall)
    return jax.shard_map(
        per_device,
        mesh=mesh,
        in_specs=(tokens, tokens, P("batch"))
        + weights * 3
        + (P("head"), P(), P(), P(None, "head")),
        out_specs=(tokens, tokens) + weights * 4 + (flat, flat, flat, P(None, ("head", "batch"))),
        check_vma=False,
    )
```

```python
import functools
import math

import jax
import jax.numpy as jnp
from jax import lax
from jax.experimental import pallas as pl
from jax.experimental.pallas import tpu as pltpu
from jax.sharding import PartitionSpec as P

HEAD_DIM = 64
SHORT = 1024

layer_eps = 1e-06
learn_rate = 0.008
beta_one = 0.9
beta_two = 0.95
adam_eps = 1e-08
bias_one = 1.0 - math.exp(100.0 * math.log(0.9))
bias_two = 1.0 - math.exp(100.0 * math.log(0.95))
score_scale = 8.0
LOG2E = math.log2(math.e)
LN2 = math.log(2.0)

bf16 = jnp.bfloat16
f32 = jnp.float32


def dot(a, b):
    return jnp.dot(a, b, preferred_element_type=f32)


def dot_t(a, b):
    return lax.dot_general(a, b, (((1,), (1,)), ((), ())), preferred_element_type=f32)


def t_dot(a, b):
    return lax.dot_general(a, b, (((0,), (0,)), ((), ())), preferred_element_type=f32)


def params(mib):
    return pltpu.CompilerParams(vmem_limit_bytes=mib * 1024 * 1024)


def full_spec(shape):
    return pl.BlockSpec(shape, lambda *_: (0,) * len(shape))


def head_sum(value, ones):
    high = value.astype(bf16)
    low = (value - high.astype(f32)).astype(bf16)
    return dot(high, ones) + dot(low, ones)


def widen(value, cols):
    return jnp.concatenate([value] * (cols // value.shape[1]), axis=1)


def swap_halves(value):
    cols = value.shape[-1]
    half = HEAD_DIM // 2
    lane = lax.broadcasted_iota(jnp.int32, value.shape, 1)
    first = (lane % HEAD_DIM) < half
    up = pltpu.roll(value, cols - half, 1)
    down = pltpu.roll(value, half, 1)
    return jnp.where(first, up, down)


def qkv_kernel(place_ref, *refs, parts):
    tokens = refs[:parts]
    w_ref, cos_ref, sin_ref, gain_ref, ones_ref, x_ref, q_ref, k_ref, v_ref, rho_ref = refs[parts:]
    cols = v_ref.shape[1]
    z = place_ref[0]
    for n in range(parts):
        at = pl.multiple_of(lax.rem(z + parts - n, parts) * cols, cols)
        x_ref[:, pl.ds(at, cols)] = tokens[n][...]
    proj = dot(x_ref[...], w_ref[...])
    cosine = widen(cos_ref[...], cols)
    sine = widen(sin_ref[...], cols)
    ones = ones_ref[...]
    gain = gain_ref[...]
    heads = cols // HEAD_DIM
    lane = lax.broadcasted_iota(jnp.int32, rho_ref.shape, 1)
    stats = jnp.zeros(rho_ref.shape, f32)
    for c, (out, scale) in enumerate(((q_ref, score_scale * LOG2E), (k_ref, 1.0))):
        part = proj[:, c * cols : (c + 1) * cols]
        rho = lax.rsqrt(head_sum(part * part, ones) + layer_eps)
        rot = part * cosine + swap_halves(part) * sine
        out[...] = (rot * rho * (gain * scale)).astype(bf16)
        for h in range(heads):
            stats = jnp.where(lane == c * heads + h, rho[:, h * HEAD_DIM : h * HEAD_DIM + 1], stats)
    rho_ref[...] = stats
    v_ref[...] = proj[:, 2 * cols :].astype(bf16)


def qkv_project(place, tokens, w, cosine, sine, gain, ones):
    rows, cols = tokens[0].shape
    parts = len(tokens)
    width = parts * cols
    blk = 512
    row = lambda n: pl.BlockSpec((blk, n), lambda i, s: (i, 0))
    return pl.pallas_call(
        functools.partial(qkv_kernel, parts=parts),
        grid_spec=pltpu.PrefetchScalarGridSpec(
            num_scalar_prefetch=1,
            grid=(rows // blk,),
            in_specs=[row(cols)] * parts
            + [full_spec((width, 3 * cols)), row(128), row(128)]
            + [full_spec((1, cols)), full_spec((cols, cols))],
            out_specs=[row(width)] + [row(cols)] * 3 + [row(128)],
        ),
        out_shape=[jax.ShapeDtypeStruct((rows, width), bf16)]
        + [jax.ShapeDtypeStruct((rows, cols), bf16)] * 3
        + [jax.ShapeDtypeStruct((rows, 128), f32)],
        compiler_params=params(56),
    )(place, *tokens, w, cosine, sine, gain, ones)


def head_masks(cols, heads):
    lane = lax.broadcasted_iota(jnp.int32, (1, cols), 1) // HEAD_DIM
    return [(lane == h) for h in range(heads)]


def masked(value, mask):
    return jnp.where(mask, value, jnp.zeros_like(value))


def attn_fwd_kernel(long_ref, q_ref, k_ref, v_ref, y_ref, l_ref, acc, mass, *, heads, blk, sub, first):
    i = first + pl.program_id(0)
    cols = q_ref.shape[1]
    masks = head_masks(cols, heads)
    per = SHORT // blk
    low = jnp.where(long_ref[0] != 0, 0, (i // per) * per)
    acc[...] = jnp.zeros_like(acc)
    mass[...] = jnp.zeros_like(mass)

    def lanes(p):
        total = p[:, 0:128]
        for n in range(1, p.shape[1] // 128):
            total = total + p[:, n * 128 : (n + 1) * 128]
        return total

    def body(j, carry):
        start = pl.multiple_of(j * blk, blk)
        keys = k_ref[pl.ds(start, blk), :]
        vals = v_ref[pl.ds(start, blk), :]
        q = q_ref[...]
        total = jnp.zeros(acc.shape, f32)
        for h in range(heads):
            p = jnp.exp2(dot_t(masked(q, masks[h]), keys))
            mass[h] += lanes(p)
            total += dot(p.astype(bf16), masked(vals, masks[h]))
        acc[...] += total
        return carry

    lax.fori_loop(low, i, body, 0)
    start = pl.multiple_of(i * blk, blk)
    causal = lax.broadcasted_iota(jnp.int32, (sub, sub), 0) >= lax.broadcasted_iota(
        jnp.int32, (sub, sub), 1
    )
    for a in range(blk // sub):
        rows = slice(a * sub, (a + 1) * sub)
        q = q_ref[rows, :]
        for b in range(a + 1):
            at = pl.multiple_of(start + b * sub, sub)
            keys = k_ref[pl.ds(at, sub), :]
            vals = v_ref[pl.ds(at, sub), :]
            total = jnp.zeros((sub, cols), f32)
            for h in range(heads):
                p = jnp.exp2(dot_t(masked(q, masks[h]), keys))
                if a == b:
                    p = jnp.where(causal, p, 0.0)
                mass[h, rows, :] += lanes(p)
                total += dot(p.astype(bf16), masked(vals, masks[h]))
            acc[rows, :] += total
    inverse = jnp.zeros(acc.shape, f32)
    logs = jnp.zeros(l_ref.shape, f32)
    lane = lax.broadcasted_iota(jnp.int32, l_ref.shape, 1)
    for h in range(heads):
        column = jnp.sum(mass[h], axis=1, keepdims=True)
        inverse = jnp.where(masks[h], 1.0 / column, inverse)
        logs = jnp.where(lane == h, jnp.log2(column), logs)
    y_ref[...] = (acc[...] * inverse).astype(bf16)
    l_ref[...] = logs


def attn_fwd(is_long, q, k, v, first, count):
    rows, cols = q.shape
    heads = cols // HEAD_DIM
    blk, sub = 512, 256
    row = lambda n: pl.BlockSpec((blk, n), lambda i, s: (i, 0))
    whole = pl.BlockSpec(((first + count) * blk, cols), lambda i, s: (0, 0))
    return pl.pallas_call(
        functools.partial(attn_fwd_kernel, heads=heads, blk=blk, sub=sub, first=first),
        grid_spec=pltpu.PrefetchScalarGridSpec(
            num_scalar_prefetch=1,
            grid=(count,),
            in_specs=[pl.BlockSpec((blk, cols), lambda i, s: (first + i, 0)), whole, whole],
            out_specs=[row(cols), row(128)],
            scratch_shapes=[pltpu.VMEM((blk, cols), f32), pltpu.VMEM((heads, blk, 128), f32)],
        ),
        out_shape=[
            jax.ShapeDtypeStruct((count * blk, cols), bf16),
            jax.ShapeDtypeStruct((count * blk, 128), f32),
        ],
        compiler_params=params(56),
    )(is_long, q, k, v)


def attn_bwd_kernel(
    long_ref, q_ref, qk_ref, dy_ref, y_ref, l_ref, k_ref, v_ref, rho_ref, cos_ref, sin_ref, gain_ref,
    ones_ref, dk_in, dv_in, out_ref, dk_out, dv_out, s_ref, acc, dk_acc, dv_acc, stats, dys, *, heads, blk, sub, first, count
):
    step = pl.program_id(0)
    local = count - 1 - step
    i = first + local
    cols = q_ref.shape[1]
    masks = head_masks(cols, heads)
    per = SHORT // blk
    low = jnp.where(long_ref[0] != 0, 0, (i // per) * per)
    ones = ones_ref[...]
    gain = gain_ref[...]

    @pl.when(step == 0)
    def _():
        dk_acc[...] = jnp.zeros_like(dk_acc)
        dv_acc[...] = jnp.zeros_like(dv_acc)
        s_ref[...] = jnp.zeros_like(s_ref)
        if dk_in is not None:
            dk_acc[...] = dk_in[...]
            dv_acc[...] = dv_in[...]

    acc[...] = jnp.zeros_like(acc)
    dys[...] = dy_ref[...].reshape(dys.shape)
    prod = dys[...].astype(f32) * y_ref[...].astype(f32)
    high = prod.astype(bf16)
    rest = (prod - high.astype(f32)).astype(bf16)
    pickers = (
        lax.broadcasted_iota(jnp.int32, (8, cols), 1) // HEAD_DIM
        == lax.broadcasted_iota(jnp.int32, (8, cols), 0)
    ).astype(bf16)
    stats[0:8, :] = dot_t(pickers, high) + dot_t(pickers, rest)
    stats[8:16, :] = l_ref[...].T[0:8, :]

    def piece(at, size, rows, causal):
        keys = k_ref[pl.ds(at, size), :]
        vals = v_ref[pl.ds(at, size), :]
        q = q_ref[rows, :]
        dy = dys[rows, :]
        total_q = jnp.zeros(q.shape, f32)
        total_k = jnp.zeros(keys.shape, f32)
        total_v = jnp.zeros(keys.shape, f32)
        for h in range(heads):
            qm = masked(q, masks[h])
            dym = masked(dy, masks[h])
            p = jnp.exp2(dot_t(keys, qm) - stats[8 + h : 9 + h, rows])
            if causal is not None:
                p = jnp.where(causal, p, 0.0)
            ds = (p * (dot_t(vals, dym) - stats[h : h + 1, rows])).astype(bf16)
            total_v += dot(p.astype(bf16), dym)
            total_k += dot(ds, qm)
            total_q += t_dot(ds, masked(keys, masks[h]))
        acc[rows, :] += total_q
        dk_acc[pl.ds(at, size), :] += total_k
        dv_acc[pl.ds(at, size), :] += total_v

    def body(j, carry):
        piece(pl.multiple_of(j * blk, blk), blk, slice(0, blk), None)
        return carry

    lax.fori_loop(low, i, body, 0)
    start = pl.multiple_of(i * blk, blk)
    causal = lax.broadcasted_iota(jnp.int32, (sub, sub), 0) <= lax.broadcasted_iota(
        jnp.int32, (sub, sub), 1
    )
    for a in range(blk // sub):
        for b in range(a + 1):
            piece(
                pl.multiple_of(start + b * sub, sub),
                sub,
                slice(a * sub, (a + 1) * sub),
                causal if a == b else None,
            )
    cosine = widen(cos_ref[...], cols)
    sine = widen(sin_ref[...], cols)
    total = jnp.zeros((1, cols), f32)
    here = pl.ds(start, blk)
    for c, (value, unit, up, scale) in enumerate(
        (
            (acc[...], q_ref[...], score_scale, score_scale * LOG2E),
            (dk_acc[here, :], k_ref[here, :], LN2, 1.0),
        )
    ):
        rho = jnp.zeros(value.shape, f32)
        for h in range(heads):
            at = c * heads + h
            rho = jnp.where(masks[h], rho_ref[:, at : at + 1], rho)
        grad = value * up
        unit = unit.astype(f32) * (1.0 / (gain * scale))
        total += jnp.sum(grad * unit, axis=0, keepdims=True)
        grad = grad * gain
        back = rho * (grad - unit * head_sum(grad * unit, ones))
        turned = back * cosine - swap_halves(back) * sine
        out_ref[:, c * cols : (c + 1) * cols] = turned.astype(bf16)
    out_ref[:, 2 * cols :] = dv_acc[here, :].astype(bf16)
    s_ref[0:1, :] += total
    if dk_out is not None:
        @pl.when(step == count - 1)
        def _():
            dk_out[...] = dk_acc[0 : first * blk, :]
            dv_out[...] = dv_acc[0 : first * blk, :]


def attn_bwd(is_long, q, k, v, dy, y, logs, rho, cosine, sine, gain, ones, first, count, carry):
    rows, cols = q.shape
    heads = cols // HEAD_DIM
    blk, sub = 512, 256
    top = (first + count) * blk
    at = lambda s: first + count - 1 - s
    row = lambda n: pl.BlockSpec((blk, n), lambda s, m: (at(s), 0))
    whole = pl.BlockSpec((top, cols), lambda s, m: (0, 0))
    ins = [q, k, dy, y, logs, k, v, rho, cosine, sine, gain, ones]
    mine = lambda n: pl.BlockSpec((blk, n), lambda s, m: (count - 1 - s, 0))
    share = dy.shape[2]
    half_at = 1 if first else 0
    in_specs = [row(cols)] * 2
    in_specs.append(
        pl.BlockSpec((blk // share, None, share, cols), lambda s, m: (count - 1 - s, half_at, 0, 0))
    )
    in_specs += [mine(cols), mine(128), whole, whole] + [row(128)] * 3
    in_specs += [full_spec((1, cols)), full_spec((cols, cols))]
    body = functools.partial(
        attn_bwd_kernel, heads=heads, blk=blk, sub=sub, first=first, count=count
    )
    outs = [jax.ShapeDtypeStruct((count * blk, 3 * cols), bf16)]
    out_specs = [pl.BlockSpec((blk, 3 * cols), lambda s, m: (count - 1 - s, 0))]
    if first:
        outs += [jax.ShapeDtypeStruct((first * blk, cols), f32)] * 2
        out_specs += [full_spec((first * blk, cols))] * 2
        inner = lambda *r: body(*r[:13], None, None, *r[13:])
    else:
        ins += carry
        in_specs += [full_spec((top, cols))] * 2
        inner = lambda *r: body(*r[:16], None, None, *r[16:])
    outs.append(jax.ShapeDtypeStruct((8, cols), f32))
    out_specs.append(full_spec((8, cols)))
    return pl.pallas_call(
        inner,
        grid_spec=pltpu.PrefetchScalarGridSpec(
            num_scalar_prefetch=1,
            grid=(count,),
            in_specs=in_specs,
            out_specs=out_specs,
            scratch_shapes=[
                pltpu.VMEM((blk, cols), f32),
                pltpu.VMEM((top, cols), f32),
                pltpu.VMEM((top, cols), f32),
                pltpu.VMEM((16, blk), f32),
                pltpu.VMEM((blk, cols), bf16),
            ],
        ),
        out_shape=outs,
        compiler_params=params(56),
    )(is_long, *ins)


def row_norm(value):
    return lax.rsqrt(jnp.mean(value * value, axis=1, keepdims=True) + layer_eps)


def norm_back(scale, result, grad):
    return scale * (grad - result * jnp.mean(grad * result, axis=1, keepdims=True))


def pack_kernel(core_ref, up_ref, gain_ref, down_ref, out_ref, mine_ref, theirs_ref):
    half = up_ref.shape[2] // 2
    low = core_ref[0] == 0
    down = down_ref[...].astype(bf16).T
    out = out_ref[...].astype(bf16).T
    for ref, first in ((mine_ref, low), (theirs_ref, jnp.logical_not(low))):
        for c in range(2):
            gain = gain_ref[c : c + 1, :]
            ref[:, c * half : (c + 1) * half] = jnp.where(
                first, up_ref[:, c, :half] * gain[:, :half], up_ref[:, c, half:] * gain[:, half:]
            ).astype(bf16)
        ref[:, 2 * half : 3 * half] = jnp.where(first, down[:, :half], down[:, half:])
        ref[:, 3 * half :] = out


def pack(core, w_up, gain, w_down, w_out):
    span, _, hid = w_up.shape
    cols = w_out.shape[0]
    vmem = pl.BlockSpec(memory_space=pltpu.VMEM)
    return pl.pallas_call(
        pack_kernel,
        in_specs=[pl.BlockSpec(memory_space=pltpu.SMEM)] + [vmem] * 4,
        out_specs=[vmem] * 2,
        out_shape=[jax.ShapeDtypeStruct((span, 3 * hid // 2 + cols), bf16)] * 2,
        compiler_params=params(16),
    )(core, w_up, gain, w_down, w_out)


def place_of(r, chip, chunk):
    return pl.ds(pl.multiple_of((r ^ chip) * chunk, chunk), chunk)


def put_relative(ref, chip, chips, fast):
    if not fast:
        return ref[...]
    if len(ref.shape) == 3:
        return jnp.concatenate([ref[r ^ chip] for r in range(chips)], axis=1)
    chunk = ref.shape[1] // chips
    return jnp.concatenate([ref[:, place_of(r, chip, chunk)] for r in range(chips)], axis=1)


def put_natural(ref, value, chip, chips, fast):
    if not fast:
        ref[...] = value
        return
    chunk = value.shape[1] // chips
    for r in range(chips):
        part = value[:, r * chunk : (r + 1) * chunk]
        if len(ref.shape) == 3:
            ref[r ^ chip] = part
        else:
            ref[:, place_of(r, chip, chunk)] = part


def attn_out_kernel(place_ref, *refs, counts, chips, fast):
    total = sum(counts)
    flat, refs = refs[:total], refs[total:]
    ya_ref, yb_ref, x_ref, alpha_ref, ha_ref, h1_ref, hb_ref, stat_ref, all_ref, half_ref, acc = refs
    z, chip, low = place_ref[0], place_ref[1], place_ref[2] == 0
    parts = len(counts)
    early = pl.program_id(0) == 0
    index = 0
    for n in range(parts):
        at = lax.rem(z + parts - n, parts)
        y = jnp.where(early, ya_ref[at], yb_ref[at])
        hc = y.shape[1] // 2
        all_ref[at] = y
        half_ref[at] = jnp.where(low, y[:, hc:], y[:, :hc])
        column = 0
        for piece in flat[index : index + counts[n]]:
            part = slice(column, column + piece.shape[0])
            if n == 0:
                acc[:, part] = dot_t(y, piece[...])
            else:
                acc[:, part] += dot_t(y, piece[...])
            column += piece.shape[0]
        index += counts[n]
    total = acc[...]
    norm = row_norm(total)
    hidden = total * norm
    start = put_relative(x_ref, chip, chips, fast).astype(f32)
    mixed = start + alpha_ref[...] * (hidden - start)
    first_norm = row_norm(mixed)
    out = mixed * first_norm
    ha_ref[...] = hidden
    h1_ref[...] = out
    hb_ref[...] = out.astype(bf16)
    lane = lax.broadcasted_iota(jnp.int32, stat_ref.shape, 1)
    stat_ref[...] = jnp.where(lane == 0, norm, first_norm)


def own_rows(blk, parts, width, fast):
    if fast:
        return pl.BlockSpec((blk, width), lambda i, s: (i * parts + s[0], 0))
    return pl.BlockSpec((blk, width), lambda i, s: (i, 0))


def out_weights(slots, cols):
    flat = [p for slot in slots for p in slot]
    last = flat[0].shape[1] // cols - 1
    return flat, [pl.BlockSpec((p.shape[0], cols), lambda i, s: (0, last)) for p in flat]


def attn_out(place, ya, yb, slots, x, alpha, chips, fast):
    parts, blk, cols = ya.shape
    width = x.shape[1]
    rows = 2 * blk
    row = lambda n: pl.BlockSpec((blk, n), lambda i, s: (i, 0))
    flat, specs = out_weights(slots, cols)
    return pl.pallas_call(
        functools.partial(attn_out_kernel, counts=[len(t) for t in slots], chips=chips, fast=fast),
        grid_spec=pltpu.PrefetchScalarGridSpec(
            num_scalar_prefetch=1,
            grid=(2,),
            in_specs=specs
            + [full_spec(ya.shape)] * 2
            + [own_rows(blk, parts, width, fast), full_spec((1, width))],
            out_specs=[row(width)] * 3
            + [row(128)]
            + [pl.BlockSpec((parts, blk, n), lambda i, s: (0, i, 0)) for n in (cols, cols // 2)],
            scratch_shapes=[pltpu.VMEM((blk, width), f32)],
        ),
        out_shape=[jax.ShapeDtypeStruct((rows, width), d) for d in (f32, f32, bf16)]
        + [jax.ShapeDtypeStruct((rows, 128), f32)]
        + [jax.ShapeDtypeStruct((parts, rows, n), bf16) for n in (cols, cols // 2)],
        compiler_params=params(56),
    )(place, *flat, ya, yb, x, alpha)


def loss_kernel(place_ref, own_ref, got_ref, h1_ref, cot_ref, alpha_ref, hidden_ref, dmo_ref, base_ref, ga_ref, *, chips, fast):
    chip = place_ref[1]
    total = own_ref[...] + got_ref[...].astype(f32)
    alpha = alpha_ref[...]
    norm = row_norm(total)
    inner = total * norm
    h1 = h1_ref[...]
    mixed = h1 + alpha * (inner - h1)
    last = row_norm(mixed)
    hidden = mixed * last
    grad = norm_back(last, hidden, put_relative(cot_ref, chip, chips, fast).astype(f32))
    put_natural(hidden_ref, hidden.astype(bf16), chip, chips, fast)
    base_ref[...] = (1.0 - alpha) * grad
    dmo_ref[...] = norm_back(norm, inner, alpha * grad).astype(bf16)

    @pl.when(pl.program_id(0) == 0)
    def _():
        ga_ref[...] = jnp.zeros_like(ga_ref)

    ga_ref[0:1, :] += jnp.sum(grad * (inner - h1), axis=0, keepdims=True)


def loss(place, own, got, h1, cot, alpha, chips, fast):
    rows, width = own.shape
    blk = rows // 2
    row = pl.BlockSpec((blk, width), lambda i, s: (i, 0))
    part = row
    if fast:
        part = pl.BlockSpec((chips, blk, width // chips), lambda i, s: (0, i, 0))
    return pl.pallas_call(
        functools.partial(loss_kernel, chips=chips, fast=fast),
        grid_spec=pltpu.PrefetchScalarGridSpec(
            num_scalar_prefetch=1,
            grid=(rows // blk,),
            in_specs=[row] * 3 + [part, full_spec((1, width))],
            out_specs=[part] + [row] * 2 + [full_spec((8, width))],
        ),
        out_shape=[jax.ShapeDtypeStruct(cot.shape, bf16)]
        + [jax.ShapeDtypeStruct((rows, width), d) for d in (bf16, f32)]
        + [jax.ShapeDtypeStruct((8, width), f32)],
        compiler_params=params(56),
    )(place, own, got, h1, cot, alpha)


def first_back_kernel(place_ref, *refs, counts, chips, fast):
    total = sum(counts)
    flat, refs = refs[:total], refs[total:]
    own_ref, got_ref, base_ref, h1_ref, ha_ref, x_ref, stat_ref, alpha_ref = refs[:8]
    do_ref, through_ref, ga_ref, dy_ref = refs[8:]
    z, chip = place_ref[0], place_ref[1]
    alpha = alpha_ref[...]
    grad = base_ref[...] + own_ref[...] + got_ref[...].astype(f32)
    grad = norm_back(stat_ref[:, 1:2], h1_ref[...], grad)
    ha = ha_ref[...]
    put_natural(through_ref, ((1.0 - alpha) * grad).astype(bf16), chip, chips, fast)
    back = norm_back(stat_ref[:, 0:1], ha, alpha * grad).astype(bf16)
    do_ref[...] = back
    parts = len(counts)
    step = pl.program_id(0)
    index = 0
    for n in range(parts):
        at = lax.rem(z + parts - n, parts)
        part = jnp.zeros(dy_ref.shape[1:], f32)
        column = 0
        for piece in flat[index : index + counts[n]]:
            part += dot(back[:, column : column + piece.shape[0]], piece[...])
            column += piece.shape[0]
        index += counts[n]
        dy_ref[at] = part.astype(bf16)

    @pl.when(step == 0)
    def _():
        ga_ref[...] = jnp.zeros_like(ga_ref)

    start = put_relative(x_ref, chip, chips, fast).astype(f32)
    ga_ref[0:1, :] += jnp.sum(grad * (ha - start), axis=0, keepdims=True)


def first_back(place, own, got, base, h1, ha, x, stat, alpha, slots, chips, fast, cols):
    rows, width = own.shape
    parts = len(slots)
    blk = rows // 2
    row = lambda n: pl.BlockSpec((blk, n), lambda i, s: (i, 0))
    flat, specs = out_weights(slots, cols)
    through, shape = row(width), (rows, width)
    if fast:
        through = pl.BlockSpec((parts, blk, cols), lambda i, s: (0, i, 0))
        shape = (parts, rows, cols)
    return pl.pallas_call(
        functools.partial(first_back_kernel, counts=[len(t) for t in slots], chips=chips, fast=fast),
        grid_spec=pltpu.PrefetchScalarGridSpec(
            num_scalar_prefetch=1,
            grid=(2,),
            in_specs=specs
            + [row(width)] * 5
            + [own_rows(blk, parts, width, fast), row(128), full_spec((1, width))],
            out_specs=[row(width), through]
            + [full_spec((8, width)), pl.BlockSpec((parts, blk, cols), lambda i, s: (0, i, 0))],
        ),
        out_shape=[jax.ShapeDtypeStruct((rows, width), bf16), jax.ShapeDtypeStruct(shape, bf16)]
        + [
            jax.ShapeDtypeStruct((8, width), f32),
            jax.ShapeDtypeStruct((parts, rows, cols), bf16),
        ],
        compiler_params=params(56),
    )(place, *flat, own, got, base, h1, ha, x, stat, alpha)


def fetch_weights(q, slots, wbuf, sems):
    def copies(j):
        at = 0
        found = []
        for p, piece in enumerate(slots[j]):
            size = piece.shape[0]
            found.append(
                pltpu.make_async_copy(
                    piece.at[:, : wbuf.shape[2]], wbuf.at[j % 2, at : at + size, :], sems.at[j % 2, p]
                )
            )
            at += size
        return found

    for j in range(len(slots)):

        @pl.when(q == j)
        def _(j=j):
            if j == 0:
                for copy in copies(0):
                    copy.start()
            if j + 1 < len(slots):
                for copy in copies(j + 1):
                    copy.start()
            for copy in copies(j):
                copy.wait()


def mlp_fwd_kernel(*refs, half, counts):
    total = sum(counts)
    flat, refs = refs[:total], refs[total:]
    slots, at = [], 0
    for n in counts:
        slots.append(flat[at : at + n])
        at += n
    ha_ref, hb_ref, act_ref, uv_ref, own_ref, got_ref, acc, wbuf, sems = refs
    rows = ha_ref.shape[0]
    q = pl.program_id(0)

    @pl.when(q == 0)
    def _():
        own_ref[...] = jnp.zeros_like(own_ref)
        acc[...] = jnp.zeros_like(acc)

    fetch_weights(q, slots, wbuf, sems)
    w = wbuf.at[lax.rem(q, 2)]
    for base, h_ref, sum_ref in ((0, ha_ref, own_ref), (rows, hb_ref, acc)):
        at = slice(base, base + rows)
        pair = dot(h_ref[...], w[:, : 2 * half])
        lifted = pair[:, :half]
        gated = pair[:, half:]
        act = (lifted * gated * jax.nn.sigmoid(gated)).astype(bf16)
        uv_ref[at, :] = pair.astype(bf16)
        act_ref[at, :] = act
        sum_ref[...] += dot_t(act, w[:, 2 * half : 3 * half])

    @pl.when(q == pl.num_programs(0) - 1)
    def _():
        got_ref[...] = acc[...].astype(bf16)


def mlp_fwd(ha, hb, slots, half):
    rows, width = ha.shape
    parts = len(slots)
    take = lambda n: pl.BlockSpec((None, 2 * rows, n), lambda q: (q, 0, 0))
    whole = full_spec((rows, width))
    anywhere = pl.BlockSpec(memory_space=pl.ANY)
    flat = [p for slot in slots for p in slot]
    return pl.pallas_call(
        functools.partial(mlp_fwd_kernel, half=half, counts=[len(s) for s in slots]),
        grid=(parts,),
        in_specs=[anywhere] * len(flat)
        + [whole, whole],
        out_specs=[take(half), take(2 * half), whole, whole],
        out_shape=[
            jax.ShapeDtypeStruct((parts, 2 * rows, half), bf16),
            jax.ShapeDtypeStruct((parts, 2 * rows, 2 * half), bf16),
            jax.ShapeDtypeStruct((rows, width), f32),
            jax.ShapeDtypeStruct((rows, width), bf16),
        ],
        scratch_shapes=[
            pltpu.VMEM((rows, width), f32),
            pltpu.VMEM((2, width, 3 * half), bf16),
            pltpu.SemaphoreType.DMA((2, max(len(s) for s in slots))),
        ],
        compiler_params=params(56),
    )(*flat, ha, hb)


def mlp_bwd_kernel(*refs, half, counts):
    total = sum(counts)
    flat, refs = refs[:total], refs[total:]
    slots, at = [], 0
    for n in counts:
        slots.append(flat[at : at + n])
        at += n
    da_ref, db_ref, uv_ref, duv_ref, own_ref, got_ref, gs_ref, acc, wbuf, sems = refs
    rows = da_ref.shape[0]
    q = pl.program_id(0)

    @pl.when(q == 0)
    def _():
        own_ref[...] = jnp.zeros_like(own_ref)
        acc[...] = jnp.zeros_like(acc)

    gs_ref[...] = jnp.zeros_like(gs_ref)
    fetch_weights(q, slots, wbuf, sems)
    w = wbuf.at[lax.rem(q, 2)]
    for base, d_ref, sum_ref in ((0, da_ref, own_ref), (rows, db_ref, acc)):
        at = slice(base, base + rows)
        grad = dot(d_ref[...], w[:, 2 * half : 3 * half])
        lifted = uv_ref[at, :half].astype(f32)
        gated = uv_ref[at, half:].astype(f32)
        sigma = jax.nn.sigmoid(gated)
        da = grad * gated * sigma
        db = grad * lifted * sigma * (1.0 + gated * (1.0 - sigma))
        gs_ref[0:1, :] += jnp.sum(da * lifted, axis=0, keepdims=True)
        gs_ref[1:2, :] += jnp.sum(db * gated, axis=0, keepdims=True)
        duv_ref[at, :half] = da.astype(bf16)
        duv_ref[at, half:] = db.astype(bf16)
        sum_ref[...] += dot_t(duv_ref[at, :], w[:, : 2 * half])

    @pl.when(q == pl.num_programs(0) - 1)
    def _():
        got_ref[...] = acc[...].astype(bf16)


def mlp_bwd(da, db, slots, uv, half):
    rows, width = da.shape
    parts = len(slots)
    take = lambda n: pl.BlockSpec((None, 2 * rows, n), lambda q: (q, 0, 0))
    whole = full_spec((rows, width))
    anywhere = pl.BlockSpec(memory_space=pl.ANY)
    flat = [p for slot in slots for p in slot]
    return pl.pallas_call(
        functools.partial(mlp_bwd_kernel, half=half, counts=[len(s) for s in slots]),
        grid=(parts,),
        in_specs=[anywhere] * len(flat)
        + [
            whole,
            whole,
            take(2 * half),
        ],
        out_specs=[
            take(2 * half),
            whole,
            whole,
            pl.BlockSpec((None, 8, half), lambda q: (q, 0, 0)),
        ],
        out_shape=[
            jax.ShapeDtypeStruct((parts, 2 * rows, 2 * half), bf16),
            jax.ShapeDtypeStruct((rows, width), f32),
            jax.ShapeDtypeStruct((rows, width), bf16),
            jax.ShapeDtypeStruct((parts, 8, half), f32),
        ],
        scratch_shapes=[
            pltpu.VMEM((rows, width), f32),
            pltpu.VMEM((2, width, 3 * half), bf16),
            pltpu.SemaphoreType.DMA((2, max(len(s) for s in slots))),
        ],
        compiler_params=params(56),
    )(*flat, da, db, uv)


EXTRA = 16


def grad_kernel(place_ref, *refs, orders, parts, chunk, more):
    ha_ref, hb_ref = refs[:2]
    refs = refs[2:]
    if more:
        oa_ref, ob_ref, ya_ref, yb_ref, gs_ref, g1_ref, g2_ref = refs[:7]
        refs = refs[7:]
    val_ref, *outs = refs[:5]
    turned = refs[5]
    rows = ha_ref.shape[0]
    k = pl.program_id(0)

    @pl.when(k == 0)
    def _():
        turned[:, :rows] = ha_ref[...].T
        turned[:, rows:] = hb_ref[...].T
        if more:
            refs[6][:, :rows] = oa_ref[...].T
            refs[6][:, rows:] = ob_ref[...].T

    if more:
        size = outs[0].shape[2]
        fill = lambda row: jnp.concatenate([row, jnp.zeros((1, size - row.shape[1]), f32)], axis=1)
        line = lax.broadcasted_iota(jnp.int32, (EXTRA, size), 0)
        units = fill(jnp.concatenate([gs_ref[0:1, :], gs_ref[1:2, :]], axis=1))
        steps = fill(jnp.concatenate([g1_ref[0:1, :], g2_ref[0:1, :]], axis=1))
        extra = jnp.where(line == 0, units, jnp.where(line == 1, steps, 0.0)).astype(bf16)

    for side in range(2):

        @pl.when((k < parts // 2) == (side == 0))
        def _(side=side):
            for which, ref in zip(orders[side], outs[2 * side : 2 * side + 2]):
                for j, r in enumerate(which):
                    at = slice(r * chunk, (r + 1) * chunk)
                    value = dot(turned[at, :], val_ref[...]).astype(bf16)
                    size = value.shape[1]
                    ref[j, :chunk, :size] = value
                    if more:
                        ref[j, :chunk, size:] = (
                            dot(refs[6][at, :rows], ya_ref[...]) + dot(refs[6][at, rows:], yb_ref[...])
                        ).astype(bf16)
                        ref[j, chunk:, :] = extra


def weight_grads(place, sends, keeps, chips, hs, value, os=None, ys=None, extra=None):
    rows, width = hs[0].shape
    chunk = width // chips
    parts, _, size = value.shape
    more = os is not None
    hc = ys[1].shape[2] if more else 0
    tall = chunk + (EXTRA if more else 0)
    middle = parts // 2
    if chunk % 128:
        result = []
        for which, lo in ((sends[0], 0), (keeps[0], 0), (sends[1], middle), (keeps[1], middle)):
            cut = lambda pair: jnp.concatenate(
                [jnp.concatenate(pair, axis=0)[:, r * chunk : (r + 1) * chunk] for r in which], axis=1
            )
            found = []
            for k in range(lo, lo + middle):
                one = t_dot(cut(hs), value[k])
                if more:
                    at = (place[0] - k) % parts
                    y = lax.dynamic_index_in_dim(ys[0], at, 0, keepdims=False)
                    y = lax.dynamic_slice_in_dim(y, place[2] * hc, hc, 1)
                    y = jnp.concatenate([y, lax.dynamic_index_in_dim(ys[1], at, 0, keepdims=False)])
                    one = jnp.concatenate([one, t_dot(cut(os), y)], axis=1)
                one = one.reshape(len(which), chunk, size + hc)
                if more:
                    wide = jnp.broadcast_to(extra[k][None], (len(which), EXTRA, size + hc))
                    one = jnp.concatenate([one, wide], axis=1)
                found.append(one.astype(bf16))
            result.append(jnp.stack(found, axis=1))
        return [result[0], result[2]], [result[1], result[3]]
    whole = full_spec((rows, width))
    ins = list(hs)
    in_specs = [whole] * 2
    scratch = [pltpu.VMEM((width, 2 * rows), bf16)]
    if more:
        slot = lambda k, p: lax.rem(p[0] + parts - k, parts)
        cols = ys[0].shape[2]
        part = pl.BlockSpec((8, cols), lambda k, p: (0, slot(k, p) ^ p[1]))
        ins += [*os, ys[0], ys[1], *extra]
        in_specs += [whole] * 2
        in_specs += [
            pl.BlockSpec((None, rows, hc), lambda k, p: (slot(k, p), 0, p[2])),
            pl.BlockSpec((None, rows, hc), lambda k, p: (slot(k, p), 0, 0)),
            pl.BlockSpec((None, 8, size // 2), lambda k, p: (k, 0, 0)),
            part,
            part,
        ]
        scratch = scratch * 2
    ins.append(value)
    in_specs.append(pl.BlockSpec((None, 2 * rows, size), lambda k, p: (k, 0, 0)))
    lists = [sends[0], keeps[0], sends[1], keeps[1]]
    block = lambda one: (len(one), None, tall, size + hc)
    early = lambda k, p: (0, jnp.minimum(k, middle - 1), 0, 0)
    late = lambda k, p: (0, jnp.maximum(k - middle, 0), 0, 0)
    out = pl.pallas_call(
        functools.partial(
            grad_kernel, orders=(lists[:2], lists[2:]), parts=parts, chunk=chunk, more=more
        ),
        grid_spec=pltpu.PrefetchScalarGridSpec(
            num_scalar_prefetch=1,
            grid=(parts,),
            in_specs=in_specs,
            out_specs=[
                pl.BlockSpec(block(one), early if n < 2 else late) for n, one in enumerate(lists)
            ],
            scratch_shapes=scratch,
        ),
        out_shape=[
            jax.ShapeDtypeStruct((len(one), middle, tall, size + hc), bf16) for one in lists
        ],
        compiler_params=params(56),
    )(place, *ins)
    return [out[0], out[2]], [out[1], out[3]]


def pair_sum_kernel(ka_ref, ga_ref, kb_ref, gb_ref, a_ref, b_ref):
    a_ref[...] = (ka_ref[...].astype(f32) + ga_ref[...].astype(f32)).astype(bf16)
    b_ref[...] = (kb_ref[...].astype(f32) + gb_ref[...].astype(f32)).astype(bf16)


def pair_sums(kept, got, at):
    _, slots, tall, wide = kept[0].shape
    spec = lambda n: pl.BlockSpec((None, None, tall, wide), lambda k, n=n: (n, k, 0, 0))
    return pl.pallas_call(
        pair_sum_kernel,
        grid=(slots,),
        in_specs=[spec(at[0]), spec(at[0]), spec(at[1]), spec(at[1])],
        out_specs=[spec(0)] * 2,
        out_shape=[jax.ShapeDtypeStruct((1, slots, tall, wide), bf16)] * 2,
        compiler_params=params(56),
    )(kept[0], got[0], kept[1], got[1])


def adam_values(weight, grad, first, second):
    first_new = beta_one * first + (1.0 - beta_one) * grad
    second_new = beta_two * second + (1.0 - beta_two) * grad * grad
    moved = weight - learn_rate * (first_new / bias_one) / (
        jnp.sqrt(second_new / bias_two) + adam_eps
    )
    return first_new, second_new, moved


def lane_sums(value):
    ones = jnp.ones((8, value.shape[1]), bf16)
    high = value.astype(bf16)
    low = (value - high.astype(f32)).astype(bf16)
    return dot_t(ones, high) + dot_t(ones, low)


def adam_wide_kernel(w_ref, g_ref, m_ref, v_ref, g_out, m_out, v_out, n_out, s_out):
    cols = w_ref.shape[2]
    for c in range(w_ref.shape[1]):
        grad = g_ref[:, c * cols : (c + 1) * cols]
        first, second, moved = adam_values(w_ref[:, c, :], grad, m_ref[:, c, :], v_ref[:, c, :])
        g_out[:, c, :] = grad
        m_out[:, c, :] = first
        v_out[:, c, :] = second
        n_out[:, c, :] = moved
        s_out[c : c + 1, :] = jnp.sum(moved * moved, axis=0, keepdims=True)


def adam_wide(w, g, m, v):
    vmem = pl.BlockSpec(memory_space=pltpu.VMEM)
    return pl.pallas_call(
        adam_wide_kernel,
        in_specs=[vmem] * 4,
        out_specs=[vmem] * 5,
        out_shape=[jax.ShapeDtypeStruct(w.shape, f32)] * 4
        + [jax.ShapeDtypeStruct(w.shape[1:], f32)],
        compiler_params=params(16),
    )(w, g, m, v)


def adam_tall_kernel(w_ref, g_ref, m_ref, v_ref, g_out, m_out, v_out, n_out, s_out):
    grad = g_ref[...].T
    first, second, moved = adam_values(w_ref[...], grad, m_ref[...], v_ref[...])
    g_out[...] = grad
    m_out[...] = first
    v_out[...] = second
    n_out[...] = moved
    s_out[...] = lane_sums(moved * moved)


def adam_tall(w, g, m, v):
    vmem = pl.BlockSpec(memory_space=pltpu.VMEM)
    return pl.pallas_call(
        adam_tall_kernel,
        in_specs=[vmem] * 4,
        out_specs=[vmem] * 5,
        out_shape=[jax.ShapeDtypeStruct(w.shape, f32)] * 4
        + [jax.ShapeDtypeStruct((8, w.shape[0]), f32)],
        compiler_params=params(16),
    )(w, g, m, v)


def scale_kernel(na_ref, nb_ref, nc_ref, nd_ref, a_ref, b_ref, c_ref, d_ref, ao_ref, bo_ref, co_ref, do_ref, *, width):
    factor = lambda value: lax.rsqrt(value / width + layer_eps)
    for norm, ref, out in ((na_ref, a_ref, ao_ref), (nc_ref, c_ref, co_ref)):
        for c in range(ref.shape[1]):
            out[:, c, :] = ref[:, c, :] * factor(norm[c : c + 1, :])
    for norm, ref, out in ((nb_ref, b_ref, bo_ref), (nd_ref, d_ref, do_ref)):
        out[...] = ref[...] * factor(norm[...]).T[:, 0:1]


def scale_weights(norms, weights, width):
    vmem = pl.BlockSpec(memory_space=pltpu.VMEM)
    return pl.pallas_call(
        functools.partial(scale_kernel, width=width),
        in_specs=[vmem] * 8,
        out_specs=[vmem] * 4,
        out_shape=[jax.ShapeDtypeStruct(w.shape, f32) for w in weights],
        compiler_params=params(16),
    )(*norms, *weights)


def after(value, *others):
    return lax.optimization_barrier((value, *others))[0]


def per_device(
    layer_input,
    cotangent,
    positions,
    w_qkv,
    w_out,
    w_up,
    w_down,
    moment_qkv,
    moment_out,
    moment_up,
    moment_down,
    square_qkv,
    square_out,
    square_up,
    square_down,
    s_qk,
    alpha_attn,
    alpha_mlp,
    s_uv,
):
    nz = lax.axis_size("head")
    nb = lax.axis_size("batch")
    z = lax.axis_index("head")
    b = lax.axis_index("batch")
    core = b % 2
    chip = b // 2
    chips = nb // 2
    bits = [1 << n for n in range(int(math.log2(chips)))]
    rows, cols = layer_input.shape
    width = cols * nz
    own = rows // nz
    hid = w_down.shape[0]
    half = hid // 2
    hc = cols // 2
    heads = cols // HEAD_DIM
    span = w_qkv.shape[0]
    chunk = width // chips
    core_s = core.reshape(1).astype(jnp.int32)
    place = jnp.stack([z, chip, core]).astype(jnp.int32)
    fast = chunk == cols and chunk % 128 == 0

    def swap_batch(value, bit):
        return lax.ppermute(value, "batch", [(i, i ^ bit) for i in range(nb)])

    def swap_core(value):
        return swap_batch(value, 1)

    def swap_chip(value, bit):
        return swap_batch(value, 2 * bit)

    def onward(value, k=1):
        return lax.ppermute(value, "head", [(i, (i + k) % nz) for i in range(nz)])

    def exchange(value):
        return lax.all_to_all(value, "head", split_axis=0, concat_axis=0)

    def pick(pair, index):
        return jnp.where(index == 0, pair[0], pair[1])

    def relative(value):
        return jnp.concatenate(
            [
                lax.dynamic_slice_in_dim(value, (chip ^ r) * chunk, chunk, value.ndim - 1)
                for r in range(chips)
            ],
            axis=-1,
        )

    def spread(value):
        if chips <= 4:
            return [value] + [swap_chip(value, r) for r in range(1, chips)]
        for bit in bits:
            value = jnp.concatenate([value, swap_chip(value, bit)], axis=0)
        return [value]

    tokens = [layer_input, onward(layer_input)]
    mine, theirs = pack(core_s, w_up, s_uv, w_down, w_out)
    qkv_own = after(w_qkv, mine).reshape(span, 3 * cols).astype(bf16)
    qkv_full = lax.all_gather(qkv_own, "batch", axis=0, tiled=True)
    theirs = swap_core(theirs)
    packet = jnp.concatenate([pick((mine, theirs), core), pick((theirs, mine), core)], axis=0)
    hops = [packet, onward(packet)]
    slots = [spread(packet)]
    tokens[1], hops[1], places, alpha_attn, alpha_mlp = lax.optimization_barrier(
        (tokens[1], hops[1], positions, alpha_attn, alpha_mlp)
    )
    come, *last = lax.optimization_barrier((hops[1], *slots[0]))
    slots[0] = list(last)

    freqs = jnp.exp(
        (jnp.arange(128) % (HEAD_DIM // 2)).astype(f32) * (-2.0 * math.log(10000.0) / HEAD_DIM)
    )
    phase = places.astype(f32)[:, None] * freqs[None, :]
    side = jnp.where(jnp.arange(128) % HEAD_DIM < HEAD_DIM // 2, -1.0, 1.0).astype(f32)
    cosine, sine = jnp.cos(phase), jnp.sin(phase) * side[None, :]
    lane = jnp.arange(cols) // HEAD_DIM
    ones = (lane[:, None] == lane[None, :]).astype(bf16)
    gain = s_qk.reshape(1, cols)
    is_long = (places[SHORT : SHORT + 1] != 0).astype(jnp.int32)
    attn_gain = relative(alpha_attn[None])
    mlp_gain = relative(alpha_mlp[None])

    for n in range(2, nz):
        slots.append(spread(come if n == 2 else hops[-1]))
        tokens.append(onward(tokens[-1]))
        if n < nz - 1:
            hops.append(onward(hops[-1]))
            tokens[-1], hops[-1], cosine, sine, ones, attn_gain, mlp_gain, *last = (
                lax.optimization_barrier(
                    (tokens[-1], hops[-1], cosine, sine, ones, attn_gain, mlp_gain, *slots[-1])
                )
            )
            slots[-1] = list(last)
    last_hop, tokens[-1] = lax.optimization_barrier((hops[-1], tokens[-1]))
    hops.append(onward(last_hop))

    blocks = rows // 512
    middle = blocks // 2
    tokens_full, q, k, v, rho = qkv_project(place, tokens, qkv_full, cosine, sine, gain, ones)
    y_a, logs_a = attn_fwd(is_long, q, k, v, 0, middle)
    q_b, hops[-1], *last = lax.optimization_barrier((after(q, y_a), hops[-1], *slots[-1]))
    slots[-1] = list(last)
    slots.append(spread(hops[-1]))
    y_b, logs_b = attn_fwd(is_long, q_b, k, v, middle, blocks - middle)
    y_one = exchange(y_a.reshape(nz, own // 2, cols))
    y_in, y_one = lax.optimization_barrier((y_b, y_one))
    y_two = exchange(y_in.reshape(nz, own // 2, cols))
    flat = lambda value: value.transpose(1, 0, 2).reshape(own, width)
    start = tokens_full
    if not fast:
        start = jnp.concatenate(
            [
                lax.dynamic_slice_in_dim(tokens_full, h * (rows // 2) + z * (own // 2), own // 2, 0)
                for h in range(2)
            ]
        )
        start = relative(start)
    y_one, y_two, *last = lax.optimization_barrier((y_one, y_two, *slots[-1]))
    slots[-1] = list(last)
    hA, h1, h_own, stat, y_mine, y_other = attn_out(place, y_one, y_two, slots, start, attn_gain, chips, fast)
    h_got = swap_core(h_own)
    y_got = swap_core(y_other)
    h_got, y_got = lax.optimization_barrier((h_got, y_got))
    cot = after(cotangent, h_own).reshape(2, nz, own // 2, cols).transpose(1, 0, 2, 3)
    cot = exchange(cot.reshape(nz, own, cols))

    act, uv, mo_own, mo_other = mlp_fwd(h_own, h_got, slots, half)
    mo_got = swap_core(mo_other)
    if not fast:
        cot = relative(flat(cot))
    hidden, d_own, base, ga_mlp = loss(place, mo_own, mo_got, h1, cot, mlp_gain, chips, fast)
    d_got = swap_core(d_own)
    if not fast:
        hidden = relative(hidden).reshape(own, nz, cols).transpose(1, 0, 2)
    hidden = exchange(hidden)

    orders = [bits, bits[::-1]]
    sent_at = [[r for r in range(chips) if r & order[0]] for order in orders]
    kept_at = [[r for r in range(chips) if not r & order[0]] for order in orders]

    def second(kept, sent):
        found, sends = [], []
        if chips == 4:
            at = [[n for n, r in enumerate(left) if r & order[1]] for order, left in zip(orders, kept_at)]
            sends = pair_sums(kept, sent, [one[0] for one in at])
            for order, one, keep, got, send in zip(orders, at, kept, sent, sends):
                cut = lambda t, n=1 - one[0]: t[n : n + 1]
                found.append([cut(keep), cut(got), swap_chip(send, order[1])])
            return found, sends
        for order, left, got, keep in zip(orders, kept_at, sent, kept):
            terms = [keep, got]
            for bit in order[1:]:
                send_at = [n for n, r in enumerate(left) if r & bit]
                keep_at = [n for n, r in enumerate(left) if not r & bit]
                left = [left[n] for n in keep_at]
                cut = lambda v, at: jnp.concatenate([v[n : n + 1] for n in at], axis=0)
                send = sum(cut(t, send_at).astype(f32) for t in terms).astype(bf16)
                terms = [cut(t, keep_at) for t in terms] + [swap_chip(send, bit)]
                sends.append(send)
            found.append(terms)
        return found, sends

    def slot_sums(found):
        return [sum(t[0, n].astype(f32) for t in terms) for terms in found for n in range(nz // 2)]

    def wait_last(found, *others):
        return [terms[:-1] + [after(terms[-1], *others)] for terms in found]

    down_made, down_kept = weight_grads(place, sent_at, kept_at, chips, (d_own, d_got), act)
    down_sent = [swap_chip(one, order[0]) for one, order in zip(down_made, orders)]
    d_own, d_got, *_ = lax.optimization_barrier((d_own, d_got, *down_made))
    duv, dh_own, dh_other, gsuv = mlp_bwd(d_own, d_got, slots, uv, half)
    dh_got = swap_core(dh_other)
    down_sent = [after(one, dh_other) for one in down_sent]
    down_part, down_next = second(down_kept, down_sent)
    dh_own, hidden, *_ = lax.optimization_barrier((dh_own, hidden, *down_next))
    do_own, through, ga_attn, dy = first_back(
        place, dh_own, dh_got, base, h1, hA, start, stat, attn_gain, slots, chips, fast, cols
    )
    dy = exchange(dy)
    do_got = swap_core(do_own)

    extra = (gsuv, ga_attn, ga_mlp)
    if not fast:
        alphas = [relative(ga_attn[0:1]), relative(ga_mlp[0:1])]
        extra = []
        wide = 2 * half + hc
        fill = lambda r: jnp.pad(r, ((0, 0), (0, wide - r.shape[1])))
        for n in range(nz):
            at = ((z - n) % nz) * cols
            line = [lax.dynamic_slice_in_dim(g, at, cols, 1) for g in alphas]
            lines = [gsuv[n, :2].reshape(1, 2 * half), jnp.concatenate(line, axis=1)]
            lines = jnp.concatenate([fill(r) for r in lines])
            extra.append(jnp.pad(lines, ((0, EXTRA - 2), (0, 0))))
        extra = jnp.stack(extra)
    up_made, up_kept = weight_grads(
        place, sent_at, kept_at, chips, (h_own, h_got), duv, (do_own, do_got), (y_mine, y_got), extra
    )
    down_part = wait_last(down_part, *up_kept)
    down_last = [terms[-1] for terms in down_part]
    dy, *both = lax.optimization_barrier((dy, *up_made, *down_last))
    up_made, down_last = both[: len(up_made)], both[len(up_made) :]
    down_slots = slot_sums([t[:-1] + [last] for t, last in zip(down_part, down_last)])
    down_along = [onward(down_slots[n].astype(bf16), nz - n) for n in range(1, nz)]
    up_sent = [swap_chip(one, order[0]) for one, order in zip(up_made, orders)]

    dy = dy.reshape(nz, 2, own // 2, cols)
    common = lambda y, logs: (
        is_long, q, k, v, dy, y, logs, rho, cosine, sine, gain, ones
    )
    dqkv_b, dk_part, dv_part, sqk_b = attn_bwd(
        *common(y_b, logs_b), middle, blocks - middle, None
    )

    if not fast:
        through = relative(through).reshape(own, nz, cols).transpose(1, 0, 2)
    mine_at = z * (own // 2)
    qkv_parts = qkv_full.reshape(nz, cols, 3 * cols)

    def input_part(dqkv, side):
        part = jnp.einsum("tn,zcn->ztc", dqkv, qkv_parts, preferred_element_type=f32).astype(bf16)
        here = lax.dynamic_slice_in_dim(part, mine_at, own // 2, 1).astype(f32)
        more = after(through, dqkv)[:, side * (own // 2) : (side + 1) * (own // 2)]
        return lax.dynamic_update_slice_in_dim(part, (here + more.astype(f32)).astype(bf16), mine_at, 1)

    part_b = input_part(dqkv_b, 1)
    down_along = [after(one, dqkv_b) for one in down_along]
    part_got = exchange(part_b)
    dk_part, *_ = lax.optimization_barrier((dk_part, part_b, *down_along))
    dqkv_a, sqk_a = attn_bwd(*common(y_a, logs_a), 0, middle, [dk_part, dv_part])
    input_b = jnp.sum(after(part_got, dqkv_a).astype(f32), axis=0)
    up_part, up_next = second(up_kept, [after(one, dqkv_a) for one in up_sent])
    dqkv_a, *_ = lax.optimization_barrier((dqkv_a, *up_next))
    part_a = input_part(dqkv_a, 0)
    dqkv = jnp.concatenate([dqkv_a, dqkv_b], axis=0)
    grad_qkv = t_dot(tokens_full, dqkv).astype(bf16)
    sqk = jnp.pad((sqk_a + sqk_b), ((0, EXTRA - 8), (0, 2 * cols)))
    shard = [lax.dynamic_slice_in_dim(grad_qkv, (b ^ r) * span, span, 0) for r in range(nb)]
    shard = [jnp.concatenate([t, sqk.astype(bf16)], axis=0) for t in shard]
    odd = [r for r in range(nb) if r & 1]
    early = swap_core(jnp.concatenate([shard[r] for r in odd], axis=0))

    def both_halves(total, *wait):
        two = (total[:span], total[span : 2 * span])
        here = jnp.concatenate([pick(two, core), total[2 * span :]], axis=0)
        there = jnp.concatenate([pick(two, 1 - core), total[2 * span :]], axis=0)
        there = swap_core(there.astype(bf16))
        if wait:
            there = after(there, *wait)
        return here, there

    def in_order(here, there):
        there = there.astype(f32)
        return [pick((here, there), core), pick((there, here), core)]

    down_along = [after(one, part_a) for one in down_along]
    down_here, down_there = both_halves(
        down_slots[0] + sum(one.astype(f32) for one in down_along)
    )
    up_part = wait_last(up_part, part_a, early, down_there, *[terms[-1] for terms in up_part])
    up_slots = slot_sums(up_part)
    passed = up_slots[1].astype(bf16)
    part_a, passed, early, down_there = lax.optimization_barrier((part_a, passed, early, down_there))
    passed = onward(passed)
    for n in range(2, nz):
        if n == nz - 2:
            passed, part_a = lax.optimization_barrier((passed, part_a))
        passed = onward((up_slots[n] + passed.astype(f32)).astype(bf16))
    sum_up_t = up_slots[0] + passed.astype(f32)
    input_a = lax.psum_scatter(part_a.reshape(-1, cols), "head", scatter_dimension=0, tiled=True)
    input_grad = jnp.concatenate([input_a.astype(f32), input_b], axis=0)
    hidden_t = after(hidden, part_a).reshape(nz, 2, own // 2, cols).transpose(1, 0, 2, 3).reshape(rows, cols)

    qbits = [1 << n for n in range(int(math.log2(nb)))]
    held = {r: shard[r] for r in range(nb)}
    for bit in qbits:
        send_at = [r for r in held if r & bit]
        send = jnp.concatenate([held[r] for r in send_at], axis=0).astype(bf16)
        got = early if bit == 1 else swap_batch(send, bit)
        size = span + EXTRA
        held = {
            r ^ bit: held[r ^ bit].astype(f32) + got[n * size : (n + 1) * size].astype(f32)
            for n, r in enumerate(send_at)
        }
    cell = width // (nz * nb)
    sum_sqk = lax.dynamic_slice_in_dim(held[0][span, :cols], b * cell, cell, 0)
    w_late, m_late, v_late, _ = lax.optimization_barrier((w_qkv, moment_qkv, square_qkv, part_a))
    qkv_new = adam_wide(w_late, held[0][:span], m_late, v_late)

    join = lambda halves, at, size: [p[:span, at : at + size] for p in halves]
    halves = in_order(down_here, down_there)
    down_new = adam_tall(w_down, jnp.concatenate(join(halves, 0, half), axis=1), moment_down, square_down)
    halves = in_order(*both_halves(sum_up_t))
    grad_up = jnp.concatenate(join(halves, 0, half) + join(halves, half, half), axis=1)
    grad_up = grad_up * s_uv.reshape(1, 2 * hid)
    up_new = adam_wide(w_up, grad_up, moment_up, square_up)
    out_new = adam_tall(w_out, jnp.concatenate(join(halves, 2 * half, hc), axis=1), moment_out, square_out)
    suv_rows = jnp.stack(
        [jnp.concatenate([p[span, c * half : (c + 1) * half] for p in halves]) for c in range(2)]
    )
    suv_rows = suv_rows / s_uv
    sum_suv = lax.dynamic_slice_in_dim(suv_rows, b * (hid // nb), hid // nb, 1)
    alphas = halves[0][span + 1] + halves[1][span + 1]
    sum_attn = lax.dynamic_slice_in_dim(alphas[:cols], b * cell, cell, 0)
    sum_mlp = lax.dynamic_slice_in_dim(alphas[cols : 2 * cols], b * cell, cell, 0)

    hidden = hidden_t.astype(f32)

    squares = [qkv_new[4], out_new[4][:1], up_new[4], down_new[4][:1]]
    sizes = [t.size for t in squares]
    norms = jnp.concatenate([t.reshape(-1) for t in squares]).reshape(-1, 128)
    for bit in qbits:
        norms = norms + swap_batch(norms, bit)
    norms = norms.reshape(-1)
    ends = [0] + [sum(sizes[: n + 1]) for n in range(4)]
    back = lambda n, shape: norms[ends[n] : ends[n + 1]].reshape(shape)
    eight = lambda value: jnp.broadcast_to(value, (8, value.shape[1]))
    new_qkv, new_out, new_up, new_down = scale_weights(
        [back(0, (3, cols)), eight(back(1, (1, cols))), back(2, (2, hid)), eight(back(3, (1, hid)))],
        [qkv_new[3], out_new[3], up_new[3], down_new[3]],
        width,
    )
    sum_qkv, first_a, second_a = qkv_new[:3]
    sum_out, first_b, second_b = out_new[:3]
    sum_up, first_c, second_c = up_new[:3]
    sum_down, first_d, second_d = down_new[:3]
    return (
        hidden,
        input_grad,
        sum_qkv,
        sum_out,
        sum_up,
        sum_down,
        first_a,
        first_b,
        first_c,
        first_d,
        second_a,
        second_b,
        second_c,
        second_d,
        new_qkv,
        new_out,
        new_up,
        new_down,
        sum_sqk,
        sum_attn,
        sum_mlp,
        sum_suv,
    )


def solution(mesh):
    tokens = P("batch", "head")
    wide = P("batch", None, "head")
    tall = P("head", "batch")
    flat = P(("head", "batch"))
    weights = (wide, tall, wide, tall)
    return jax.shard_map(
        per_device,
        mesh=mesh,
        in_specs=(tokens, tokens, P("batch"))
        + weights * 3
        + (P("head"), P(), P(), P(None, "head")),
        out_specs=(tokens, tokens) + weights * 4 + (flat, flat, flat, P(None, ("head", "batch"))),
        check_vma=False,
    )
```

```python
import functools
import math

import jax
import jax.numpy as jnp
from jax import lax
from jax.experimental import pallas as pl
from jax.experimental.pallas import tpu as pltpu
from jax.sharding import PartitionSpec as P

HEAD_DIM = 64
SHORT = 1024

layer_eps = 1e-06
learn_rate = 0.008
beta_one = 0.9
beta_two = 0.95
adam_eps = 1e-08
bias_one = 1.0 - math.exp(100.0 * math.log(0.9))
bias_two = 1.0 - math.exp(100.0 * math.log(0.95))
score_scale = 8.0
LOG2E = math.log2(math.e)
LN2 = math.log(2.0)

bf16 = jnp.bfloat16
f32 = jnp.float32


def dot(a, b):
    return jnp.dot(a, b, preferred_element_type=f32)


def dot_t(a, b):
    return lax.dot_general(a, b, (((1,), (1,)), ((), ())), preferred_element_type=f32)


def t_dot(a, b):
    return lax.dot_general(a, b, (((0,), (0,)), ((), ())), preferred_element_type=f32)


def params(mib):
    return pltpu.CompilerParams(vmem_limit_bytes=mib * 1024 * 1024)


def full_spec(shape):
    return pl.BlockSpec(shape, lambda *_: (0,) * len(shape))


def head_sum(value, ones):
    high = value.astype(bf16)
    low = (value - high.astype(f32)).astype(bf16)
    return dot(high, ones) + dot(low, ones)


def widen(value, cols):
    return jnp.concatenate([value] * (cols // value.shape[1]), axis=1)


def swap_halves(value):
    cols = value.shape[-1]
    half = HEAD_DIM // 2
    lane = lax.broadcasted_iota(jnp.int32, value.shape, 1)
    first = (lane % HEAD_DIM) < half
    up = pltpu.roll(value, cols - half, 1)
    down = pltpu.roll(value, half, 1)
    return jnp.where(first, up, down)


def qkv_kernel(place_ref, *refs, parts):
    tokens = refs[:parts]
    w_ref, cos_ref, sin_ref, gain_ref, ones_ref, x_ref, q_ref, k_ref, v_ref, rho_ref = refs[parts:]
    cols = v_ref.shape[1]
    z = place_ref[0]
    for n in range(parts):
        at = pl.multiple_of(lax.rem(z + parts - n, parts) * cols, cols)
        x_ref[:, pl.ds(at, cols)] = tokens[n][...]
    proj = dot(x_ref[...], w_ref[...])
    cosine = widen(cos_ref[...], cols)
    sine = widen(sin_ref[...], cols)
    ones = ones_ref[...]
    gain = gain_ref[...]
    heads = cols // HEAD_DIM
    lane = lax.broadcasted_iota(jnp.int32, rho_ref.shape, 1)
    stats = jnp.zeros(rho_ref.shape, f32)
    for c, (out, scale) in enumerate(((q_ref, score_scale * LOG2E), (k_ref, 1.0))):
        part = proj[:, c * cols : (c + 1) * cols]
        rho = lax.rsqrt(head_sum(part * part, ones) + layer_eps)
        rot = part * cosine + swap_halves(part) * sine
        out[...] = (rot * rho * (gain * scale)).astype(bf16)
        for h in range(heads):
            stats = jnp.where(lane == c * heads + h, rho[:, h * HEAD_DIM : h * HEAD_DIM + 1], stats)
    rho_ref[...] = stats
    v_ref[...] = proj[:, 2 * cols :].astype(bf16)


def qkv_project(place, tokens, w, cosine, sine, gain, ones):
    rows, cols = tokens[0].shape
    parts = len(tokens)
    width = parts * cols
    blk = 512
    row = lambda n: pl.BlockSpec((blk, n), lambda i, s: (i, 0))
    return pl.pallas_call(
        functools.partial(qkv_kernel, parts=parts),
        grid_spec=pltpu.PrefetchScalarGridSpec(
            num_scalar_prefetch=1,
            grid=(rows // blk,),
            in_specs=[row(cols)] * parts
            + [full_spec((width, 3 * cols)), row(128), row(128)]
            + [full_spec((1, cols)), full_spec((cols, cols))],
            out_specs=[row(width)] + [row(cols)] * 3 + [row(128)],
        ),
        out_shape=[jax.ShapeDtypeStruct((rows, width), bf16)]
        + [jax.ShapeDtypeStruct((rows, cols), bf16)] * 3
        + [jax.ShapeDtypeStruct((rows, 128), f32)],
        compiler_params=params(56),
    )(place, *tokens, w, cosine, sine, gain, ones)


def head_masks(cols, heads):
    lane = lax.broadcasted_iota(jnp.int32, (1, cols), 1) // HEAD_DIM
    return [(lane == h) for h in range(heads)]


def masked(value, mask):
    return jnp.where(mask, value, jnp.zeros_like(value))


def attn_fwd_kernel(long_ref, q_ref, k_ref, v_ref, y_ref, l_ref, acc, mass, *, heads, blk, sub, first):
    i = first + pl.program_id(0)
    cols = q_ref.shape[1]
    masks = head_masks(cols, heads)
    per = SHORT // blk
    low = jnp.where(long_ref[0] != 0, 0, (i // per) * per)
    acc[...] = jnp.zeros_like(acc)
    mass[...] = jnp.zeros_like(mass)

    def lanes(p):
        total = p[:, 0:128]
        for n in range(1, p.shape[1] // 128):
            total = total + p[:, n * 128 : (n + 1) * 128]
        return total

    def body(j, carry):
        start = pl.multiple_of(j * blk, blk)
        keys = k_ref[pl.ds(start, blk), :]
        vals = v_ref[pl.ds(start, blk), :]
        q = q_ref[...]
        total = jnp.zeros(acc.shape, f32)
        for h in range(heads):
            p = jnp.exp2(dot_t(masked(q, masks[h]), keys))
            mass[h] += lanes(p)
            total += dot(p.astype(bf16), masked(vals, masks[h]))
        acc[...] += total
        return carry

    lax.fori_loop(low, i, body, 0)
    start = pl.multiple_of(i * blk, blk)
    causal = lax.broadcasted_iota(jnp.int32, (sub, sub), 0) >= lax.broadcasted_iota(
        jnp.int32, (sub, sub), 1
    )
    for a in range(blk // sub):
        rows = slice(a * sub, (a + 1) * sub)
        q = q_ref[rows, :]
        for b in range(a + 1):
            at = pl.multiple_of(start + b * sub, sub)
            keys = k_ref[pl.ds(at, sub), :]
            vals = v_ref[pl.ds(at, sub), :]
            total = jnp.zeros((sub, cols), f32)
            for h in range(heads):
                p = jnp.exp2(dot_t(masked(q, masks[h]), keys))
                if a == b:
                    p = jnp.where(causal, p, 0.0)
                mass[h, rows, :] += lanes(p)
                total += dot(p.astype(bf16), masked(vals, masks[h]))
            acc[rows, :] += total
    inverse = jnp.zeros(acc.shape, f32)
    logs = jnp.zeros(l_ref.shape, f32)
    lane = lax.broadcasted_iota(jnp.int32, l_ref.shape, 1)
    for h in range(heads):
        column = jnp.sum(mass[h], axis=1, keepdims=True)
        inverse = jnp.where(masks[h], 1.0 / column, inverse)
        logs = jnp.where(lane == h, jnp.log2(column), logs)
    y_ref[...] = (acc[...] * inverse).astype(bf16)
    l_ref[...] = logs


def attn_fwd(is_long, q, k, v, first, count):
    rows, cols = q.shape
    heads = cols // HEAD_DIM
    blk, sub = 512, 256
    row = lambda n: pl.BlockSpec((blk, n), lambda i, s: (i, 0))
    whole = pl.BlockSpec(((first + count) * blk, cols), lambda i, s: (0, 0))
    return pl.pallas_call(
        functools.partial(attn_fwd_kernel, heads=heads, blk=blk, sub=sub, first=first),
        grid_spec=pltpu.PrefetchScalarGridSpec(
            num_scalar_prefetch=1,
            grid=(count,),
            in_specs=[pl.BlockSpec((blk, cols), lambda i, s: (first + i, 0)), whole, whole],
            out_specs=[row(cols), row(128)],
            scratch_shapes=[pltpu.VMEM((blk, cols), f32), pltpu.VMEM((heads, blk, 128), f32)],
        ),
        out_shape=[
            jax.ShapeDtypeStruct((count * blk, cols), bf16),
            jax.ShapeDtypeStruct((count * blk, 128), f32),
        ],
        compiler_params=params(56),
    )(is_long, q, k, v)


def attn_bwd_kernel(
    long_ref, q_ref, qk_ref, dy_ref, y_ref, l_ref, k_ref, v_ref, rho_ref, cos_ref, sin_ref, gain_ref,
    ones_ref, dk_in, dv_in, out_ref, dk_out, dv_out, s_ref, acc, dk_acc, dv_acc, stats, dys, *, heads, blk, sub, first, count
):
    step = pl.program_id(0)
    local = count - 1 - step
    i = first + local
    cols = q_ref.shape[1]
    masks = head_masks(cols, heads)
    per = SHORT // blk
    low = jnp.where(long_ref[0] != 0, 0, (i // per) * per)
    ones = ones_ref[...]
    gain = gain_ref[...]

    @pl.when(step == 0)
    def _():
        dk_acc[...] = jnp.zeros_like(dk_acc)
        dv_acc[...] = jnp.zeros_like(dv_acc)
        s_ref[...] = jnp.zeros_like(s_ref)
        if dk_in is not None:
            dk_acc[...] = dk_in[...]
            dv_acc[...] = dv_in[...]

    acc[...] = jnp.zeros_like(acc)
    dys[...] = dy_ref[...].reshape(dys.shape)
    prod = dys[...].astype(f32) * y_ref[...].astype(f32)
    high = prod.astype(bf16)
    rest = (prod - high.astype(f32)).astype(bf16)
    pickers = (
        lax.broadcasted_iota(jnp.int32, (8, cols), 1) // HEAD_DIM
        == lax.broadcasted_iota(jnp.int32, (8, cols), 0)
    ).astype(bf16)
    stats[0:8, :] = dot_t(pickers, high) + dot_t(pickers, rest)
    stats[8:16, :] = l_ref[...].T[0:8, :]

    def piece(at, size, rows, causal):
        keys = k_ref[pl.ds(at, size), :]
        vals = v_ref[pl.ds(at, size), :]
        q = q_ref[rows, :]
        dy = dys[rows, :]
        total_q = jnp.zeros(q.shape, f32)
        total_k = jnp.zeros(keys.shape, f32)
        total_v = jnp.zeros(keys.shape, f32)
        for h in range(heads):
            qm = masked(q, masks[h])
            dym = masked(dy, masks[h])
            p = jnp.exp2(dot_t(keys, qm) - stats[8 + h : 9 + h, rows])
            if causal is not None:
                p = jnp.where(causal, p, 0.0)
            ds = (p * (dot_t(vals, dym) - stats[h : h + 1, rows])).astype(bf16)
            total_v += dot(p.astype(bf16), dym)
            total_k += dot(ds, qm)
            total_q += t_dot(ds, masked(keys, masks[h]))
        acc[rows, :] += total_q
        dk_acc[pl.ds(at, size), :] += total_k
        dv_acc[pl.ds(at, size), :] += total_v

    def body(j, carry):
        piece(pl.multiple_of(j * blk, blk), blk, slice(0, blk), None)
        return carry

    lax.fori_loop(low, i, body, 0)
    start = pl.multiple_of(i * blk, blk)
    causal = lax.broadcasted_iota(jnp.int32, (sub, sub), 0) <= lax.broadcasted_iota(
        jnp.int32, (sub, sub), 1
    )
    for a in range(blk // sub):
        for b in range(a + 1):
            piece(
                pl.multiple_of(start + b * sub, sub),
                sub,
                slice(a * sub, (a + 1) * sub),
                causal if a == b else None,
            )
    cosine = widen(cos_ref[...], cols)
    sine = widen(sin_ref[...], cols)
    total = jnp.zeros((1, cols), f32)
    here = pl.ds(start, blk)
    for c, (value, unit, up, scale) in enumerate(
        (
            (acc[...], q_ref[...], score_scale, score_scale * LOG2E),
            (dk_acc[here, :], k_ref[here, :], LN2, 1.0),
        )
    ):
        rho = jnp.zeros(value.shape, f32)
        for h in range(heads):
            at = c * heads + h
            rho = jnp.where(masks[h], rho_ref[:, at : at + 1], rho)
        grad = value * up
        unit = unit.astype(f32) * (1.0 / (gain * scale))
        total += jnp.sum(grad * unit, axis=0, keepdims=True)
        grad = grad * gain
        back = rho * (grad - unit * head_sum(grad * unit, ones))
        turned = back * cosine - swap_halves(back) * sine
        out_ref[:, c * cols : (c + 1) * cols] = turned.astype(bf16)
    out_ref[:, 2 * cols :] = dv_acc[here, :].astype(bf16)
    s_ref[0:1, :] += total
    if dk_out is not None:
        @pl.when(step == count - 1)
        def _():
            dk_out[...] = dk_acc[0 : first * blk, :]
            dv_out[...] = dv_acc[0 : first * blk, :]


def attn_bwd(is_long, q, k, v, dy, y, logs, rho, cosine, sine, gain, ones, first, count, carry):
    rows, cols = q.shape
    heads = cols // HEAD_DIM
    blk, sub = 512, 256
    top = (first + count) * blk
    at = lambda s: first + count - 1 - s
    row = lambda n: pl.BlockSpec((blk, n), lambda s, m: (at(s), 0))
    whole = pl.BlockSpec((top, cols), lambda s, m: (0, 0))
    ins = [q, k, dy, y, logs, k, v, rho, cosine, sine, gain, ones]
    mine = lambda n: pl.BlockSpec((blk, n), lambda s, m: (count - 1 - s, 0))
    share = dy.shape[2]
    half_at = 1 if first else 0
    in_specs = [row(cols)] * 2
    in_specs.append(
        pl.BlockSpec((blk // share, None, share, cols), lambda s, m: (count - 1 - s, half_at, 0, 0))
    )
    in_specs += [mine(cols), mine(128), whole, whole] + [row(128)] * 3
    in_specs += [full_spec((1, cols)), full_spec((cols, cols))]
    body = functools.partial(
        attn_bwd_kernel, heads=heads, blk=blk, sub=sub, first=first, count=count
    )
    outs = [jax.ShapeDtypeStruct((count * blk, 3 * cols), bf16)]
    out_specs = [pl.BlockSpec((blk, 3 * cols), lambda s, m: (count - 1 - s, 0))]
    if first:
        outs += [jax.ShapeDtypeStruct((first * blk, cols), f32)] * 2
        out_specs += [full_spec((first * blk, cols))] * 2
        inner = lambda *r: body(*r[:13], None, None, *r[13:])
    else:
        ins += carry
        in_specs += [full_spec((top, cols))] * 2
        inner = lambda *r: body(*r[:16], None, None, *r[16:])
    outs.append(jax.ShapeDtypeStruct((8, cols), f32))
    out_specs.append(full_spec((8, cols)))
    return pl.pallas_call(
        inner,
        grid_spec=pltpu.PrefetchScalarGridSpec(
            num_scalar_prefetch=1,
            grid=(count,),
            in_specs=in_specs,
            out_specs=out_specs,
            scratch_shapes=[
                pltpu.VMEM((blk, cols), f32),
                pltpu.VMEM((top, cols), f32),
                pltpu.VMEM((top, cols), f32),
                pltpu.VMEM((16, blk), f32),
                pltpu.VMEM((blk, cols), bf16),
            ],
        ),
        out_shape=outs,
        compiler_params=params(56),
    )(is_long, *ins)


def row_norm(value):
    return lax.rsqrt(jnp.mean(value * value, axis=1, keepdims=True) + layer_eps)


def norm_back(scale, result, grad):
    return scale * (grad - result * jnp.mean(grad * result, axis=1, keepdims=True))


def pack_kernel(core_ref, up_ref, gain_ref, down_ref, out_ref, mine_ref, theirs_ref):
    half = up_ref.shape[2] // 2
    low = core_ref[0] == 0
    down = down_ref[...].astype(bf16).T
    out = out_ref[...].astype(bf16).T
    for ref, first in ((mine_ref, low), (theirs_ref, jnp.logical_not(low))):
        for c in range(2):
            gain = gain_ref[c : c + 1, :]
            ref[:, c * half : (c + 1) * half] = jnp.where(
                first, up_ref[:, c, :half] * gain[:, :half], up_ref[:, c, half:] * gain[:, half:]
            ).astype(bf16)
        ref[:, 2 * half : 3 * half] = jnp.where(first, down[:, :half], down[:, half:])
        ref[:, 3 * half :] = out


def pack(core, w_up, gain, w_down, w_out):
    span, _, hid = w_up.shape
    cols = w_out.shape[0]
    vmem = pl.BlockSpec(memory_space=pltpu.VMEM)
    return pl.pallas_call(
        pack_kernel,
        in_specs=[pl.BlockSpec(memory_space=pltpu.SMEM)] + [vmem] * 4,
        out_specs=[vmem] * 2,
        out_shape=[jax.ShapeDtypeStruct((span, 3 * hid // 2 + cols), bf16)] * 2,
        compiler_params=params(16),
    )(core, w_up, gain, w_down, w_out)


def place_of(r, chip, chunk):
    return pl.ds(pl.multiple_of((r ^ chip) * chunk, chunk), chunk)


def put_relative(ref, chip, chips, fast):
    if not fast:
        return ref[...]
    if len(ref.shape) == 3:
        return jnp.concatenate([ref[r ^ chip] for r in range(chips)], axis=1)
    chunk = ref.shape[1] // chips
    return jnp.concatenate([ref[:, place_of(r, chip, chunk)] for r in range(chips)], axis=1)


def put_natural(ref, value, chip, chips, fast):
    if not fast:
        ref[...] = value
        return
    chunk = value.shape[1] // chips
    for r in range(chips):
        part = value[:, r * chunk : (r + 1) * chunk]
        if len(ref.shape) == 3:
            ref[r ^ chip] = part
        else:
            ref[:, place_of(r, chip, chunk)] = part


def attn_out_kernel(place_ref, *refs, counts, chips, fast):
    total = sum(counts)
    flat, refs = refs[:total], refs[total:]
    ya_ref, yb_ref, x_ref, alpha_ref, ha_ref, h1_ref, hb_ref, stat_ref, all_ref, half_ref, acc = refs
    z, chip, low = place_ref[0], place_ref[1], place_ref[2] == 0
    parts = len(counts)
    early = pl.program_id(0) == 0
    index = 0
    for n in range(parts):
        at = lax.rem(z + parts - n, parts)
        y = jnp.where(early, ya_ref[at], yb_ref[at])
        hc = y.shape[1] // 2
        all_ref[at] = y
        half_ref[at] = jnp.where(low, y[:, hc:], y[:, :hc])
        column = 0
        for piece in flat[index : index + counts[n]]:
            part = slice(column, column + piece.shape[0])
            if n == 0:
                acc[:, part] = dot_t(y, piece[...])
            else:
                acc[:, part] += dot_t(y, piece[...])
            column += piece.shape[0]
        index += counts[n]
    total = acc[...]
    norm = row_norm(total)
    hidden = total * norm
    start = put_relative(x_ref, chip, chips, fast).astype(f32)
    mixed = start + alpha_ref[...] * (hidden - start)
    first_norm = row_norm(mixed)
    out = mixed * first_norm
    ha_ref[...] = hidden
    h1_ref[...] = out
    hb_ref[...] = out.astype(bf16)
    lane = lax.broadcasted_iota(jnp.int32, stat_ref.shape, 1)
    stat_ref[...] = jnp.where(lane == 0, norm, first_norm)


def own_rows(blk, parts, width, fast):
    if fast:
        return pl.BlockSpec((blk, width), lambda i, s: (i * parts + s[0], 0))
    return pl.BlockSpec((blk, width), lambda i, s: (i, 0))


def out_weights(slots, cols):
    flat = [p for slot in slots for p in slot]
    last = flat[0].shape[1] // cols - 1
    return flat, [pl.BlockSpec((p.shape[0], cols), lambda i, s: (0, last)) for p in flat]


def attn_out(place, ya, yb, slots, x, alpha, chips, fast):
    parts, blk, cols = ya.shape
    width = x.shape[1]
    rows = 2 * blk
    row = lambda n: pl.BlockSpec((blk, n), lambda i, s: (i, 0))
    flat, specs = out_weights(slots, cols)
    return pl.pallas_call(
        functools.partial(attn_out_kernel, counts=[len(t) for t in slots], chips=chips, fast=fast),
        grid_spec=pltpu.PrefetchScalarGridSpec(
            num_scalar_prefetch=1,
            grid=(2,),
            in_specs=specs
            + [full_spec(ya.shape)] * 2
            + [own_rows(blk, parts, width, fast), full_spec((1, width))],
            out_specs=[row(width)] * 3
            + [row(128)]
            + [pl.BlockSpec((parts, blk, n), lambda i, s: (0, i, 0)) for n in (cols, cols // 2)],
            scratch_shapes=[pltpu.VMEM((blk, width), f32)],
        ),
        out_shape=[jax.ShapeDtypeStruct((rows, width), d) for d in (f32, f32, bf16)]
        + [jax.ShapeDtypeStruct((rows, 128), f32)]
        + [jax.ShapeDtypeStruct((parts, rows, n), bf16) for n in (cols, cols // 2)],
        compiler_params=params(56),
    )(place, *flat, ya, yb, x, alpha)


def loss_kernel(place_ref, own_ref, got_ref, h1_ref, cot_ref, alpha_ref, hidden_ref, dmo_ref, base_ref, ga_ref, *, chips, fast):
    chip = place_ref[1]
    total = own_ref[...] + got_ref[...].astype(f32)
    alpha = alpha_ref[...]
    norm = row_norm(total)
    inner = total * norm
    h1 = h1_ref[...]
    mixed = h1 + alpha * (inner - h1)
    last = row_norm(mixed)
    hidden = mixed * last
    grad = norm_back(last, hidden, put_relative(cot_ref, chip, chips, fast).astype(f32))
    put_natural(hidden_ref, hidden.astype(bf16), chip, chips, fast)
    base_ref[...] = (1.0 - alpha) * grad
    dmo_ref[...] = norm_back(norm, inner, alpha * grad).astype(bf16)

    @pl.when(pl.program_id(0) == 0)
    def _():
        ga_ref[...] = jnp.zeros_like(ga_ref)

    ga_ref[0:1, :] += jnp.sum(grad * (inner - h1), axis=0, keepdims=True)


def loss(place, own, got, h1, cot, alpha, chips, fast):
    rows, width = own.shape
    blk = rows // 2
    row = pl.BlockSpec((blk, width), lambda i, s: (i, 0))
    part = row
    if fast:
        part = pl.BlockSpec((chips, blk, width // chips), lambda i, s: (0, i, 0))
    return pl.pallas_call(
        functools.partial(loss_kernel, chips=chips, fast=fast),
        grid_spec=pltpu.PrefetchScalarGridSpec(
            num_scalar_prefetch=1,
            grid=(rows // blk,),
            in_specs=[row] * 3 + [part, full_spec((1, width))],
            out_specs=[part] + [row] * 2 + [full_spec((8, width))],
        ),
        out_shape=[jax.ShapeDtypeStruct(cot.shape, bf16)]
        + [jax.ShapeDtypeStruct((rows, width), d) for d in (bf16, f32)]
        + [jax.ShapeDtypeStruct((8, width), f32)],
        compiler_params=params(56),
    )(place, own, got, h1, cot, alpha)


def first_back_kernel(place_ref, *refs, counts, chips, fast):
    total = sum(counts)
    flat, refs = refs[:total], refs[total:]
    own_ref, got_ref, base_ref, h1_ref, ha_ref, x_ref, stat_ref, alpha_ref = refs[:8]
    do_ref, through_ref, ga_ref, dy_ref = refs[8:]
    z, chip = place_ref[0], place_ref[1]
    alpha = alpha_ref[...]
    grad = base_ref[...] + own_ref[...] + got_ref[...].astype(f32)
    grad = norm_back(stat_ref[:, 1:2], h1_ref[...], grad)
    ha = ha_ref[...]
    put_natural(through_ref, ((1.0 - alpha) * grad).astype(bf16), chip, chips, fast)
    back = norm_back(stat_ref[:, 0:1], ha, alpha * grad).astype(bf16)
    do_ref[...] = back
    parts = len(counts)
    step = pl.program_id(0)
    index = 0
    for n in range(parts):
        at = lax.rem(z + parts - n, parts)
        part = jnp.zeros(dy_ref.shape[1:], f32)
        column = 0
        for piece in flat[index : index + counts[n]]:
            part += dot(back[:, column : column + piece.shape[0]], piece[...])
            column += piece.shape[0]
        index += counts[n]
        dy_ref[at] = part.astype(bf16)

    @pl.when(step == 0)
    def _():
        ga_ref[...] = jnp.zeros_like(ga_ref)

    start = put_relative(x_ref, chip, chips, fast).astype(f32)
    ga_ref[0:1, :] += jnp.sum(grad * (ha - start), axis=0, keepdims=True)


def first_back(place, own, got, base, h1, ha, x, stat, alpha, slots, chips, fast, cols):
    rows, width = own.shape
    parts = len(slots)
    blk = rows // 2
    row = lambda n: pl.BlockSpec((blk, n), lambda i, s: (i, 0))
    flat, specs = out_weights(slots, cols)
    through, shape = row(width), (rows, width)
    if fast:
        through = pl.BlockSpec((parts, blk, cols), lambda i, s: (0, i, 0))
        shape = (parts, rows, cols)
    return pl.pallas_call(
        functools.partial(first_back_kernel, counts=[len(t) for t in slots], chips=chips, fast=fast),
        grid_spec=pltpu.PrefetchScalarGridSpec(
            num_scalar_prefetch=1,
            grid=(2,),
            in_specs=specs
            + [row(width)] * 5
            + [own_rows(blk, parts, width, fast), row(128), full_spec((1, width))],
            out_specs=[row(width), through]
            + [full_spec((8, width)), pl.BlockSpec((parts, blk, cols), lambda i, s: (0, i, 0))],
        ),
        out_shape=[jax.ShapeDtypeStruct((rows, width), bf16), jax.ShapeDtypeStruct(shape, bf16)]
        + [
            jax.ShapeDtypeStruct((8, width), f32),
            jax.ShapeDtypeStruct((parts, rows, cols), bf16),
        ],
        compiler_params=params(56),
    )(place, *flat, own, got, base, h1, ha, x, stat, alpha)


def fetch_weights(q, slots, wbuf, sems):
    def copies(j):
        at = 0
        found = []
        for p, piece in enumerate(slots[j]):
            size = piece.shape[0]
            found.append(
                pltpu.make_async_copy(
                    piece.at[:, : wbuf.shape[2]], wbuf.at[j % 2, at : at + size, :], sems.at[j % 2, p]
                )
            )
            at += size
        return found

    for j in range(len(slots)):

        @pl.when(q == j)
        def _(j=j):
            if j == 0:
                for copy in copies(0):
                    copy.start()
            if j + 1 < len(slots):
                for copy in copies(j + 1):
                    copy.start()
            for copy in copies(j):
                copy.wait()


def mlp_fwd_kernel(*refs, half, counts):
    total = sum(counts)
    flat, refs = refs[:total], refs[total:]
    slots, at = [], 0
    for n in counts:
        slots.append(flat[at : at + n])
        at += n
    ha_ref, hb_ref, act_ref, uv_ref, own_ref, got_ref, acc, wbuf, sems = refs
    rows = ha_ref.shape[0]
    q = pl.program_id(0)

    @pl.when(q == 0)
    def _():
        own_ref[...] = jnp.zeros_like(own_ref)
        acc[...] = jnp.zeros_like(acc)

    fetch_weights(q, slots, wbuf, sems)
    w = wbuf.at[lax.rem(q, 2)]
    for base, h_ref, sum_ref in ((0, ha_ref, own_ref), (rows, hb_ref, acc)):
        at = slice(base, base + rows)
        pair = dot(h_ref[...], w[:, : 2 * half])
        lifted = pair[:, :half]
        gated = pair[:, half:]
        act = (lifted * gated * jax.nn.sigmoid(gated)).astype(bf16)
        uv_ref[at, :] = pair.astype(bf16)
        act_ref[at, :] = act
        sum_ref[...] += dot_t(act, w[:, 2 * half : 3 * half])

    @pl.when(q == pl.num_programs(0) - 1)
    def _():
        got_ref[...] = acc[...].astype(bf16)


def mlp_fwd(ha, hb, slots, half):
    rows, width = ha.shape
    parts = len(slots)
    take = lambda n: pl.BlockSpec((None, 2 * rows, n), lambda q: (q, 0, 0))
    whole = full_spec((rows, width))
    anywhere = pl.BlockSpec(memory_space=pl.ANY)
    flat = [p for slot in slots for p in slot]
    return pl.pallas_call(
        functools.partial(mlp_fwd_kernel, half=half, counts=[len(s) for s in slots]),
        grid=(parts,),
        in_specs=[anywhere] * len(flat)
        + [whole, whole],
        out_specs=[take(half), take(2 * half), whole, whole],
        out_shape=[
            jax.ShapeDtypeStruct((parts, 2 * rows, half), bf16),
            jax.ShapeDtypeStruct((parts, 2 * rows, 2 * half), bf16),
            jax.ShapeDtypeStruct((rows, width), f32),
            jax.ShapeDtypeStruct((rows, width), bf16),
        ],
        scratch_shapes=[
            pltpu.VMEM((rows, width), f32),
            pltpu.VMEM((2, width, 3 * half), bf16),
            pltpu.SemaphoreType.DMA((2, max(len(s) for s in slots))),
        ],
        compiler_params=params(56),
    )(*flat, ha, hb)


def mlp_bwd_kernel(*refs, half, counts):
    total = sum(counts)
    flat, refs = refs[:total], refs[total:]
    slots, at = [], 0
    for n in counts:
        slots.append(flat[at : at + n])
        at += n
    da_ref, db_ref, uv_ref, duv_ref, own_ref, got_ref, gs_ref, acc, wbuf, sems = refs
    rows = da_ref.shape[0]
    q = pl.program_id(0)

    @pl.when(q == 0)
    def _():
        own_ref[...] = jnp.zeros_like(own_ref)
        acc[...] = jnp.zeros_like(acc)

    gs_ref[...] = jnp.zeros_like(gs_ref)
    fetch_weights(q, slots, wbuf, sems)
    w = wbuf.at[lax.rem(q, 2)]
    for base, d_ref, sum_ref in ((0, da_ref, own_ref), (rows, db_ref, acc)):
        at = slice(base, base + rows)
        grad = dot(d_ref[...], w[:, 2 * half : 3 * half])
        lifted = uv_ref[at, :half].astype(f32)
        gated = uv_ref[at, half:].astype(f32)
        sigma = jax.nn.sigmoid(gated)
        da = grad * gated * sigma
        db = grad * lifted * sigma * (1.0 + gated * (1.0 - sigma))
        gs_ref[0:1, :] += jnp.sum(da * lifted, axis=0, keepdims=True)
        gs_ref[1:2, :] += jnp.sum(db * gated, axis=0, keepdims=True)
        duv_ref[at, :half] = da.astype(bf16)
        duv_ref[at, half:] = db.astype(bf16)
        sum_ref[...] += dot_t(duv_ref[at, :], w[:, : 2 * half])

    @pl.when(q == pl.num_programs(0) - 1)
    def _():
        got_ref[...] = acc[...].astype(bf16)


def mlp_bwd(da, db, slots, uv, half):
    rows, width = da.shape
    parts = len(slots)
    take = lambda n: pl.BlockSpec((None, 2 * rows, n), lambda q: (q, 0, 0))
    whole = full_spec((rows, width))
    anywhere = pl.BlockSpec(memory_space=pl.ANY)
    flat = [p for slot in slots for p in slot]
    return pl.pallas_call(
        functools.partial(mlp_bwd_kernel, half=half, counts=[len(s) for s in slots]),
        grid=(parts,),
        in_specs=[anywhere] * len(flat)
        + [
            whole,
            whole,
            take(2 * half),
        ],
        out_specs=[
            take(2 * half),
            whole,
            whole,
            pl.BlockSpec((None, 8, half), lambda q: (q, 0, 0)),
        ],
        out_shape=[
            jax.ShapeDtypeStruct((parts, 2 * rows, 2 * half), bf16),
            jax.ShapeDtypeStruct((rows, width), f32),
            jax.ShapeDtypeStruct((rows, width), bf16),
            jax.ShapeDtypeStruct((parts, 8, half), f32),
        ],
        scratch_shapes=[
            pltpu.VMEM((rows, width), f32),
            pltpu.VMEM((2, width, 3 * half), bf16),
            pltpu.SemaphoreType.DMA((2, max(len(s) for s in slots))),
        ],
        compiler_params=params(56),
    )(*flat, da, db, uv)


EXTRA = 16


def grad_kernel(place_ref, *refs, orders, parts, chunk, more):
    ha_ref, hb_ref = refs[:2]
    refs = refs[2:]
    if more:
        oa_ref, ob_ref, ya_ref, yb_ref, gs_ref, g1_ref, g2_ref = refs[:7]
        refs = refs[7:]
    val_ref, *outs = refs[:5]
    turned = refs[5]
    rows = ha_ref.shape[0]
    k = pl.program_id(0)

    @pl.when(k == 0)
    def _():
        turned[:, :rows] = ha_ref[...].T
        turned[:, rows:] = hb_ref[...].T
        if more:
            refs[6][:, :rows] = oa_ref[...].T
            refs[6][:, rows:] = ob_ref[...].T

    if more:
        size = outs[0].shape[2]
        fill = lambda row: jnp.concatenate([row, jnp.zeros((1, size - row.shape[1]), f32)], axis=1)
        line = lax.broadcasted_iota(jnp.int32, (EXTRA, size), 0)
        units = fill(jnp.concatenate([gs_ref[0:1, :], gs_ref[1:2, :]], axis=1))
        steps = fill(jnp.concatenate([g1_ref[0:1, :], g2_ref[0:1, :]], axis=1))
        extra = jnp.where(line == 0, units, jnp.where(line == 1, steps, 0.0)).astype(bf16)

    for side in range(2):

        @pl.when((k < parts // 2) == (side == 0))
        def _(side=side):
            for which, ref in zip(orders[side], outs[2 * side : 2 * side + 2]):
                for j, r in enumerate(which):
                    at = slice(r * chunk, (r + 1) * chunk)
                    value = dot(turned[at, :], val_ref[...]).astype(bf16)
                    size = value.shape[1]
                    ref[j, :chunk, :size] = value
                    if more:
                        ref[j, :chunk, size:] = (
                            dot(refs[6][at, :rows], ya_ref[...]) + dot(refs[6][at, rows:], yb_ref[...])
                        ).astype(bf16)
                        ref[j, chunk:, :] = extra


def weight_grads(place, sends, keeps, chips, hs, value, os=None, ys=None, extra=None):
    rows, width = hs[0].shape
    chunk = width // chips
    parts, _, size = value.shape
    more = os is not None
    hc = ys[1].shape[2] if more else 0
    tall = chunk + (EXTRA if more else 0)
    middle = parts // 2
    if chunk % 128:
        result = []
        for which, lo in ((sends[0], 0), (keeps[0], 0), (sends[1], middle), (keeps[1], middle)):
            cut = lambda pair: jnp.concatenate(
                [jnp.concatenate(pair, axis=0)[:, r * chunk : (r + 1) * chunk] for r in which], axis=1
            )
            found = []
            for k in range(lo, lo + middle):
                one = t_dot(cut(hs), value[k])
                if more:
                    at = (place[0] - k) % parts
                    y = lax.dynamic_index_in_dim(ys[0], at, 0, keepdims=False)
                    y = lax.dynamic_slice_in_dim(y, place[2] * hc, hc, 1)
                    y = jnp.concatenate([y, lax.dynamic_index_in_dim(ys[1], at, 0, keepdims=False)])
                    one = jnp.concatenate([one, t_dot(cut(os), y)], axis=1)
                one = one.reshape(len(which), chunk, size + hc)
                if more:
                    wide = jnp.broadcast_to(extra[k][None], (len(which), EXTRA, size + hc))
                    one = jnp.concatenate([one, wide], axis=1)
                found.append(one.astype(bf16))
            result.append(jnp.stack(found, axis=1))
        return [result[0], result[2]], [result[1], result[3]]
    whole = full_spec((rows, width))
    ins = list(hs)
    in_specs = [whole] * 2
    scratch = [pltpu.VMEM((width, 2 * rows), bf16)]
    if more:
        slot = lambda k, p: lax.rem(p[0] + parts - k, parts)
        cols = ys[0].shape[2]
        part = pl.BlockSpec((8, cols), lambda k, p: (0, slot(k, p) ^ p[1]))
        ins += [*os, ys[0], ys[1], *extra]
        in_specs += [whole] * 2
        in_specs += [
            pl.BlockSpec((None, rows, hc), lambda k, p: (slot(k, p), 0, p[2])),
            pl.BlockSpec((None, rows, hc), lambda k, p: (slot(k, p), 0, 0)),
            pl.BlockSpec((None, 8, size // 2), lambda k, p: (k, 0, 0)),
            part,
            part,
        ]
        scratch = scratch * 2
    ins.append(value)
    in_specs.append(pl.BlockSpec((None, 2 * rows, size), lambda k, p: (k, 0, 0)))
    lists = [sends[0], keeps[0], sends[1], keeps[1]]
    block = lambda one: (len(one), None, tall, size + hc)
    early = lambda k, p: (0, jnp.minimum(k, middle - 1), 0, 0)
    late = lambda k, p: (0, jnp.maximum(k - middle, 0), 0, 0)
    out = pl.pallas_call(
        functools.partial(
            grad_kernel, orders=(lists[:2], lists[2:]), parts=parts, chunk=chunk, more=more
        ),
        grid_spec=pltpu.PrefetchScalarGridSpec(
            num_scalar_prefetch=1,
            grid=(parts,),
            in_specs=in_specs,
            out_specs=[
                pl.BlockSpec(block(one), early if n < 2 else late) for n, one in enumerate(lists)
            ],
            scratch_shapes=scratch,
        ),
        out_shape=[
            jax.ShapeDtypeStruct((len(one), middle, tall, size + hc), bf16) for one in lists
        ],
        compiler_params=params(56),
    )(place, *ins)
    return [out[0], out[2]], [out[1], out[3]]


def pair_sum_kernel(ka_ref, ga_ref, kb_ref, gb_ref, a_ref, b_ref):
    a_ref[...] = (ka_ref[...].astype(f32) + ga_ref[...].astype(f32)).astype(bf16)
    b_ref[...] = (kb_ref[...].astype(f32) + gb_ref[...].astype(f32)).astype(bf16)


def pair_sums(kept, got, at):
    _, slots, tall, wide = kept[0].shape
    spec = lambda n: pl.BlockSpec((None, None, tall, wide), lambda k, n=n: (n, k, 0, 0))
    return pl.pallas_call(
        pair_sum_kernel,
        grid=(slots,),
        in_specs=[spec(at[0]), spec(at[0]), spec(at[1]), spec(at[1])],
        out_specs=[spec(0)] * 2,
        out_shape=[jax.ShapeDtypeStruct((1, slots, tall, wide), bf16)] * 2,
        compiler_params=params(56),
    )(kept[0], got[0], kept[1], got[1])


def adam_values(weight, grad, first, second):
    first_new = beta_one * first + (1.0 - beta_one) * grad
    second_new = beta_two * second + (1.0 - beta_two) * grad * grad
    moved = weight - learn_rate * (first_new / bias_one) / (
        jnp.sqrt(second_new / bias_two) + adam_eps
    )
    return first_new, second_new, moved


def lane_sums(value):
    ones = jnp.ones((8, value.shape[1]), bf16)
    high = value.astype(bf16)
    low = (value - high.astype(f32)).astype(bf16)
    return dot_t(ones, high) + dot_t(ones, low)


def adam_wide_kernel(w_ref, g_ref, m_ref, v_ref, g_out, m_out, v_out, n_out, s_out):
    cols = w_ref.shape[2]
    for c in range(w_ref.shape[1]):
        grad = g_ref[:, c * cols : (c + 1) * cols]
        first, second, moved = adam_values(w_ref[:, c, :], grad, m_ref[:, c, :], v_ref[:, c, :])
        g_out[:, c, :] = grad
        m_out[:, c, :] = first
        v_out[:, c, :] = second
        n_out[:, c, :] = moved
        s_out[c : c + 1, :] = jnp.sum(moved * moved, axis=0, keepdims=True)


def adam_wide(w, g, m, v):
    vmem = pl.BlockSpec(memory_space=pltpu.VMEM)
    return pl.pallas_call(
        adam_wide_kernel,
        in_specs=[vmem] * 4,
        out_specs=[vmem] * 5,
        out_shape=[jax.ShapeDtypeStruct(w.shape, f32)] * 4
        + [jax.ShapeDtypeStruct(w.shape[1:], f32)],
        compiler_params=params(16),
    )(w, g, m, v)


def adam_tall_kernel(w_ref, g_ref, m_ref, v_ref, g_out, m_out, v_out, n_out, s_out):
    grad = g_ref[...].T
    first, second, moved = adam_values(w_ref[...], grad, m_ref[...], v_ref[...])
    g_out[...] = grad
    m_out[...] = first
    v_out[...] = second
    n_out[...] = moved
    s_out[...] = lane_sums(moved * moved)


def adam_tall(w, g, m, v):
    vmem = pl.BlockSpec(memory_space=pltpu.VMEM)
    return pl.pallas_call(
        adam_tall_kernel,
        in_specs=[vmem] * 4,
        out_specs=[vmem] * 5,
        out_shape=[jax.ShapeDtypeStruct(w.shape, f32)] * 4
        + [jax.ShapeDtypeStruct((8, w.shape[0]), f32)],
        compiler_params=params(16),
    )(w, g, m, v)


def scale_kernel(na_ref, nb_ref, nc_ref, nd_ref, a_ref, b_ref, c_ref, d_ref, ao_ref, bo_ref, co_ref, do_ref, *, width):
    factor = lambda value: lax.rsqrt(value / width + layer_eps)
    for norm, ref, out in ((na_ref, a_ref, ao_ref), (nc_ref, c_ref, co_ref)):
        for c in range(ref.shape[1]):
            out[:, c, :] = ref[:, c, :] * factor(norm[c : c + 1, :])
    for norm, ref, out in ((nb_ref, b_ref, bo_ref), (nd_ref, d_ref, do_ref)):
        out[...] = ref[...] * factor(norm[...]).T[:, 0:1]


def scale_weights(norms, weights, width):
    vmem = pl.BlockSpec(memory_space=pltpu.VMEM)
    return pl.pallas_call(
        functools.partial(scale_kernel, width=width),
        in_specs=[vmem] * 8,
        out_specs=[vmem] * 4,
        out_shape=[jax.ShapeDtypeStruct(w.shape, f32) for w in weights],
        compiler_params=params(16),
    )(*norms, *weights)


def after(value, *others):
    return lax.optimization_barrier((value, *others))[0]


def per_device(
    layer_input,
    cotangent,
    positions,
    w_qkv,
    w_out,
    w_up,
    w_down,
    moment_qkv,
    moment_out,
    moment_up,
    moment_down,
    square_qkv,
    square_out,
    square_up,
    square_down,
    s_qk,
    alpha_attn,
    alpha_mlp,
    s_uv,
):
    nz = lax.axis_size("head")
    nb = lax.axis_size("batch")
    z = lax.axis_index("head")
    b = lax.axis_index("batch")
    core = b % 2
    chip = b // 2
    chips = nb // 2
    bits = [1 << n for n in range(int(math.log2(chips)))]
    rows, cols = layer_input.shape
    width = cols * nz
    own = rows // nz
    hid = w_down.shape[0]
    half = hid // 2
    hc = cols // 2
    heads = cols // HEAD_DIM
    span = w_qkv.shape[0]
    chunk = width // chips
    core_s = core.reshape(1).astype(jnp.int32)
    place = jnp.stack([z, chip, core]).astype(jnp.int32)
    fast = chunk == cols and chunk % 128 == 0

    def swap_batch(value, bit):
        return lax.ppermute(value, "batch", [(i, i ^ bit) for i in range(nb)])

    def swap_core(value):
        return swap_batch(value, 1)

    def swap_chip(value, bit):
        return swap_batch(value, 2 * bit)

    def onward(value, k=1):
        return lax.ppermute(value, "head", [(i, (i + k) % nz) for i in range(nz)])

    def exchange(value):
        return lax.all_to_all(value, "head", split_axis=0, concat_axis=0)

    def pick(pair, index):
        return jnp.where(index == 0, pair[0], pair[1])

    def relative(value):
        return jnp.concatenate(
            [
                lax.dynamic_slice_in_dim(value, (chip ^ r) * chunk, chunk, value.ndim - 1)
                for r in range(chips)
            ],
            axis=-1,
        )

    def spread(value):
        if chips <= 4:
            return [value] + [swap_chip(value, r) for r in range(1, chips)]
        for bit in bits:
            value = jnp.concatenate([value, swap_chip(value, bit)], axis=0)
        return [value]

    tokens = [layer_input, onward(layer_input)]
    mine, theirs = pack(core_s, w_up, s_uv, w_down, w_out)
    qkv_own = after(w_qkv, mine).reshape(span, 3 * cols).astype(bf16)
    qkv_full = lax.all_gather(qkv_own, "batch", axis=0, tiled=True)
    theirs = swap_core(theirs)
    packet = jnp.concatenate([pick((mine, theirs), core), pick((theirs, mine), core)], axis=0)
    hops = [packet, onward(packet)]
    slots = [spread(packet)]
    tokens[1], hops[1], places, alpha_attn, alpha_mlp, *last = lax.optimization_barrier(
        (tokens[1], hops[1], positions, alpha_attn, alpha_mlp, *slots[0])
    )
    slots[0] = list(last)

    freqs = jnp.exp(
        (jnp.arange(128) % (HEAD_DIM // 2)).astype(f32) * (-2.0 * math.log(10000.0) / HEAD_DIM)
    )
    phase = places.astype(f32)[:, None] * freqs[None, :]
    side = jnp.where(jnp.arange(128) % HEAD_DIM < HEAD_DIM // 2, -1.0, 1.0).astype(f32)
    cosine, sine = jnp.cos(phase), jnp.sin(phase) * side[None, :]
    lane = jnp.arange(cols) // HEAD_DIM
    ones = (lane[:, None] == lane[None, :]).astype(bf16)
    gain = s_qk.reshape(1, cols)
    is_long = (places[SHORT : SHORT + 1] != 0).astype(jnp.int32)
    attn_gain = relative(alpha_attn[None])
    mlp_gain = relative(alpha_mlp[None])

    for n in range(2, nz):
        slots.append(spread(hops[-1]))
        tokens.append(onward(tokens[-1]))
        if n < nz - 1:
            hops.append(onward(hops[-1]))
            tokens[-1], hops[-1], cosine, sine, ones, attn_gain, mlp_gain, *last = (
                lax.optimization_barrier(
                    (tokens[-1], hops[-1], cosine, sine, ones, attn_gain, mlp_gain, *slots[-1])
                )
            )
            slots[-1] = list(last)
    last_hop, tokens[-1] = lax.optimization_barrier((hops[-1], tokens[-1]))
    hops.append(onward(last_hop))

    blocks = rows // 512
    middle = blocks // 2
    tokens_full, q, k, v, rho = qkv_project(place, tokens, qkv_full, cosine, sine, gain, ones)
    y_a, logs_a = attn_fwd(is_long, q, k, v, 0, middle)
    q_b, hops[-1], *last = lax.optimization_barrier((after(q, y_a), hops[-1], *slots[-1]))
    slots[-1] = list(last)
    slots.append(spread(hops[-1]))
    y_b, logs_b = attn_fwd(is_long, q_b, k, v, middle, blocks - middle)
    y_one = exchange(y_a.reshape(nz, own // 2, cols))
    y_in, y_one = lax.optimization_barrier((y_b, y_one))
    y_two = exchange(y_in.reshape(nz, own // 2, cols))
    flat = lambda value: value.transpose(1, 0, 2).reshape(own, width)
    start = tokens_full
    if not fast:
        start = jnp.concatenate(
            [
                lax.dynamic_slice_in_dim(tokens_full, h * (rows // 2) + z * (own // 2), own // 2, 0)
                for h in range(2)
            ]
        )
        start = relative(start)
    y_one, y_two, *last = lax.optimization_barrier((y_one, y_two, *slots[-1]))
    slots[-1] = list(last)
    hA, h1, h_own, stat, y_mine, y_other = attn_out(place, y_one, y_two, slots, start, attn_gain, chips, fast)
    h_got = swap_core(h_own)
    y_got = swap_core(y_other)
    h_got, y_got = lax.optimization_barrier((h_got, y_got))
    cot = after(cotangent, h_own).reshape(2, nz, own // 2, cols).transpose(1, 0, 2, 3)
    cot = exchange(cot.reshape(nz, own, cols))

    act, uv, mo_own, mo_other = mlp_fwd(h_own, h_got, slots, half)
    mo_got = swap_core(mo_other)
    if not fast:
        cot = relative(flat(cot))
    hidden, d_own, base, ga_mlp = loss(place, mo_own, mo_got, h1, cot, mlp_gain, chips, fast)
    d_got = swap_core(d_own)
    if not fast:
        hidden = relative(hidden).reshape(own, nz, cols).transpose(1, 0, 2)
    hidden = exchange(hidden)

    orders = [bits, bits[::-1]]
    sent_at = [[r for r in range(chips) if r & order[0]] for order in orders]
    kept_at = [[r for r in range(chips) if not r & order[0]] for order in orders]

    def second(kept, sent):
        found, sends = [], []
        if chips == 4:
            at = [[n for n, r in enumerate(left) if r & order[1]] for order, left in zip(orders, kept_at)]
            sends = pair_sums(kept, sent, [one[0] for one in at])
            for order, one, keep, got, send in zip(orders, at, kept, sent, sends):
                cut = lambda t, n=1 - one[0]: t[n : n + 1]
                found.append([cut(keep), cut(got), swap_chip(send, order[1])])
            return found, sends
        for order, left, got, keep in zip(orders, kept_at, sent, kept):
            terms = [keep, got]
            for bit in order[1:]:
                send_at = [n for n, r in enumerate(left) if r & bit]
                keep_at = [n for n, r in enumerate(left) if not r & bit]
                left = [left[n] for n in keep_at]
                cut = lambda v, at: jnp.concatenate([v[n : n + 1] for n in at], axis=0)
                send = sum(cut(t, send_at).astype(f32) for t in terms).astype(bf16)
                terms = [cut(t, keep_at) for t in terms] + [swap_chip(send, bit)]
                sends.append(send)
            found.append(terms)
        return found, sends

    def slot_sums(found):
        return [sum(t[0, n].astype(f32) for t in terms) for terms in found for n in range(nz // 2)]

    def wait_last(found, *others):
        return [terms[:-1] + [after(terms[-1], *others)] for terms in found]

    down_made, down_kept = weight_grads(place, sent_at, kept_at, chips, (d_own, d_got), act)
    down_sent = [swap_chip(one, order[0]) for one, order in zip(down_made, orders)]
    d_own, d_got, *_ = lax.optimization_barrier((d_own, d_got, *down_made))
    duv, dh_own, dh_other, gsuv = mlp_bwd(d_own, d_got, slots, uv, half)
    dh_got = swap_core(dh_other)
    down_sent = [after(one, dh_other) for one in down_sent]
    down_part, down_next = second(down_kept, down_sent)
    dh_own, hidden, *_ = lax.optimization_barrier((dh_own, hidden, *down_next))
    do_own, through, ga_attn, dy = first_back(
        place, dh_own, dh_got, base, h1, hA, start, stat, attn_gain, slots, chips, fast, cols
    )
    dy = exchange(dy)
    do_got = swap_core(do_own)

    extra = (gsuv, ga_attn, ga_mlp)
    if not fast:
        alphas = [relative(ga_attn[0:1]), relative(ga_mlp[0:1])]
        extra = []
        wide = 2 * half + hc
        fill = lambda r: jnp.pad(r, ((0, 0), (0, wide - r.shape[1])))
        for n in range(nz):
            at = ((z - n) % nz) * cols
            line = [lax.dynamic_slice_in_dim(g, at, cols, 1) for g in alphas]
            lines = [gsuv[n, :2].reshape(1, 2 * half), jnp.concatenate(line, axis=1)]
            lines = jnp.concatenate([fill(r) for r in lines])
            extra.append(jnp.pad(lines, ((0, EXTRA - 2), (0, 0))))
        extra = jnp.stack(extra)
    up_made, up_kept = weight_grads(
        place, sent_at, kept_at, chips, (h_own, h_got), duv, (do_own, do_got), (y_mine, y_got), extra
    )
    down_part = wait_last(down_part, *up_kept)
    down_last = [terms[-1] for terms in down_part]
    dy, *both = lax.optimization_barrier((dy, *up_made, *down_last))
    up_made, down_last = both[: len(up_made)], both[len(up_made) :]
    down_slots = slot_sums([t[:-1] + [last] for t, last in zip(down_part, down_last)])
    down_along = [onward(down_slots[n].astype(bf16), nz - n) for n in range(1, nz)]
    up_sent = [swap_chip(one, order[0]) for one, order in zip(up_made, orders)]

    dy = dy.reshape(nz, 2, own // 2, cols)
    common = lambda y, logs: (
        is_long, q, k, v, dy, y, logs, rho, cosine, sine, gain, ones
    )
    dqkv_b, dk_part, dv_part, sqk_b = attn_bwd(
        *common(y_b, logs_b), middle, blocks - middle, None
    )

    if not fast:
        through = relative(through).reshape(own, nz, cols).transpose(1, 0, 2)
    mine_at = z * (own // 2)
    qkv_parts = qkv_full.reshape(nz, cols, 3 * cols)

    def input_part(dqkv, side):
        part = jnp.einsum("tn,zcn->ztc", dqkv, qkv_parts, preferred_element_type=f32).astype(bf16)
        here = lax.dynamic_slice_in_dim(part, mine_at, own // 2, 1).astype(f32)
        more = after(through, dqkv)[:, side * (own // 2) : (side + 1) * (own // 2)]
        return lax.dynamic_update_slice_in_dim(part, (here + more.astype(f32)).astype(bf16), mine_at, 1)

    part_b = input_part(dqkv_b, 1)
    down_along = [after(one, dqkv_b) for one in down_along]
    part_got = exchange(part_b)
    dk_part, *_ = lax.optimization_barrier((dk_part, part_b, *down_along))
    dqkv_a, sqk_a = attn_bwd(*common(y_a, logs_a), 0, middle, [dk_part, dv_part])
    input_b = jnp.sum(after(part_got, dqkv_a).astype(f32), axis=0)
    up_part, up_next = second(up_kept, [after(one, dqkv_a) for one in up_sent])
    dqkv_a, *_ = lax.optimization_barrier((dqkv_a, *up_next))
    part_a = input_part(dqkv_a, 0)
    dqkv = jnp.concatenate([dqkv_a, dqkv_b], axis=0)
    grad_qkv = t_dot(tokens_full, dqkv).astype(bf16)
    sqk = jnp.pad((sqk_a + sqk_b), ((0, EXTRA - 8), (0, 2 * cols)))
    shard = [lax.dynamic_slice_in_dim(grad_qkv, (b ^ r) * span, span, 0) for r in range(nb)]
    shard = [jnp.concatenate([t, sqk.astype(bf16)], axis=0) for t in shard]
    odd = [r for r in range(nb) if r & 1]
    early = swap_core(jnp.concatenate([shard[r] for r in odd], axis=0))

    def both_halves(total, *wait):
        two = (total[:span], total[span : 2 * span])
        here = jnp.concatenate([pick(two, core), total[2 * span :]], axis=0)
        there = jnp.concatenate([pick(two, 1 - core), total[2 * span :]], axis=0)
        there = swap_core(there.astype(bf16))
        if wait:
            there = after(there, *wait)
        return here, there

    def in_order(here, there):
        there = there.astype(f32)
        return [pick((here, there), core), pick((there, here), core)]

    down_along = [after(one, part_a) for one in down_along]
    down_here, down_there = both_halves(
        down_slots[0] + sum(one.astype(f32) for one in down_along)
    )
    up_part = wait_last(up_part, part_a, early, down_there, *[terms[-1] for terms in up_part])
    up_slots = slot_sums(up_part)
    passed = up_slots[1].astype(bf16)
    part_a, passed, early, down_there = lax.optimization_barrier((part_a, passed, early, down_there))
    passed = onward(passed)
    for n in range(2, nz):
        if n == nz - 1:
            passed, part_a = lax.optimization_barrier((passed, part_a))
        passed = onward((up_slots[n] + passed.astype(f32)).astype(bf16))
    sum_up_t = up_slots[0] + passed.astype(f32)
    input_a = lax.psum_scatter(part_a.reshape(-1, cols), "head", scatter_dimension=0, tiled=True)
    input_grad = jnp.concatenate([input_a.astype(f32), input_b], axis=0)
    hidden_t = after(hidden, part_a).reshape(nz, 2, own // 2, cols).transpose(1, 0, 2, 3).reshape(rows, cols)

    qbits = [1 << n for n in range(int(math.log2(nb)))]
    held = {r: shard[r] for r in range(nb)}
    for bit in qbits:
        send_at = [r for r in held if r & bit]
        send = jnp.concatenate([held[r] for r in send_at], axis=0).astype(bf16)
        got = early if bit == 1 else swap_batch(send, bit)
        size = span + EXTRA
        held = {
            r ^ bit: held[r ^ bit].astype(f32) + got[n * size : (n + 1) * size].astype(f32)
            for n, r in enumerate(send_at)
        }
    cell = width // (nz * nb)
    sum_sqk = lax.dynamic_slice_in_dim(held[0][span, :cols], b * cell, cell, 0)
    w_late, m_late, v_late, _ = lax.optimization_barrier((w_qkv, moment_qkv, square_qkv, part_a))
    qkv_new = adam_wide(w_late, held[0][:span], m_late, v_late)

    join = lambda halves, at, size: [p[:span, at : at + size] for p in halves]
    halves = in_order(down_here, down_there)
    down_new = adam_tall(w_down, jnp.concatenate(join(halves, 0, half), axis=1), moment_down, square_down)
    halves = in_order(*both_halves(sum_up_t))
    grad_up = jnp.concatenate(join(halves, 0, half) + join(halves, half, half), axis=1)
    grad_up = grad_up * s_uv.reshape(1, 2 * hid)
    up_new = adam_wide(w_up, grad_up, moment_up, square_up)
    out_new = adam_tall(w_out, jnp.concatenate(join(halves, 2 * half, hc), axis=1), moment_out, square_out)
    suv_rows = jnp.stack(
        [jnp.concatenate([p[span, c * half : (c + 1) * half] for p in halves]) for c in range(2)]
    )
    suv_rows = suv_rows / s_uv
    sum_suv = lax.dynamic_slice_in_dim(suv_rows, b * (hid // nb), hid // nb, 1)
    alphas = halves[0][span + 1] + halves[1][span + 1]
    sum_attn = lax.dynamic_slice_in_dim(alphas[:cols], b * cell, cell, 0)
    sum_mlp = lax.dynamic_slice_in_dim(alphas[cols : 2 * cols], b * cell, cell, 0)

    hidden = hidden_t.astype(f32)

    squares = [qkv_new[4], out_new[4][:1], up_new[4], down_new[4][:1]]
    sizes = [t.size for t in squares]
    norms = jnp.concatenate([t.reshape(-1) for t in squares]).reshape(-1, 128)
    for bit in qbits:
        norms = norms + swap_batch(norms, bit)
    norms = norms.reshape(-1)
    ends = [0] + [sum(sizes[: n + 1]) for n in range(4)]
    back = lambda n, shape: norms[ends[n] : ends[n + 1]].reshape(shape)
    eight = lambda value: jnp.broadcast_to(value, (8, value.shape[1]))
    new_qkv, new_out, new_up, new_down = scale_weights(
        [back(0, (3, cols)), eight(back(1, (1, cols))), back(2, (2, hid)), eight(back(3, (1, hid)))],
        [qkv_new[3], out_new[3], up_new[3], down_new[3]],
        width,
    )
    sum_qkv, first_a, second_a = qkv_new[:3]
    sum_out, first_b, second_b = out_new[:3]
    sum_up, first_c, second_c = up_new[:3]
    sum_down, first_d, second_d = down_new[:3]
    return (
        hidden,
        input_grad,
        sum_qkv,
        sum_out,
        sum_up,
        sum_down,
        first_a,
        first_b,
        first_c,
        first_d,
        second_a,
        second_b,
        second_c,
        second_d,
        new_qkv,
        new_out,
        new_up,
        new_down,
        sum_sqk,
        sum_attn,
        sum_mlp,
        sum_suv,
    )


def solution(mesh):
    tokens = P("batch", "head")
    wide = P("batch", None, "head")
    tall = P("head", "batch")
    flat = P(("head", "batch"))
    weights = (wide, tall, wide, tall)
    return jax.shard_map(
        per_device,
        mesh=mesh,
        in_specs=(tokens, tokens, P("batch"))
        + weights * 3
        + (P("head"), P(), P(), P(None, "head")),
        out_specs=(tokens, tokens) + weights * 4 + (flat, flat, flat, P(None, ("head", "batch"))),
        check_vma=False,
    )
```

```python
import functools
import math

import jax
import jax.numpy as jnp
from jax import lax
from jax.experimental import pallas as pl
from jax.experimental.pallas import tpu as pltpu
from jax.sharding import PartitionSpec as P

HEAD_DIM = 64
SHORT = 1024

layer_eps = 1e-06
learn_rate = 0.008
beta_one = 0.9
beta_two = 0.95
adam_eps = 1e-08
bias_one = 1.0 - math.exp(100.0 * math.log(0.9))
bias_two = 1.0 - math.exp(100.0 * math.log(0.95))
score_scale = 8.0
LOG2E = math.log2(math.e)
LN2 = math.log(2.0)

bf16 = jnp.bfloat16
f32 = jnp.float32


def dot(a, b):
    return jnp.dot(a, b, preferred_element_type=f32)


def dot_t(a, b):
    return lax.dot_general(a, b, (((1,), (1,)), ((), ())), preferred_element_type=f32)


def t_dot(a, b):
    return lax.dot_general(a, b, (((0,), (0,)), ((), ())), preferred_element_type=f32)


def params(mib):
    return pltpu.CompilerParams(vmem_limit_bytes=mib * 1024 * 1024)


def full_spec(shape):
    return pl.BlockSpec(shape, lambda *_: (0,) * len(shape))


def head_sum(value, ones):
    high = value.astype(bf16)
    low = (value - high.astype(f32)).astype(bf16)
    return dot(high, ones) + dot(low, ones)


def widen(value, cols):
    return jnp.concatenate([value] * (cols // value.shape[1]), axis=1)


def swap_halves(value):
    cols = value.shape[-1]
    half = HEAD_DIM // 2
    lane = lax.broadcasted_iota(jnp.int32, value.shape, 1)
    first = (lane % HEAD_DIM) < half
    up = pltpu.roll(value, cols - half, 1)
    down = pltpu.roll(value, half, 1)
    return jnp.where(first, up, down)


def qkv_kernel(place_ref, *refs, parts):
    tokens = refs[:parts]
    w_ref, cos_ref, sin_ref, gain_ref, ones_ref, x_ref, q_ref, k_ref, v_ref, rho_ref = refs[parts:]
    cols = v_ref.shape[1]
    z = place_ref[0]
    for n in range(parts):
        at = pl.multiple_of(lax.rem(z + parts - n, parts) * cols, cols)
        x_ref[:, pl.ds(at, cols)] = tokens[n][...]
    proj = dot(x_ref[...], w_ref[...])
    cosine = widen(cos_ref[...], cols)
    sine = widen(sin_ref[...], cols)
    ones = ones_ref[...]
    gain = gain_ref[...]
    heads = cols // HEAD_DIM
    lane = lax.broadcasted_iota(jnp.int32, rho_ref.shape, 1)
    stats = jnp.zeros(rho_ref.shape, f32)
    for c, (out, scale) in enumerate(((q_ref, score_scale * LOG2E), (k_ref, 1.0))):
        part = proj[:, c * cols : (c + 1) * cols]
        rho = lax.rsqrt(head_sum(part * part, ones) + layer_eps)
        rot = part * cosine + swap_halves(part) * sine
        out[...] = (rot * rho * (gain * scale)).astype(bf16)
        for h in range(heads):
            stats = jnp.where(lane == c * heads + h, rho[:, h * HEAD_DIM : h * HEAD_DIM + 1], stats)
    rho_ref[...] = stats
    v_ref[...] = proj[:, 2 * cols :].astype(bf16)


def qkv_project(place, tokens, w, cosine, sine, gain, ones):
    rows, cols = tokens[0].shape
    parts = len(tokens)
    width = parts * cols
    blk = 512
    row = lambda n: pl.BlockSpec((blk, n), lambda i, s: (i, 0))
    return pl.pallas_call(
        functools.partial(qkv_kernel, parts=parts),
        grid_spec=pltpu.PrefetchScalarGridSpec(
            num_scalar_prefetch=1,
            grid=(rows // blk,),
            in_specs=[row(cols)] * parts
            + [full_spec((width, 3 * cols)), row(128), row(128)]
            + [full_spec((1, cols)), full_spec((cols, cols))],
            out_specs=[row(width)] + [row(cols)] * 3 + [row(128)],
        ),
        out_shape=[jax.ShapeDtypeStruct((rows, width), bf16)]
        + [jax.ShapeDtypeStruct((rows, cols), bf16)] * 3
        + [jax.ShapeDtypeStruct((rows, 128), f32)],
        compiler_params=params(50),
    )(place, *tokens, w, cosine, sine, gain, ones)


def head_masks(cols, heads):
    lane = lax.broadcasted_iota(jnp.int32, (1, cols), 1) // HEAD_DIM
    return [(lane == h) for h in range(heads)]


def masked(value, mask):
    return jnp.where(mask, value, jnp.zeros_like(value))


def attn_fwd_kernel(long_ref, q_ref, k_ref, v_ref, y_ref, l_ref, acc, mass, *, heads, blk, sub, first):
    i = first + pl.program_id(0)
    cols = q_ref.shape[1]
    masks = head_masks(cols, heads)
    per = SHORT // blk
    low = jnp.where(long_ref[0] != 0, 0, (i // per) * per)
    acc[...] = jnp.zeros_like(acc)
    mass[...] = jnp.zeros_like(mass)

    def lanes(p):
        total = p[:, 0:128]
        for n in range(1, p.shape[1] // 128):
            total = total + p[:, n * 128 : (n + 1) * 128]
        return total

    def body(j, carry):
        start = pl.multiple_of(j * blk, blk)
        keys = k_ref[pl.ds(start, blk), :]
        vals = v_ref[pl.ds(start, blk), :]
        q = q_ref[...]
        total = jnp.zeros(acc.shape, f32)
        for h in range(heads):
            p = jnp.exp2(dot_t(masked(q, masks[h]), keys))
            mass[h] += lanes(p)
            total += dot(p.astype(bf16), masked(vals, masks[h]))
        acc[...] += total
        return carry

    lax.fori_loop(low, i, body, 0)
    start = pl.multiple_of(i * blk, blk)
    causal = lax.broadcasted_iota(jnp.int32, (sub, sub), 0) >= lax.broadcasted_iota(
        jnp.int32, (sub, sub), 1
    )
    for a in range(blk // sub):
        rows = slice(a * sub, (a + 1) * sub)
        q = q_ref[rows, :]
        for b in range(a + 1):
            at = pl.multiple_of(start + b * sub, sub)
            keys = k_ref[pl.ds(at, sub), :]
            vals = v_ref[pl.ds(at, sub), :]
            total = jnp.zeros((sub, cols), f32)
            for h in range(heads):
                p = jnp.exp2(dot_t(masked(q, masks[h]), keys))
                if a == b:
                    p = jnp.where(causal, p, 0.0)
                mass[h, rows, :] += lanes(p)
                total += dot(p.astype(bf16), masked(vals, masks[h]))
            acc[rows, :] += total
    inverse = jnp.zeros(acc.shape, f32)
    logs = jnp.zeros(l_ref.shape, f32)
    lane = lax.broadcasted_iota(jnp.int32, l_ref.shape, 1)
    for h in range(heads):
        column = jnp.sum(mass[h], axis=1, keepdims=True)
        inverse = jnp.where(masks[h], 1.0 / column, inverse)
        logs = jnp.where(lane == h, jnp.log2(column), logs)
    y_ref[...] = (acc[...] * inverse).astype(bf16)
    l_ref[...] = logs


def attn_fwd(is_long, q, k, v, first, count):
    rows, cols = q.shape
    heads = cols // HEAD_DIM
    blk, sub = 512, 256
    row = lambda n: pl.BlockSpec((blk, n), lambda i, s: (i, 0))
    whole = pl.BlockSpec(((first + count) * blk, cols), lambda i, s: (0, 0))
    return pl.pallas_call(
        functools.partial(attn_fwd_kernel, heads=heads, blk=blk, sub=sub, first=first),
        grid_spec=pltpu.PrefetchScalarGridSpec(
            num_scalar_prefetch=1,
            grid=(count,),
            in_specs=[pl.BlockSpec((blk, cols), lambda i, s: (first + i, 0)), whole, whole],
            out_specs=[row(cols), row(128)],
            scratch_shapes=[pltpu.VMEM((blk, cols), f32), pltpu.VMEM((heads, blk, 128), f32)],
        ),
        out_shape=[
            jax.ShapeDtypeStruct((count * blk, cols), bf16),
            jax.ShapeDtypeStruct((count * blk, 128), f32),
        ],
        compiler_params=params(50),
    )(is_long, q, k, v)


def attn_bwd_kernel(
    long_ref, q_ref, qk_ref, dy_ref, y_ref, l_ref, k_ref, v_ref, rho_ref, cos_ref, sin_ref, gain_ref,
    ones_ref, dk_in, dv_in, out_ref, dk_out, dv_out, s_ref, acc, dk_acc, dv_acc, stats, dys, *, heads, blk, sub, first, count
):
    step = pl.program_id(0)
    local = count - 1 - step
    i = first + local
    cols = q_ref.shape[1]
    masks = head_masks(cols, heads)
    per = SHORT // blk
    low = jnp.where(long_ref[0] != 0, 0, (i // per) * per)
    ones = ones_ref[...]
    gain = gain_ref[...]

    @pl.when(step == 0)
    def _():
        dk_acc[...] = jnp.zeros_like(dk_acc)
        dv_acc[...] = jnp.zeros_like(dv_acc)
        s_ref[...] = jnp.zeros_like(s_ref)
        if dk_in is not None:
            dk_acc[...] = dk_in[...]
            dv_acc[...] = dv_in[...]

    acc[...] = jnp.zeros_like(acc)
    dys[...] = dy_ref[...].reshape(dys.shape)
    prod = dys[...].astype(f32) * y_ref[...].astype(f32)
    high = prod.astype(bf16)
    rest = (prod - high.astype(f32)).astype(bf16)
    pickers = (
        lax.broadcasted_iota(jnp.int32, (8, cols), 1) // HEAD_DIM
        == lax.broadcasted_iota(jnp.int32, (8, cols), 0)
    ).astype(bf16)
    stats[0:8, :] = dot_t(pickers, high) + dot_t(pickers, rest)
    stats[8:16, :] = l_ref[...].T[0:8, :]

    def piece(at, size, rows, causal):
        keys = k_ref[pl.ds(at, size), :]
        vals = v_ref[pl.ds(at, size), :]
        q = q_ref[rows, :]
        dy = dys[rows, :]
        total_q = jnp.zeros(q.shape, f32)
        total_k = jnp.zeros(keys.shape, f32)
        total_v = jnp.zeros(keys.shape, f32)
        for h in range(heads):
            qm = masked(q, masks[h])
            dym = masked(dy, masks[h])
            p = jnp.exp2(dot_t(keys, qm) - stats[8 + h : 9 + h, rows])
            if causal is not None:
                p = jnp.where(causal, p, 0.0)
            ds = (p * (dot_t(vals, dym) - stats[h : h + 1, rows])).astype(bf16)
            total_v += dot(p.astype(bf16), dym)
            total_k += dot(ds, qm)
            total_q += t_dot(ds, masked(keys, masks[h]))
        acc[rows, :] += total_q
        dk_acc[pl.ds(at, size), :] += total_k
        dv_acc[pl.ds(at, size), :] += total_v

    def body(j, carry):
        piece(pl.multiple_of(j * blk, blk), blk, slice(0, blk), None)
        return carry

    lax.fori_loop(low, i, body, 0)
    start = pl.multiple_of(i * blk, blk)
    causal = lax.broadcasted_iota(jnp.int32, (sub, sub), 0) <= lax.broadcasted_iota(
        jnp.int32, (sub, sub), 1
    )
    for a in range(blk // sub):
        for b in range(a + 1):
            piece(
                pl.multiple_of(start + b * sub, sub),
                sub,
                slice(a * sub, (a + 1) * sub),
                causal if a == b else None,
            )
    cosine = widen(cos_ref[...], cols)
    sine = widen(sin_ref[...], cols)
    total = jnp.zeros((1, cols), f32)
    here = pl.ds(start, blk)
    for c, (value, unit, up, scale) in enumerate(
        (
            (acc[...], q_ref[...], score_scale, score_scale * LOG2E),
            (dk_acc[here, :], k_ref[here, :], LN2, 1.0),
        )
    ):
        rho = jnp.zeros(value.shape, f32)
        for h in range(heads):
            at = c * heads + h
            rho = jnp.where(masks[h], rho_ref[:, at : at + 1], rho)
        grad = value * up
        unit = unit.astype(f32) * (1.0 / (gain * scale))
        total += jnp.sum(grad * unit, axis=0, keepdims=True)
        grad = grad * gain
        back = rho * (grad - unit * head_sum(grad * unit, ones))
        turned = back * cosine - swap_halves(back) * sine
        out_ref[:, c * cols : (c + 1) * cols] = turned.astype(bf16)
    out_ref[:, 2 * cols :] = dv_acc[here, :].astype(bf16)
    s_ref[0:1, :] += total
    if dk_out is not None:
        @pl.when(step == count - 1)
        def _():
            dk_out[...] = dk_acc[0 : first * blk, :]
            dv_out[...] = dv_acc[0 : first * blk, :]


def attn_bwd(is_long, q, k, v, dy, y, logs, rho, cosine, sine, gain, ones, first, count, carry):
    rows, cols = q.shape
    heads = cols // HEAD_DIM
    blk, sub = 512, 256
    top = (first + count) * blk
    at = lambda s: first + count - 1 - s
    row = lambda n: pl.BlockSpec((blk, n), lambda s, m: (at(s), 0))
    whole = pl.BlockSpec((top, cols), lambda s, m: (0, 0))
    ins = [q, k, dy, y, logs, k, v, rho, cosine, sine, gain, ones]
    mine = lambda n: pl.BlockSpec((blk, n), lambda s, m: (count - 1 - s, 0))
    share = dy.shape[2]
    half_at = 1 if first else 0
    in_specs = [row(cols)] * 2
    in_specs.append(
        pl.BlockSpec((blk // share, None, share, cols), lambda s, m: (count - 1 - s, half_at, 0, 0))
    )
    in_specs += [mine(cols), mine(128), whole, whole] + [row(128)] * 3
    in_specs += [full_spec((1, cols)), full_spec((cols, cols))]
    body = functools.partial(
        attn_bwd_kernel, heads=heads, blk=blk, sub=sub, first=first, count=count
    )
    outs = [jax.ShapeDtypeStruct((count * blk, 3 * cols), bf16)]
    out_specs = [pl.BlockSpec((blk, 3 * cols), lambda s, m: (count - 1 - s, 0))]
    if first:
        outs += [jax.ShapeDtypeStruct((first * blk, cols), f32)] * 2
        out_specs += [full_spec((first * blk, cols))] * 2
        inner = lambda *r: body(*r[:13], None, None, *r[13:])
    else:
        ins += carry
        in_specs += [full_spec((top, cols))] * 2
        inner = lambda *r: body(*r[:16], None, None, *r[16:])
    outs.append(jax.ShapeDtypeStruct((8, cols), f32))
    out_specs.append(full_spec((8, cols)))
    return pl.pallas_call(
        inner,
        grid_spec=pltpu.PrefetchScalarGridSpec(
            num_scalar_prefetch=1,
            grid=(count,),
            in_specs=in_specs,
            out_specs=out_specs,
            scratch_shapes=[
                pltpu.VMEM((blk, cols), f32),
                pltpu.VMEM((top, cols), f32),
                pltpu.VMEM((top, cols), f32),
                pltpu.VMEM((16, blk), f32),
                pltpu.VMEM((blk, cols), bf16),
            ],
        ),
        out_shape=outs,
        compiler_params=params(50),
    )(is_long, *ins)


def row_norm(value):
    return lax.rsqrt(jnp.mean(value * value, axis=1, keepdims=True) + layer_eps)


def norm_back(scale, result, grad):
    return scale * (grad - result * jnp.mean(grad * result, axis=1, keepdims=True))


def pack_kernel(core_ref, up_ref, gain_ref, down_ref, out_ref, mine_ref, theirs_ref):
    half = up_ref.shape[2] // 2
    low = core_ref[0] == 0
    down = down_ref[...].astype(bf16).T
    out = out_ref[...].astype(bf16).T
    for ref, first in ((mine_ref, low), (theirs_ref, jnp.logical_not(low))):
        for c in range(2):
            gain = gain_ref[c : c + 1, :]
            ref[:, c * half : (c + 1) * half] = jnp.where(
                first, up_ref[:, c, :half] * gain[:, :half], up_ref[:, c, half:] * gain[:, half:]
            ).astype(bf16)
        ref[:, 2 * half : 3 * half] = jnp.where(first, down[:, :half], down[:, half:])
        ref[:, 3 * half :] = out


def pack(core, w_up, gain, w_down, w_out):
    span, _, hid = w_up.shape
    cols = w_out.shape[0]
    vmem = pl.BlockSpec(memory_space=pltpu.VMEM)
    return pl.pallas_call(
        pack_kernel,
        in_specs=[pl.BlockSpec(memory_space=pltpu.SMEM)] + [vmem] * 4,
        out_specs=[vmem] * 2,
        out_shape=[jax.ShapeDtypeStruct((span, 3 * hid // 2 + cols), bf16)] * 2,
        compiler_params=params(16),
    )(core, w_up, gain, w_down, w_out)


def place_of(r, chip, chunk):
    return pl.ds(pl.multiple_of((r ^ chip) * chunk, chunk), chunk)


def put_relative(ref, chip, chips, fast):
    if not fast:
        return ref[...]
    if len(ref.shape) == 3:
        return jnp.concatenate([ref[r ^ chip] for r in range(chips)], axis=1)
    chunk = ref.shape[1] // chips
    return jnp.concatenate([ref[:, place_of(r, chip, chunk)] for r in range(chips)], axis=1)


def put_natural(ref, value, chip, chips, fast):
    if not fast:
        ref[...] = value
        return
    chunk = value.shape[1] // chips
    for r in range(chips):
        part = value[:, r * chunk : (r + 1) * chunk]
        if len(ref.shape) == 3:
            ref[r ^ chip] = part
        else:
            ref[:, place_of(r, chip, chunk)] = part


def attn_out_kernel(place_ref, *refs, counts, chips, fast):
    total = sum(counts)
    flat, refs = refs[:total], refs[total:]
    ya_ref, yb_ref, x_ref, alpha_ref, ha_ref, h1_ref, hb_ref, stat_ref, all_ref, half_ref, acc = refs
    z, chip, low = place_ref[0], place_ref[1], place_ref[2] == 0
    parts = len(counts)
    early = pl.program_id(0) == 0
    index = 0
    for n in range(parts):
        at = lax.rem(z + parts - n, parts)
        y = jnp.where(early, ya_ref[at], yb_ref[at])
        hc = y.shape[1] // 2
        all_ref[at] = y
        half_ref[at] = jnp.where(low, y[:, hc:], y[:, :hc])
        column = 0
        for piece in flat[index : index + counts[n]]:
            part = slice(column, column + piece.shape[0])
            if n == 0:
                acc[:, part] = dot_t(y, piece[...])
            else:
                acc[:, part] += dot_t(y, piece[...])
            column += piece.shape[0]
        index += counts[n]
    total = acc[...]
    norm = row_norm(total)
    hidden = total * norm
    start = put_relative(x_ref, chip, chips, fast).astype(f32)
    mixed = start + alpha_ref[...] * (hidden - start)
    first_norm = row_norm(mixed)
    out = mixed * first_norm
    ha_ref[...] = hidden
    h1_ref[...] = out
    hb_ref[...] = out.astype(bf16)
    lane = lax.broadcasted_iota(jnp.int32, stat_ref.shape, 1)
    stat_ref[...] = jnp.where(lane == 0, norm, first_norm)


def own_rows(blk, parts, width, fast):
    if fast:
        return pl.BlockSpec((blk, width), lambda i, s: (i * parts + s[0], 0))
    return pl.BlockSpec((blk, width), lambda i, s: (i, 0))


def out_weights(slots, cols):
    flat = [p for slot in slots for p in slot]
    last = flat[0].shape[1] // cols - 1
    return flat, [pl.BlockSpec((p.shape[0], cols), lambda i, s: (0, last)) for p in flat]


def attn_out(place, ya, yb, slots, x, alpha, chips, fast):
    parts, blk, cols = ya.shape
    width = x.shape[1]
    rows = 2 * blk
    row = lambda n: pl.BlockSpec((blk, n), lambda i, s: (i, 0))
    flat, specs = out_weights(slots, cols)
    return pl.pallas_call(
        functools.partial(attn_out_kernel, counts=[len(t) for t in slots], chips=chips, fast=fast),
        grid_spec=pltpu.PrefetchScalarGridSpec(
            num_scalar_prefetch=1,
            grid=(2,),
            in_specs=specs
            + [full_spec(ya.shape)] * 2
            + [own_rows(blk, parts, width, fast), full_spec((1, width))],
            out_specs=[row(width)] * 3
            + [row(128)]
            + [pl.BlockSpec((parts, blk, n), lambda i, s: (0, i, 0)) for n in (cols, cols // 2)],
            scratch_shapes=[pltpu.VMEM((blk, width), f32)],
        ),
        out_shape=[jax.ShapeDtypeStruct((rows, width), d) for d in (f32, f32, bf16)]
        + [jax.ShapeDtypeStruct((rows, 128), f32)]
        + [jax.ShapeDtypeStruct((parts, rows, n), bf16) for n in (cols, cols // 2)],
        compiler_params=params(50),
    )(place, *flat, ya, yb, x, alpha)


def loss_kernel(place_ref, own_ref, got_ref, h1_ref, cot_ref, alpha_ref, hidden_ref, dmo_ref, base_ref, ga_ref, *, chips, fast):
    chip = place_ref[1]
    total = own_ref[...] + got_ref[...].astype(f32)
    alpha = alpha_ref[...]
    norm = row_norm(total)
    inner = total * norm
    h1 = h1_ref[...]
    mixed = h1 + alpha * (inner - h1)
    last = row_norm(mixed)
    hidden = mixed * last
    grad = norm_back(last, hidden, put_relative(cot_ref, chip, chips, fast).astype(f32))
    put_natural(hidden_ref, hidden.astype(bf16), chip, chips, fast)
    base_ref[...] = (1.0 - alpha) * grad
    dmo_ref[...] = norm_back(norm, inner, alpha * grad).astype(bf16)

    @pl.when(pl.program_id(0) == 0)
    def _():
        ga_ref[...] = jnp.zeros_like(ga_ref)

    ga_ref[0:1, :] += jnp.sum(grad * (inner - h1), axis=0, keepdims=True)


def loss(place, own, got, h1, cot, alpha, chips, fast):
    rows, width = own.shape
    blk = rows // 2
    row = pl.BlockSpec((blk, width), lambda i, s: (i, 0))
    part = row
    if fast:
        part = pl.BlockSpec((chips, blk, width // chips), lambda i, s: (0, i, 0))
    return pl.pallas_call(
        functools.partial(loss_kernel, chips=chips, fast=fast),
        grid_spec=pltpu.PrefetchScalarGridSpec(
            num_scalar_prefetch=1,
            grid=(rows // blk,),
            in_specs=[row] * 3 + [part, full_spec((1, width))],
            out_specs=[part] + [row] * 2 + [full_spec((8, width))],
        ),
        out_shape=[jax.ShapeDtypeStruct(cot.shape, bf16)]
        + [jax.ShapeDtypeStruct((rows, width), d) for d in (bf16, f32)]
        + [jax.ShapeDtypeStruct((8, width), f32)],
        compiler_params=params(50),
    )(place, own, got, h1, cot, alpha)


def first_back_kernel(place_ref, *refs, counts, chips, fast):
    total = sum(counts)
    flat, refs = refs[:total], refs[total:]
    own_ref, got_ref, base_ref, h1_ref, ha_ref, x_ref, stat_ref, alpha_ref = refs[:8]
    do_ref, through_ref, ga_ref, dy_ref = refs[8:]
    z, chip = place_ref[0], place_ref[1]
    alpha = alpha_ref[...]
    grad = base_ref[...] + own_ref[...] + got_ref[...].astype(f32)
    grad = norm_back(stat_ref[:, 1:2], h1_ref[...], grad)
    ha = ha_ref[...]
    put_natural(through_ref, ((1.0 - alpha) * grad).astype(bf16), chip, chips, fast)
    back = norm_back(stat_ref[:, 0:1], ha, alpha * grad).astype(bf16)
    do_ref[...] = back
    parts = len(counts)
    step = pl.program_id(0)
    index = 0
    for n in range(parts):
        at = lax.rem(z + parts - n, parts)
        part = jnp.zeros(dy_ref.shape[1:], f32)
        column = 0
        for piece in flat[index : index + counts[n]]:
            part += dot(back[:, column : column + piece.shape[0]], piece[...])
            column += piece.shape[0]
        index += counts[n]
        dy_ref[at] = part.astype(bf16)

    @pl.when(step == 0)
    def _():
        ga_ref[...] = jnp.zeros_like(ga_ref)

    start = put_relative(x_ref, chip, chips, fast).astype(f32)
    ga_ref[0:1, :] += jnp.sum(grad * (ha - start), axis=0, keepdims=True)


def first_back(place, own, got, base, h1, ha, x, stat, alpha, slots, chips, fast, cols):
    rows, width = own.shape
    parts = len(slots)
    blk = rows // 2
    row = lambda n: pl.BlockSpec((blk, n), lambda i, s: (i, 0))
    flat, specs = out_weights(slots, cols)
    through, shape = row(width), (rows, width)
    if fast:
        through = pl.BlockSpec((parts, blk, cols), lambda i, s: (0, i, 0))
        shape = (parts, rows, cols)
    return pl.pallas_call(
        functools.partial(first_back_kernel, counts=[len(t) for t in slots], chips=chips, fast=fast),
        grid_spec=pltpu.PrefetchScalarGridSpec(
            num_scalar_prefetch=1,
            grid=(2,),
            in_specs=specs
            + [row(width)] * 5
            + [own_rows(blk, parts, width, fast), row(128), full_spec((1, width))],
            out_specs=[row(width), through]
            + [full_spec((8, width)), pl.BlockSpec((parts, blk, cols), lambda i, s: (0, i, 0))],
        ),
        out_shape=[jax.ShapeDtypeStruct((rows, width), bf16), jax.ShapeDtypeStruct(shape, bf16)]
        + [
            jax.ShapeDtypeStruct((8, width), f32),
            jax.ShapeDtypeStruct((parts, rows, cols), bf16),
        ],
        compiler_params=params(50),
    )(place, *flat, own, got, base, h1, ha, x, stat, alpha)


def fetch_weights(q, slots, wbuf, sems):
    def copies(j):
        at = 0
        found = []
        for p, piece in enumerate(slots[j]):
            size = piece.shape[0]
            found.append(
                pltpu.make_async_copy(
                    piece.at[:, : wbuf.shape[2]], wbuf.at[j % 2, at : at + size, :], sems.at[j % 2, p]
                )
            )
            at += size
        return found

    for j in range(len(slots)):

        @pl.when(q == j)
        def _(j=j):
            if j == 0:
                for copy in copies(0):
                    copy.start()
            if j + 1 < len(slots):
                for copy in copies(j + 1):
                    copy.start()
            for copy in copies(j):
                copy.wait()


def mlp_fwd_kernel(*refs, half, counts):
    total = sum(counts)
    flat, refs = refs[:total], refs[total:]
    slots, at = [], 0
    for n in counts:
        slots.append(flat[at : at + n])
        at += n
    ha_ref, hb_ref, act_ref, uv_ref, own_ref, got_ref, acc, wbuf, sems = refs
    rows = ha_ref.shape[0]
    q = pl.program_id(0)

    @pl.when(q == 0)
    def _():
        own_ref[...] = jnp.zeros_like(own_ref)
        acc[...] = jnp.zeros_like(acc)

    fetch_weights(q, slots, wbuf, sems)
    w = wbuf.at[lax.rem(q, 2)]
    for base, h_ref, sum_ref in ((0, ha_ref, own_ref), (rows, hb_ref, acc)):
        at = slice(base, base + rows)
        pair = dot(h_ref[...], w[:, : 2 * half])
        lifted = pair[:, :half]
        gated = pair[:, half:]
        act = (lifted * gated * jax.nn.sigmoid(gated)).astype(bf16)
        uv_ref[at, :] = pair.astype(bf16)
        act_ref[at, :] = act
        sum_ref[...] += dot_t(act, w[:, 2 * half : 3 * half])

    @pl.when(q == pl.num_programs(0) - 1)
    def _():
        got_ref[...] = acc[...].astype(bf16)


def mlp_fwd(ha, hb, slots, half):
    rows, width = ha.shape
    parts = len(slots)
    take = lambda n: pl.BlockSpec((None, 2 * rows, n), lambda q: (q, 0, 0))
    whole = full_spec((rows, width))
    anywhere = pl.BlockSpec(memory_space=pl.ANY)
    flat = [p for slot in slots for p in slot]
    return pl.pallas_call(
        functools.partial(mlp_fwd_kernel, half=half, counts=[len(s) for s in slots]),
        grid=(parts,),
        in_specs=[anywhere] * len(flat)
        + [whole, whole],
        out_specs=[take(half), take(2 * half), whole, whole],
        out_shape=[
            jax.ShapeDtypeStruct((parts, 2 * rows, half), bf16),
            jax.ShapeDtypeStruct((parts, 2 * rows, 2 * half), bf16),
            jax.ShapeDtypeStruct((rows, width), f32),
            jax.ShapeDtypeStruct((rows, width), bf16),
        ],
        scratch_shapes=[
            pltpu.VMEM((rows, width), f32),
            pltpu.VMEM((2, width, 3 * half), bf16),
            pltpu.SemaphoreType.DMA((2, max(len(s) for s in slots))),
        ],
        compiler_params=params(50),
    )(*flat, ha, hb)


def mlp_bwd_kernel(*refs, half, counts):
    total = sum(counts)
    flat, refs = refs[:total], refs[total:]
    slots, at = [], 0
    for n in counts:
        slots.append(flat[at : at + n])
        at += n
    da_ref, db_ref, uv_ref, duv_ref, own_ref, got_ref, gs_ref, acc, wbuf, sems = refs
    rows = da_ref.shape[0]
    q = pl.program_id(0)

    @pl.when(q == 0)
    def _():
        own_ref[...] = jnp.zeros_like(own_ref)
        acc[...] = jnp.zeros_like(acc)

    gs_ref[...] = jnp.zeros_like(gs_ref)
    fetch_weights(q, slots, wbuf, sems)
    w = wbuf.at[lax.rem(q, 2)]
    for base, d_ref, sum_ref in ((0, da_ref, own_ref), (rows, db_ref, acc)):
        at = slice(base, base + rows)
        grad = dot(d_ref[...], w[:, 2 * half : 3 * half])
        lifted = uv_ref[at, :half].astype(f32)
        gated = uv_ref[at, half:].astype(f32)
        sigma = jax.nn.sigmoid(gated)
        da = grad * gated * sigma
        db = grad * lifted * sigma * (1.0 + gated * (1.0 - sigma))
        gs_ref[0:1, :] += jnp.sum(da * lifted, axis=0, keepdims=True)
        gs_ref[1:2, :] += jnp.sum(db * gated, axis=0, keepdims=True)
        duv_ref[at, :half] = da.astype(bf16)
        duv_ref[at, half:] = db.astype(bf16)
        sum_ref[...] += dot_t(duv_ref[at, :], w[:, : 2 * half])

    @pl.when(q == pl.num_programs(0) - 1)
    def _():
        got_ref[...] = acc[...].astype(bf16)


def mlp_bwd(da, db, slots, uv, half):
    rows, width = da.shape
    parts = len(slots)
    take = lambda n: pl.BlockSpec((None, 2 * rows, n), lambda q: (q, 0, 0))
    whole = full_spec((rows, width))
    anywhere = pl.BlockSpec(memory_space=pl.ANY)
    flat = [p for slot in slots for p in slot]
    return pl.pallas_call(
        functools.partial(mlp_bwd_kernel, half=half, counts=[len(s) for s in slots]),
        grid=(parts,),
        in_specs=[anywhere] * len(flat)
        + [
            whole,
            whole,
            take(2 * half),
        ],
        out_specs=[
            take(2 * half),
            whole,
            whole,
            pl.BlockSpec((None, 8, half), lambda q: (q, 0, 0)),
        ],
        out_shape=[
            jax.ShapeDtypeStruct((parts, 2 * rows, 2 * half), bf16),
            jax.ShapeDtypeStruct((rows, width), f32),
            jax.ShapeDtypeStruct((rows, width), bf16),
            jax.ShapeDtypeStruct((parts, 8, half), f32),
        ],
        scratch_shapes=[
            pltpu.VMEM((rows, width), f32),
            pltpu.VMEM((2, width, 3 * half), bf16),
            pltpu.SemaphoreType.DMA((2, max(len(s) for s in slots))),
        ],
        compiler_params=params(50),
    )(*flat, da, db, uv)


EXTRA = 16


def grad_kernel(place_ref, *refs, orders, parts, chunk, more):
    ha_ref, hb_ref = refs[:2]
    refs = refs[2:]
    if more:
        oa_ref, ob_ref, ya_ref, yb_ref, gs_ref, g1_ref, g2_ref = refs[:7]
        refs = refs[7:]
    val_ref, *outs = refs[:5]
    turned = refs[5]
    rows = ha_ref.shape[0]
    k = pl.program_id(0)

    @pl.when(k == 0)
    def _():
        turned[:, :rows] = ha_ref[...].T
        turned[:, rows:] = hb_ref[...].T
        if more:
            refs[6][:, :rows] = oa_ref[...].T
            refs[6][:, rows:] = ob_ref[...].T

    if more:
        size = outs[0].shape[2]
        fill = lambda row: jnp.concatenate([row, jnp.zeros((1, size - row.shape[1]), f32)], axis=1)
        line = lax.broadcasted_iota(jnp.int32, (EXTRA, size), 0)
        units = fill(jnp.concatenate([gs_ref[0:1, :], gs_ref[1:2, :]], axis=1))
        steps = fill(jnp.concatenate([g1_ref[0:1, :], g2_ref[0:1, :]], axis=1))
        extra = jnp.where(line == 0, units, jnp.where(line == 1, steps, 0.0)).astype(bf16)

    for side in range(2):

        @pl.when((k < parts // 2) == (side == 0))
        def _(side=side):
            for which, ref in zip(orders[side], outs[2 * side : 2 * side + 2]):
                for j, r in enumerate(which):
                    at = slice(r * chunk, (r + 1) * chunk)
                    value = dot(turned[at, :], val_ref[...]).astype(bf16)
                    size = value.shape[1]
                    ref[j, :chunk, :size] = value
                    if more:
                        ref[j, :chunk, size:] = (
                            dot(refs[6][at, :rows], ya_ref[...]) + dot(refs[6][at, rows:], yb_ref[...])
                        ).astype(bf16)
                        ref[j, chunk:, :] = extra


def weight_grads(place, sends, keeps, chips, hs, value, os=None, ys=None, extra=None):
    rows, width = hs[0].shape
    chunk = width // chips
    parts, _, size = value.shape
    more = os is not None
    hc = ys[1].shape[2] if more else 0
    tall = chunk + (EXTRA if more else 0)
    middle = parts // 2
    if chunk % 128:
        result = []
        for which, lo in ((sends[0], 0), (keeps[0], 0), (sends[1], middle), (keeps[1], middle)):
            cut = lambda pair: jnp.concatenate(
                [jnp.concatenate(pair, axis=0)[:, r * chunk : (r + 1) * chunk] for r in which], axis=1
            )
            found = []
            for k in range(lo, lo + middle):
                one = t_dot(cut(hs), value[k])
                if more:
                    at = (place[0] - k) % parts
                    y = lax.dynamic_index_in_dim(ys[0], at, 0, keepdims=False)
                    y = lax.dynamic_slice_in_dim(y, place[2] * hc, hc, 1)
                    y = jnp.concatenate([y, lax.dynamic_index_in_dim(ys[1], at, 0, keepdims=False)])
                    one = jnp.concatenate([one, t_dot(cut(os), y)], axis=1)
                one = one.reshape(len(which), chunk, size + hc)
                if more:
                    wide = jnp.broadcast_to(extra[k][None], (len(which), EXTRA, size + hc))
                    one = jnp.concatenate([one, wide], axis=1)
                found.append(one.astype(bf16))
            result.append(jnp.stack(found, axis=1))
        return [result[0], result[2]], [result[1], result[3]]
    whole = full_spec((rows, width))
    ins = list(hs)
    in_specs = [whole] * 2
    scratch = [pltpu.VMEM((width, 2 * rows), bf16)]
    if more:
        slot = lambda k, p: lax.rem(p[0] + parts - k, parts)
        cols = ys[0].shape[2]
        part = pl.BlockSpec((8, cols), lambda k, p: (0, slot(k, p) ^ p[1]))
        ins += [*os, ys[0], ys[1], *extra]
        in_specs += [whole] * 2
        in_specs += [
            pl.BlockSpec((None, rows, hc), lambda k, p: (slot(k, p), 0, p[2])),
            pl.BlockSpec((None, rows, hc), lambda k, p: (slot(k, p), 0, 0)),
            pl.BlockSpec((None, 8, size // 2), lambda k, p: (k, 0, 0)),
            part,
            part,
        ]
        scratch = scratch * 2
    ins.append(value)
    in_specs.append(pl.BlockSpec((None, 2 * rows, size), lambda k, p: (k, 0, 0)))
    lists = [sends[0], keeps[0], sends[1], keeps[1]]
    block = lambda one: (len(one), None, tall, size + hc)
    early = lambda k, p: (0, jnp.minimum(k, middle - 1), 0, 0)
    late = lambda k, p: (0, jnp.maximum(k - middle, 0), 0, 0)
    out = pl.pallas_call(
        functools.partial(
            grad_kernel, orders=(lists[:2], lists[2:]), parts=parts, chunk=chunk, more=more
        ),
        grid_spec=pltpu.PrefetchScalarGridSpec(
            num_scalar_prefetch=1,
            grid=(parts,),
            in_specs=in_specs,
            out_specs=[
                pl.BlockSpec(block(one), early if n < 2 else late) for n, one in enumerate(lists)
            ],
            scratch_shapes=scratch,
        ),
        out_shape=[
            jax.ShapeDtypeStruct((len(one), middle, tall, size + hc), bf16) for one in lists
        ],
        compiler_params=params(50),
    )(place, *ins)
    return [out[0], out[2]], [out[1], out[3]]


def pair_sum_kernel(ka_ref, ga_ref, kb_ref, gb_ref, a_ref, b_ref):
    a_ref[...] = (ka_ref[...].astype(f32) + ga_ref[...].astype(f32)).astype(bf16)
    b_ref[...] = (kb_ref[...].astype(f32) + gb_ref[...].astype(f32)).astype(bf16)


def pair_sums(kept, got, at):
    _, slots, tall, wide = kept[0].shape
    spec = lambda n: pl.BlockSpec((None, None, tall, wide), lambda k, n=n: (n, k, 0, 0))
    return pl.pallas_call(
        pair_sum_kernel,
        grid=(slots,),
        in_specs=[spec(at[0]), spec(at[0]), spec(at[1]), spec(at[1])],
        out_specs=[spec(0)] * 2,
        out_shape=[jax.ShapeDtypeStruct((1, slots, tall, wide), bf16)] * 2,
        compiler_params=params(50),
    )(kept[0], got[0], kept[1], got[1])


def adam_values(weight, grad, first, second):
    first_new = beta_one * first + (1.0 - beta_one) * grad
    second_new = beta_two * second + (1.0 - beta_two) * grad * grad
    moved = weight - learn_rate * (first_new / bias_one) / (
        jnp.sqrt(second_new / bias_two) + adam_eps
    )
    return first_new, second_new, moved


def lane_sums(value):
    ones = jnp.ones((8, value.shape[1]), bf16)
    high = value.astype(bf16)
    low = (value - high.astype(f32)).astype(bf16)
    return dot_t(ones, high) + dot_t(ones, low)


def adam_wide_kernel(w_ref, g_ref, m_ref, v_ref, g_out, m_out, v_out, n_out, s_out):
    cols = w_ref.shape[2]
    for c in range(w_ref.shape[1]):
        grad = g_ref[:, c * cols : (c + 1) * cols]
        first, second, moved = adam_values(w_ref[:, c, :], grad, m_ref[:, c, :], v_ref[:, c, :])
        g_out[:, c, :] = grad
        m_out[:, c, :] = first
        v_out[:, c, :] = second
        n_out[:, c, :] = moved
        s_out[c : c + 1, :] = jnp.sum(moved * moved, axis=0, keepdims=True)


def adam_wide(w, g, m, v):
    vmem = pl.BlockSpec(memory_space=pltpu.VMEM)
    return pl.pallas_call(
        adam_wide_kernel,
        in_specs=[vmem] * 4,
        out_specs=[vmem] * 5,
        out_shape=[jax.ShapeDtypeStruct(w.shape, f32)] * 4
        + [jax.ShapeDtypeStruct(w.shape[1:], f32)],
        compiler_params=params(16),
    )(w, g, m, v)


def adam_tall_kernel(w_ref, g_ref, m_ref, v_ref, g_out, m_out, v_out, n_out, s_out):
    grad = g_ref[...].T
    first, second, moved = adam_values(w_ref[...], grad, m_ref[...], v_ref[...])
    g_out[...] = grad
    m_out[...] = first
    v_out[...] = second
    n_out[...] = moved
    s_out[...] = lane_sums(moved * moved)


def adam_tall(w, g, m, v):
    vmem = pl.BlockSpec(memory_space=pltpu.VMEM)
    return pl.pallas_call(
        adam_tall_kernel,
        in_specs=[vmem] * 4,
        out_specs=[vmem] * 5,
        out_shape=[jax.ShapeDtypeStruct(w.shape, f32)] * 4
        + [jax.ShapeDtypeStruct((8, w.shape[0]), f32)],
        compiler_params=params(16),
    )(w, g, m, v)


def scale_kernel(na_ref, nb_ref, nc_ref, nd_ref, a_ref, b_ref, c_ref, d_ref, ao_ref, bo_ref, co_ref, do_ref, *, width):
    factor = lambda value: lax.rsqrt(value / width + layer_eps)
    for norm, ref, out in ((na_ref, a_ref, ao_ref), (nc_ref, c_ref, co_ref)):
        for c in range(ref.shape[1]):
            out[:, c, :] = ref[:, c, :] * factor(norm[c : c + 1, :])
    for norm, ref, out in ((nb_ref, b_ref, bo_ref), (nd_ref, d_ref, do_ref)):
        out[...] = ref[...] * factor(norm[...]).T[:, 0:1]


def scale_weights(norms, weights, width):
    vmem = pl.BlockSpec(memory_space=pltpu.VMEM)
    return pl.pallas_call(
        functools.partial(scale_kernel, width=width),
        in_specs=[vmem] * 8,
        out_specs=[vmem] * 4,
        out_shape=[jax.ShapeDtypeStruct(w.shape, f32) for w in weights],
        compiler_params=params(16),
    )(*norms, *weights)


def after(value, *others):
    return lax.optimization_barrier((value, *others))[0]


def per_device(
    layer_input,
    cotangent,
    positions,
    w_qkv,
    w_out,
    w_up,
    w_down,
    moment_qkv,
    moment_out,
    moment_up,
    moment_down,
    square_qkv,
    square_out,
    square_up,
    square_down,
    s_qk,
    alpha_attn,
    alpha_mlp,
    s_uv,
):
    nz = lax.axis_size("head")
    nb = lax.axis_size("batch")
    z = lax.axis_index("head")
    b = lax.axis_index("batch")
    core = b % 2
    chip = b // 2
    chips = nb // 2
    bits = [1 << n for n in range(int(math.log2(chips)))]
    rows, cols = layer_input.shape
    width = cols * nz
    own = rows // nz
    hid = w_down.shape[0]
    half = hid // 2
    hc = cols // 2
    heads = cols // HEAD_DIM
    span = w_qkv.shape[0]
    chunk = width // chips
    core_s = core.reshape(1).astype(jnp.int32)
    place = jnp.stack([z, chip, core]).astype(jnp.int32)
    fast = chunk == cols and chunk % 128 == 0

    def swap_batch(value, bit):
        return lax.ppermute(value, "batch", [(i, i ^ bit) for i in range(nb)])

    def swap_core(value):
        return swap_batch(value, 1)

    def swap_chip(value, bit):
        return swap_batch(value, 2 * bit)

    def onward(value, k=1):
        return lax.ppermute(value, "head", [(i, (i + k) % nz) for i in range(nz)])

    def exchange(value):
        return lax.all_to_all(value, "head", split_axis=0, concat_axis=0)

    def pick(pair, index):
        return jnp.where(index == 0, pair[0], pair[1])

    def relative(value):
        return jnp.concatenate(
            [
                lax.dynamic_slice_in_dim(value, (chip ^ r) * chunk, chunk, value.ndim - 1)
                for r in range(chips)
            ],
            axis=-1,
        )

    def spread(value):
        if chips <= 4:
            return [value] + [swap_chip(value, r) for r in range(1, chips)]
        for bit in bits:
            value = jnp.concatenate([value, swap_chip(value, bit)], axis=0)
        return [value]

    tokens = [layer_input, onward(layer_input)]
    mine, theirs = pack(core_s, w_up, s_uv, w_down, w_out)
    qkv_own = after(w_qkv, mine).reshape(span, 3 * cols).astype(bf16)
    qkv_full = lax.all_gather(qkv_own, "batch", axis=0, tiled=True)
    theirs = swap_core(theirs)
    packet = jnp.concatenate([pick((mine, theirs), core), pick((theirs, mine), core)], axis=0)
    hops = [packet, onward(packet)]
    slots = [spread(packet)]
    tokens[1], hops[1], places, alpha_attn, alpha_mlp, *last = lax.optimization_barrier(
        (tokens[1], hops[1], positions, alpha_attn, alpha_mlp, *slots[0])
    )
    slots[0] = list(last)

    freqs = jnp.exp(
        (jnp.arange(128) % (HEAD_DIM // 2)).astype(f32) * (-2.0 * math.log(10000.0) / HEAD_DIM)
    )
    phase = places.astype(f32)[:, None] * freqs[None, :]
    side = jnp.where(jnp.arange(128) % HEAD_DIM < HEAD_DIM // 2, -1.0, 1.0).astype(f32)
    cosine, sine = jnp.cos(phase), jnp.sin(phase) * side[None, :]
    lane = jnp.arange(cols) // HEAD_DIM
    ones = (lane[:, None] == lane[None, :]).astype(bf16)
    gain = s_qk.reshape(1, cols)
    is_long = (places[SHORT : SHORT + 1] != 0).astype(jnp.int32)
    attn_gain = relative(alpha_attn[None])
    mlp_gain = relative(alpha_mlp[None])

    for n in range(2, nz):
        slots.append(spread(hops[-1]))
        tokens.append(onward(tokens[-1]))
        if n < nz - 1:
            hops.append(onward(hops[-1]))
            tokens[-1], hops[-1], cosine, sine, ones, attn_gain, mlp_gain, *last = (
                lax.optimization_barrier(
                    (tokens[-1], hops[-1], cosine, sine, ones, attn_gain, mlp_gain, *slots[-1])
                )
            )
            slots[-1] = list(last)
    last_hop, tokens[-1] = lax.optimization_barrier((hops[-1], tokens[-1]))
    hops.append(onward(last_hop))

    blocks = rows // 512
    middle = blocks // 2
    tokens_full, q, k, v, rho = qkv_project(place, tokens, qkv_full, cosine, sine, gain, ones)
    y_a, logs_a = attn_fwd(is_long, q, k, v, 0, middle)
    q_b, hops[-1], *last = lax.optimization_barrier((after(q, y_a), hops[-1], *slots[-1]))
    slots[-1] = list(last)
    slots.append(spread(hops[-1]))
    y_b, logs_b = attn_fwd(is_long, q_b, k, v, middle, blocks - middle)
    y_one = exchange(y_a.reshape(nz, own // 2, cols))
    y_in, y_one = lax.optimization_barrier((y_b, y_one))
    y_two = exchange(y_in.reshape(nz, own // 2, cols))
    flat = lambda value: value.transpose(1, 0, 2).reshape(own, width)
    start = tokens_full
    if not fast:
        start = jnp.concatenate(
            [
                lax.dynamic_slice_in_dim(tokens_full, h * (rows // 2) + z * (own // 2), own // 2, 0)
                for h in range(2)
            ]
        )
        start = relative(start)
    y_one, y_two, *last = lax.optimization_barrier((y_one, y_two, *slots[-1]))
    slots[-1] = list(last)
    hA, h1, h_own, stat, y_mine, y_other = attn_out(place, y_one, y_two, slots, start, attn_gain, chips, fast)
    h_got = swap_core(h_own)
    y_got = swap_core(y_other)
    h_got, y_got = lax.optimization_barrier((h_got, y_got))
    cot = after(cotangent, h_own).reshape(2, nz, own // 2, cols).transpose(1, 0, 2, 3)
    cot = exchange(cot.reshape(nz, own, cols))

    act, uv, mo_own, mo_other = mlp_fwd(h_own, h_got, slots, half)
    mo_got = swap_core(mo_other)
    if not fast:
        cot = relative(flat(cot))
    hidden, d_own, base, ga_mlp = loss(place, mo_own, mo_got, h1, cot, mlp_gain, chips, fast)
    d_got = swap_core(d_own)
    if not fast:
        hidden = relative(hidden).reshape(own, nz, cols).transpose(1, 0, 2)
    hidden = exchange(hidden)

    orders = [bits, bits[::-1]]
    sent_at = [[r for r in range(chips) if r & order[0]] for order in orders]
    kept_at = [[r for r in range(chips) if not r & order[0]] for order in orders]

    def second(kept, sent):
        found, sends = [], []
        if chips == 4:
            at = [[n for n, r in enumerate(left) if r & order[1]] for order, left in zip(orders, kept_at)]
            sends = pair_sums(kept, sent, [one[0] for one in at])
            for order, one, keep, got, send in zip(orders, at, kept, sent, sends):
                cut = lambda t, n=1 - one[0]: t[n : n + 1]
                found.append([cut(keep), cut(got), swap_chip(send, order[1])])
            return found, sends
        for order, left, got, keep in zip(orders, kept_at, sent, kept):
            terms = [keep, got]
            for bit in order[1:]:
                send_at = [n for n, r in enumerate(left) if r & bit]
                keep_at = [n for n, r in enumerate(left) if not r & bit]
                left = [left[n] for n in keep_at]
                cut = lambda v, at: jnp.concatenate([v[n : n + 1] for n in at], axis=0)
                send = sum(cut(t, send_at).astype(f32) for t in terms).astype(bf16)
                terms = [cut(t, keep_at) for t in terms] + [swap_chip(send, bit)]
                sends.append(send)
            found.append(terms)
        return found, sends

    def slot_sums(found):
        return [sum(t[0, n].astype(f32) for t in terms) for terms in found for n in range(nz // 2)]

    def wait_last(found, *others):
        return [terms[:-1] + [after(terms[-1], *others)] for terms in found]

    down_made, down_kept = weight_grads(place, sent_at, kept_at, chips, (d_own, d_got), act)
    down_sent = [swap_chip(one, order[0]) for one, order in zip(down_made, orders)]
    d_own, d_got, *_ = lax.optimization_barrier((d_own, d_got, *down_made))
    duv, dh_own, dh_other, gsuv = mlp_bwd(d_own, d_got, slots, uv, half)
    dh_got = swap_core(dh_other)
    down_sent = [after(one, dh_other) for one in down_sent]
    down_part, down_next = second(down_kept, down_sent)
    dh_own, hidden, *_ = lax.optimization_barrier((dh_own, hidden, *down_next))
    do_own, through, ga_attn, dy = first_back(
        place, dh_own, dh_got, base, h1, hA, start, stat, attn_gain, slots, chips, fast, cols
    )
    dy = exchange(dy)
    do_got = swap_core(do_own)

    extra = (gsuv, ga_attn, ga_mlp)
    if not fast:
        alphas = [relative(ga_attn[0:1]), relative(ga_mlp[0:1])]
        extra = []
        wide = 2 * half + hc
        fill = lambda r: jnp.pad(r, ((0, 0), (0, wide - r.shape[1])))
        for n in range(nz):
            at = ((z - n) % nz) * cols
            line = [lax.dynamic_slice_in_dim(g, at, cols, 1) for g in alphas]
            lines = [gsuv[n, :2].reshape(1, 2 * half), jnp.concatenate(line, axis=1)]
            lines = jnp.concatenate([fill(r) for r in lines])
            extra.append(jnp.pad(lines, ((0, EXTRA - 2), (0, 0))))
        extra = jnp.stack(extra)
    up_made, up_kept = weight_grads(
        place, sent_at, kept_at, chips, (h_own, h_got), duv, (do_own, do_got), (y_mine, y_got), extra
    )
    down_part = wait_last(down_part, *up_kept)
    down_last = [terms[-1] for terms in down_part]
    dy, *both = lax.optimization_barrier((dy, *up_made, *down_last))
    up_made, down_last = both[: len(up_made)], both[len(up_made) :]
    down_slots = slot_sums([t[:-1] + [last] for t, last in zip(down_part, down_last)])
    down_along = [onward(down_slots[n].astype(bf16), nz - n) for n in range(1, nz)]
    up_sent = [swap_chip(one, order[0]) for one, order in zip(up_made, orders)]

    dy = dy.reshape(nz, 2, own // 2, cols)
    common = lambda y, logs: (
        is_long, q, k, v, dy, y, logs, rho, cosine, sine, gain, ones
    )
    dqkv_b, dk_part, dv_part, sqk_b = attn_bwd(
        *common(y_b, logs_b), middle, blocks - middle, None
    )

    if not fast:
        through = relative(through).reshape(own, nz, cols).transpose(1, 0, 2)
    mine_at = z * (own // 2)
    qkv_parts = qkv_full.reshape(nz, cols, 3 * cols)

    def input_part(dqkv, side):
        part = jnp.einsum("tn,zcn->ztc", dqkv, qkv_parts, preferred_element_type=f32).astype(bf16)
        here = lax.dynamic_slice_in_dim(part, mine_at, own // 2, 1).astype(f32)
        more = after(through, dqkv)[:, side * (own // 2) : (side + 1) * (own // 2)]
        return lax.dynamic_update_slice_in_dim(part, (here + more.astype(f32)).astype(bf16), mine_at, 1)

    part_b = input_part(dqkv_b, 1)
    down_along = [after(one, dqkv_b) for one in down_along]
    part_got = exchange(part_b)
    dk_part, *_ = lax.optimization_barrier((dk_part, part_b, *down_along))
    dqkv_a, sqk_a = attn_bwd(*common(y_a, logs_a), 0, middle, [dk_part, dv_part])
    input_b = jnp.sum(after(part_got, dqkv_a).astype(f32), axis=0)
    up_part, up_next = second(up_kept, [after(one, dqkv_a) for one in up_sent])
    dqkv_a, *_ = lax.optimization_barrier((dqkv_a, *up_next))
    part_a = input_part(dqkv_a, 0)
    dqkv = jnp.concatenate([dqkv_a, dqkv_b], axis=0)
    grad_qkv = t_dot(tokens_full, dqkv).astype(bf16)
    up_part = wait_last(up_part, part_a, grad_qkv, *[terms[-1] for terms in up_part])
    up_slots = slot_sums(up_part)
    passed = up_slots[1].astype(bf16)
    part_a, grad_qkv, passed = lax.optimization_barrier((part_a, grad_qkv, passed))
    passed = onward(passed)
    for n in range(2, nz):
        if n == nz - 1:
            passed, part_a = lax.optimization_barrier((passed, part_a))
        passed = onward((up_slots[n] + passed.astype(f32)).astype(bf16))
    sum_up_t = up_slots[0] + passed.astype(f32)
    input_a = lax.psum_scatter(part_a.reshape(-1, cols), "head", scatter_dimension=0, tiled=True)
    input_grad = jnp.concatenate([input_a.astype(f32), input_b], axis=0)
    hidden_t = after(hidden, part_a).reshape(nz, 2, own // 2, cols).transpose(1, 0, 2, 3).reshape(rows, cols)

    sqk = jnp.pad((sqk_a + sqk_b), ((0, EXTRA - 8), (0, 2 * cols)))
    shard = [lax.dynamic_slice_in_dim(grad_qkv, (b ^ r) * span, span, 0) for r in range(nb)]
    shard = [jnp.concatenate([s, sqk.astype(bf16)], axis=0) for s in shard]
    qbits = [1 << n for n in range(int(math.log2(nb)))]
    held = {r: shard[r] for r in range(nb)}
    for bit in qbits:
        send_at = [r for r in held if r & bit]
        send = jnp.concatenate([held[r] for r in send_at], axis=0).astype(bf16)
        got = swap_batch(send, bit)
        size = span + EXTRA
        held = {
            r ^ bit: held[r ^ bit].astype(f32) + got[n * size : (n + 1) * size].astype(f32)
            for n, r in enumerate(send_at)
        }
    cell = width // (nz * nb)
    sum_sqk = lax.dynamic_slice_in_dim(held[0][span, :cols], b * cell, cell, 0)
    w_late, m_late, v_late, _ = lax.optimization_barrier((w_qkv, moment_qkv, square_qkv, part_a))
    qkv_new = adam_wide(w_late, held[0][:span], m_late, v_late)

    def both_halves(total):
        two = (total[:span], total[span : 2 * span])
        here = jnp.concatenate([pick(two, core), total[2 * span :]], axis=0)
        there = jnp.concatenate([pick(two, 1 - core), total[2 * span :]], axis=0)
        there = swap_core(there.astype(bf16)).astype(f32)
        return [pick((here, there), core), pick((there, here), core)]

    join = lambda halves, at, size: [p[:span, at : at + size] for p in halves]
    down_along = [after(one, part_a) for one in down_along]
    halves = both_halves(down_slots[0] + sum(one.astype(f32) for one in down_along))
    down_new = adam_tall(w_down, jnp.concatenate(join(halves, 0, half), axis=1), moment_down, square_down)
    halves = both_halves(sum_up_t)
    grad_up = jnp.concatenate(join(halves, 0, half) + join(halves, half, half), axis=1)
    grad_up = grad_up * s_uv.reshape(1, 2 * hid)
    up_new = adam_wide(w_up, grad_up, moment_up, square_up)
    out_new = adam_tall(w_out, jnp.concatenate(join(halves, 2 * half, hc), axis=1), moment_out, square_out)
    suv_rows = jnp.stack(
        [jnp.concatenate([p[span, c * half : (c + 1) * half] for p in halves]) for c in range(2)]
    )
    suv_rows = suv_rows / s_uv
    sum_suv = lax.dynamic_slice_in_dim(suv_rows, b * (hid // nb), hid // nb, 1)
    alphas = halves[0][span + 1] + halves[1][span + 1]
    sum_attn = lax.dynamic_slice_in_dim(alphas[:cols], b * cell, cell, 0)
    sum_mlp = lax.dynamic_slice_in_dim(alphas[cols : 2 * cols], b * cell, cell, 0)

    hidden = hidden_t.astype(f32)

    squares = [qkv_new[4], out_new[4][:1], up_new[4], down_new[4][:1]]
    sizes = [t.size for t in squares]
    norms = jnp.concatenate([t.reshape(-1) for t in squares]).reshape(-1, 128)
    for bit in qbits:
        norms = norms + swap_batch(norms, bit)
    norms = norms.reshape(-1)
    ends = [0] + [sum(sizes[: n + 1]) for n in range(4)]
    back = lambda n, shape: norms[ends[n] : ends[n + 1]].reshape(shape)
    eight = lambda value: jnp.broadcast_to(value, (8, value.shape[1]))
    new_qkv, new_out, new_up, new_down = scale_weights(
        [back(0, (3, cols)), eight(back(1, (1, cols))), back(2, (2, hid)), eight(back(3, (1, hid)))],
        [qkv_new[3], out_new[3], up_new[3], down_new[3]],
        width,
    )
    sum_qkv, first_a, second_a = qkv_new[:3]
    sum_out, first_b, second_b = out_new[:3]
    sum_up, first_c, second_c = up_new[:3]
    sum_down, first_d, second_d = down_new[:3]
    return (
        hidden,
        input_grad,
        sum_qkv,
        sum_out,
        sum_up,
        sum_down,
        first_a,
        first_b,
        first_c,
        first_d,
        second_a,
        second_b,
        second_c,
        second_d,
        new_qkv,
        new_out,
        new_up,
        new_down,
        sum_sqk,
        sum_attn,
        sum_mlp,
        sum_suv,
    )


def solution(mesh):
    tokens = P("batch", "head")
    wide = P("batch", None, "head")
    tall = P("head", "batch")
    flat = P(("head", "batch"))
    weights = (wide, tall, wide, tall)
    return jax.shard_map(
        per_device,
        mesh=mesh,
        in_specs=(tokens, tokens, P("batch"))
        + weights * 3
        + (P("head"), P(), P(), P(None, "head")),
        out_specs=(tokens, tokens) + weights * 4 + (flat, flat, flat, P(None, ("head", "batch"))),
        check_vma=False,
    )
```
